32 devices in a mesh: sector: 4 (over y, x), dom: 8 (over z, core).
Axes of the slice: x: 2, y: 2, z: 4, core: 2. Of those that a mesh axis runs over, the one named last changes fastest.
Arguments:
- strain_map: float32 [36, 8192], P(None, ('sector', 'dom')), may hold values from -1.75 to 1.75
- corner_nodes: int32 [4, 8192], P(None, ('sector', 'dom')), may hold values from 0 to 4095, as said below
- counts: int32 [32], P(('sector', 'dom')), may hold values from 64 to 256, as said below
- seam_nodes: int32 [4, 2048], P('sector'), may hold values from 0 to 2047
- velocity: float32 [3, 8192], P(None, ('sector', 'dom')), may hold values from -6 to 6
- dual_state: float32 [3, 8192], P(None, ('sector', 'dom')), may hold values from -6 to 6
- nodal_load: float32 [3, 8192], P(None, ('sector', 'dom')), may hold values from -6 to 6
- mobility: float32 [8192], P(('sector', 'dom')), may hold values from 0.1 to 0.5
- past_dual: float32 [8, 3, 8192], P(None, None, ('sector', 'dom')), may hold values from -6 to 6
- past_dual_gap: float32 [8, 3, 8192], P(None, None, ('sector', 'dom')), may hold values from -12 to 12
- past_velocity: float32 [8, 3, 8192], P(None, None, ('sector', 'dom')), may hold values from -6 to 6
- past_velocity_gap: float32 [8, 3, 8192], P(None, None, ('sector', 'dom')), may hold values from -12 to 12
Outputs:
- new_velocity: float32 [3, 8192], P(None, ('sector', 'dom'))
- new_dual: float32 [3, 8192], P(None, ('sector', 'dom'))
The draws below stay inside these ranges and needn't reach their ends.
Inputs may be any that keep to these rules, and one draw needn't show every extreme that they name: `counts`: each block has between 64 and 256 live elements; some block is full and some has exactly the least. `corner_nodes`: an element of block d of a sector (d = its slot's block index along dom) names either a seam position (2048 and up) or a node from d * 256 - 32 to (d + 1) * 256 + 31, within 0 to 2047; both ends of that range are named in every draw where they exist.
All inputs are finite; a program needn't handle non-finite values.
Results may differ from the reference program's by a relative error of at most 0.0003.
Values sent between devices are 32-bit elements; how exact they have to be, the bound alone decides.
No kernel may reach another device: no remote copies, remote signals or barrier semaphores. Data moves between devices by JAX's collectives and lax.ppermute only.
A program may use at most 64 MiB of HBM per device.

```python
import math
import jax
import jax.numpy as jnp
from jax import lax

E_DEV = 256
SEAM = 2048
ITERS = 2
DEPTH = 8
BAND = 32
SECTORS = 4
BLOCKS = 32
ESEC = 2048
NODES_SEC = 2048
NREF = 4096
ELEMS = 8192
NODES = 8192


def regional_gap(key, columns):
    first = jax.random.fold_in(key, 0)
    base = jax.random.normal(first, (DEPTH, 3, columns), jnp.float32)
    base = jnp.clip(base, -6.0, 6.0)
    position = jnp.arange(columns, dtype=jnp.float32)[None, None, :] / columns
    position = position + jnp.arange(DEPTH, dtype=jnp.float32)[:, None, None] / DEPTH
    fraction = jnp.mod(position, 1.0)
    return 0.2 * jnp.power(10.0, fraction) * base


def draw_past_dual_gap(key, part):
    return regional_gap(jax.random.fold_in(key, 11), ELEMS)


def draw_past_velocity_gap(key, part):
    return regional_gap(jax.random.fold_in(key, 23), NODES)


def draw_counts(key, part):
    first, second = jax.random.split(jax.random.fold_in(key, 37))
    values = jax.random.randint(first, (BLOCKS,), E_DEV // 4, E_DEV + 1, dtype=jnp.int32)
    order = jax.random.permutation(second, BLOCKS)
    values = values.at[order[0]].set(E_DEV)
    values = values.at[order[1]].set(E_DEV // 4)
    return values.astype(jnp.int32)


def draw_corner_nodes(key, part):
    keys = jax.random.split(jax.random.fold_in(key, 53), 4)
    elem_index = jnp.arange(ELEMS, dtype=jnp.int32)
    blocks_sec = ESEC // E_DEV
    block_pos = elem_index // E_DEV % blocks_sec
    slot = elem_index % E_DEV
    kind = jax.random.randint(keys[0], (4, ELEMS), 0, 20, dtype=jnp.int32)
    own = block_pos[None, :] * E_DEV + jax.random.randint(keys[1], (4, ELEMS), 0, E_DEV, dtype=jnp.int32)
    offset = jax.random.randint(keys[2], (4, ELEMS), 0, BAND, dtype=jnp.int32)
    left = block_pos[None, :] * E_DEV - 1 - offset
    right = (block_pos[None, :] + 1) * E_DEV + offset
    seam = NODES_SEC + jax.random.randint(keys[3], (4, ELEMS), 0, SEAM, dtype=jnp.int32)
    left = jnp.where(left >= 0, left, own)
    right = jnp.where(right < NODES_SEC, right, own)
    chosen = jnp.where(kind < 16, own, jnp.where(kind == 16, left, jnp.where(kind == 17, right, seam)))
    far_right = (block_pos + 1) * E_DEV + BAND - 1
    far_left = block_pos * E_DEV - BAND
    row_one = jnp.where((slot == 1) & (far_right < NODES_SEC), far_right, chosen[1])
    row_two = jnp.where((slot == 2) & (far_left >= 0), far_left, chosen[2])
    chosen = chosen.at[1].set(row_one).at[2].set(row_two)
    chosen = chosen.at[0, 0].set(0).at[0, ELEMS - 1].set(NREF - 1)
    return chosen.astype(jnp.int32)


def set_ends(array, own_key, low, high):
    extent = array.shape
    index_at = [jax.random.randint(jax.random.fold_in(own_key, axis), (), 0, extent[axis]) for axis in range(len(extent))]
    array = array.at[tuple(index_at)].set(low)
    longest = extent.index(max(extent))
    index_at[longest] = (index_at[longest] + 1) % extent[longest]
    return array.at[tuple(index_at)].set(high)


def shard_levels(stream_key, shape, pieces, low, high):
    factor_of, own = 1.0, jax.random.fold_in(stream_key, 6)
    for dim, parts in pieces:
        draws = jnp.exp(jax.random.uniform(jax.random.fold_in(own, dim), (parts,), jnp.float32, low / len(pieces), high / len(pieces)))
        factor_of = factor_of * jnp.repeat(draws, shape[dim] // parts).reshape([-1 if axis == dim else 1 for axis in range(len(shape))])
    return factor_of


def normal_values(own_key, extent, scale, most, shards=(), held_as=jnp.bfloat16):
    values = jax.random.normal(own_key, extent, jnp.float32) * scale
    if len(shards) > 0:
        values = shard_levels(own_key, extent, shards, -0.22, 0.18) * values
    return jnp.clip(values, min=-most, max=most).astype(held_as)


def setup_inputs(seed: int = 0) -> dict:
    key_of = jax.random.split(jax.random.key(seed), 13)
    return {
        "strain_map": normal_values(key_of[0], (36, ELEMS), 12 ** -0.5, 1.75, ((1, 32),), jnp.float32),
        "corner_nodes": draw_corner_nodes(jax.random.fold_in(key_of[12], 71), 0),
        "counts": draw_counts(jax.random.fold_in(key_of[12], 71), 0),
        "seam_nodes": set_ends(jax.random.randint(key_of[3], (SECTORS, SEAM), 0, NODES_SEC), jax.random.fold_in(key_of[3], 1), 0, NODES_SEC - 1).astype(jnp.int32),
        "velocity": normal_values(key_of[4], (3, NODES), 1.0, 6.0, ((1, 32),), jnp.float32),
        "dual_state": normal_values(key_of[5], (3, ELEMS), 1.0, 6.0, ((1, 32),), jnp.float32),
        "nodal_load": normal_values(key_of[6], (3, NODES), 1.0, 6.0, ((1, 32),), jnp.float32),
        "mobility": jnp.clip(jnp.exp(math.log(0.5) - 1.609438 * jax.random.uniform(key_of[7], (NODES,), jnp.float32) ** shard_levels(key_of[7], (NODES,), ((0, 32),), -0.2, 0.2)), 0.1, 0.5),
        "past_dual": normal_values(key_of[8], (DEPTH, 3, ELEMS), 1.0, 6.0, ((2, 32),), jnp.float32),
        "past_dual_gap": draw_past_dual_gap(jax.random.fold_in(key_of[12], 71), 0),
        "past_velocity": normal_values(key_of[10], (DEPTH, 3, NODES), 1.0, 6.0, ((2, 32),), jnp.float32),
        "past_velocity_gap": draw_past_velocity_gap(jax.random.fold_in(key_of[12], 71), 0),
    }


def project_cone(trial):
    center = 0.5 * (trial[0] + trial[1])
    spread = 0.5 * (trial[0] - trial[1])
    shear = trial[2]
    radius = jnp.sqrt(spread * spread + shear * shear)
    upper = center + radius
    lower = center - radius
    iso_part = 0.5 * (jnp.maximum(upper, 0.0) + jnp.maximum(lower, 0.0))
    factor = jnp.clip((center + radius) / (2.0 * jnp.maximum(radius, 0.05)), 0.0, 1.0)
    return jnp.stack([iso_part + factor * spread, iso_part - factor * spread, factor * shear])

def reference(strain_map, corner_nodes, counts, seam_nodes, velocity, dual_state, nodal_load, mobility, past_dual, past_dual_gap, past_velocity, past_velocity_gap):
    highest = lax.Precision.HIGHEST
    elem_count = strain_map.shape[1]
    elem_index = jnp.arange(elem_count, dtype=jnp.int32)
    alive_mask = (elem_index % E_DEV < counts[elem_index // E_DEV]).astype(jnp.float32)
    sector_index = elem_index // ESEC
    next_sector = (sector_index + 1) % SECTORS
    seam_pos = jnp.clip(corner_nodes - NODES_SEC, 0, SEAM - 1).astype(jnp.int32)
    seam_node = seam_nodes[jnp.broadcast_to(next_sector[None, :], corner_nodes.shape), seam_pos]
    glob = jnp.where(corner_nodes < NODES_SEC, sector_index[None, :] * NODES_SEC + corner_nodes, next_sector[None, :] * NODES_SEC + seam_node).astype(jnp.int32)
    flat_nodes = glob.reshape(-1)
    strain_blocks = strain_map.reshape(3, 4, 3, elem_count)

    def sweep_once(dual, speed):
        corner_vel = speed[:, flat_nodes].reshape(3, 4, elem_count).transpose(1, 0, 2)
        rate = lax.optimization_barrier(jnp.sum(strain_blocks * corner_vel[None], axis=(1, 2)))
        trial = rate + dual
        cone = project_cone(trial)
        dual_next = alive_mask * (trial - cone)
        misfit = alive_mask * (rate - cone + dual_next)
        elem_force = lax.optimization_barrier(jnp.sum(strain_blocks * misfit[:, None, None, :], axis=0))
        spread_force = elem_force.transpose(1, 0, 2).reshape(3, -1)
        forces = jnp.zeros((3, NODES), jnp.float32).at[:, flat_nodes].add(spread_force)
        speed_next = speed - mobility[None, :] * (forces - nodal_load)
        return (dual_next, speed_next)
    dual, speed = (dual_state, velocity)
    dual_prev, speed_prev = (dual, speed)
    for sweep in range(ITERS):
        dual_prev, speed_prev = (dual, speed)
        dual, speed = sweep_once(dual, speed)
    res_w = dual - dual_prev
    res_u = speed - speed_prev
    gap_w = res_w[None] - past_dual_gap
    gap_u = res_u[None] - past_velocity_gap
    gram = jnp.einsum('iab,jab->ij', gap_w, gap_w, precision=highest) + jnp.einsum('iab,jab->ij', gap_u, gap_u, precision=highest)
    rhs = jnp.einsum('iab,ab->i', gap_w, res_w, precision=highest) + jnp.einsum('iab,ab->i', gap_u, res_u, precision=highest)
    ridge_term = 0.0001 * jnp.trace(gram) / DEPTH
    factor = jnp.linalg.cholesky(gram + ridge_term * jnp.eye(DEPTH, dtype=gram.dtype))
    coeffs = jax.scipy.linalg.cho_solve((factor, True), rhs)
    new_dual = dual - jnp.einsum('i,iab->ab', coeffs, dual[None] - past_dual - past_dual_gap, precision=highest)
    new_velocity = speed - jnp.einsum('i,iab->ab', coeffs, speed[None] - past_velocity - past_velocity_gap, precision=highest)
    return (new_velocity, new_dual)
```

```python
import functools
import itertools

import jax
import jax.numpy as jnp
from jax import lax
from jax.experimental import pallas as pl
from jax.experimental.pallas import tpu as pltpu
from jax.sharding import PartitionSpec as P

LANES = 128
VMEM_LIMIT = 24 * 1024 * 1024

STRAIN, DUAL, ALIVE, OWN, ROWS_ONE = 0, 36, 39, 40, 48
INDEX, NEXT, ROWS_TWO = 0, 4, 16
STATE_OWN, STATE_NEXT, STATE_ROWS = 40, 47, 54


def vmem():
    return pl.BlockSpec(memory_space=pltpu.VMEM)


def smem():
    return pl.BlockSpec(memory_space=pltpu.SMEM)


def call(kernel, outs, args, scalars=0, scratch=()):
    return pl.pallas_call(
        kernel,
        out_shape=outs,
        in_specs=[smem()] * scalars + [vmem()] * (len(args) - scalars),
        out_specs=jax.tree.map(lambda _: vmem(), outs),
        scratch_shapes=list(scratch),
        compiler_params=pltpu.CompilerParams(vmem_limit_bytes=VMEM_LIMIT),
    )(*args)


def f32(*shape):
    return jax.ShapeDtypeStruct(shape, jnp.float32)


def repeat(blocks, body, init):
    if blocks == 8:
        return body(slice(0, 8), 0, init)
    return lax.fori_loop(
        0, blocks // 8, lambda step, carry: body(pl.ds(pl.multiple_of(8 * step, 8), 8), 8 * step, carry), init
    )


def project_cone(trial):
    center = 0.5 * (trial[0] + trial[1])
    spread = 0.5 * (trial[0] - trial[1])
    shear = trial[2]
    radius = jnp.sqrt(spread * spread + shear * shear)
    upper = center + radius
    lower = center - radius
    iso_part = 0.5 * (jnp.maximum(upper, 0.0) + jnp.maximum(lower, 0.0))
    factor = jnp.clip((center + radius) / (2.0 * jnp.maximum(radius, 0.05)), 0.0, 1.0)
    return (iso_part + factor * spread, iso_part - factor * spread, factor * shear)


def pack_kernel(counts, strain, dual, speed, load, mobility, seam, gap_w, gap_u, one, ahead, history):
    own = speed.shape[1]
    slot = lax.broadcasted_iota(jnp.int32, (1, own), 1)
    one[STRAIN:DUAL, :] = strain[...]
    one[DUAL:ALIVE, :] = dual[...]
    one[ALIVE:OWN, :] = (slot < counts[0]).astype(jnp.float32)
    nodes = jnp.concatenate([speed[...], load[...], mobility[...], jnp.zeros((1, own), jnp.float32)], axis=0)
    one[OWN:ROWS_ONE, :] = nodes
    ahead[0:8, :] = nodes
    for row in range(ahead.shape[0] - 8):
        ahead[8 + row : 9 + row, :] = seam[:, row * own : (row + 1) * own].astype(jnp.float32)
    depth = gap_w.shape[0]
    for i in range(depth):
        history[3 * i : 3 * i + 3, :] = gap_w[i]
        history[3 * (depth + i) : 3 * (depth + i) + 3, :] = gap_u[i]


def resolve_kernel(sector_nodes, ahead, corners, two):
    own = corners.shape[1]
    halves = own // LANES
    corner = jnp.concatenate([corners[:, h * LANES : (h + 1) * LANES] for h in range(halves)], axis=0)
    seam_rows = ahead.shape[0] - 8
    place = jnp.clip(corner - sector_nodes, 0, seam_rows * own - 1)
    high, low = place // LANES, place % LANES
    found = jnp.zeros(corner.shape, jnp.float32)
    for row in range(seam_rows):
        for h in range(halves):
            table = jnp.broadcast_to(ahead[8 + row : 9 + row, h * LANES : (h + 1) * LANES], corner.shape)
            value = jnp.take_along_axis(table, low, axis=1, mode="promise_in_bounds")
            found = jnp.where(high == row * halves + h, value, found)
    node = jnp.where(corner < sector_nodes, corner.astype(jnp.float32), found + float(sector_nodes))
    for h in range(halves):
        two[INDEX:NEXT, h * LANES : (h + 1) * LANES] = node[4 * h : 4 * h + 4]
    two[NEXT : NEXT + 8, :] = ahead[0:8, :]
    two[NEXT + 8 : ROWS_TWO, :] = jnp.zeros((ROWS_TWO - NEXT - 8, own), jnp.float32)


def sweep(strain_row, index, table, terms, dual, alive):
    blocks, own = index.shape[1:]
    halves = own // LANES
    count = 2 * blocks * halves
    high = [[index[k, :, h * LANES : (h + 1) * LANES] // LANES for h in range(halves)] for k in range(4)]
    low = [[index[k, :, h * LANES : (h + 1) * LANES] % LANES for h in range(halves)] for k in range(4)]

    def take_group(group, first, found):
        found = list(found)
        for side, part, block in itertools.product(range(2), range(halves), range(8)):
            number = (side * blocks + first + block) * halves + part
            rows = [
                jnp.broadcast_to(
                    table[3 * side + j, group, part * LANES : (part + 1) * LANES][block : block + 1],
                    (blocks, LANES),
                )
                for j in range(3)
            ]
            at = 0
            for k in range(4):
                for h in range(halves):
                    here = high[k][h] == number
                    for j in range(3):
                        value = jnp.take_along_axis(rows[j], low[k][h], axis=1, mode="promise_in_bounds")
                        found[at] = jnp.where(here, value, found[at])
                        at += 1
        return tuple(found)

    found = repeat(blocks, take_group, tuple(jnp.zeros((blocks, LANES), jnp.float32) for _ in range(12 * halves)))
    speed = [
        [jnp.concatenate([found[(k * halves + h) * 3 + j] for h in range(halves)], axis=1) for j in range(3)]
        for k in range(4)
    ]
    rate = []
    for c in range(3):
        total = None
        for k in range(4):
            for j in range(3):
                term = strain_row(12 * c + 3 * k + j) * speed[k][j]
                total = term if total is None else total + term
        rate.append(total)
    trial = [rate[c] + dual[c] for c in range(3)]
    cone = project_cone(trial)
    dual_next = [alive * (trial[c] - cone[c]) for c in range(3)]
    misfit = [alive * (rate[c] - cone[c] + dual_next[c]) for c in range(3)]
    for k in range(4):
        for j in range(3):
            rest = sum(strain_row(12 * c + 3 * k + j) * misfit[c] for c in range(3))
            for split in range(3):
                term = rest.astype(jnp.bfloat16).astype(jnp.float32)
                terms[3 * j + split, k] = term
                rest = rest - term

    node_rows = 2 * blocks
    high_iota = lax.broadcasted_iota(jnp.int32, (node_rows, 4 * own), 0)
    low_iota = lax.broadcasted_iota(jnp.int32, (own, 4 * own), 0)

    def add_group(group, first, total):
        for block in range(8):
            number = jnp.concatenate([index[k, group, :][block : block + 1] for k in range(4)], axis=1)
            here = high_iota == number // own
            spread = (low_iota == number % own).astype(jnp.float32).astype(jnp.bfloat16)
            weights = []
            for row in range(9):
                value = jnp.concatenate([terms[row, k, group, :][block : block + 1] for k in range(4)], axis=1)
                weights.append(jnp.where(here, value, 0.0).astype(jnp.bfloat16))
            total += lax.dot_general(
                jnp.concatenate(weights, axis=0),
                spread,
                (((1,), (1,)), ((), ())),
                preferred_element_type=jnp.float32,
            )
        return total

    total = repeat(blocks, add_group, jnp.zeros((9 * node_rows, own), jnp.float32))
    force = []
    for j in range(3):
        at = 3 * j * node_rows
        force.append(total[at : at + node_rows] + total[at + node_rows : at + 2 * node_rows] + total[at + 2 * node_rows : at + 3 * node_rows])
    return dual_next, [value[:blocks] for value in force], [value[blocks:] for value in force]


def by_block(ref, row, rows, blocks):
    return ref[pl.ds(row, blocks, stride=rows), :]


def first_kernel(blocks, *refs):
    ones, twos = refs[:blocks], refs[blocks : 2 * blocks]
    state, index, force_own, force_next, stack_one, stack_two, table, terms = refs[2 * blocks :]
    own = index.shape[2]
    halves = own // LANES
    for block in range(blocks):
        for h in range(halves):
            lanes = slice(h * LANES, (h + 1) * LANES)
            stack_one[h, block * ROWS_ONE : (block + 1) * ROWS_ONE, :] = ones[block][:, lanes]
            stack_two[h, block * ROWS_TWO : (block + 1) * ROWS_TWO, :] = twos[block][:, lanes]

    def row_one(row):
        return jnp.concatenate([by_block(stack_one.at[h], row, ROWS_ONE, blocks) for h in range(halves)], axis=1)

    def row_two(row):
        return jnp.concatenate([by_block(stack_two.at[h], row, ROWS_TWO, blocks) for h in range(halves)], axis=1)

    flip = lax.axis_index("dom") * own
    for k in range(4):
        index[k] = row_two(INDEX + k).astype(jnp.int32) ^ flip
    for row in range(36):
        state[row] = row_one(STRAIN + row)
    alive = row_one(ALIVE)
    state[ALIVE] = alive
    for row in range(7):
        state[STATE_OWN + row] = row_one(OWN + row)
        state[STATE_NEXT + row] = row_two(NEXT + row)
    for j in range(3):
        table[j] = state[STATE_OWN + j]
        table[3 + j] = state[STATE_NEXT + j]
    dual = [row_one(DUAL + c) for c in range(3)]
    dual, out_own, out_next = sweep(lambda row: state[row], index, table, terms, dual, alive)
    for c in range(3):
        state[DUAL + c] = dual[c]
        force_own[c] = out_own[c]
        force_next[c] = out_next[c]


def second_kernel(state, index, force_own, force_next, from_prev, from_next, out_next, keep, table, terms):
    for j in range(3):
        own_force = force_own[j] + from_prev[j]
        next_force = from_next[j] + force_next[j]
        table[j] = state[STATE_OWN + j] - state[STATE_OWN + 6] * (own_force - state[STATE_OWN + 3 + j])
        table[3 + j] = state[STATE_NEXT + j] - state[STATE_NEXT + 6] * (next_force - state[STATE_NEXT + 3 + j])
    dual = [state[DUAL + c] for c in range(3)]
    dual_next, own_force, next_force = sweep(
        lambda row: state[row], index, table, terms, dual, state[ALIVE]
    )
    for c in range(3):
        out_next[c] = next_force[c]
        keep[c] = dual_next[c]
        keep[3 + c] = dual_next[c] - dual[c]
        keep[6 + c] = table[c]
        keep[9 + c] = own_force[c]


def gram_kernel(blocks, depth, state, keep, from_prev, *refs):
    pieces = refs[:blocks]
    part, last, stack = refs[blocks:]
    own = keep.shape[2]
    halves = own // LANES
    rows = 6 * depth
    for block in range(blocks):
        for h in range(halves):
            stack[h, block * rows : (block + 1) * rows, :] = pieces[block][:, h * LANES : (h + 1) * LANES]
    speed, change = [], []
    for j in range(3):
        force = keep[9 + j] + from_prev[j]
        before = keep[6 + j]
        after = before - state[STATE_OWN + 6] * (force - state[STATE_OWN + 3 + j])
        speed.append(after)
        change.append(after - before)
        last[j : j + 1, :] = after[0:1]
        last[3 + j : 4 + j, :] = keep[j][0:1]
    last[6:8, :] = jnp.zeros((2, own), jnp.float32)
    sums = {}
    for kind in range(2):
        for c in range(3):
            whole = keep[3 + c] if kind == 0 else change[c]
            for h in range(halves):
                for top in range(0, blocks, 8):
                    moved = whole[top : top + 8, h * LANES : (h + 1) * LANES]
                    gaps = [
                        moved - stack[h, pl.ds(top * rows + 3 * (depth * kind + i) + c, 8, stride=rows), :]
                        for i in range(depth)
                    ]
                    for i in range(depth):
                        for l in range(i, depth + 1):
                            term = gaps[i] * (gaps[l] if l < depth else moved)
                            sums[i, l] = sums[i, l] + term if (i, l) in sums else term
    row = lax.broadcasted_iota(jnp.int32, (depth, LANES), 0)
    lane = lax.broadcasted_iota(jnp.int32, (depth, LANES), 1)
    out = jnp.zeros((depth, LANES), jnp.float32)
    for (i, l), value in sums.items():
        value = jnp.sum(jnp.sum(value, axis=0, keepdims=True), axis=1, keepdims=True)
        here = (row == i) & (lane == l)
        if i < l < depth:
            here = here | ((row == l) & (lane == i))
        out = jnp.where(here, value, out)
    part[...] = out


def solve_kernel(depth, *refs):
    parts = refs[:-7]
    last, past_w, gap_w, past_u, gap_u, new_u, new_w = refs[-7:]
    matrix = parts[0][...]
    for other in parts[1:]:
        matrix = matrix + other[...]
    row = lax.broadcasted_iota(jnp.int32, (depth, LANES), 0)
    lane = lax.broadcasted_iota(jnp.int32, (depth, LANES), 1)
    diagonal = jnp.where(row == lane, matrix, 0.0)
    trace = jnp.sum(jnp.sum(diagonal, axis=0, keepdims=True), axis=1, keepdims=True)
    matrix = matrix + jnp.where(row == lane, 0.0001 * trace / depth, 0.0)
    for step in range(depth):
        pivot = matrix[step : step + 1, :]
        pivot = pivot / pivot[:, step : step + 1]
        matrix = jnp.where(row == step, pivot, matrix - matrix[:, step : step + 1] * pivot)
    speed, dual = last[0:3, :], last[3:6, :]
    out_u, out_w = speed, dual
    for i in range(depth):
        weight = matrix[i : i + 1, depth : depth + 1]
        out_u = out_u - weight * (speed - past_u[i] - gap_u[i])
        out_w = out_w - weight * (dual - past_w[i] - gap_w[i])
    new_u[...] = out_u
    new_w[...] = out_w


def per_device(
    strain_map,
    corner_nodes,
    counts,
    seam_nodes,
    velocity,
    dual_state,
    nodal_load,
    mobility,
    past_dual,
    past_dual_gap,
    past_velocity,
    past_velocity_gap,
):
    own = velocity.shape[1]
    halves = own // LANES
    blocks = lax.axis_size("dom")
    sectors = lax.axis_size("sector")
    depth = past_dual.shape[0]
    seam_rows = seam_nodes.shape[1] // own

    def to_next(value):
        return lax.ppermute(value, "sector", [(i, (i + 1) % sectors) for i in range(sectors)])

    def to_prev(value):
        return lax.ppermute(value, "sector", [(i, (i - 1) % sectors) for i in range(sectors)])

    def swap(value, bits):
        return lax.ppermute(value, "dom", [(i, i ^ bits) for i in range(blocks)])

    def gather_blocks(value):
        even = [value] + [swap(value, bits) for bits in range(2, blocks, 2)]
        odd = [swap(piece, 1) for piece in even]
        return [piece for pair in zip(even, odd) for piece in pair]

    one, ahead, history = call(
        pack_kernel,
        (f32(ROWS_ONE, own), f32(8 + seam_rows, own), f32(6 * depth, own)),
        (
            counts,
            strain_map,
            dual_state,
            velocity,
            nodal_load,
            mobility.reshape(1, own),
            seam_nodes,
            past_dual_gap,
            past_velocity_gap,
        ),
        scalars=1,
    )
    ahead = to_prev(ahead)
    ones = gather_blocks(one)
    two = call(
        functools.partial(resolve_kernel, own * blocks),
        f32(ROWS_TWO, own),
        (ahead, corner_nodes),
    )
    twos = gather_blocks(two)
    histories = gather_blocks(history)
    sector = f32(3, blocks, own)
    work = [pltpu.VMEM((6, blocks, own), jnp.float32), pltpu.VMEM((9, 4, blocks, own), jnp.float32)]
    state, index, force_own, force_next = call(
        functools.partial(first_kernel, blocks),
        (f32(STATE_ROWS, blocks, own), jax.ShapeDtypeStruct((4, blocks, own), jnp.int32), sector, sector),
        (*ones, *twos),
        scratch=[
            pltpu.VMEM((halves, blocks * ROWS_ONE, LANES), jnp.float32),
            pltpu.VMEM((halves, blocks * ROWS_TWO, LANES), jnp.float32),
            *work,
        ],
    )
    force_next_two, keep = call(
        second_kernel,
        (sector, f32(12, blocks, own)),
        (state, index, force_own, force_next, to_next(force_next), to_prev(force_own)),
        scratch=work,
    )
    part, last = call(
        functools.partial(gram_kernel, blocks, depth),
        (f32(depth, LANES), f32(8, own)),
        (state, keep, to_next(force_next_two), *histories),
        scratch=[pltpu.VMEM((halves, blocks * 6 * depth, LANES), jnp.float32)],
    )
    parts = [part] + [
        lax.ppermute(part, "sector", [(i, (i + by) % sectors) for i in range(sectors)]) for by in range(1, sectors)
    ]
    return call(
        functools.partial(solve_kernel, depth),
        (f32(3, own), f32(3, own)),
        (*parts, last, past_dual, past_dual_gap, past_velocity, past_velocity_gap),
    )


def solution(mesh):
    in_specs = (
        P(None, ("sector", "dom")),
        P(None, ("sector", "dom")),
        P(("sector", "dom")),
        P("sector", None),
        P(None, ("sector", "dom")),
        P(None, ("sector", "dom")),
        P(None, ("sector", "dom")),
        P(("sector", "dom")),
        P(None, None, ("sector", "dom")),
        P(None, None, ("sector", "dom")),
        P(None, None, ("sector", "dom")),
        P(None, None, ("sector", "dom")),
    )
    out_specs = (P(None, ("sector", "dom")), P(None, ("sector", "dom")))
    return jax.shard_map(
        per_device, mesh=mesh, in_specs=in_specs, out_specs=out_specs, check_vma=False
    )
```

```python
import functools
import itertools

import jax
import jax.numpy as jnp
from jax import lax
from jax.experimental import pallas as pl
from jax.experimental.pallas import tpu as pltpu
from jax.sharding import PartitionSpec as P

LANES = 128
VMEM_LIMIT = 24 * 1024 * 1024

STRAIN, DUAL, STEP, SPEED, LOAD, NEXT_STEP, NEXT_SPEED, INDEX, ROWS = 0, 36, 39, 40, 43, 46, 48, 51, 56
KEPT_NEXT_STEP, KEPT_LOAD, KEPT = 40, 41, 44
SPLITS = 3


def vmem():
    return pl.BlockSpec(memory_space=pltpu.VMEM)


def smem():
    return pl.BlockSpec(memory_space=pltpu.SMEM)


def call(kernel, outs, args, scalars=0, loose=0, scratch=()):
    return pl.pallas_call(
        kernel,
        out_shape=outs,
        in_specs=[smem()] * scalars
        + [pl.BlockSpec(memory_space=pl.ANY)] * loose
        + [vmem()] * (len(args) - scalars - loose),
        out_specs=jax.tree.map(lambda _: vmem(), outs),
        scratch_shapes=list(scratch),
        compiler_params=pltpu.CompilerParams(vmem_limit_bytes=VMEM_LIMIT),
    )(*args)


def f32(*shape):
    return jax.ShapeDtypeStruct(shape, jnp.float32)


def repeat(blocks, body, init):
    if blocks == 8:
        return body(slice(0, 8), 0, init)
    return lax.fori_loop(
        0, blocks // 8, lambda step, carry: body(pl.ds(pl.multiple_of(8 * step, 8), 8), 8 * step, carry), init
    )


def project_cone(trial):
    center = 0.5 * (trial[0] + trial[1])
    spread = 0.5 * (trial[0] - trial[1])
    shear = trial[2]
    radius = jnp.sqrt(spread * spread + shear * shear)
    upper = center + radius
    lower = center - radius
    iso_part = 0.5 * (jnp.maximum(upper, 0.0) + jnp.maximum(lower, 0.0))
    factor = jnp.clip((center + radius) / (2.0 * jnp.maximum(radius, 0.05)), 0.0, 1.0)
    return (iso_part + factor * spread, iso_part - factor * spread, factor * shear)


def nodes_kernel(speed, mobility, seam, ahead):
    own = speed.shape[1]
    ahead[0:3, :] = speed[...]
    ahead[3:4, :] = mobility[...]
    ahead[4:8, :] = jnp.zeros((4, own), jnp.float32)
    for row in range(ahead.shape[0] - 8):
        ahead[8 + row : 9 + row, :] = seam[:, row * own : (row + 1) * own].astype(jnp.float32)


def message_kernel(sector_nodes, counts, ahead, corners, strain, dual, speed, load, mobility, message):
    own = corners.shape[1]
    halves = own // LANES
    slot = lax.broadcasted_iota(jnp.int32, (1, own), 1)
    alive = (slot < counts[0]).astype(jnp.float32)
    message[STRAIN:DUAL, :] = strain[...] * alive
    message[DUAL : DUAL + 3, :] = dual[...] * alive
    message[STEP : STEP + 1, :] = mobility[...]
    message[SPEED : SPEED + 3, :] = speed[...]
    message[LOAD : LOAD + 3, :] = load[...]
    message[NEXT_STEP : NEXT_STEP + 1, :] = ahead[3:4, :]
    message[NEXT_STEP + 1 : NEXT_SPEED, :] = jnp.zeros((1, own), jnp.float32)
    message[NEXT_SPEED : NEXT_SPEED + 3, :] = ahead[0:3, :]
    message[ROWS - 1 : ROWS, :] = jnp.zeros((1, own), jnp.float32)
    corner = jnp.concatenate([corners[:, h * LANES : (h + 1) * LANES] for h in range(halves)], axis=0)
    seam_rows = ahead.shape[0] - 8
    place = jnp.clip(corner - sector_nodes, 0, seam_rows * own - 1)
    high, low = place // LANES, place % LANES
    found = jnp.zeros(corner.shape, jnp.float32)
    for row in range(seam_rows):
        for h in range(halves):
            table = jnp.broadcast_to(ahead[8 + row : 9 + row, h * LANES : (h + 1) * LANES], corner.shape)
            value = jnp.take_along_axis(table, low, axis=1, mode="promise_in_bounds")
            found = jnp.where(high == row * halves + h, value, found)
    node = jnp.where(corner < sector_nodes, corner.astype(jnp.float32), found + float(sector_nodes))
    for h in range(halves):
        message[INDEX : INDEX + 4, h * LANES : (h + 1) * LANES] = node[4 * h : 4 * h + 4]


def history_kernel(after, gap_w, gap_u, history):
    depth = gap_w.shape[1]
    for c in range(3):
        history[depth * c : depth * (c + 1), :] = gap_w[c]
        history[depth * (3 + c) : depth * (4 + c), :] = gap_u[c]


def join_kernel(after, left, right, joined):
    rows = left.shape[0]
    joined[:rows, :] = left[...]
    joined[rows:, :] = right[...]


def sweep(strain_row, index, table, terms, dual):
    blocks, own = index.shape[1:]
    halves = own // LANES
    high = [[index[k, :, h * LANES : (h + 1) * LANES] // LANES for h in range(halves)] for k in range(4)]
    low = [[index[k, :, h * LANES : (h + 1) * LANES] % LANES for h in range(halves)] for k in range(4)]

    def take_group(group, first, found):
        found = list(found)
        for side, part, block in itertools.product(range(2), range(halves), range(8)):
            number = (side * blocks + first + block) * halves + part
            rows = [
                jnp.broadcast_to(
                    table[3 * side + j, group, part * LANES : (part + 1) * LANES][block : block + 1],
                    (blocks, LANES),
                )
                for j in range(3)
            ]
            at = 0
            for k in range(4):
                for h in range(halves):
                    here = high[k][h] == number
                    for j in range(3):
                        value = jnp.take_along_axis(rows[j], low[k][h], axis=1, mode="promise_in_bounds")
                        found[at] = jnp.where(here, value, found[at])
                        at += 1
        return tuple(found)

    found = repeat(blocks, take_group, tuple(jnp.zeros((blocks, LANES), jnp.float32) for _ in range(12 * halves)))
    speed = [
        [jnp.concatenate([found[(k * halves + h) * 3 + j] for h in range(halves)], axis=1) for j in range(3)]
        for k in range(4)
    ]
    rate = []
    for c in range(3):
        total = None
        for k in range(4):
            for j in range(3):
                term = strain_row(12 * c + 3 * k + j) * speed[k][j]
                total = term if total is None else total + term
        rate.append(total)
    trial = [rate[c] + dual[c] for c in range(3)]
    cone = project_cone(trial)
    dual_next = [trial[c] - cone[c] for c in range(3)]
    misfit = [rate[c] - cone[c] + dual_next[c] for c in range(3)]
    for k in range(4):
        for j in range(3):
            rest = sum(strain_row(12 * c + 3 * k + j) * misfit[c] for c in range(3))
            for split in range(SPLITS):
                term = rest.astype(jnp.bfloat16).astype(jnp.float32)
                terms[SPLITS * j + split, k] = term
                rest = rest - term

    node_rows = 2 * blocks
    iota = lax.broadcasted_iota(jnp.int32, (16, 4 * own), 0).astype(jnp.float32)
    low_iota = [(iota + float(16 * g)).astype(jnp.bfloat16) for g in range(own // 16)]
    high_iota = [(iota + float(16 * g)).astype(jnp.bfloat16) for g in range(node_rows // 16)]
    one = jnp.ones((16, 4 * own), jnp.bfloat16)
    zero = jnp.zeros((16, 4 * own), jnp.bfloat16)

    def spread_row(rows):
        return jnp.broadcast_to(jnp.concatenate(rows, axis=1), (16, 4 * own)).astype(jnp.bfloat16)

    def add_group(group, first, total):
        for block in range(8):
            number = [index[k, group, :][block : block + 1] for k in range(4)]
            low_row = spread_row([(value % own).astype(jnp.float32) for value in number])
            high_row = spread_row([(value // own).astype(jnp.float32) for value in number])
            spread = jnp.concatenate([jnp.where(low_row == value, one, zero) for value in low_iota], axis=0)
            here = [high_row == value for value in high_iota]
            weights = []
            for row in range(3 * SPLITS):
                value = spread_row([terms[row, k, group, :][block : block + 1] for k in range(4)])
                weights += [jnp.where(mask, value, zero) for mask in here]
            total += lax.dot_general(
                jnp.concatenate(weights, axis=0),
                spread,
                (((1,), (1,)), ((), ())),
                preferred_element_type=jnp.float32,
            )
        return total

    total = repeat(blocks, add_group, jnp.zeros((3 * SPLITS * node_rows, own), jnp.float32))
    force = [
        sum(total[(SPLITS * j + split) * node_rows : (SPLITS * j + split + 1) * node_rows] for split in range(SPLITS))
        for j in range(3)
    ]
    return dual_next, [value[:blocks] for value in force], [value[blocks:] for value in force]


def stack_blocks(pieces, slots, rows, stack):
    for piece, own_slots in zip(pieces, slots):
        for at, slot in enumerate(own_slots):
            for h in range(stack.shape[0]):
                stack[h, slot * rows : (slot + 1) * rows, :] = piece[
                    at * rows : (at + 1) * rows, h * LANES : (h + 1) * LANES
                ]


def across(stack, row, rows):
    blocks = stack.shape[1] // rows
    return jnp.concatenate(
        [stack[h, pl.ds(row, blocks, stride=rows), :] for h in range(stack.shape[0])], axis=1
    )


def first_kernel(blocks, *refs):
    pieces = refs[:blocks]
    state, index, to_near, to_far, stack, table, terms = refs[blocks:]
    own = index.shape[2]
    stack_blocks(pieces, [(block,) for block in range(blocks)], ROWS, stack)
    flip = lax.axis_index("dom") * own
    even = lax.axis_index("sector") % 2 == 0
    for k in range(4):
        index[k] = across(stack, INDEX + k, ROWS).astype(jnp.int32) ^ flip
    for row in range(36):
        state[row] = across(stack, STRAIN + row, ROWS)
    step = across(stack, STEP, ROWS)
    state[STEP] = step
    state[KEPT_NEXT_STEP] = across(stack, NEXT_STEP, ROWS)
    for j in range(3):
        state[KEPT_LOAD + j] = across(stack, LOAD + j, ROWS)
        table[j] = across(stack, SPEED + j, ROWS)
        table[3 + j] = across(stack, NEXT_SPEED + j, ROWS)
    dual = [across(stack, DUAL + c, ROWS) for c in range(3)]
    dual, force_own, force_next = sweep(lambda row: state[row], index, table, terms, dual)
    for c in range(3):
        state[DUAL + c] = dual[c]
        mine = table[c] - step * (force_own[c] - state[KEPT_LOAD + c])
        to_near[c] = jnp.where(even, force_next[c], mine)
        to_far[c] = jnp.where(even, mine, force_next[c])


def second_kernel(state, index, to_near, to_far, from_near, from_far, out_next, keep, table, terms):
    even = lax.axis_index("sector") % 2 == 0
    step, next_step = state[STEP], state[KEPT_NEXT_STEP]
    for j in range(3):
        near, far = to_near[j], to_far[j]
        near_in, far_in = from_near[j], from_far[j]
        table[j] = jnp.where(even, far, near) - step * jnp.where(even, far_in, near_in)
        table[3 + j] = jnp.where(even, near_in, far_in) - next_step * jnp.where(even, near, far)
    dual = [state[DUAL + c] for c in range(3)]
    dual_next, force_own, force_next = sweep(lambda row: state[row], index, table, terms, dual)
    for c in range(3):
        out_next[c] = force_next[c]
        keep[c] = dual_next[c]
        keep[3 + c] = dual_next[c] - dual[c]
        keep[6 + c] = table[c]
        keep[9 + c] = table[c] - step * (force_own[c] - state[KEPT_LOAD + c])


def pairs(depth):
    return [(i, l) for i in range(depth) for l in range(i, depth + 1)]


def gram_kernel(depth, slots, state, keep, from_prev, left, right, part, last, stack):
    blocks, own = keep.shape[1:]
    halves = own // LANES
    rows = 6 * depth
    stack_blocks((left, right), slots, rows, stack)
    change = []
    for j in range(3):
        after = keep[9 + j] - state[STEP] * from_prev[j]
        change.append(after - keep[6 + j])
        last[j : j + 1, :] = after[0:1]
        last[3 + j : 4 + j, :] = keep[j][0:1]
    last[6:8, :] = jnp.zeros((2, own), jnp.float32)
    sums = {}
    for kind in range(2):
        for c in range(3):
            whole = keep[3 + c] if kind == 0 else change[c]
            for h in range(halves):
                for top in range(0, blocks, 8):
                    moved = whole[top : top + 8, h * LANES : (h + 1) * LANES]
                    gaps = [
                        moved - stack[h, pl.ds(top * rows + depth * (3 * kind + c) + i, 8, stride=rows), :]
                        for i in range(depth)
                    ] + [moved]
                    for i, l in pairs(depth):
                        term = gaps[i] * gaps[l]
                        sums[i, l] = sums[i, l] + term if (i, l) in sums else term
    for at, pair in enumerate(pairs(depth)):
        part[at : at + 1, :] = jnp.sum(sums[pair], axis=0, keepdims=True)
    count = len(pairs(depth))
    if part.shape[0] > count:
        part[count:, :] = jnp.zeros((part.shape[0] - count, LANES), jnp.float32)
    part[...] = jnp.broadcast_to(jnp.sum(part[...], axis=1, keepdims=True), part.shape)


def add_kernel(left, right, total):
    total[...] = left[...] + right[...]


def solve_kernel(depth, left, right, last, past_w, gap_w, past_u, gap_u, new_u, new_w, total):
    own = last.shape[1]
    total[...] = left[...] + right[...]
    matrix = {
        pair: jnp.broadcast_to(total[at : at + 1, :], (depth, LANES)) for at, pair in enumerate(pairs(depth))
    }
    ridge = 0.0001 * sum(matrix[i, i] for i in range(depth)) / depth
    for i in range(depth):
        matrix[i, i] = matrix[i, i] + ridge
    inverse = []
    for step in range(depth):
        inverse.append(1.0 / matrix[step, step])
        for i in range(step + 1, depth):
            factor = matrix[step, i] * inverse[step]
            for l in range(i, depth + 1):
                matrix[i, l] = matrix[i, l] - factor * matrix[step, l]
    weights = [None] * depth
    for i in reversed(range(depth)):
        value = matrix[i, depth]
        for l in range(i + 1, depth):
            value = value - matrix[i, l] * weights[l]
        weights[i] = value * inverse[i]
    row = lax.broadcasted_iota(jnp.int32, (depth, LANES), 0)
    weight = weights[0]
    for i in range(1, depth):
        weight = jnp.where(row == i, weights[i], weight)
    for start in range(0, own, LANES):
        lanes = slice(start, start + LANES)
        for at, (past, gap, out) in enumerate(((past_u, gap_u, new_u), (past_w, gap_w, new_w))):
            for c in range(3):
                value = jnp.broadcast_to(last[3 * at + c : 3 * at + c + 1, lanes], (depth, LANES))
                change = weight * (value - past[c, :, lanes] - gap[c, :, lanes])
                out[c : c + 1, lanes] = value[0:1] - jnp.sum(change, axis=0, keepdims=True)


def per_device(
    strain_map,
    corner_nodes,
    counts,
    seam_nodes,
    velocity,
    dual_state,
    nodal_load,
    mobility,
    past_dual,
    past_dual_gap,
    past_velocity,
    past_velocity_gap,
):
    own = velocity.shape[1]
    halves = own // LANES
    blocks = lax.axis_size("dom")
    sectors = lax.axis_size("sector")
    depth = past_dual.shape[0]
    seam_rows = seam_nodes.shape[1] // own
    mobility = mobility.reshape(1, own)
    past_dual, past_dual_gap, past_velocity, past_velocity_gap = (
        value.transpose(1, 0, 2) for value in (past_dual, past_dual_gap, past_velocity, past_velocity_gap)
    )

    def send(value, target):
        return lax.ppermute(value, "sector", [(i, target(i) % sectors) for i in range(sectors)])

    def swap(value, bits):
        return lax.ppermute(value, "dom", [(i, i ^ bits) for i in range(blocks)])

    ahead = call(nodes_kernel, f32(8 + seam_rows, own), (velocity, mobility, seam_nodes))
    ahead = send(ahead, lambda i: i - 1)
    message = call(
        functools.partial(message_kernel, own * blocks),
        f32(ROWS, own),
        (counts, ahead, corner_nodes, strain_map, dual_state, velocity, nodal_load, mobility),
        scalars=1,
    )
    pieces = {0: message}
    for bits in range(blocks - 2, 0, -2):
        pieces[bits] = swap(message, bits)
    history = call(history_kernel, f32(6 * depth, own), (message, past_dual_gap, past_velocity_gap), loose=1)
    slots = [0]
    bits = blocks // 2
    history_in = swap(history, bits)
    for even in range(0, blocks, 2):
        pieces[even + 1] = swap(pieces[even], 1)
    sector = f32(3, blocks, own)
    work = [
        pltpu.VMEM((6, blocks, own), jnp.float32),
        pltpu.VMEM((3 * SPLITS, 4, blocks, own), jnp.float32),
    ]
    state, index, to_near, to_far = call(
        functools.partial(first_kernel, blocks),
        (f32(KEPT, blocks, own), jax.ShapeDtypeStruct((4, blocks, own), jnp.int32), sector, sector),
        tuple(pieces[block] for block in range(blocks)),
        scratch=[pltpu.VMEM((halves, blocks * ROWS, LANES), jnp.float32), *work],
    )
    from_far = send(to_far, lambda i: i + 1 if i % 2 else i - 1)
    from_near = send(to_near, lambda i: i ^ 1)
    after = to_near
    while True:
        history = call(join_kernel, f32(2 * history.shape[0], own), (after, history, history_in), loose=1)
        slots += [slot ^ bits for slot in slots]
        bits //= 2
        if bits == 1:
            break
        history_in = swap(history, bits)
        after = from_near if bits == 2 else to_near
    force_next, keep = call(
        second_kernel,
        (sector, f32(12, blocks, own)),
        (state, index, to_near, to_far, from_near, from_far),
        scratch=work,
    )
    from_prev = send(force_next, lambda i: i + 1)
    history_in = swap(history, 1)
    count = -(-len(pairs(depth)) // 8) * 8
    part, last = call(
        functools.partial(gram_kernel, depth, (tuple(slots), tuple(slot ^ 1 for slot in slots))),
        (f32(count, LANES), f32(8, own)),
        (state, keep, from_prev, history, history_in),
        scratch=[pltpu.VMEM((halves, blocks * 6 * depth, LANES), jnp.float32)],
    )
    bits = 1
    other = send(part, lambda i: i ^ 1)
    while 2 * bits < sectors:
        bits *= 2
        part = call(add_kernel, f32(count, LANES), (part, other))
        other = send(part, lambda i: i ^ bits)
    return call(
        functools.partial(solve_kernel, depth),
        (f32(3, own), f32(3, own)),
        (part, other, last, past_dual, past_dual_gap, past_velocity, past_velocity_gap),
        scratch=[pltpu.VMEM((count, LANES), jnp.float32)],
    )


def solution(mesh):
    in_specs = (
        P(None, ("sector", "dom")),
        P(None, ("sector", "dom")),
        P(("sector", "dom")),
        P("sector", None),
        P(None, ("sector", "dom")),
        P(None, ("sector", "dom")),
        P(None, ("sector", "dom")),
        P(("sector", "dom")),
        P(None, None, ("sector", "dom")),
        P(None, None, ("sector", "dom")),
        P(None, None, ("sector", "dom")),
        P(None, None, ("sector", "dom")),
    )
    out_specs = (P(None, ("sector", "dom")), P(None, ("sector", "dom")))
    return jax.shard_map(
        per_device, mesh=mesh, in_specs=in_specs, out_specs=out_specs, check_vma=False
    )
```

```python
import functools
import itertools

import jax
import jax.numpy as jnp
from jax import lax
from jax.experimental import pallas as pl
from jax.experimental.pallas import tpu as pltpu
from jax.sharding import PartitionSpec as P

LANES = 128
VMEM_LIMIT = 24 * 1024 * 1024

STRAIN, DUAL, STEP, SPEED, LOAD, NEXT_STEP, NEXT_SPEED, INDEX, ROWS = 0, 36, 39, 40, 43, 46, 48, 51, 56
KEPT_NEXT_STEP, KEPT_LOAD, KEPT = 40, 41, 44
SPLITS = 2


def vmem():
    return pl.BlockSpec(memory_space=pltpu.VMEM)


def smem():
    return pl.BlockSpec(memory_space=pltpu.SMEM)


def call(kernel, outs, args, scalars=0, loose=0, scratch=()):
    return pl.pallas_call(
        kernel,
        out_shape=outs,
        in_specs=[smem()] * scalars
        + [pl.BlockSpec(memory_space=pl.ANY)] * loose
        + [vmem()] * (len(args) - scalars - loose),
        out_specs=jax.tree.map(lambda _: vmem(), outs),
        scratch_shapes=list(scratch),
        compiler_params=pltpu.CompilerParams(vmem_limit_bytes=VMEM_LIMIT),
    )(*args)


def f32(*shape):
    return jax.ShapeDtypeStruct(shape, jnp.float32)


def repeat(blocks, body, init):
    if blocks == 8:
        return body(slice(0, 8), 0, init)
    return lax.fori_loop(
        0, blocks // 8, lambda step, carry: body(pl.ds(pl.multiple_of(8 * step, 8), 8), 8 * step, carry), init
    )


def project_cone(trial):
    center = 0.5 * (trial[0] + trial[1])
    spread = 0.5 * (trial[0] - trial[1])
    shear = trial[2]
    radius = jnp.sqrt(spread * spread + shear * shear)
    upper = center + radius
    lower = center - radius
    iso_part = 0.5 * (jnp.maximum(upper, 0.0) + jnp.maximum(lower, 0.0))
    factor = jnp.clip((center + radius) / (2.0 * jnp.maximum(radius, 0.05)), 0.0, 1.0)
    return (iso_part + factor * spread, iso_part - factor * spread, factor * shear)


def base_kernel(counts, strain, dual, speed, load, mobility, base):
    own = speed.shape[1]
    slot = lax.broadcasted_iota(jnp.int32, (1, own), 1)
    alive = (slot < counts[0]).astype(jnp.float32)
    base[STRAIN:DUAL, :] = strain[...] * alive
    base[DUAL : DUAL + 3, :] = dual[...] * alive
    base[STEP : STEP + 1, :] = mobility[...]
    base[SPEED : SPEED + 3, :] = speed[...]
    base[LOAD : LOAD + 3, :] = load[...]
    base[LOAD + 3 :, :] = jnp.zeros((base.shape[0] - LOAD - 3, own), jnp.float32)


def message_kernel(sector_nodes, ahead, corners, base, message):
    own = corners.shape[1]
    halves = own // LANES
    message[:NEXT_STEP, :] = base[:NEXT_STEP, :]
    message[NEXT_STEP : NEXT_STEP + 1, :] = ahead[3:4, :]
    message[NEXT_STEP + 1 : NEXT_SPEED, :] = jnp.zeros((1, own), jnp.float32)
    message[NEXT_SPEED : NEXT_SPEED + 3, :] = ahead[0:3, :]
    message[ROWS - 1 : ROWS, :] = jnp.zeros((1, own), jnp.float32)
    corner = jnp.concatenate([corners[:, h * LANES : (h + 1) * LANES] for h in range(halves)], axis=0)
    seam_rows = ahead.shape[0] - 8
    place = jnp.clip(corner - sector_nodes, 0, seam_rows * own - 1)
    high, low = place // LANES, place % LANES
    found = jnp.zeros(corner.shape, jnp.float32)
    for row in range(seam_rows):
        for h in range(halves):
            table = jnp.broadcast_to(ahead[8 + row : 9 + row, h * LANES : (h + 1) * LANES], corner.shape)
            value = jnp.take_along_axis(table, low, axis=1, mode="promise_in_bounds")
            found = jnp.where(high == row * halves + h, value, found)
    node = jnp.where(corner < sector_nodes, corner.astype(jnp.float32), found + float(sector_nodes))
    for h in range(halves):
        message[INDEX : INDEX + 4, h * LANES : (h + 1) * LANES] = node[4 * h : 4 * h + 4]


def history_kernel(after, gap_w, gap_u, history):
    depth = gap_w.shape[1]
    for c in range(3):
        history[depth * c : depth * (c + 1), :] = gap_w[c]
        history[depth * (3 + c) : depth * (4 + c), :] = gap_u[c]


def join_kernel(after, left, right, joined):
    rows = left.shape[0]
    joined[:rows, :] = left[...]
    joined[rows:, :] = right[...]


def sweep(strain_row, index, table, terms, dual):
    blocks, own = index.shape[1:]
    halves = own // LANES
    here = lax.axis_index("dom")
    row = lax.broadcasted_iota(jnp.int32, (blocks, LANES), 0)
    left_block = ((row ^ here) - 1) ^ here
    right_block = ((row ^ here) + 1) ^ here

    def wide(j, group, block, part):
        piece = table[j, group, part * LANES : (part + 1) * LANES][block : block + 1]
        return jnp.broadcast_to(piece, (blocks, LANES))

    def take_sides(group, first, sides):
        left, right = (list(side) for side in sides)
        for block in range(8):
            for j in range(3):
                left[j] = jnp.where(left_block == first + block, wide(j, group, block, halves - 1), left[j])
                right[j] = jnp.where(right_block == first + block, wide(j, group, block, 0), right[j])
        return tuple(left), tuple(right)

    blank = tuple(jnp.zeros((blocks, LANES), jnp.float32) for _ in range(3))
    left, right = repeat(blocks, take_sides, (blank, blank))
    speed = []
    for k in range(4):
        parts = []
        for h in range(halves):
            number = index[k, :, h * LANES : (h + 1) * LANES]
            high, low = number // LANES, number % LANES

            def take(value):
                return jnp.take_along_axis(value, low, axis=1, mode="promise_in_bounds")

            found = [take(table[j, :, 0:LANES]) for j in range(3)]
            for part in range(1, halves):
                mask = high % halves == part
                found = [
                    jnp.where(mask, take(table[j, :, part * LANES : (part + 1) * LANES]), found[j]) for j in range(3)
                ]
            mask = number // own == left_block
            found = [jnp.where(mask, take(left[j]), found[j]) for j in range(3)]
            mask = number // own == right_block
            found = [jnp.where(mask, take(right[j]), found[j]) for j in range(3)]

            def take_group(group, first, found):
                for part, block in itertools.product(range(halves), range(8)):
                    mask = high == (blocks + first + block) * halves + part
                    found = [jnp.where(mask, take(wide(3 + j, group, block, part)), found[j]) for j in range(3)]
                return tuple(found)

            parts.append(repeat(blocks, take_group, tuple(found)))
        speed.append([jnp.concatenate([found[j] for found in parts], axis=1) for j in range(3)])
    rate = []
    for c in range(3):
        total = None
        for k in range(4):
            for j in range(3):
                term = strain_row(12 * c + 3 * k + j) * speed[k][j]
                total = term if total is None else total + term
        rate.append(total)
    trial = [rate[c] + dual[c] for c in range(3)]
    cone = project_cone(trial)
    dual_next = [trial[c] - cone[c] for c in range(3)]
    misfit = [rate[c] - cone[c] + dual_next[c] for c in range(3)]
    for k in range(4):
        for j in range(3):
            rest = sum(strain_row(12 * c + 3 * k + j) * misfit[c] for c in range(3))
            for split in range(SPLITS):
                term = rest.astype(jnp.bfloat16).astype(jnp.float32)
                terms[SPLITS * j + split, k] = term
                rest = rest - term

    node_rows = 2 * blocks
    iota = lax.broadcasted_iota(jnp.int32, (16, own), 0).astype(jnp.float32)
    low_iota = [(iota + float(16 * g)).astype(jnp.bfloat16) for g in range(own // 16)]
    high_iota = [(iota + float(16 * g)).astype(jnp.bfloat16) for g in range(node_rows // 16)]
    one = jnp.ones((16, own), jnp.bfloat16)
    zero = jnp.zeros((16, own), jnp.bfloat16)

    def spread_row(value):
        return jnp.broadcast_to(value, (16, own)).astype(jnp.bfloat16)

    def add_group(group, first, total):
        for block, k in itertools.product(range(8), range(4)):
            number = index[k, group, :][block : block + 1]
            low_row = spread_row((number % own).astype(jnp.float32))
            high_row = spread_row((number // own).astype(jnp.float32))
            spread = jnp.concatenate([jnp.where(low_row == value, one, zero) for value in low_iota], axis=0)
            masks = [high_row == value for value in high_iota]
            weights = []
            for row in range(3 * SPLITS):
                value = spread_row(terms[row, k, group, :][block : block + 1])
                weights += [jnp.where(mask, value, zero) for mask in masks]
            total += lax.dot_general(
                jnp.concatenate(weights, axis=0),
                spread,
                (((1,), (1,)), ((), ())),
                preferred_element_type=jnp.float32,
            )
        return total

    total = repeat(blocks, add_group, jnp.zeros((3 * SPLITS * node_rows, own), jnp.float32))
    force = [
        sum(total[(SPLITS * j + split) * node_rows : (SPLITS * j + split + 1) * node_rows] for split in range(SPLITS))
        for j in range(3)
    ]
    return dual_next, [value[:blocks] for value in force], [value[blocks:] for value in force]


def stack_blocks(pieces, slots, rows, stack):
    for piece, own_slots in zip(pieces, slots):
        for at, slot in enumerate(own_slots):
            for h in range(stack.shape[0]):
                stack[h, slot * rows : (slot + 1) * rows, :] = piece[
                    at * rows : (at + 1) * rows, h * LANES : (h + 1) * LANES
                ]


def across(stack, row, rows):
    blocks = stack.shape[1] // rows
    return jnp.concatenate(
        [stack[h, pl.ds(row, blocks, stride=rows), :] for h in range(stack.shape[0])], axis=1
    )


def first_kernel(order, *refs):
    blocks = len(order)
    pieces = refs[:blocks]
    state, index, to_near, to_far, stack, table, terms = refs[blocks:]
    own = index.shape[2]
    stack_blocks(pieces, [(block,) for block in order], ROWS, stack)
    flip = lax.axis_index("dom") * own
    even = lax.axis_index("sector") % 2 == 0
    for k in range(4):
        index[k] = across(stack, INDEX + k, ROWS).astype(jnp.int32) ^ flip
    for row in range(36):
        state[row] = across(stack, STRAIN + row, ROWS)
    step = across(stack, STEP, ROWS)
    state[STEP] = step
    state[KEPT_NEXT_STEP] = across(stack, NEXT_STEP, ROWS)
    for j in range(3):
        state[KEPT_LOAD + j] = across(stack, LOAD + j, ROWS)
        table[j] = across(stack, SPEED + j, ROWS)
        table[3 + j] = across(stack, NEXT_SPEED + j, ROWS)
    dual = [across(stack, DUAL + c, ROWS) for c in range(3)]
    dual, force_own, force_next = sweep(lambda row: state[row], index, table, terms, dual)
    for c in range(3):
        state[DUAL + c] = dual[c]
        mine = table[c] - step * (force_own[c] - state[KEPT_LOAD + c])
        to_near[c] = jnp.where(even, force_next[c], mine)
        to_far[c] = jnp.where(even, mine, force_next[c])


def second_kernel(state, index, to_near, to_far, from_far, from_near, out_next, keep, table, terms):
    even = lax.axis_index("sector") % 2 == 0
    step, next_step = state[STEP], state[KEPT_NEXT_STEP]
    for j in range(3):
        near, far = to_near[j], to_far[j]
        near_in, far_in = from_near[j], from_far[j]
        table[j] = jnp.where(even, far, near) - step * jnp.where(even, far_in, near_in)
        table[3 + j] = jnp.where(even, near_in, far_in) - next_step * jnp.where(even, near, far)
    dual = [state[DUAL + c] for c in range(3)]
    dual_next, force_own, force_next = sweep(lambda row: state[row], index, table, terms, dual)
    for c in range(3):
        out_next[c] = force_next[c]
        keep[c] = dual_next[c]
        keep[3 + c] = dual_next[c] - dual[c]
        keep[6 + c] = table[c]
        keep[9 + c] = table[c] - step * (force_own[c] - state[KEPT_LOAD + c])


def pairs(depth):
    return [(i, l) for i in range(depth) for l in range(i, depth + 1)]


def gram_kernel(depth, slots, state, keep, from_prev, left, right, part, last, stack, rows_sum):
    blocks, own = keep.shape[1:]
    halves = own // LANES
    rows = 6 * depth
    stack_blocks((left, right), slots, rows, stack)
    change = []
    for j in range(3):
        after = keep[9 + j] - state[STEP] * from_prev[j]
        change.append(after - keep[6 + j])
        last[j : j + 1, :] = after[0:1]
        last[3 + j : 4 + j, :] = keep[j][0:1]
    last[6:8, :] = jnp.zeros((2, own), jnp.float32)
    sums = {}
    for kind in range(2):
        for c in range(3):
            whole = keep[3 + c] if kind == 0 else change[c]
            for h in range(halves):
                for top in range(0, blocks, 8):
                    moved = whole[top : top + 8, h * LANES : (h + 1) * LANES]
                    gaps = [
                        moved - stack[h, pl.ds(top * rows + depth * (3 * kind + c) + i, 8, stride=rows), :]
                        for i in range(depth)
                    ] + [moved]
                    for i, l in pairs(depth):
                        term = gaps[i] * gaps[l]
                        sums[i, l] = sums[i, l] + term if (i, l) in sums else term
    for at, pair in enumerate(pairs(depth)):
        rows_sum[at : at + 1, :] = jnp.sum(sums[pair], axis=0, keepdims=True)
    count = len(pairs(depth))
    if rows_sum.shape[0] > count:
        rows_sum[count:, :] = jnp.zeros((rows_sum.shape[0] - count, LANES), jnp.float32)
    whole = jnp.broadcast_to(jnp.sum(rows_sum[...], axis=1, keepdims=True), rows_sum.shape)
    lane = lax.broadcasted_iota(jnp.int32, (8, LANES), 1)
    out = whole[0:8]
    for group in range(1, rows_sum.shape[0] // 8):
        out = jnp.where(lane == group, whole[8 * group : 8 * group + 8], out)
    part[...] = out


def solve_kernel(depth, *refs):
    parts = refs[:-8]
    last, past_w, gap_w, past_u, gap_u, new_u, new_w, total = refs[-8:]
    own = last.shape[1]
    tile = parts[0][...]
    for other in parts[1:]:
        tile = tile + other[...]
    for group in range(total.shape[0] // 8):
        total[8 * group : 8 * group + 8, :] = jnp.broadcast_to(tile[:, group : group + 1], (8, LANES))
    matrix = {
        pair: jnp.broadcast_to(total[at : at + 1, :], (depth, LANES)) for at, pair in enumerate(pairs(depth))
    }
    ridge = 0.0001 * sum(matrix[i, i] for i in range(depth)) / depth
    for i in range(depth):
        matrix[i, i] = matrix[i, i] + ridge
    inverse = []
    for step in range(depth):
        inverse.append(1.0 / matrix[step, step])
        for i in range(step + 1, depth):
            factor = matrix[step, i] * inverse[step]
            for l in range(i, depth + 1):
                matrix[i, l] = matrix[i, l] - factor * matrix[step, l]
    weights = [None] * depth
    for i in reversed(range(depth)):
        value = matrix[i, depth]
        for l in range(i + 1, depth):
            value = value - matrix[i, l] * weights[l]
        weights[i] = value * inverse[i]
    row = lax.broadcasted_iota(jnp.int32, (depth, LANES), 0)
    weight = weights[0]
    for i in range(1, depth):
        weight = jnp.where(row == i, weights[i], weight)
    for start in range(0, own, LANES):
        lanes = slice(start, start + LANES)
        for at, (past, gap, out) in enumerate(((past_u, gap_u, new_u), (past_w, gap_w, new_w))):
            for c in range(3):
                value = jnp.broadcast_to(last[3 * at + c : 3 * at + c + 1, lanes], (depth, LANES))
                change = weight * (value - past[c, :, lanes] - gap[c, :, lanes])
                out[c : c + 1, lanes] = value[0:1] - jnp.sum(change, axis=0, keepdims=True)


def per_device(
    strain_map,
    corner_nodes,
    counts,
    seam_nodes,
    velocity,
    dual_state,
    nodal_load,
    mobility,
    past_dual,
    past_dual_gap,
    past_velocity,
    past_velocity_gap,
):
    own = velocity.shape[1]
    halves = own // LANES
    blocks = lax.axis_size("dom")
    sectors = lax.axis_size("sector")
    depth = past_dual.shape[0]
    seam_rows = seam_nodes.shape[1] // own
    mobility = mobility.reshape(1, own)
    past_dual, past_dual_gap, past_velocity, past_velocity_gap = (
        value.transpose(1, 0, 2) for value in (past_dual, past_dual_gap, past_velocity, past_velocity_gap)
    )

    def send(value, target):
        return lax.ppermute(value, "sector", [(i, target(i) % sectors) for i in range(sectors)])

    def swap(value, bits):
        return lax.ppermute(value, "dom", [(i, i ^ bits) for i in range(blocks)])

    ahead = jnp.concatenate(
        [velocity, mobility, jnp.zeros((4, own), jnp.float32), seam_nodes.reshape(seam_rows, own).astype(jnp.float32)],
        axis=0,
    )
    base = call(
        base_kernel,
        f32(NEXT_STEP + 2, own),
        (counts, strain_map, dual_state, velocity, nodal_load, mobility),
        scalars=1,
    )
    ahead = send(ahead, lambda i: i - 1)
    message = call(functools.partial(message_kernel, own * blocks), f32(ROWS, own), (ahead, corner_nodes, base))
    pieces = {0: message}
    for bits in range(blocks - 2, 0, -2):
        pieces[bits] = swap(message, bits)
    history = call(history_kernel, f32(6 * depth, own), (message, past_dual_gap, past_velocity_gap), loose=1)
    slots = [0]
    bits = blocks // 2
    history_in = swap(history, bits)
    for even in range(0, blocks, 2):
        pieces[even + 1] = swap(pieces[even], 1)
    sector = f32(3, blocks, own)
    order = tuple(reversed(range(blocks)))
    work = [
        pltpu.VMEM((6, blocks, own), jnp.float32),
        pltpu.VMEM((3 * SPLITS, 4, blocks, own), jnp.float32),
    ]
    state, index, to_near, to_far = call(
        functools.partial(first_kernel, order),
        (f32(KEPT, blocks, own), jax.ShapeDtypeStruct((4, blocks, own), jnp.int32), sector, sector),
        tuple(pieces[block] for block in order),
        scratch=[pltpu.VMEM((halves, blocks * ROWS, LANES), jnp.float32), *work],
    )
    from_far = send(to_far, lambda i: i + 1 if i % 2 else i - 1)
    from_near = send(to_near, lambda i: i ^ 1)
    while bits > 2:
        history = call(join_kernel, f32(2 * history.shape[0], own), (to_near, history, history_in), loose=1)
        slots += [slot ^ bits for slot in slots]
        bits //= 2
        history_in = swap(history, bits)
    force_next, keep = call(
        second_kernel,
        (sector, f32(12, blocks, own)),
        (state, index, to_near, to_far, from_far, from_near),
        scratch=work,
    )
    from_prev = send(force_next, lambda i: i + 1)
    history = call(join_kernel, f32(2 * history.shape[0], own), (keep, history, history_in), loose=1)
    slots += [slot ^ bits for slot in slots]
    history_in = swap(history, 1)
    count = -(-len(pairs(depth)) // 8) * 8
    part, last = call(
        functools.partial(gram_kernel, depth, (tuple(slots), tuple(slot ^ 1 for slot in slots))),
        (f32(8, LANES), f32(8, own)),
        (state, keep, from_prev, history, history_in),
        scratch=[
            pltpu.VMEM((halves, blocks * 6 * depth, LANES), jnp.float32),
            pltpu.VMEM((count, LANES), jnp.float32),
        ],
    )
    parts = [part] + [send(part, lambda i: i ^ by) for by in range(sectors - 1, 0, -1)]
    return call(
        functools.partial(solve_kernel, depth),
        (f32(3, own), f32(3, own)),
        (*parts, last, past_dual, past_dual_gap, past_velocity, past_velocity_gap),
        scratch=[pltpu.VMEM((count, LANES), jnp.float32)],
    )


def solution(mesh):
    in_specs = (
        P(None, ("sector", "dom")),
        P(None, ("sector", "dom")),
        P(("sector", "dom")),
        P("sector", None),
        P(None, ("sector", "dom")),
        P(None, ("sector", "dom")),
        P(None, ("sector", "dom")),
        P(("sector", "dom")),
        P(None, None, ("sector", "dom")),
        P(None, None, ("sector", "dom")),
        P(None, None, ("sector", "dom")),
        P(None, None, ("sector", "dom")),
    )
    out_specs = (P(None, ("sector", "dom")), P(None, ("sector", "dom")))
    return jax.shard_map(
        per_device, mesh=mesh, in_specs=in_specs, out_specs=out_specs, check_vma=False
    )
```

```python
import functools
import itertools

import jax
import jax.numpy as jnp
from jax import lax
from jax.experimental import pallas as pl
from jax.experimental.pallas import tpu as pltpu
from jax.sharding import PartitionSpec as P

LANES = 128
VMEM_LIMIT = 24 * 1024 * 1024

STRAIN, DUAL, STEP, SPEED, LOAD, NEXT_STEP, NEXT_SPEED, INDEX, ROWS = 0, 36, 39, 40, 43, 46, 48, 51, 56
KEPT_NEXT_STEP, KEPT_LOAD, KEPT = 40, 41, 44
SPLITS = 2


def vmem():
    return pl.BlockSpec(memory_space=pltpu.VMEM)


def smem():
    return pl.BlockSpec(memory_space=pltpu.SMEM)


def call(kernel, outs, args, scalars=0, loose=0, scratch=()):
    return pl.pallas_call(
        kernel,
        out_shape=outs,
        in_specs=[smem()] * scalars
        + [pl.BlockSpec(memory_space=pl.ANY)] * loose
        + [vmem()] * (len(args) - scalars - loose),
        out_specs=jax.tree.map(lambda _: vmem(), outs),
        scratch_shapes=list(scratch),
        compiler_params=pltpu.CompilerParams(vmem_limit_bytes=VMEM_LIMIT),
    )(*args)


def f32(*shape):
    return jax.ShapeDtypeStruct(shape, jnp.float32)


def repeat(blocks, body, init):
    if blocks == 8:
        return body(slice(0, 8), 0, init)
    return lax.fori_loop(
        0, blocks // 8, lambda step, carry: body(pl.ds(pl.multiple_of(8 * step, 8), 8), 8 * step, carry), init
    )


def project_cone(trial):
    center = 0.5 * (trial[0] + trial[1])
    spread = 0.5 * (trial[0] - trial[1])
    shear = trial[2]
    radius = jnp.sqrt(spread * spread + shear * shear)
    upper = center + radius
    lower = center - radius
    iso_part = 0.5 * (jnp.maximum(upper, 0.0) + jnp.maximum(lower, 0.0))
    factor = jnp.clip((center + radius) / (2.0 * jnp.maximum(radius, 0.05)), 0.0, 1.0)
    return (iso_part + factor * spread, iso_part - factor * spread, factor * shear)


def fetch(pairs, sems):
    copies = [pltpu.make_async_copy(source, target, sems.at[at]) for at, (source, target) in enumerate(pairs)]
    for copy in copies:
        copy.start()
    for copy in copies:
        copy.wait()


def in_hbm(*values):
    return tuple(pltpu.with_memory_space_constraint(value, pltpu.HBM) for value in values)


def pack_kernel(counts, *refs):
    held = refs[8:14]
    fetch(zip(refs[:6], held), refs[14])
    strain, dual, speed, load, mobility, seam = held
    ahead, base = refs[6:8]
    own = speed.shape[1]
    ahead[0:3, :] = speed[...]
    ahead[3:4, :] = mobility[...]
    ahead[4:8, :] = jnp.zeros((4, own), jnp.float32)
    for row in range(ahead.shape[0] - 8):
        ahead[8 + row : 9 + row, :] = seam[:, row * own : (row + 1) * own].astype(jnp.float32)
    slot = lax.broadcasted_iota(jnp.int32, (1, own), 1)
    alive = (slot < counts[0]).astype(jnp.float32)
    base[STRAIN:DUAL, :] = strain[...] * alive
    base[DUAL : DUAL + 3, :] = dual[...] * alive
    base[STEP : STEP + 1, :] = mobility[...]
    base[SPEED : SPEED + 3, :] = speed[...]
    base[LOAD : LOAD + 3, :] = load[...]
    base[LOAD + 3 :, :] = jnp.zeros((base.shape[0] - LOAD - 3, own), jnp.float32)


def message_kernel(sector_nodes, after, ahead, corners, base, message):
    own = corners.shape[1]
    halves = own // LANES
    message[:NEXT_STEP, :] = base[:NEXT_STEP, :]
    message[NEXT_STEP : NEXT_STEP + 1, :] = ahead[3:4, :]
    message[NEXT_STEP + 1 : NEXT_SPEED, :] = jnp.zeros((1, own), jnp.float32)
    message[NEXT_SPEED : NEXT_SPEED + 3, :] = ahead[0:3, :]
    message[ROWS - 1 : ROWS, :] = jnp.zeros((1, own), jnp.float32)
    corner = jnp.concatenate([corners[:, h * LANES : (h + 1) * LANES] for h in range(halves)], axis=0)
    seam_rows = ahead.shape[0] - 8
    place = jnp.clip(corner - sector_nodes, 0, seam_rows * own - 1)
    high, low = place // LANES, place % LANES
    found = jnp.zeros(corner.shape, jnp.float32)
    for row in range(seam_rows):
        for h in range(halves):
            table = jnp.broadcast_to(ahead[8 + row : 9 + row, h * LANES : (h + 1) * LANES], corner.shape)
            value = jnp.take_along_axis(table, low, axis=1, mode="promise_in_bounds")
            found = jnp.where(high == row * halves + h, value, found)
    node = jnp.where(corner < sector_nodes, corner.astype(jnp.float32), found + float(sector_nodes))
    for h in range(halves):
        message[INDEX : INDEX + 4, h * LANES : (h + 1) * LANES] = node[4 * h : 4 * h + 4]


def history_kernel(after, gap_w, gap_u, history, sems):
    fetch(((gap_w, history.at[0:3]), (gap_u, history.at[3:6])), sems)


def sweep(strain_row, index, table, terms, dual):
    blocks, own = index.shape[1:]
    halves = own // LANES
    here = lax.axis_index("dom")
    row = lax.broadcasted_iota(jnp.int32, (blocks, LANES), 0)
    left_block = ((row ^ here) - 1) ^ here
    right_block = ((row ^ here) + 1) ^ here

    def wide(j, group, block, part):
        piece = table[j, group, part * LANES : (part + 1) * LANES][block : block + 1]
        return jnp.broadcast_to(piece, (blocks, LANES))

    def take_sides(group, first, sides):
        left, right = (list(side) for side in sides)
        for block in range(8):
            for j in range(3):
                left[j] = jnp.where(left_block == first + block, wide(j, group, block, halves - 1), left[j])
                right[j] = jnp.where(right_block == first + block, wide(j, group, block, 0), right[j])
        return tuple(left), tuple(right)

    blank = tuple(jnp.zeros((blocks, LANES), jnp.float32) for _ in range(3))
    left, right = repeat(blocks, take_sides, (blank, blank))
    speed = []
    for k in range(4):
        parts = []
        for h in range(halves):
            number = index[k, :, h * LANES : (h + 1) * LANES]
            high, low = number // LANES, number % LANES

            def take(value):
                return jnp.take_along_axis(value, low, axis=1, mode="promise_in_bounds")

            found = [take(table[j, :, 0:LANES]) for j in range(3)]
            for part in range(1, halves):
                mask = high % halves == part
                found = [
                    jnp.where(mask, take(table[j, :, part * LANES : (part + 1) * LANES]), found[j]) for j in range(3)
                ]
            mask = number // own == left_block
            found = [jnp.where(mask, take(left[j]), found[j]) for j in range(3)]
            mask = number // own == right_block
            found = [jnp.where(mask, take(right[j]), found[j]) for j in range(3)]

            def take_group(group, first, found):
                for part, block in itertools.product(range(halves), range(8)):
                    mask = high == (blocks + first + block) * halves + part
                    found = [jnp.where(mask, take(wide(3 + j, group, block, part)), found[j]) for j in range(3)]
                return tuple(found)

            parts.append(repeat(blocks, take_group, tuple(found)))
        speed.append([jnp.concatenate([found[j] for found in parts], axis=1) for j in range(3)])
    rate = []
    for c in range(3):
        total = None
        for k in range(4):
            for j in range(3):
                term = strain_row(12 * c + 3 * k + j) * speed[k][j]
                total = term if total is None else total + term
        rate.append(total)
    trial = [rate[c] + dual[c] for c in range(3)]
    cone = project_cone(trial)
    dual_next = [trial[c] - cone[c] for c in range(3)]
    misfit = [rate[c] - cone[c] + dual_next[c] for c in range(3)]
    for k in range(4):
        for j in range(3):
            rest = sum(strain_row(12 * c + 3 * k + j) * misfit[c] for c in range(3))
            for split in range(SPLITS):
                term = rest.astype(jnp.bfloat16).astype(jnp.float32)
                terms[SPLITS * j + split, k] = term
                rest = rest - term

    side_rows = 2 * blocks
    node_rows = halves * side_rows
    iota = lax.broadcasted_iota(jnp.int32, (16, own), 0).astype(jnp.float32)
    low_iota = [(iota + float(16 * g)).astype(jnp.bfloat16) for g in range(LANES // 16)]
    high_iota = [(iota + float(16 * g)).astype(jnp.bfloat16) for g in range(node_rows // 16)]
    one = jnp.ones((16, own), jnp.bfloat16)
    zero = jnp.zeros((16, own), jnp.bfloat16)

    def spread_row(value):
        return jnp.broadcast_to(value, (16, own)).astype(jnp.bfloat16)

    def add_group(group, first, total):
        for block, k in itertools.product(range(8), range(4)):
            number = index[k, group, :][block : block + 1]
            low_row = spread_row((number % LANES).astype(jnp.float32))
            high_row = spread_row((number // own + (number // LANES % halves) * side_rows).astype(jnp.float32))
            spread = jnp.concatenate([jnp.where(low_row == value, one, zero) for value in low_iota], axis=0)
            masks = [high_row == value for value in high_iota]
            weights = []
            for row in range(3 * SPLITS):
                value = spread_row(terms[row, k, group, :][block : block + 1])
                weights += [jnp.where(mask, value, zero) for mask in masks]
            total += lax.dot_general(
                jnp.concatenate(weights, axis=0),
                spread,
                (((1,), (1,)), ((), ())),
                preferred_element_type=jnp.float32,
            )
        return total

    total = repeat(blocks, add_group, jnp.zeros((3 * SPLITS * node_rows, LANES), jnp.float32))
    force = []
    for j in range(3):
        whole = sum(total[(SPLITS * j + split) * node_rows : (SPLITS * j + split + 1) * node_rows] for split in range(SPLITS))
        force.append(jnp.concatenate([whole[h * side_rows : (h + 1) * side_rows] for h in range(halves)], axis=1))
    return dual_next, [value[:blocks] for value in force], [value[blocks:] for value in force]


def stack_blocks(pieces, slots, rows, stack):
    for piece, slot in zip(pieces, slots):
        for h in range(stack.shape[0]):
            stack[h, slot * rows : (slot + 1) * rows, :] = piece[:, h * LANES : (h + 1) * LANES]


def across(stack, row, rows):
    blocks = stack.shape[1] // rows
    return jnp.concatenate(
        [stack[h, pl.ds(row, blocks, stride=rows), :] for h in range(stack.shape[0])], axis=1
    )


def first_kernel(order, *refs):
    blocks = len(order)
    pieces = refs[:blocks]
    state, index, to_near, to_far, stack, table, terms = refs[blocks:]
    own = index.shape[2]
    stack_blocks(pieces, order, ROWS, stack)
    flip = lax.axis_index("dom") * own
    even = lax.axis_index("sector") % 2 == 0
    for k in range(4):
        index[k] = across(stack, INDEX + k, ROWS).astype(jnp.int32) ^ flip
    for row in range(36):
        state[row] = across(stack, STRAIN + row, ROWS)
    step = across(stack, STEP, ROWS)
    state[STEP] = step
    state[KEPT_NEXT_STEP] = across(stack, NEXT_STEP, ROWS)
    for j in range(3):
        state[KEPT_LOAD + j] = across(stack, LOAD + j, ROWS)
        table[j] = across(stack, SPEED + j, ROWS)
        table[3 + j] = across(stack, NEXT_SPEED + j, ROWS)
    dual = [across(stack, DUAL + c, ROWS) for c in range(3)]
    dual, force_own, force_next = sweep(lambda row: state[row], index, table, terms, dual)
    for c in range(3):
        state[DUAL + c] = dual[c]
        mine = table[c] - step * (force_own[c] - state[KEPT_LOAD + c])
        to_near[c] = jnp.where(even, force_next[c], mine)
        to_far[c] = jnp.where(even, mine, force_next[c])


def second_kernel(state, index, to_near, to_far, from_far, from_near, out_next, keep, table, terms):
    even = lax.axis_index("sector") % 2 == 0
    step, next_step = state[STEP], state[KEPT_NEXT_STEP]
    for j in range(3):
        near, far = to_near[j], to_far[j]
        near_in, far_in = from_near[j], from_far[j]
        table[j] = jnp.where(even, far, near) - step * jnp.where(even, far_in, near_in)
        table[3 + j] = jnp.where(even, near_in, far_in) - next_step * jnp.where(even, near, far)
    dual = [state[DUAL + c] for c in range(3)]
    dual_next, force_own, force_next = sweep(lambda row: state[row], index, table, terms, dual)
    for c in range(3):
        out_next[c] = force_next[c]
        keep[c] = dual_next[c]
        keep[3 + c] = dual_next[c] - dual[c]
        keep[6 + c] = table[c]
        keep[9 + c] = table[c] - step * (force_own[c] - state[KEPT_LOAD + c])


def pairs(depth):
    return [(i, l) for i in range(depth) for l in range(i, depth + 1)]


def gram_kernel(depth, state, keep, from_prev, histories, part, last, stack, rows_sum):
    blocks, own = keep.shape[1:]
    halves = own // LANES
    rows = 6 * depth
    here = lax.axis_index("dom")
    for slot, kind, h in itertools.product(range(blocks), range(6), range(halves)):
        start = slot * rows + kind * depth
        stack[h, start : start + depth, :] = histories[slot ^ here, kind, :, h * LANES : (h + 1) * LANES]
    change = []
    for j in range(3):
        after = keep[9 + j] - state[STEP] * from_prev[j]
        change.append(after - keep[6 + j])
        last[j : j + 1, :] = after[0:1]
        last[3 + j : 4 + j, :] = keep[j][0:1]
    last[6:8, :] = jnp.zeros((2, own), jnp.float32)
    sums = {}
    for kind in range(2):
        for c in range(3):
            whole = keep[3 + c] if kind == 0 else change[c]
            for h in range(halves):
                for top in range(0, blocks, 8):
                    moved = whole[top : top + 8, h * LANES : (h + 1) * LANES]
                    gaps = [
                        moved - stack[h, pl.ds(top * rows + depth * (3 * kind + c) + i, 8, stride=rows), :]
                        for i in range(depth)
                    ] + [moved]
                    for i, l in pairs(depth):
                        term = gaps[i] * gaps[l]
                        sums[i, l] = sums[i, l] + term if (i, l) in sums else term
    for at, pair in enumerate(pairs(depth)):
        rows_sum[at : at + 1, :] = jnp.sum(sums[pair], axis=0, keepdims=True)
    count = len(pairs(depth))
    if rows_sum.shape[0] > count:
        rows_sum[count:, :] = jnp.zeros((rows_sum.shape[0] - count, LANES), jnp.float32)
    whole = jnp.broadcast_to(jnp.sum(rows_sum[...], axis=1, keepdims=True), rows_sum.shape)
    lane = lax.broadcasted_iota(jnp.int32, (8, LANES), 1)
    out = whole[0:8]
    for group in range(1, rows_sum.shape[0] // 8):
        out = jnp.where(lane == group, whole[8 * group : 8 * group + 8], out)
    part[...] = out


def solve_kernel(depth, *refs):
    parts = refs[:-8]
    last, past_w, gap_w, past_u, gap_u, new_u, new_w, total = refs[-8:]
    own = last.shape[1]
    tile = parts[0][...]
    for other in parts[1:]:
        tile = tile + other[...]
    for group in range(total.shape[0] // 8):
        total[8 * group : 8 * group + 8, :] = jnp.broadcast_to(tile[:, group : group + 1], (8, LANES))
    matrix = {
        pair: jnp.broadcast_to(total[at : at + 1, :], (depth, LANES)) for at, pair in enumerate(pairs(depth))
    }
    ridge = 0.0001 * sum(matrix[i, i] for i in range(depth)) / depth
    for i in range(depth):
        matrix[i, i] = matrix[i, i] + ridge
    inverse = []
    for step in range(depth):
        inverse.append(1.0 / matrix[step, step])
        for i in range(step + 1, depth):
            factor = matrix[step, i] * inverse[step]
            for l in range(i, depth + 1):
                matrix[i, l] = matrix[i, l] - factor * matrix[step, l]
    weights = [None] * depth
    for i in reversed(range(depth)):
        value = matrix[i, depth]
        for l in range(i + 1, depth):
            value = value - matrix[i, l] * weights[l]
        weights[i] = value * inverse[i]
    row = lax.broadcasted_iota(jnp.int32, (depth, LANES), 0)
    weight = weights[0]
    for i in range(1, depth):
        weight = jnp.where(row == i, weights[i], weight)
    for start in range(0, own, LANES):
        lanes = slice(start, start + LANES)
        for at, (past, gap, out) in enumerate(((past_u, gap_u, new_u), (past_w, gap_w, new_w))):
            for c in range(3):
                value = jnp.broadcast_to(last[3 * at + c : 3 * at + c + 1, lanes], (depth, LANES))
                change = weight * (value - past[c, :, lanes] - gap[c, :, lanes])
                out[c : c + 1, lanes] = value[0:1] - jnp.sum(change, axis=0, keepdims=True)


def per_device(
    strain_map,
    corner_nodes,
    counts,
    seam_nodes,
    velocity,
    dual_state,
    nodal_load,
    mobility,
    past_dual,
    past_dual_gap,
    past_velocity,
    past_velocity_gap,
):
    own = velocity.shape[1]
    halves = own // LANES
    blocks = lax.axis_size("dom")
    sectors = lax.axis_size("sector")
    depth = past_dual.shape[0]
    seam_rows = seam_nodes.shape[1] // own
    mobility = mobility.reshape(1, own)
    past_dual, past_dual_gap, past_velocity, past_velocity_gap = (
        value.transpose(1, 0, 2) for value in (past_dual, past_dual_gap, past_velocity, past_velocity_gap)
    )

    def send(value, target):
        return lax.ppermute(value, "sector", [(i, target(i) % sectors) for i in range(sectors)])

    def swap(value, bits):
        return lax.ppermute(value, "dom", [(i, i ^ bits) for i in range(blocks)])

    held = (strain_map, dual_state, velocity, nodal_load, mobility, seam_nodes)
    ahead, base = call(
        pack_kernel,
        (f32(8 + seam_rows, own), f32(NEXT_STEP + 2, own)),
        (counts, *in_hbm(*held)),
        scalars=1,
        loose=len(held),
        scratch=[pltpu.VMEM(value.shape, value.dtype) for value in held] + [pltpu.SemaphoreType.DMA((len(held),))],
    )
    history = call(
        history_kernel,
        f32(6, depth, own),
        (ahead, *in_hbm(past_dual_gap, past_velocity_gap)),
        loose=3,
        scratch=[pltpu.SemaphoreType.DMA((2,))],
    )
    ahead = send(ahead, lambda i: i - 1)
    histories = lax.all_gather(history, "dom")
    message = call(functools.partial(message_kernel, own * blocks), f32(ROWS, own), (history, ahead, corner_nodes, base), loose=1)
    pieces = {0: message}
    for apart in range(blocks - 2, 0, -2):
        pieces[apart] = swap(message, apart)
    for even in range(0, blocks, 2):
        pieces[even + 1] = swap(pieces[even], 1)
    sector = f32(3, blocks, own)
    order = tuple(reversed(range(blocks)))
    work = [
        pltpu.VMEM((6, blocks, own), jnp.float32),
        pltpu.VMEM((3 * SPLITS, 4, blocks, own), jnp.float32),
    ]
    state, index, to_near, to_far = call(
        functools.partial(first_kernel, order),
        (f32(KEPT, blocks, own), jax.ShapeDtypeStruct((4, blocks, own), jnp.int32), sector, sector),
        tuple(pieces[block] for block in order),
        scratch=[pltpu.VMEM((halves, blocks * ROWS, LANES), jnp.float32), *work],
    )
    from_far = send(to_far, lambda i: i + 1 if i % 2 else i - 1)
    from_near = send(to_near, lambda i: i ^ 1)
    force_next, keep = call(
        second_kernel,
        (sector, f32(12, blocks, own)),
        (state, index, to_near, to_far, from_far, from_near),
        scratch=work,
    )
    from_prev = send(force_next, lambda i: i + 1)
    count = -(-len(pairs(depth)) // 8) * 8
    part, last = call(
        functools.partial(gram_kernel, depth),
        (f32(8, LANES), f32(8, own)),
        (state, keep, from_prev, histories),
        scratch=[
            pltpu.VMEM((halves, blocks * 6 * depth, LANES), jnp.float32),
            pltpu.VMEM((count, LANES), jnp.float32),
        ],
    )
    parts = [part] + [send(part, lambda i: i ^ by) for by in range(sectors - 1, 0, -1)]
    return call(
        functools.partial(solve_kernel, depth),
        (f32(3, own), f32(3, own)),
        (*parts, last, past_dual, past_dual_gap, past_velocity, past_velocity_gap),
        scratch=[pltpu.VMEM((count, LANES), jnp.float32)],
    )


def solution(mesh):
    in_specs = (
        P(None, ("sector", "dom")),
        P(None, ("sector", "dom")),
        P(("sector", "dom")),
        P("sector", None),
        P(None, ("sector", "dom")),
        P(None, ("sector", "dom")),
        P(None, ("sector", "dom")),
        P(("sector", "dom")),
        P(None, None, ("sector", "dom")),
        P(None, None, ("sector", "dom")),
        P(None, None, ("sector", "dom")),
        P(None, None, ("sector", "dom")),
    )
    out_specs = (P(None, ("sector", "dom")), P(None, ("sector", "dom")))
    return jax.shard_map(
        per_device, mesh=mesh, in_specs=in_specs, out_specs=out_specs, check_vma=False
    )
```

```python
import functools
import itertools

import jax
import jax.numpy as jnp
from jax import lax
from jax.experimental import pallas as pl
from jax.experimental.pallas import tpu as pltpu
from jax.sharding import PartitionSpec as P

LANES = 128
VMEM_LIMIT = 24 * 1024 * 1024

STRAIN, DUAL, STEP, SPEED, LOAD, NEXT_STEP, NEXT_SPEED, INDEX, ROWS = 0, 36, 39, 40, 43, 46, 48, 51, 56
KEPT_NEXT_STEP, KEPT_LOAD, KEPT = 40, 41, 44
SPLITS = 2


def vmem():
    return pl.BlockSpec(memory_space=pltpu.VMEM)


def smem():
    return pl.BlockSpec(memory_space=pltpu.SMEM)


def call(kernel, outs, args, scalars=0, loose=0, scratch=()):
    return pl.pallas_call(
        kernel,
        out_shape=outs,
        in_specs=[smem()] * scalars
        + [pl.BlockSpec(memory_space=pl.ANY)] * loose
        + [vmem()] * (len(args) - scalars - loose),
        out_specs=jax.tree.map(lambda _: vmem(), outs),
        scratch_shapes=list(scratch),
        compiler_params=pltpu.CompilerParams(vmem_limit_bytes=VMEM_LIMIT),
    )(*args)


def f32(*shape):
    return jax.ShapeDtypeStruct(shape, jnp.float32)


def repeat(blocks, body, init):
    if blocks == 8:
        return body(slice(0, 8), 0, init)
    return lax.fori_loop(
        0, blocks // 8, lambda step, carry: body(pl.ds(pl.multiple_of(8 * step, 8), 8), 8 * step, carry), init
    )


def project_cone(trial):
    center = 0.5 * (trial[0] + trial[1])
    spread = 0.5 * (trial[0] - trial[1])
    shear = trial[2]
    radius = jnp.sqrt(spread * spread + shear * shear)
    upper = center + radius
    lower = center - radius
    iso_part = 0.5 * (jnp.maximum(upper, 0.0) + jnp.maximum(lower, 0.0))
    factor = jnp.clip((center + radius) / (2.0 * jnp.maximum(radius, 0.05)), 0.0, 1.0)
    return (iso_part + factor * spread, iso_part - factor * spread, factor * shear)


def fetch(pairs, sems):
    copies = [pltpu.make_async_copy(source, target, sems.at[at]) for at, (source, target) in enumerate(pairs)]
    for copy in copies:
        copy.start()
    for copy in copies:
        copy.wait()


def in_hbm(*values):
    return tuple(pltpu.with_memory_space_constraint(value, pltpu.HBM) for value in values)


def pack_kernel(counts, *refs):
    count = (len(refs) - 3) // 2
    sources, (ahead, carry), held, sems = refs[: count + 1], refs[count + 1 : count + 3], refs[count + 3 : -1], refs[-1]
    gap_w, gap_u = sources[-2:]
    depth = gap_w.shape[1]
    pairs = list(zip(sources[:-2], held))
    for c in range(3):
        for kind, gap in enumerate((gap_w, gap_u)):
            pairs.append((gap.at[c], carry.at[pl.ds(ROWS + depth * (3 * kind + c), depth)]))
    fetch(pairs, sems)
    strain, dual, speed, load, mobility, seam, corners = held
    own = speed.shape[1]
    ahead[0:3, :] = speed[...]
    ahead[3:4, :] = mobility[...]
    ahead[4:8, :] = jnp.zeros((4, own), jnp.float32)
    for row in range(ahead.shape[0] - 8):
        ahead[8 + row : 9 + row, :] = seam[:, row * own : (row + 1) * own].astype(jnp.float32)
    slot = lax.broadcasted_iota(jnp.int32, (1, own), 1)
    alive = (slot < counts[0]).astype(jnp.float32)
    carry[STRAIN:DUAL, :] = strain[...] * alive
    carry[DUAL : DUAL + 3, :] = dual[...] * alive
    carry[STEP : STEP + 1, :] = mobility[...]
    carry[SPEED : SPEED + 3, :] = speed[...]
    carry[LOAD : LOAD + 3, :] = load[...]
    carry[NEXT_STEP:INDEX, :] = jnp.zeros((INDEX - NEXT_STEP, own), jnp.float32)
    carry[INDEX : INDEX + 4, :] = corners[...].astype(jnp.float32)
    carry[INDEX + 4 : ROWS, :] = jnp.zeros((ROWS - INDEX - 4, own), jnp.float32)


def message_kernel(moved, sector_nodes, ahead_own, ahead_in, carry_own, carry_in, message, wide):
    own = message.shape[1]
    halves = own // LANES
    place = lax.axis_index("sector")
    ahead, carry = ahead_in[...], carry_own[...]
    for sector, (stays, comes) in enumerate(moved):
        if stays:
            ahead = jnp.where(place == sector, ahead_own[...], ahead)
        if comes:
            carry = jnp.where(place == sector, carry_in[...], carry)
    wide[:NEXT_STEP, :] = carry[:NEXT_STEP]
    wide[NEXT_STEP : NEXT_STEP + 1, :] = ahead[3:4]
    wide[NEXT_STEP + 1 : NEXT_SPEED, :] = jnp.zeros((1, own), jnp.float32)
    wide[NEXT_SPEED : NEXT_SPEED + 3, :] = ahead[0:3]
    wide[ROWS - 1 :, :] = carry[ROWS - 1 :]
    corners = carry[INDEX : INDEX + 4].astype(jnp.int32)
    corner = jnp.concatenate([corners[:, h * LANES : (h + 1) * LANES] for h in range(halves)], axis=0)
    seam_rows = ahead.shape[0] - 8
    spot = jnp.clip(corner - sector_nodes, 0, seam_rows * own - 1)
    high, low = spot // LANES, spot % LANES
    found = jnp.zeros(corner.shape, jnp.float32)
    for row in range(seam_rows):
        for h in range(halves):
            table = jnp.broadcast_to(ahead[8 + row : 9 + row, h * LANES : (h + 1) * LANES], corner.shape)
            value = jnp.take_along_axis(table, low, axis=1, mode="promise_in_bounds")
            found = jnp.where(high == row * halves + h, value, found)
    node = jnp.where(corner < sector_nodes, corner.astype(jnp.float32), found + float(sector_nodes))
    for h in range(halves):
        wide[INDEX : INDEX + 4, h * LANES : (h + 1) * LANES] = node[4 * h : 4 * h + 4]
    message[...] = wide[:ROWS, :]


def pair_kernel(*refs):
    left, right, joined = refs[-3:]
    joined[0] = left[ROWS:, :]
    joined[1] = right[ROWS:, :]


def copy_kernel(after, value, copied):
    copied[...] = value[...]


def join_kernel(left, right, joined):
    count = left.shape[0]
    joined[:count] = left[...]
    joined[count:] = right[...]


def sweep(strain_row, index, table, terms, dual):
    blocks, own = index.shape[1:]
    halves = own // LANES
    here = lax.axis_index("dom")
    row = lax.broadcasted_iota(jnp.int32, (blocks, LANES), 0)
    left_block = ((row ^ here) - 1) ^ here
    right_block = ((row ^ here) + 1) ^ here

    def wide(j, group, block, part):
        piece = table[j, group, part * LANES : (part + 1) * LANES][block : block + 1]
        return jnp.broadcast_to(piece, (blocks, LANES))

    def take_sides(group, first, sides):
        left, right = (list(side) for side in sides)
        for block in range(8):
            for j in range(3):
                left[j] = jnp.where(left_block == first + block, wide(j, group, block, halves - 1), left[j])
                right[j] = jnp.where(right_block == first + block, wide(j, group, block, 0), right[j])
        return tuple(left), tuple(right)

    blank = tuple(jnp.zeros((blocks, LANES), jnp.float32) for _ in range(3))
    left, right = repeat(blocks, take_sides, (blank, blank))
    speed = []
    for k in range(4):
        parts = []
        for h in range(halves):
            number = index[k, :, h * LANES : (h + 1) * LANES]
            high, low = number // LANES, number % LANES

            def take(value):
                return jnp.take_along_axis(value, low, axis=1, mode="promise_in_bounds")

            found = [take(table[j, :, 0:LANES]) for j in range(3)]
            for part in range(1, halves):
                mask = high % halves == part
                found = [
                    jnp.where(mask, take(table[j, :, part * LANES : (part + 1) * LANES]), found[j]) for j in range(3)
                ]
            mask = number // own == left_block
            found = [jnp.where(mask, take(left[j]), found[j]) for j in range(3)]
            mask = number // own == right_block
            found = [jnp.where(mask, take(right[j]), found[j]) for j in range(3)]

            def take_group(group, first, found):
                for part, block in itertools.product(range(halves), range(8)):
                    mask = high == (blocks + first + block) * halves + part
                    found = [jnp.where(mask, take(wide(3 + j, group, block, part)), found[j]) for j in range(3)]
                return tuple(found)

            parts.append(repeat(blocks, take_group, tuple(found)))
        speed.append([jnp.concatenate([found[j] for found in parts], axis=1) for j in range(3)])
    rate = []
    for c in range(3):
        total = None
        for k in range(4):
            for j in range(3):
                term = strain_row(12 * c + 3 * k + j) * speed[k][j]
                total = term if total is None else total + term
        rate.append(total)
    trial = [rate[c] + dual[c] for c in range(3)]
    cone = project_cone(trial)
    dual_next = [trial[c] - cone[c] for c in range(3)]
    misfit = [rate[c] - cone[c] + dual_next[c] for c in range(3)]
    for k in range(4):
        for j in range(3):
            rest = sum(strain_row(12 * c + 3 * k + j) * misfit[c] for c in range(3))
            for split in range(SPLITS):
                term = rest.astype(jnp.bfloat16).astype(jnp.float32)
                terms[SPLITS * j + split, k] = term
                rest = rest - term

    side_rows = 2 * blocks
    node_rows = halves * side_rows
    iota = lax.broadcasted_iota(jnp.int32, (16, own), 0).astype(jnp.float32)
    low_iota = [(iota + float(16 * g)).astype(jnp.bfloat16) for g in range(LANES // 16)]
    high_iota = [(iota + float(16 * g)).astype(jnp.bfloat16) for g in range(node_rows // 16)]
    one = jnp.ones((16, own), jnp.bfloat16)
    zero = jnp.zeros((16, own), jnp.bfloat16)

    def spread_row(value):
        return jnp.broadcast_to(value, (16, own)).astype(jnp.bfloat16)

    def add_group(group, first, total):
        for block, k in itertools.product(range(8), range(4)):
            number = index[k, group, :][block : block + 1]
            low_row = spread_row((number % LANES).astype(jnp.float32))
            high_row = spread_row((number // own + (number // LANES % halves) * side_rows).astype(jnp.float32))
            spread = jnp.concatenate([jnp.where(low_row == value, one, zero) for value in low_iota], axis=0)
            masks = [high_row == value for value in high_iota]
            weights = []
            for row in range(3 * SPLITS):
                value = spread_row(terms[row, k, group, :][block : block + 1])
                weights += [jnp.where(mask, value, zero) for mask in masks]
            total += lax.dot_general(
                jnp.concatenate(weights, axis=0),
                spread,
                (((1,), (1,)), ((), ())),
                preferred_element_type=jnp.float32,
            )
        return total

    total = repeat(blocks, add_group, jnp.zeros((3 * SPLITS * node_rows, LANES), jnp.float32))
    force = []
    for j in range(3):
        whole = sum(total[(SPLITS * j + split) * node_rows : (SPLITS * j + split + 1) * node_rows] for split in range(SPLITS))
        force.append(jnp.concatenate([whole[h * side_rows : (h + 1) * side_rows] for h in range(halves)], axis=1))
    return dual_next, [value[:blocks] for value in force], [value[blocks:] for value in force]


def stack_block(piece, slot, rows, stack):
    for h in range(stack.shape[0]):
        stack[h, slot * rows : (slot + 1) * rows, :] = piece[:rows, h * LANES : (h + 1) * LANES]


def across(stack, row, rows):
    blocks = stack.shape[1] // rows
    return jnp.concatenate(
        [stack[h, pl.ds(row, blocks, stride=rows), :] for h in range(stack.shape[0])], axis=1
    )


def first_kernel(role, order, *refs):
    blocks = len(order)
    pieces = refs[:blocks]
    state, index, to_near, to_far, stack, table, terms = refs[blocks:]
    own = index.shape[2]
    for piece, slot in zip(pieces, order):
        stack_block(piece, slot, ROWS, stack)
    flip = lax.axis_index("dom") * own
    even = role() % 2 == 0
    for k in range(4):
        index[k] = across(stack, INDEX + k, ROWS).astype(jnp.int32) ^ flip
    for row in range(36):
        state[row] = across(stack, STRAIN + row, ROWS)
    step = across(stack, STEP, ROWS)
    state[STEP] = step
    state[KEPT_NEXT_STEP] = across(stack, NEXT_STEP, ROWS)
    for j in range(3):
        state[KEPT_LOAD + j] = across(stack, LOAD + j, ROWS)
        table[j] = across(stack, SPEED + j, ROWS)
        table[3 + j] = across(stack, NEXT_SPEED + j, ROWS)
    dual = [across(stack, DUAL + c, ROWS) for c in range(3)]
    dual, force_own, force_next = sweep(lambda row: state[row], index, table, terms, dual)
    for c in range(3):
        state[DUAL + c] = dual[c]
        mine = table[c] - step * (force_own[c] - state[KEPT_LOAD + c])
        to_near[c] = jnp.where(even, force_next[c], mine)
        to_far[c] = jnp.where(even, mine, force_next[c])


def second_kernel(role, state, index, to_near, to_far, from_far, from_near, out_next, keep, table, terms):
    even = role() % 2 == 0
    step, next_step = state[STEP], state[KEPT_NEXT_STEP]
    for j in range(3):
        near, far = to_near[j], to_far[j]
        near_in, far_in = from_near[j], from_far[j]
        table[j] = jnp.where(even, far, near) - step * jnp.where(even, far_in, near_in)
        table[3 + j] = jnp.where(even, near_in, far_in) - next_step * jnp.where(even, near, far)
    dual = [state[DUAL + c] for c in range(3)]
    dual_next, force_own, force_next = sweep(lambda row: state[row], index, table, terms, dual)
    for c in range(3):
        out_next[c] = force_next[c]
        keep[c] = dual_next[c]
        keep[3 + c] = dual_next[c] - dual[c]
        keep[6 + c] = table[c]
        keep[9 + c] = table[c] - step * (force_own[c] - state[KEPT_LOAD + c])


def pairs(depth):
    return [(i, l) for i in range(depth) for l in range(i, depth + 1)]


def gram_kernel(depth, slots, state, keep, from_prev, *refs):
    blocks, own = keep.shape[1:]
    halves = own // LANES
    rows = 6 * depth
    pieces = refs[: len(slots)]
    part, both, stack, rows_sum = refs[len(slots) :]
    for piece, own_slots in zip(pieces, slots):
        for at, slot in enumerate(own_slots):
            stack_block(piece.at[at] if len(piece.shape) == 3 else piece.at[ROWS:], slot, rows, stack)
    change = []
    for j in range(3):
        after = keep[9 + j] - state[STEP] * from_prev[j]
        change.append(after - keep[6 + j])
        both[j : j + 1, LANES:] = after[0:1]
        both[3 + j : 4 + j, LANES:] = keep[j][0:1]
    both[6:8, LANES:] = jnp.zeros((2, own), jnp.float32)
    sums = {}
    for kind in range(2):
        for c in range(3):
            whole = keep[3 + c] if kind == 0 else change[c]
            for h in range(halves):
                for top in range(0, blocks, 8):
                    moved = whole[top : top + 8, h * LANES : (h + 1) * LANES]
                    gaps = [
                        moved - stack[h, pl.ds(top * rows + depth * (3 * kind + c) + i, 8, stride=rows), :]
                        for i in range(depth)
                    ] + [moved]
                    for i, l in pairs(depth):
                        term = gaps[i] * gaps[l]
                        sums[i, l] = sums[i, l] + term if (i, l) in sums else term
    for at, pair in enumerate(pairs(depth)):
        rows_sum[at : at + 1, :] = jnp.sum(sums[pair], axis=0, keepdims=True)
    count = len(pairs(depth))
    if rows_sum.shape[0] > count:
        rows_sum[count:, :] = jnp.zeros((rows_sum.shape[0] - count, LANES), jnp.float32)
    whole = jnp.broadcast_to(jnp.sum(rows_sum[...], axis=1, keepdims=True), rows_sum.shape)
    lane = lax.broadcasted_iota(jnp.int32, (8, LANES), 1)
    out = whole[0:8]
    for group in range(1, rows_sum.shape[0] // 8):
        out = jnp.where(lane == group, whole[8 * group : 8 * group + 8], out)
    part[...] = out
    both[:, :LANES] = out


def solve_kernel(depth, away, *refs):
    parts = refs[:-7]
    past_w, gap_w, past_u, gap_u, new_u, new_w, total = refs[-7:]
    own = new_u.shape[1]
    tile = parts[0][:, :LANES]
    for other in parts[1:]:
        tile = tile + other[:, :LANES]
    last = parts[0][:, LANES:]
    for sector in away:
        last = jnp.where(lax.axis_index("sector") == sector, parts[1][:, LANES:], last)
    for group in range(total.shape[0] // 8):
        total[8 * group : 8 * group + 8, :] = jnp.broadcast_to(tile[:, group : group + 1], (8, LANES))
    matrix = {
        pair: jnp.broadcast_to(total[at : at + 1, :], (depth, LANES)) for at, pair in enumerate(pairs(depth))
    }
    ridge = 0.0001 * sum(matrix[i, i] for i in range(depth)) / depth
    for i in range(depth):
        matrix[i, i] = matrix[i, i] + ridge
    inverse = []
    for step in range(depth):
        inverse.append(1.0 / matrix[step, step])
        for i in range(step + 1, depth):
            factor = matrix[step, i] * inverse[step]
            for l in range(i, depth + 1):
                matrix[i, l] = matrix[i, l] - factor * matrix[step, l]
    weights = [None] * depth
    for i in reversed(range(depth)):
        value = matrix[i, depth]
        for l in range(i + 1, depth):
            value = value - matrix[i, l] * weights[l]
        weights[i] = value * inverse[i]
    row = lax.broadcasted_iota(jnp.int32, (depth, LANES), 0)
    weight = weights[0]
    for i in range(1, depth):
        weight = jnp.where(row == i, weights[i], weight)
    for start in range(0, own, LANES):
        lanes = slice(start, start + LANES)
        for at, (past, gap, out) in enumerate(((past_u, gap_u, new_u), (past_w, gap_w, new_w))):
            for c in range(3):
                value = jnp.broadcast_to(last[3 * at + c : 3 * at + c + 1, lanes], (depth, LANES))
                change = weight * (value - past[c, :, lanes] - gap[c, :, lanes])
                out[c : c + 1, lanes] = value[0:1] - jnp.sum(change, axis=0, keepdims=True)


def per_device(
    strain_map,
    corner_nodes,
    counts,
    seam_nodes,
    velocity,
    dual_state,
    nodal_load,
    mobility,
    past_dual,
    past_dual_gap,
    past_velocity,
    past_velocity_gap,
):
    own = velocity.shape[1]
    halves = own // LANES
    blocks = lax.axis_size("dom")
    sectors = lax.axis_size("sector")
    depth = past_dual.shape[0]
    seam_rows = seam_nodes.shape[1] // own
    mobility = mobility.reshape(1, own)
    past_dual, past_dual_gap, past_velocity, past_velocity_gap = (
        value.transpose(1, 0, 2) for value in (past_dual, past_dual_gap, past_velocity, past_velocity_gap)
    )

    places = (0, 1, 3, 2) if sectors == 4 else tuple(range(sectors))
    moved = tuple((place == (places.index(place) + 1) % sectors, places[place] != place) for place in range(sectors))
    away = tuple(place for place in range(sectors) if places[place] != place)

    def role():
        place = lax.axis_index("sector")
        return place ^ (place >> 1) if away else place

    def to_places(value, pairs):
        return lax.ppermute(value, "sector", [pair for pair in pairs if pair[0] != pair[1]])

    def send(value, target):
        return to_places(value, [(places[i], places[target(i) % sectors]) for i in range(sectors)])

    def swap(value, bits):
        return lax.ppermute(value, "dom", [(i, i ^ bits) for i in range(blocks)])

    history_rows = 6 * depth
    wide_rows = ROWS + history_rows
    held = (strain_map, dual_state, velocity, nodal_load, mobility, seam_nodes, corner_nodes)
    ahead, carry = call(
        pack_kernel,
        (f32(8 + seam_rows, own), f32(wide_rows, own)),
        (counts, *in_hbm(*held, past_dual_gap, past_velocity_gap)),
        scalars=1,
        loose=len(held) + 2,
        scratch=[pltpu.VMEM(value.shape, value.dtype) for value in held]
        + [pltpu.SemaphoreType.DMA((len(held) + 6,))],
    )
    ahead_in = to_places(ahead, [((i + 1) % sectors, places[i]) for i in range(sectors)])
    carry_in = to_places(carry, [(i, places[i]) for i in range(sectors)]) if away else carry
    message, wide = call(
        functools.partial(message_kernel, moved, own * blocks),
        (f32(ROWS, own), f32(wide_rows, own)),
        (ahead, ahead_in, carry, carry_in),
    )
    pieces = {0: wide}
    for apart in range(blocks - 2, 0, -2):
        pieces[apart] = swap(wide if apart == 2 else message, apart)
    for even in range(0, blocks, 2):
        pieces[even + 1] = swap(pieces[even], 1)
    order = tuple(reversed(range(blocks)))
    sector = f32(3, blocks, own)
    work = [
        pltpu.VMEM((6, blocks, own), jnp.float32),
        pltpu.VMEM((3 * SPLITS, 4, blocks, own), jnp.float32),
    ]
    state, index, to_near, to_far = call(
        functools.partial(first_kernel, role, order),
        (f32(KEPT, blocks, own), jax.ShapeDtypeStruct((4, blocks, own), jnp.int32), sector, sector),
        tuple(pieces[block] for block in order),
        scratch=[pltpu.VMEM((halves, blocks * ROWS, LANES), jnp.float32), *work],
    )
    from_far = send(to_far, lambda i: i + 1 if i % 2 else i - 1)
    from_near = send(to_near, lambda i: i ^ 1)
    ahead_of = [pieces[blocks - 2]]
    history = call(pair_kernel, f32(2, history_rows, own), (*ahead_of, wide, pieces[2]), loose=len(ahead_of))
    slots = [(block,) for block in range(4)]
    histories = [pieces[block] for block in range(4)]
    known = (0, 2)
    bits = 4
    while bits < blocks:
        other = swap(history, bits)
        far = tuple(slot ^ bits for slot in known)
        histories.append(other)
        slots.append(far)
        known += far
        bits *= 2
        if bits < blocks:
            history = call(join_kernel, f32(2 * history.shape[0], history_rows, own), (history, other))
    force_next, keep = call(
        functools.partial(second_kernel, role),
        (sector, f32(12, blocks, own)),
        (state, index, to_near, to_far, from_far, from_near),
        scratch=work,
    )
    from_prev = send(force_next, lambda i: i + 1)
    for other, far in list(zip(histories, slots))[4:]:
        histories.append(swap(call(copy_kernel, f32(*other.shape), (keep, other), loose=1), 1))
        slots.append(tuple(slot ^ 1 for slot in far))
    count = -(-len(pairs(depth)) // 8) * 8
    part, both = call(
        functools.partial(gram_kernel, depth, tuple(slots)),
        (f32(8, LANES), f32(8, LANES + own)),
        (state, keep, from_prev, *histories),
        scratch=[
            pltpu.VMEM((halves, blocks * history_rows, LANES), jnp.float32),
            pltpu.VMEM((count, LANES), jnp.float32),
        ],
    )
    parts = [both]
    for by in range(1, sectors):
        parts.append(to_places(both if by == 1 else part, [(i, i ^ by) for i in range(sectors)]))
    return call(
        functools.partial(solve_kernel, depth, away),
        (f32(3, own), f32(3, own)),
        (*parts, past_dual, past_dual_gap, past_velocity, past_velocity_gap),
        scratch=[pltpu.VMEM((count, LANES), jnp.float32)],
    )


def solution(mesh):
    in_specs = (
        P(None, ("sector", "dom")),
        P(None, ("sector", "dom")),
        P(("sector", "dom")),
        P("sector", None),
        P(None, ("sector", "dom")),
        P(None, ("sector", "dom")),
        P(None, ("sector", "dom")),
        P(("sector", "dom")),
        P(None, None, ("sector", "dom")),
        P(None, None, ("sector", "dom")),
        P(None, None, ("sector", "dom")),
        P(None, None, ("sector", "dom")),
    )
    out_specs = (P(None, ("sector", "dom")), P(None, ("sector", "dom")))
    return jax.shard_map(
        per_device, mesh=mesh, in_specs=in_specs, out_specs=out_specs, check_vma=False
    )
```

```python
import functools
import itertools

import jax
import jax.numpy as jnp
from jax import lax
from jax.experimental import pallas as pl
from jax.experimental.pallas import tpu as pltpu
from jax.sharding import PartitionSpec as P

LANES = 128
VMEM_LIMIT = 24 * 1024 * 1024

STRAIN, DUAL, STEP, SPEED, LOAD, NEXT_STEP, NEXT_SPEED, INDEX, ROWS = 0, 36, 39, 40, 43, 46, 47, 50, 56
KEPT_NEXT_STEP, KEPT_LOAD, KEPT = 40, 41, 44
SPLITS = 2


def vmem():
    return pl.BlockSpec(memory_space=pltpu.VMEM)


def smem():
    return pl.BlockSpec(memory_space=pltpu.SMEM)


def call(kernel, outs, args, scalars=0, loose=0, scratch=()):
    return pl.pallas_call(
        kernel,
        out_shape=outs,
        in_specs=[smem()] * scalars
        + [pl.BlockSpec(memory_space=pl.ANY)] * loose
        + [vmem()] * (len(args) - scalars - loose),
        out_specs=jax.tree.map(lambda _: vmem(), outs),
        scratch_shapes=list(scratch),
        compiler_params=pltpu.CompilerParams(vmem_limit_bytes=VMEM_LIMIT),
    )(*args)


def f32(*shape):
    return jax.ShapeDtypeStruct(shape, jnp.float32)


def repeat(blocks, body, init):
    if blocks == 8:
        return body(slice(0, 8), 0, init)
    return lax.fori_loop(
        0, blocks // 8, lambda step, carry: body(pl.ds(pl.multiple_of(8 * step, 8), 8), 8 * step, carry), init
    )


def project_cone(trial):
    center = 0.5 * (trial[0] + trial[1])
    spread = 0.5 * (trial[0] - trial[1])
    shear = trial[2]
    radius = jnp.sqrt(spread * spread + shear * shear)
    upper = center + radius
    lower = center - radius
    iso_part = 0.5 * (jnp.maximum(upper, 0.0) + jnp.maximum(lower, 0.0))
    factor = jnp.clip((center + radius) / (2.0 * jnp.maximum(radius, 0.05)), 0.0, 1.0)
    return (iso_part + factor * spread, iso_part - factor * spread, factor * shear)


def fetch(pairs, sems):
    copies = [pltpu.make_async_copy(source, target, sems.at[at]) for at, (source, target) in enumerate(pairs)]
    for copy in copies:
        copy.start()
    for copy in copies:
        copy.wait()


def in_hbm(*values):
    return tuple(pltpu.with_memory_space_constraint(value, pltpu.HBM) for value in values)


def nodes_kernel(speed_in, mobility_in, seam_in, ahead, speed, mobility, seam, sems):
    fetch(((speed_in, speed), (mobility_in, mobility), (seam_in, seam)), sems)
    own = speed.shape[1]
    ahead[0:3, :] = speed[...]
    ahead[3:4, :] = mobility[...]
    ahead[4:8, :] = jnp.zeros((4, own), jnp.float32)
    for row in range(ahead.shape[0] - 8):
        ahead[8 + row : 9 + row, :] = seam[:, row * own : (row + 1) * own].astype(jnp.float32)


def base_kernel(counts, after, *refs):
    count = (len(refs) - 2) // 2
    sources, base, held, sems = refs[:count], refs[count], refs[count + 1 : -1], refs[-1]
    fetch(zip(sources, held), sems)
    strain, dual, speed, load, mobility, corners = held
    own = speed.shape[1]
    slot = lax.broadcasted_iota(jnp.int32, (1, own), 1)
    alive = (slot < counts[0]).astype(jnp.float32)
    base[STRAIN:DUAL, :] = strain[...] * alive
    base[DUAL : DUAL + 3, :] = dual[...] * alive
    base[STEP : STEP + 1, :] = mobility[...]
    base[SPEED : SPEED + 3, :] = speed[...]
    base[LOAD : LOAD + 3, :] = load[...]
    base[NEXT_STEP:INDEX, :] = jnp.zeros((INDEX - NEXT_STEP, own), jnp.float32)
    base[INDEX : INDEX + 4, :] = corners[...].astype(jnp.float32)


def message_kernel(sector_nodes, after, ahead, base, message, *shorter):
    own = message.shape[1]
    halves = own // LANES
    message[:NEXT_STEP, :] = base[:NEXT_STEP, :]
    message[NEXT_STEP : NEXT_STEP + 1, :] = ahead[3:4, :]
    message[NEXT_SPEED : NEXT_SPEED + 3, :] = ahead[0:3, :]
    message[INDEX + 4 :, :] = jnp.zeros((ROWS - INDEX - 4, own), jnp.float32)
    corners = base[INDEX : INDEX + 4, :].astype(jnp.int32)
    corner = jnp.concatenate([corners[:, h * LANES : (h + 1) * LANES] for h in range(halves)], axis=0)
    seam_rows = ahead.shape[0] - 8
    place = jnp.clip(corner - sector_nodes, 0, seam_rows * own - 1)
    high, low = place // LANES, place % LANES
    found = jnp.zeros(corner.shape, jnp.float32)
    for row in range(seam_rows):
        for h in range(halves):
            table = jnp.broadcast_to(ahead[8 + row : 9 + row, h * LANES : (h + 1) * LANES], corner.shape)
            value = jnp.take_along_axis(table, low, axis=1, mode="promise_in_bounds")
            found = jnp.where(high == row * halves + h, value, found)
    node = jnp.where(corner < sector_nodes, corner.astype(jnp.float32), found + float(sector_nodes))
    for h in range(halves):
        message[INDEX : INDEX + 4, h * LANES : (h + 1) * LANES] = node[4 * h : 4 * h + 4]
    for other in shorter:
        other[...] = message[: other.shape[0], :]


def history_kernel(after, gap_w, gap_u, history, sems):
    fetch(((gap_w, history.at[0:3]), (gap_u, history.at[3:6])), sems)


def join_kernel(after, left, right, joined):
    count = left.shape[0]
    joined[:count] = left[...]
    joined[count:] = right[...]


def sweep(strain_row, index, table, terms, dual):
    blocks, own = index.shape[1:]
    halves = own // LANES
    here = lax.axis_index("dom")
    row = lax.broadcasted_iota(jnp.int32, (blocks, LANES), 0)
    left_block = ((row ^ here) - 1) ^ here
    right_block = ((row ^ here) + 1) ^ here

    def wide(j, group, block, part):
        piece = table[j, group, part * LANES : (part + 1) * LANES][block : block + 1]
        return jnp.broadcast_to(piece, (blocks, LANES))

    def take_sides(group, first, sides):
        left, right = (list(side) for side in sides)
        for block in range(8):
            for j in range(3):
                left[j] = jnp.where(left_block == first + block, wide(j, group, block, halves - 1), left[j])
                right[j] = jnp.where(right_block == first + block, wide(j, group, block, 0), right[j])
        return tuple(left), tuple(right)

    blank = tuple(jnp.zeros((blocks, LANES), jnp.float32) for _ in range(3))
    left, right = repeat(blocks, take_sides, (blank, blank))
    speed = []
    for k in range(4):
        parts = []
        for h in range(halves):
            number = index[k, :, h * LANES : (h + 1) * LANES]
            high, low = number // LANES, number % LANES

            def take(value):
                return jnp.take_along_axis(value, low, axis=1, mode="promise_in_bounds")

            found = [take(table[j, :, 0:LANES]) for j in range(3)]
            for part in range(1, halves):
                mask = high % halves == part
                found = [
                    jnp.where(mask, take(table[j, :, part * LANES : (part + 1) * LANES]), found[j]) for j in range(3)
                ]
            mask = number // own == left_block
            found = [jnp.where(mask, take(left[j]), found[j]) for j in range(3)]
            mask = number // own == right_block
            found = [jnp.where(mask, take(right[j]), found[j]) for j in range(3)]

            def take_group(group, first, found):
                for part, block in itertools.product(range(halves), range(8)):
                    mask = high == (blocks + first + block) * halves + part
                    found = [jnp.where(mask, take(wide(3 + j, group, block, part)), found[j]) for j in range(3)]
                return tuple(found)

            parts.append(repeat(blocks, take_group, tuple(found)))
        speed.append([jnp.concatenate([found[j] for found in parts], axis=1) for j in range(3)])
    rate = []
    for c in range(3):
        total = None
        for k in range(4):
            for j in range(3):
                term = strain_row(12 * c + 3 * k + j) * speed[k][j]
                total = term if total is None else total + term
        rate.append(total)
    trial = [rate[c] + dual[c] for c in range(3)]
    cone = project_cone(trial)
    dual_next = [trial[c] - cone[c] for c in range(3)]
    misfit = [rate[c] - cone[c] + dual_next[c] for c in range(3)]
    for k in range(4):
        for j in range(3):
            rest = sum(strain_row(12 * c + 3 * k + j) * misfit[c] for c in range(3))
            for split in range(SPLITS):
                term = rest.astype(jnp.bfloat16).astype(jnp.float32)
                terms[SPLITS * j + split, k] = term
                rest = rest - term

    side_rows = 2 * blocks
    node_rows = halves * side_rows
    iota = lax.broadcasted_iota(jnp.int32, (16, own), 0).astype(jnp.float32)
    low_iota = [(iota + float(16 * g)).astype(jnp.bfloat16) for g in range(LANES // 16)]
    high_iota = [(iota + float(16 * g)).astype(jnp.bfloat16) for g in range(node_rows // 16)]
    one = jnp.ones((16, own), jnp.bfloat16)
    zero = jnp.zeros((16, own), jnp.bfloat16)

    def spread_row(value):
        return jnp.broadcast_to(value, (16, own)).astype(jnp.bfloat16)

    def add_group(group, first, total):
        for block, k in itertools.product(range(8), range(4)):
            number = index[k, group, :][block : block + 1]
            low_row = spread_row((number % LANES).astype(jnp.float32))
            high_row = spread_row((number // own + (number // LANES % halves) * side_rows).astype(jnp.float32))
            spread = jnp.concatenate([jnp.where(low_row == value, one, zero) for value in low_iota], axis=0)
            masks = [high_row == value for value in high_iota]
            weights = []
            for row in range(3 * SPLITS):
                value = spread_row(terms[row, k, group, :][block : block + 1])
                weights += [jnp.where(mask, value, zero) for mask in masks]
            total += lax.dot_general(
                jnp.concatenate(weights, axis=0),
                spread,
                (((1,), (1,)), ((), ())),
                preferred_element_type=jnp.float32,
            )
        return total

    total = repeat(blocks, add_group, jnp.zeros((3 * SPLITS * node_rows, LANES), jnp.float32))
    force = []
    for j in range(3):
        whole = sum(total[(SPLITS * j + split) * node_rows : (SPLITS * j + split + 1) * node_rows] for split in range(SPLITS))
        force.append(jnp.concatenate([whole[h * side_rows : (h + 1) * side_rows] for h in range(halves)], axis=1))
    return dual_next, [value[:blocks] for value in force], [value[blocks:] for value in force]


def stack_block(piece, slot, rows, stack):
    held = min(rows, piece.shape[0])
    for h in range(stack.shape[0]):
        stack[h, slot * rows : slot * rows + held, :] = piece[:held, h * LANES : (h + 1) * LANES]


def across(stack, row, rows):
    blocks = stack.shape[1] // rows
    return jnp.concatenate(
        [stack[h, pl.ds(row, blocks, stride=rows), :] for h in range(stack.shape[0])], axis=1
    )


def first_kernel(order, *refs):
    blocks = len(order)
    pieces = refs[:blocks]
    state, index, to_near, to_far, stack, table, terms = refs[blocks:]
    own = index.shape[2]
    for piece, slot in zip(pieces, order):
        stack_block(piece, slot, ROWS, stack)
    flip = lax.axis_index("dom") * own
    even = lax.axis_index("sector") % 2 == 0
    for k in range(4):
        index[k] = across(stack, INDEX + k, ROWS).astype(jnp.int32) ^ flip
    for row in range(36):
        state[row] = across(stack, STRAIN + row, ROWS)
    step = across(stack, STEP, ROWS)
    state[STEP] = step
    state[KEPT_NEXT_STEP] = across(stack, NEXT_STEP, ROWS)
    for j in range(3):
        state[KEPT_LOAD + j] = across(stack, LOAD + j, ROWS)
        table[j] = across(stack, SPEED + j, ROWS)
        table[3 + j] = across(stack, NEXT_SPEED + j, ROWS)
    dual = [across(stack, DUAL + c, ROWS) for c in range(3)]
    dual, force_own, force_next = sweep(lambda row: state[row], index, table, terms, dual)
    for c in range(3):
        state[DUAL + c] = dual[c]
        mine = table[c] - step * (force_own[c] - state[KEPT_LOAD + c])
        to_near[c] = jnp.where(even, force_next[c], mine)
        to_far[c] = jnp.where(even, mine, force_next[c])


def second_kernel(state, index, to_near, to_far, from_far, from_near, out_next, keep, table, terms):
    even = lax.axis_index("sector") % 2 == 0
    step, next_step = state[STEP], state[KEPT_NEXT_STEP]
    for j in range(3):
        near, far = to_near[j], to_far[j]
        near_in, far_in = from_near[j], from_far[j]
        table[j] = jnp.where(even, far, near) - step * jnp.where(even, far_in, near_in)
        table[3 + j] = jnp.where(even, near_in, far_in) - next_step * jnp.where(even, near, far)
    dual = [state[DUAL + c] for c in range(3)]
    dual_next, force_own, force_next = sweep(lambda row: state[row], index, table, terms, dual)
    for c in range(3):
        out_next[c] = force_next[c]
        keep[c] = dual_next[c]
        keep[3 + c] = dual_next[c] - dual[c]
        keep[6 + c] = table[c]
        keep[9 + c] = table[c] - step * (force_own[c] - state[KEPT_LOAD + c])


def pairs(depth):
    return [(i, l) for i in range(depth) for l in range(i, depth + 1)]


def gram_kernel(depth, slots, state, keep, from_prev, left, right, part, last, stack, rows_sum):
    blocks, own = keep.shape[1:]
    halves = own // LANES
    rows = 6 * depth
    for piece, own_slots in zip((left, right), slots):
        for at, slot in enumerate(own_slots):
            for kind in range(6):
                for h in range(halves):
                    start = slot * rows + kind * depth
                    stack[h, start : start + depth, :] = piece[at, kind, :, h * LANES : (h + 1) * LANES]
    change = []
    for j in range(3):
        after = keep[9 + j] - state[STEP] * from_prev[j]
        change.append(after - keep[6 + j])
        last[j : j + 1, :] = after[0:1]
        last[3 + j : 4 + j, :] = keep[j][0:1]
    last[6:8, :] = jnp.zeros((2, own), jnp.float32)
    sums = {}
    for kind in range(2):
        for c in range(3):
            whole = keep[3 + c] if kind == 0 else change[c]
            for h in range(halves):
                for top in range(0, blocks, 8):
                    moved = whole[top : top + 8, h * LANES : (h + 1) * LANES]
                    gaps = [
                        moved - stack[h, pl.ds(top * rows + depth * (3 * kind + c) + i, 8, stride=rows), :]
                        for i in range(depth)
                    ] + [moved]
                    for i, l in pairs(depth):
                        term = gaps[i] * gaps[l]
                        sums[i, l] = sums[i, l] + term if (i, l) in sums else term
    for at, pair in enumerate(pairs(depth)):
        rows_sum[at : at + 1, :] = jnp.sum(sums[pair], axis=0, keepdims=True)
    count = len(pairs(depth))
    if rows_sum.shape[0] > count:
        rows_sum[count:, :] = jnp.zeros((rows_sum.shape[0] - count, LANES), jnp.float32)
    whole = jnp.broadcast_to(jnp.sum(rows_sum[...], axis=1, keepdims=True), rows_sum.shape)
    lane = lax.broadcasted_iota(jnp.int32, (8, LANES), 1)
    out = whole[0:8]
    for group in range(1, rows_sum.shape[0] // 8):
        out = jnp.where(lane == group, whole[8 * group : 8 * group + 8], out)
    part[...] = out


def solve_kernel(depth, *refs):
    parts = refs[:-8]
    last, past_w, gap_w, past_u, gap_u, new_u, new_w, total = refs[-8:]
    own = last.shape[1]
    tile = parts[0][...]
    for other in parts[1:]:
        tile = tile + other[...]
    for group in range(total.shape[0] // 8):
        total[8 * group : 8 * group + 8, :] = jnp.broadcast_to(tile[:, group : group + 1], (8, LANES))
    matrix = {
        pair: jnp.broadcast_to(total[at : at + 1, :], (depth, LANES)) for at, pair in enumerate(pairs(depth))
    }
    ridge = 0.0001 * sum(matrix[i, i] for i in range(depth)) / depth
    for i in range(depth):
        matrix[i, i] = matrix[i, i] + ridge
    inverse = []
    for step in range(depth):
        inverse.append(1.0 / matrix[step, step])
        for i in range(step + 1, depth):
            factor = matrix[step, i] * inverse[step]
            for l in range(i, depth + 1):
                matrix[i, l] = matrix[i, l] - factor * matrix[step, l]
    weights = [None] * depth
    for i in reversed(range(depth)):
        value = matrix[i, depth]
        for l in range(i + 1, depth):
            value = value - matrix[i, l] * weights[l]
        weights[i] = value * inverse[i]
    row = lax.broadcasted_iota(jnp.int32, (depth, LANES), 0)
    weight = weights[0]
    for i in range(1, depth):
        weight = jnp.where(row == i, weights[i], weight)
    for start in range(0, own, LANES):
        lanes = slice(start, start + LANES)
        for at, (past, gap, out) in enumerate(((past_u, gap_u, new_u), (past_w, gap_w, new_w))):
            for c in range(3):
                value = jnp.broadcast_to(last[3 * at + c : 3 * at + c + 1, lanes], (depth, LANES))
                change = weight * (value - past[c, :, lanes] - gap[c, :, lanes])
                out[c : c + 1, lanes] = value[0:1] - jnp.sum(change, axis=0, keepdims=True)


def per_device(
    strain_map,
    corner_nodes,
    counts,
    seam_nodes,
    velocity,
    dual_state,
    nodal_load,
    mobility,
    past_dual,
    past_dual_gap,
    past_velocity,
    past_velocity_gap,
):
    own = velocity.shape[1]
    halves = own // LANES
    blocks = lax.axis_size("dom")
    sectors = lax.axis_size("sector")
    depth = past_dual.shape[0]
    seam_rows = seam_nodes.shape[1] // own
    mobility = mobility.reshape(1, own)
    past_dual, past_dual_gap, past_velocity, past_velocity_gap = (
        value.transpose(1, 0, 2) for value in (past_dual, past_dual_gap, past_velocity, past_velocity_gap)
    )

    def send(value, target):
        return lax.ppermute(value, "sector", [(i, target(i) % sectors) for i in range(sectors)])

    def swap(value, bits):
        return lax.ppermute(value, "dom", [(i, i ^ bits) for i in range(blocks)])

    nodes = (velocity, mobility, seam_nodes)
    ahead = call(
        nodes_kernel,
        f32(8 + seam_rows, own),
        in_hbm(*nodes),
        loose=len(nodes),
        scratch=[pltpu.VMEM(value.shape, value.dtype) for value in nodes] + [pltpu.SemaphoreType.DMA((len(nodes),))],
    )
    held = (strain_map, dual_state, velocity, nodal_load, mobility, corner_nodes)
    base = call(
        base_kernel,
        f32(INDEX + 4, own),
        (counts, ahead, *in_hbm(*held)),
        scalars=1,
        loose=len(held) + 1,
        scratch=[pltpu.VMEM(value.shape, value.dtype) for value in held] + [pltpu.SemaphoreType.DMA((len(held),))],
    )
    ahead = send(ahead, lambda i: i - 1)
    history = call(
        history_kernel,
        f32(6, depth, own),
        (base, *in_hbm(past_dual_gap, past_velocity_gap)),
        loose=3,
        scratch=[pltpu.SemaphoreType.DMA((2,))],
    )
    partners = range(2, blocks, 2)
    lengths = [max(INDEX + 4, ROWS - (blocks - 2 - bits) // 2) for bits in partners]
    messages = call(
        functools.partial(message_kernel, own * blocks),
        tuple(f32(rows, own) for rows in sorted(set(lengths), reverse=True)),
        (history, ahead, base),
        loose=1,
    )
    pieces = {0: messages[0]}
    for bits, rows in zip(partners, lengths):
        pieces[bits] = swap(next(value for value in messages if value.shape[0] == rows), bits)
    slots = [0]
    apart, after = 2, pieces[blocks - 2]
    history = history[None]
    history_in = swap(history, apart)
    for even in range(0, blocks, 2):
        pieces[even + 1] = swap(pieces[even], 1)
    sector = f32(3, blocks, own)
    order = tuple(reversed(range(blocks)))
    work = [
        pltpu.VMEM((6, blocks, own), jnp.float32),
        pltpu.VMEM((3 * SPLITS, 4, blocks, own), jnp.float32),
    ]
    state, index, to_near, to_far = call(
        functools.partial(first_kernel, order),
        (f32(KEPT, blocks, own), jax.ShapeDtypeStruct((4, blocks, own), jnp.int32), sector, sector),
        tuple(pieces[block] for block in order),
        scratch=[pltpu.VMEM((halves, blocks * ROWS, LANES), jnp.float32), *work],
    )
    from_far = send(to_far, lambda i: i + 1 if i % 2 else i - 1)
    from_near = send(to_near, lambda i: i ^ 1)
    while 2 * apart < blocks:
        history = call(join_kernel, f32(2 * history.shape[0], 6, depth, own), (after, history, history_in), loose=1)
        slots += [slot ^ apart for slot in slots]
        apart, after = 2 * apart, to_near
        history_in = swap(history, apart)
    force_next, keep = call(
        second_kernel,
        (sector, f32(12, blocks, own)),
        (state, index, to_near, to_far, from_far, from_near),
        scratch=work,
    )
    from_prev = send(force_next, lambda i: i + 1)
    history = call(join_kernel, f32(2 * history.shape[0], 6, depth, own), (keep, history, history_in), loose=1)
    slots += [slot ^ apart for slot in slots]
    history_in = swap(history, 1)
    count = -(-len(pairs(depth)) // 8) * 8
    part, last = call(
        functools.partial(gram_kernel, depth, (tuple(slots), tuple(slot ^ 1 for slot in slots))),
        (f32(8, LANES), f32(8, own)),
        (state, keep, from_prev, history, history_in),
        scratch=[
            pltpu.VMEM((halves, blocks * 6 * depth, LANES), jnp.float32),
            pltpu.VMEM((count, LANES), jnp.float32),
        ],
    )
    parts = [part] + [send(part, lambda i: i ^ by) for by in range(sectors - 1, 0, -1)]
    return call(
        functools.partial(solve_kernel, depth),
        (f32(3, own), f32(3, own)),
        (*parts, last, past_dual, past_dual_gap, past_velocity, past_velocity_gap),
        scratch=[pltpu.VMEM((count, LANES), jnp.float32)],
    )


def solution(mesh):
    in_specs = (
        P(None, ("sector", "dom")),
        P(None, ("sector", "dom")),
        P(("sector", "dom")),
        P("sector", None),
        P(None, ("sector", "dom")),
        P(None, ("sector", "dom")),
        P(None, ("sector", "dom")),
        P(("sector", "dom")),
        P(None, None, ("sector", "dom")),
        P(None, None, ("sector", "dom")),
        P(None, None, ("sector", "dom")),
        P(None, None, ("sector", "dom")),
    )
    out_specs = (P(None, ("sector", "dom")), P(None, ("sector", "dom")))
    return jax.shard_map(
        per_device, mesh=mesh, in_specs=in_specs, out_specs=out_specs, check_vma=False
    )
```

```python
import functools
import itertools

import jax
import jax.numpy as jnp
from jax import lax
from jax.experimental import pallas as pl
from jax.experimental.pallas import tpu as pltpu
from jax.sharding import PartitionSpec as P

LANES = 128
VMEM_LIMIT = 24 * 1024 * 1024

STRAIN, DUAL, STEP, SPEED, LOAD, NEXT_STEP, NEXT_SPEED, INDEX, ROWS = 0, 36, 39, 40, 43, 46, 47, 50, 56
KEPT_NEXT_STEP, KEPT_LOAD, KEPT = 40, 41, 44
SPLITS = 2


def vmem():
    return pl.BlockSpec(memory_space=pltpu.VMEM)


def smem():
    return pl.BlockSpec(memory_space=pltpu.SMEM)


def call(kernel, outs, args, scalars=0, loose=0, scratch=()):
    return pl.pallas_call(
        kernel,
        out_shape=outs,
        in_specs=[smem()] * scalars
        + [pl.BlockSpec(memory_space=pl.ANY)] * loose
        + [vmem()] * (len(args) - scalars - loose),
        out_specs=jax.tree.map(lambda _: vmem(), outs),
        scratch_shapes=list(scratch),
        compiler_params=pltpu.CompilerParams(vmem_limit_bytes=VMEM_LIMIT),
    )(*args)


def f32(*shape):
    return jax.ShapeDtypeStruct(shape, jnp.float32)


def repeat(blocks, body, init):
    if blocks == 8:
        return body(slice(0, 8), 0, init)
    return lax.fori_loop(
        0, blocks // 8, lambda step, carry: body(pl.ds(pl.multiple_of(8 * step, 8), 8), 8 * step, carry), init
    )


def project_cone(trial):
    center = 0.5 * (trial[0] + trial[1])
    spread = 0.5 * (trial[0] - trial[1])
    shear = trial[2]
    radius = jnp.sqrt(spread * spread + shear * shear)
    upper = center + radius
    lower = center - radius
    iso_part = 0.5 * (jnp.maximum(upper, 0.0) + jnp.maximum(lower, 0.0))
    factor = jnp.clip((center + radius) / (2.0 * jnp.maximum(radius, 0.05)), 0.0, 1.0)
    return (iso_part + factor * spread, iso_part - factor * spread, factor * shear)


def fetch(pairs, sems):
    copies = [pltpu.make_async_copy(source, target, sems.at[at]) for at, (source, target) in enumerate(pairs)]
    for copy in copies:
        copy.start()
    for copy in copies:
        copy.wait()


def in_hbm(*values):
    return tuple(pltpu.with_memory_space_constraint(value, pltpu.HBM) for value in values)


def nodes_kernel(speed_in, mobility_in, seam_in, ahead, speed, mobility, seam, sems):
    fetch(((speed_in, speed), (mobility_in, mobility), (seam_in, seam)), sems)
    own = speed.shape[1]
    ahead[0:3, :] = speed[...]
    ahead[3:4, :] = mobility[...]
    ahead[4:8, :] = jnp.zeros((4, own), jnp.float32)
    for row in range(ahead.shape[0] - 8):
        ahead[8 + row : 9 + row, :] = seam[:, row * own : (row + 1) * own].astype(jnp.float32)


def base_kernel(counts, after, *refs):
    count = (len(refs) - 2) // 2
    sources, base, held, sems = refs[:count], refs[count], refs[count + 1 : -1], refs[-1]
    fetch(zip(sources, held), sems)
    strain, dual, speed, load, mobility, corners = held
    own = speed.shape[1]
    slot = lax.broadcasted_iota(jnp.int32, (1, own), 1)
    alive = (slot < counts[0]).astype(jnp.float32)
    base[STRAIN:DUAL, :] = strain[...] * alive
    base[DUAL : DUAL + 3, :] = dual[...] * alive
    base[STEP : STEP + 1, :] = mobility[...]
    base[SPEED : SPEED + 3, :] = speed[...]
    base[LOAD : LOAD + 3, :] = load[...]
    base[NEXT_STEP:INDEX, :] = jnp.zeros((INDEX - NEXT_STEP, own), jnp.float32)
    base[INDEX : INDEX + 4, :] = corners[...].astype(jnp.float32)


def message_kernel(sector_nodes, after, ahead, base, message, *shorter):
    own = message.shape[1]
    halves = own // LANES
    message[:NEXT_STEP, :] = base[:NEXT_STEP, :]
    message[NEXT_STEP : NEXT_STEP + 1, :] = ahead[3:4, :]
    message[NEXT_SPEED : NEXT_SPEED + 3, :] = ahead[0:3, :]
    message[INDEX + 4 :, :] = jnp.zeros((ROWS - INDEX - 4, own), jnp.float32)
    corners = base[INDEX : INDEX + 4, :].astype(jnp.int32)
    corner = jnp.concatenate([corners[:, h * LANES : (h + 1) * LANES] for h in range(halves)], axis=0)
    seam_rows = ahead.shape[0] - 8
    place = jnp.clip(corner - sector_nodes, 0, seam_rows * own - 1)
    high, low = place // LANES, place % LANES
    found = jnp.zeros(corner.shape, jnp.float32)
    for row in range(seam_rows):
        for h in range(halves):
            table = jnp.broadcast_to(ahead[8 + row : 9 + row, h * LANES : (h + 1) * LANES], corner.shape)
            value = jnp.take_along_axis(table, low, axis=1, mode="promise_in_bounds")
            found = jnp.where(high == row * halves + h, value, found)
    node = jnp.where(corner < sector_nodes, corner.astype(jnp.float32), found + float(sector_nodes))
    for h in range(halves):
        message[INDEX : INDEX + 4, h * LANES : (h + 1) * LANES] = node[4 * h : 4 * h + 4]
    for other in shorter:
        other[...] = message[: other.shape[0], :]


def history_kernel(after, gap_w, gap_u, history, sems):
    fetch(((gap_w, history.at[0:3]), (gap_u, history.at[3:6])), sems)


def join_kernel(after, left, right, joined):
    count = left.shape[0]
    joined[:count] = left[...]
    joined[count:] = right[...]


def sweep(strain_row, index, work, dual):
    table, terms, codes, nearby = work
    blocks, own = index.shape[1:]
    halves = own // LANES
    here = lax.axis_index("dom")
    row = lax.broadcasted_iota(jnp.int32, (blocks, LANES), 0)
    left_block = ((row ^ here) - 1) ^ here
    right_block = ((row ^ here) + 1) ^ here

    def wide(j, group, block, part):
        piece = table[j, group, part * LANES : (part + 1) * LANES][block : block + 1]
        return jnp.broadcast_to(piece, (blocks, LANES))

    def take_sides(group, first, sides):
        left, right = (list(side) for side in sides)
        for block in range(8):
            for j in range(3):
                left[j] = jnp.where(left_block == first + block, wide(j, group, block, halves - 1), left[j])
                right[j] = jnp.where(right_block == first + block, wide(j, group, block, 0), right[j])
        return tuple(left), tuple(right)

    blank = tuple(jnp.zeros((blocks, LANES), jnp.float32) for _ in range(3))
    left, right = repeat(blocks, take_sides, (blank, blank))
    speed = []
    for k in range(4):
        parts = []
        for h in range(halves):
            number = index[k, :, h * LANES : (h + 1) * LANES]
            high, low = number // LANES, number % LANES

            def take(value):
                return jnp.take_along_axis(value, low, axis=1, mode="promise_in_bounds")

            found = [take(table[j, :, 0:LANES]) for j in range(3)]
            for part in range(1, halves):
                mask = high % halves == part
                found = [
                    jnp.where(mask, take(table[j, :, part * LANES : (part + 1) * LANES]), found[j]) for j in range(3)
                ]
            mask = number // own == left_block
            found = [jnp.where(mask, take(left[j]), found[j]) for j in range(3)]
            mask = number // own == right_block
            found = [jnp.where(mask, take(right[j]), found[j]) for j in range(3)]

            def take_group(group, first, found):
                for part, block in itertools.product(range(halves), range(8)):
                    mask = high == (blocks + first + block) * halves + part
                    found = [jnp.where(mask, take(wide(3 + j, group, block, part)), found[j]) for j in range(3)]
                return tuple(found)

            parts.append(repeat(blocks, take_group, tuple(found)))
        speed.append([jnp.concatenate([found[j] for found in parts], axis=1) for j in range(3)])
    rate = []
    for c in range(3):
        total = None
        for k in range(4):
            for j in range(3):
                term = strain_row(12 * c + 3 * k + j) * speed[k][j]
                total = term if total is None else total + term
        rate.append(total)
    trial = [rate[c] + dual[c] for c in range(3)]
    cone = project_cone(trial)
    dual_next = [trial[c] - cone[c] for c in range(3)]
    misfit = [rate[c] - cone[c] + dual_next[c] for c in range(3)]
    for k in range(4):
        for j in range(3):
            rest = sum(strain_row(12 * c + 3 * k + j) * misfit[c] for c in range(3))
            for split in range(SPLITS):
                term = rest.astype(jnp.bfloat16).astype(jnp.float32)
                terms[SPLITS * j + split, k] = term
                rest = rest - term

    near_rows = halves + 2
    next_rows = halves * blocks
    row_wide = lax.broadcasted_iota(jnp.int32, (blocks, own), 0) ^ here
    for k in range(4):
        number = index[k]
        block_of, half = number // own, number // LANES % halves
        near = jnp.where(block_of == ((row_wide - 1) ^ here), 0, 1 + half)
        near = jnp.where(block_of == ((row_wide + 1) ^ here), 1 + halves, near)
        codes[0, k] = (number % LANES).astype(jnp.float32)
        codes[1, k] = jnp.where(block_of < blocks, near, -1).astype(jnp.float32)
        codes[2, k] = jnp.where(block_of < blocks, -1, half * blocks + block_of - blocks).astype(jnp.float32)

    values = 3 * SPLITS
    per_tile = 16 // near_rows
    near_tiles = -(-values // per_tile)
    iota = lax.broadcasted_iota(jnp.int32, (16, own), 0)
    near_iota = (iota % near_rows).astype(jnp.float32).astype(jnp.bfloat16)
    value_iota = (iota // near_rows).astype(jnp.float32).astype(jnp.bfloat16)
    value_masks = [value_iota == jnp.full((16, own), float(at), jnp.bfloat16) for at in range(per_tile)]
    iota = iota.astype(jnp.float32)
    low_iota = [(iota + float(16 * g)).astype(jnp.bfloat16) for g in range(LANES // 16)]
    next_iota = [(iota + float(16 * g)).astype(jnp.bfloat16) for g in range(next_rows // 16)]
    one = jnp.ones((16, own), jnp.bfloat16)
    zero = jnp.zeros((16, own), jnp.bfloat16)

    def spread_row(value):
        return jnp.broadcast_to(value, (16, own)).astype(jnp.bfloat16)

    def add_group(group, first, total):
        for block in range(8):
            part = None
            for k in range(4):
                low_row, near_row, next_row = (
                    spread_row(codes[at, k, group, :][block : block + 1]) for at in range(3)
                )
                rows = [spread_row(terms[at, k, group, :][block : block + 1]) for at in range(values)]
                spread = jnp.concatenate([jnp.where(low_row == value, one, zero) for value in low_iota], axis=0)
                mask = near_row == near_iota
                weights = []
                for tile in range(near_tiles):
                    inside = rows[tile * per_tile : (tile + 1) * per_tile]
                    value = inside[-1]
                    for at in range(len(inside) - 1):
                        value = jnp.where(value_masks[at], inside[at], value)
                    weights.append(jnp.where(mask, value, zero))
                masks = [next_row == value for value in next_iota]
                weights += [jnp.where(mask, row, zero) for row in rows for mask in masks]
                product = lax.dot_general(
                    jnp.concatenate(weights, axis=0),
                    spread,
                    (((1,), (1,)), ((), ())),
                    preferred_element_type=jnp.float32,
                )
                part = product if part is None else part + product
            start = (first + block) * 16 * near_tiles
            if not isinstance(start, int):
                start = pl.multiple_of(start, 16)
            nearby[pl.ds(start, 16 * near_tiles), :] = part[: 16 * near_tiles]
            total += part[16 * near_tiles :]
        return total

    total = repeat(blocks, add_group, jnp.zeros((values * next_rows, LANES), jnp.float32))

    def near_force(j, row):
        return sum(
            nearby[pl.ds((SPLITS * j + split) * near_rows + row, blocks, stride=16 * near_tiles), :]
            for split in range(SPLITS)
        )

    force_own, force_next = [], []
    for j in range(3):
        halves_own = [near_force(j, 1 + h) for h in range(halves)]
        to_left, to_right = near_force(j, 0), near_force(j, 1 + halves)
        from_right = from_left = jnp.zeros((blocks, LANES), jnp.float32)
        for block in range(blocks):
            wide_left = jnp.broadcast_to(to_left[block : block + 1], (blocks, LANES))
            wide_right = jnp.broadcast_to(to_right[block : block + 1], (blocks, LANES))
            from_right = jnp.where(right_block == block, wide_left, from_right)
            from_left = jnp.where(left_block == block, wide_right, from_left)
        halves_own[-1] = halves_own[-1] + from_right
        halves_own[0] = halves_own[0] + from_left
        force_own.append(jnp.concatenate(halves_own, axis=1))
        whole = sum(
            total[(SPLITS * j + split) * next_rows : (SPLITS * j + split + 1) * next_rows] for split in range(SPLITS)
        )
        force_next.append(jnp.concatenate([whole[h * blocks : (h + 1) * blocks] for h in range(halves)], axis=1))
    return dual_next, force_own, force_next


def stack_block(piece, slot, rows, stack):
    held = min(rows, piece.shape[0])
    for h in range(stack.shape[0]):
        stack[h, slot * rows : slot * rows + held, :] = piece[:held, h * LANES : (h + 1) * LANES]


def across(stack, row, rows):
    blocks = stack.shape[1] // rows
    return jnp.concatenate(
        [stack[h, pl.ds(row, blocks, stride=rows), :] for h in range(stack.shape[0])], axis=1
    )


def first_kernel(order, *refs):
    blocks = len(order)
    pieces = refs[:blocks]
    state, index, to_near, to_far, stack = refs[blocks : blocks + 5]
    work = refs[blocks + 5 :]
    table = work[0]
    own = index.shape[2]
    for piece, slot in zip(pieces, order):
        stack_block(piece, slot, ROWS, stack)
    flip = lax.axis_index("dom") * own
    even = lax.axis_index("sector") % 2 == 0
    for k in range(4):
        index[k] = across(stack, INDEX + k, ROWS).astype(jnp.int32) ^ flip
    for row in range(36):
        state[row] = across(stack, STRAIN + row, ROWS)
    step = across(stack, STEP, ROWS)
    state[STEP] = step
    state[KEPT_NEXT_STEP] = across(stack, NEXT_STEP, ROWS)
    for j in range(3):
        state[KEPT_LOAD + j] = across(stack, LOAD + j, ROWS)
        table[j] = across(stack, SPEED + j, ROWS)
        table[3 + j] = across(stack, NEXT_SPEED + j, ROWS)
    dual = [across(stack, DUAL + c, ROWS) for c in range(3)]
    dual, force_own, force_next = sweep(lambda row: state[row], index, work, dual)
    for c in range(3):
        state[DUAL + c] = dual[c]
        mine = table[c] - step * (force_own[c] - state[KEPT_LOAD + c])
        to_near[c] = jnp.where(even, force_next[c], mine)
        to_far[c] = jnp.where(even, mine, force_next[c])


def second_kernel(state, index, to_near, to_far, from_far, from_near, out_next, keep, *work):
    table = work[0]
    even = lax.axis_index("sector") % 2 == 0
    step, next_step = state[STEP], state[KEPT_NEXT_STEP]
    for j in range(3):
        near, far = to_near[j], to_far[j]
        near_in, far_in = from_near[j], from_far[j]
        table[j] = jnp.where(even, far, near) - step * jnp.where(even, far_in, near_in)
        table[3 + j] = jnp.where(even, near_in, far_in) - next_step * jnp.where(even, near, far)
    dual = [state[DUAL + c] for c in range(3)]
    dual_next, force_own, force_next = sweep(lambda row: state[row], index, work, dual)
    for c in range(3):
        out_next[c] = force_next[c]
        keep[c] = dual_next[c]
        keep[3 + c] = dual_next[c] - dual[c]
        keep[6 + c] = table[c]
        keep[9 + c] = table[c] - step * (force_own[c] - state[KEPT_LOAD + c])


def pairs(depth):
    return [(i, l) for i in range(depth) for l in range(i, depth + 1)]


def gram_kernel(depth, slots, state, keep, from_prev, left, right, part, last, stack, rows_sum):
    blocks, own = keep.shape[1:]
    halves = own // LANES
    rows = 6 * depth
    for piece, own_slots in zip((left, right), slots):
        for at, slot in enumerate(own_slots):
            for kind in range(6):
                for h in range(halves):
                    start = slot * rows + kind * depth
                    stack[h, start : start + depth, :] = piece[at, kind, :, h * LANES : (h + 1) * LANES]
    change = []
    for j in range(3):
        after = keep[9 + j] - state[STEP] * from_prev[j]
        change.append(after - keep[6 + j])
        last[j : j + 1, :] = after[0:1]
        last[3 + j : 4 + j, :] = keep[j][0:1]
    last[6:8, :] = jnp.zeros((2, own), jnp.float32)
    sums = {}
    for kind in range(2):
        for c in range(3):
            whole = keep[3 + c] if kind == 0 else change[c]
            for h in range(halves):
                for top in range(0, blocks, 8):
                    moved = whole[top : top + 8, h * LANES : (h + 1) * LANES]
                    gaps = [
                        moved - stack[h, pl.ds(top * rows + depth * (3 * kind + c) + i, 8, stride=rows), :]
                        for i in range(depth)
                    ] + [moved]
                    for i, l in pairs(depth):
                        term = gaps[i] * gaps[l]
                        sums[i, l] = sums[i, l] + term if (i, l) in sums else term
    for at, pair in enumerate(pairs(depth)):
        rows_sum[at : at + 1, :] = jnp.sum(sums[pair], axis=0, keepdims=True)
    count = len(pairs(depth))
    if rows_sum.shape[0] > count:
        rows_sum[count:, :] = jnp.zeros((rows_sum.shape[0] - count, LANES), jnp.float32)
    whole = jnp.broadcast_to(jnp.sum(rows_sum[...], axis=1, keepdims=True), rows_sum.shape)
    lane = lax.broadcasted_iota(jnp.int32, (8, LANES), 1)
    out = whole[0:8]
    for group in range(1, rows_sum.shape[0] // 8):
        out = jnp.where(lane == group, whole[8 * group : 8 * group + 8], out)
    part[...] = out


def solve_kernel(depth, *refs):
    parts = refs[:-8]
    last, past_w, gap_w, past_u, gap_u, new_u, new_w, total = refs[-8:]
    own = last.shape[1]
    tile = parts[0][...]
    for other in parts[1:]:
        tile = tile + other[...]
    for group in range(total.shape[0] // 8):
        total[8 * group : 8 * group + 8, :] = jnp.broadcast_to(tile[:, group : group + 1], (8, LANES))
    matrix = {
        pair: jnp.broadcast_to(total[at : at + 1, :], (depth, LANES)) for at, pair in enumerate(pairs(depth))
    }
    ridge = 0.0001 * sum(matrix[i, i] for i in range(depth)) / depth
    for i in range(depth):
        matrix[i, i] = matrix[i, i] + ridge
    inverse = []
    for step in range(depth):
        inverse.append(1.0 / matrix[step, step])
        for i in range(step + 1, depth):
            factor = matrix[step, i] * inverse[step]
            for l in range(i, depth + 1):
                matrix[i, l] = matrix[i, l] - factor * matrix[step, l]
    weights = [None] * depth
    for i in reversed(range(depth)):
        value = matrix[i, depth]
        for l in range(i + 1, depth):
            value = value - matrix[i, l] * weights[l]
        weights[i] = value * inverse[i]
    row = lax.broadcasted_iota(jnp.int32, (depth, LANES), 0)
    weight = weights[0]
    for i in range(1, depth):
        weight = jnp.where(row == i, weights[i], weight)
    for start in range(0, own, LANES):
        lanes = slice(start, start + LANES)
        for at, (past, gap, out) in enumerate(((past_u, gap_u, new_u), (past_w, gap_w, new_w))):
            for c in range(3):
                value = jnp.broadcast_to(last[3 * at + c : 3 * at + c + 1, lanes], (depth, LANES))
                change = weight * (value - past[c, :, lanes] - gap[c, :, lanes])
                out[c : c + 1, lanes] = value[0:1] - jnp.sum(change, axis=0, keepdims=True)


def per_device(
    strain_map,
    corner_nodes,
    counts,
    seam_nodes,
    velocity,
    dual_state,
    nodal_load,
    mobility,
    past_dual,
    past_dual_gap,
    past_velocity,
    past_velocity_gap,
):
    own = velocity.shape[1]
    halves = own // LANES
    blocks = lax.axis_size("dom")
    sectors = lax.axis_size("sector")
    depth = past_dual.shape[0]
    seam_rows = seam_nodes.shape[1] // own
    mobility = mobility.reshape(1, own)
    past_dual, past_dual_gap, past_velocity, past_velocity_gap = (
        value.transpose(1, 0, 2) for value in (past_dual, past_dual_gap, past_velocity, past_velocity_gap)
    )

    def send(value, target):
        return lax.ppermute(value, "sector", [(i, target(i) % sectors) for i in range(sectors)])

    def swap(value, bits):
        return lax.ppermute(value, "dom", [(i, i ^ bits) for i in range(blocks)])

    nodes = (velocity, mobility, seam_nodes)
    ahead = call(
        nodes_kernel,
        f32(8 + seam_rows, own),
        in_hbm(*nodes),
        loose=len(nodes),
        scratch=[pltpu.VMEM(value.shape, value.dtype) for value in nodes] + [pltpu.SemaphoreType.DMA((len(nodes),))],
    )
    held = (strain_map, dual_state, velocity, nodal_load, mobility, corner_nodes)
    base = call(
        base_kernel,
        f32(INDEX + 4, own),
        (counts, ahead, *in_hbm(*held)),
        scalars=1,
        loose=len(held) + 1,
        scratch=[pltpu.VMEM(value.shape, value.dtype) for value in held] + [pltpu.SemaphoreType.DMA((len(held),))],
    )
    ahead = send(ahead, lambda i: i - 1)
    history = call(
        history_kernel,
        f32(6, depth, own),
        (base, *in_hbm(past_dual_gap, past_velocity_gap)),
        loose=3,
        scratch=[pltpu.SemaphoreType.DMA((2,))],
    )
    partners = sorted(range(2, blocks, 2), key=lambda bits: (bits == 2, bits))
    lengths = [max(INDEX + 4, ROWS - place) for place in range(len(partners))]
    messages = call(
        functools.partial(message_kernel, own * blocks),
        tuple(f32(rows, own) for rows in sorted(set(lengths), reverse=True)),
        (history, ahead, base),
        loose=1,
    )
    pieces = {0: messages[0]}
    for bits, rows in zip(partners, lengths):
        pieces[bits] = swap(next(value for value in messages if value.shape[0] == rows), bits)
    slots = [0]
    apart, after = 2, pieces[partners[0]]
    history = history[None]
    history_in = swap(history, apart)
    for even in range(0, blocks, 2):
        pieces[even + 1] = swap(pieces[even], 1)
    sector = f32(3, blocks, own)
    order = tuple(reversed(range(blocks)))
    work = [
        pltpu.VMEM((6, blocks, own), jnp.float32),
        pltpu.VMEM((3 * SPLITS, 4, blocks, own), jnp.float32),
        pltpu.VMEM((3, 4, blocks, own), jnp.float32),
        pltpu.VMEM((blocks * 16 * -(-3 * SPLITS * (halves + 2) // 16), LANES), jnp.float32),
    ]
    state, index, to_near, to_far = call(
        functools.partial(first_kernel, order),
        (f32(KEPT, blocks, own), jax.ShapeDtypeStruct((4, blocks, own), jnp.int32), sector, sector),
        tuple(pieces[block] for block in order),
        scratch=[pltpu.VMEM((halves, blocks * ROWS, LANES), jnp.float32), *work],
    )
    from_far = send(to_far, lambda i: i + 1 if i % 2 else i - 1)
    from_near = send(to_near, lambda i: i ^ 1)
    while 2 * apart < blocks:
        history = call(join_kernel, f32(2 * history.shape[0], 6, depth, own), (after, history, history_in), loose=1)
        slots += [slot ^ apart for slot in slots]
        apart, after = 2 * apart, to_near
        history_in = swap(history, apart)
    force_next, keep = call(
        second_kernel,
        (sector, f32(12, blocks, own)),
        (state, index, to_near, to_far, from_far, from_near),
        scratch=work,
    )
    from_prev = send(force_next, lambda i: i + 1)
    history = call(join_kernel, f32(2 * history.shape[0], 6, depth, own), (keep, history, history_in), loose=1)
    slots += [slot ^ apart for slot in slots]
    history_in = swap(history, 1)
    count = -(-len(pairs(depth)) // 8) * 8
    part, last = call(
        functools.partial(gram_kernel, depth, (tuple(slots), tuple(slot ^ 1 for slot in slots))),
        (f32(8, LANES), f32(8, own)),
        (state, keep, from_prev, history, history_in),
        scratch=[
            pltpu.VMEM((halves, blocks * 6 * depth, LANES), jnp.float32),
            pltpu.VMEM((count, LANES), jnp.float32),
        ],
    )
    parts = [part] + [send(part, lambda i: i ^ by) for by in range(sectors - 1, 0, -1)]
    return call(
        functools.partial(solve_kernel, depth),
        (f32(3, own), f32(3, own)),
        (*parts, last, past_dual, past_dual_gap, past_velocity, past_velocity_gap),
        scratch=[pltpu.VMEM((count, LANES), jnp.float32)],
    )


def solution(mesh):
    in_specs = (
        P(None, ("sector", "dom")),
        P(None, ("sector", "dom")),
        P(("sector", "dom")),
        P("sector", None),
        P(None, ("sector", "dom")),
        P(None, ("sector", "dom")),
        P(None, ("sector", "dom")),
        P(("sector", "dom")),
        P(None, None, ("sector", "dom")),
        P(None, None, ("sector", "dom")),
        P(None, None, ("sector", "dom")),
        P(None, None, ("sector", "dom")),
    )
    out_specs = (P(None, ("sector", "dom")), P(None, ("sector", "dom")))
    return jax.shard_map(
        per_device, mesh=mesh, in_specs=in_specs, out_specs=out_specs, check_vma=False
    )
```

```python
import functools
import itertools

import jax
import jax.numpy as jnp
from jax import lax
from jax.experimental import pallas as pl
from jax.experimental.pallas import tpu as pltpu
from jax.sharding import PartitionSpec as P

LANES = 128
VMEM_LIMIT = 24 * 1024 * 1024

STRAIN, DUAL, STEP, SPEED, LOAD, NEXT_STEP, NEXT_SPEED, INDEX, ROWS = 0, 36, 39, 40, 43, 46, 47, 50, 56
KEPT_NEXT_STEP, KEPT_LOAD, KEPT = 40, 41, 44
SPLITS = 2


def vmem():
    return pl.BlockSpec(memory_space=pltpu.VMEM)


def smem():
    return pl.BlockSpec(memory_space=pltpu.SMEM)


def call(kernel, outs, args, scalars=0, loose=0, scratch=()):
    return pl.pallas_call(
        kernel,
        out_shape=outs,
        in_specs=[smem()] * scalars
        + [pl.BlockSpec(memory_space=pl.ANY)] * loose
        + [vmem()] * (len(args) - scalars - loose),
        out_specs=jax.tree.map(lambda _: vmem(), outs),
        scratch_shapes=list(scratch),
        compiler_params=pltpu.CompilerParams(vmem_limit_bytes=VMEM_LIMIT),
    )(*args)


def f32(*shape):
    return jax.ShapeDtypeStruct(shape, jnp.float32)


def repeat(blocks, body, init):
    if blocks == 8:
        return body(slice(0, 8), 0, init)
    return lax.fori_loop(
        0, blocks // 8, lambda step, carry: body(pl.ds(pl.multiple_of(8 * step, 8), 8), 8 * step, carry), init
    )


def project_cone(trial):
    center = 0.5 * (trial[0] + trial[1])
    spread = 0.5 * (trial[0] - trial[1])
    shear = trial[2]
    radius = jnp.sqrt(spread * spread + shear * shear)
    upper = center + radius
    lower = center - radius
    iso_part = 0.5 * (jnp.maximum(upper, 0.0) + jnp.maximum(lower, 0.0))
    factor = jnp.clip((center + radius) / (2.0 * jnp.maximum(radius, 0.05)), 0.0, 1.0)
    return (iso_part + factor * spread, iso_part - factor * spread, factor * shear)


def fetch(pairs, sems):
    copies = [pltpu.make_async_copy(source, target, sems.at[at]) for at, (source, target) in enumerate(pairs)]
    for copy in copies:
        copy.start()
    for copy in copies:
        copy.wait()


def in_hbm(*values):
    return tuple(pltpu.with_memory_space_constraint(value, pltpu.HBM) for value in values)


def nodes_kernel(speed_in, mobility_in, seam_in, gap_u, ahead, speed, mobility, seam, sems):
    depth = gap_u.shape[1]
    start = ahead.shape[0] - 3 * depth
    gaps = [(gap_u.at[c], ahead.at[pl.ds(start + depth * c, depth)]) for c in range(3)]
    fetch(((speed_in, speed), (mobility_in, mobility), (seam_in, seam), *gaps), sems)
    own = speed.shape[1]
    ahead[0:3, :] = speed[...]
    ahead[3:4, :] = mobility[...]
    ahead[4:8, :] = jnp.zeros((4, own), jnp.float32)
    for row in range(8, start):
        ahead[row : row + 1, :] = seam[:, (row - 8) * own : (row - 7) * own].astype(jnp.float32)


def base_kernel(counts, after, *refs):
    count = (len(refs) - 2) // 2
    sources, base, held, sems = refs[:count], refs[count], refs[count + 1 : -1], refs[-1]
    fetch(zip(sources, held), sems)
    strain, dual, speed, load, mobility, corners = held
    own = speed.shape[1]
    slot = lax.broadcasted_iota(jnp.int32, (1, own), 1)
    alive = (slot < counts[0]).astype(jnp.float32)
    base[STRAIN:DUAL, :] = strain[...] * alive
    base[DUAL : DUAL + 3, :] = dual[...] * alive
    base[STEP : STEP + 1, :] = mobility[...]
    base[SPEED : SPEED + 3, :] = speed[...]
    base[LOAD : LOAD + 3, :] = load[...]
    base[NEXT_STEP:INDEX, :] = jnp.zeros((INDEX - NEXT_STEP, own), jnp.float32)
    base[INDEX : INDEX + 4, :] = corners[...].astype(jnp.float32)


def message_kernel(sector_nodes, depth, after, ahead, base, message, *shorter):
    own = message.shape[1]
    halves = own // LANES
    message[:NEXT_STEP, :] = base[:NEXT_STEP, :]
    message[NEXT_STEP : NEXT_STEP + 1, :] = ahead[3:4, :]
    message[NEXT_SPEED : NEXT_SPEED + 3, :] = ahead[0:3, :]
    message[INDEX + 4 :, :] = jnp.zeros((ROWS - INDEX - 4, own), jnp.float32)
    corners = base[INDEX : INDEX + 4, :].astype(jnp.int32)
    corner = jnp.concatenate([corners[:, h * LANES : (h + 1) * LANES] for h in range(halves)], axis=0)
    seam_rows = ahead.shape[0] - 8 - 3 * depth
    place = jnp.clip(corner - sector_nodes, 0, seam_rows * own - 1)
    high, low = place // LANES, place % LANES
    found = jnp.zeros(corner.shape, jnp.float32)
    for row in range(seam_rows):
        for h in range(halves):
            table = jnp.broadcast_to(ahead[8 + row : 9 + row, h * LANES : (h + 1) * LANES], corner.shape)
            value = jnp.take_along_axis(table, low, axis=1, mode="promise_in_bounds")
            found = jnp.where(high == row * halves + h, value, found)
    node = jnp.where(corner < sector_nodes, corner.astype(jnp.float32), found + float(sector_nodes))
    for h in range(halves):
        message[INDEX : INDEX + 4, h * LANES : (h + 1) * LANES] = node[4 * h : 4 * h + 4]
    for other in shorter:
        other[...] = message[: other.shape[0], :]


def history_kernel(after, gap_w, gap_u, history, sems):
    fetch(((gap_w, history.at[0:3]), (gap_u, history.at[3:6])), sems)


def gaps_kernel(after, gaps, ahead, history):
    depth = gaps.shape[1]
    start = ahead.shape[0] - 3 * depth
    for kind in range(6):
        history[0, kind] = gaps[kind]
    for c in range(3):
        history[0, 6 + c] = ahead[start + depth * c : start + depth * (c + 1), :]


def join_kernel(*refs):
    left, right, joined = refs[-3:]
    count = left.shape[0]
    joined[:count] = left[...]
    joined[count:] = right[...]


def sweep(strain_row, index, work, dual):
    table, terms, codes, nearby = work
    blocks, own = index.shape[1:]
    halves = own // LANES
    here = lax.axis_index("dom")
    row = lax.broadcasted_iota(jnp.int32, (blocks, LANES), 0)
    left_block = ((row ^ here) - 1) ^ here
    right_block = ((row ^ here) + 1) ^ here

    def wide(j, group, block, part):
        piece = table[j, group, part * LANES : (part + 1) * LANES][block : block + 1]
        return jnp.broadcast_to(piece, (blocks, LANES))

    def take_sides(group, first, sides):
        left, right = (list(side) for side in sides)
        for block in range(8):
            for j in range(3):
                left[j] = jnp.where(left_block == first + block, wide(j, group, block, halves - 1), left[j])
                right[j] = jnp.where(right_block == first + block, wide(j, group, block, 0), right[j])
        return tuple(left), tuple(right)

    blank = tuple(jnp.zeros((blocks, LANES), jnp.float32) for _ in range(3))
    left, right = repeat(blocks, take_sides, (blank, blank))
    speed = []
    for k in range(4):
        parts = []
        for h in range(halves):
            number = index[k, :, h * LANES : (h + 1) * LANES]
            high, low = number // LANES, number % LANES

            def take(value):
                return jnp.take_along_axis(value, low, axis=1, mode="promise_in_bounds")

            found = [take(table[j, :, 0:LANES]) for j in range(3)]
            for part in range(1, halves):
                mask = high % halves == part
                found = [
                    jnp.where(mask, take(table[j, :, part * LANES : (part + 1) * LANES]), found[j]) for j in range(3)
                ]
            mask = number // own == left_block
            found = [jnp.where(mask, take(left[j]), found[j]) for j in range(3)]
            mask = number // own == right_block
            found = [jnp.where(mask, take(right[j]), found[j]) for j in range(3)]

            def take_group(group, first, found):
                for part, block in itertools.product(range(halves), range(8)):
                    mask = high == (blocks + first + block) * halves + part
                    found = [jnp.where(mask, take(wide(3 + j, group, block, part)), found[j]) for j in range(3)]
                return tuple(found)

            parts.append(repeat(blocks, take_group, tuple(found)))
        speed.append([jnp.concatenate([found[j] for found in parts], axis=1) for j in range(3)])
    rate = []
    for c in range(3):
        total = None
        for k in range(4):
            for j in range(3):
                term = strain_row(12 * c + 3 * k + j) * speed[k][j]
                total = term if total is None else total + term
        rate.append(total)
    trial = [rate[c] + dual[c] for c in range(3)]
    cone = project_cone(trial)
    dual_next = [trial[c] - cone[c] for c in range(3)]
    misfit = [rate[c] - cone[c] + dual_next[c] for c in range(3)]
    for k in range(4):
        for j in range(3):
            rest = sum(strain_row(12 * c + 3 * k + j) * misfit[c] for c in range(3))
            for split in range(SPLITS):
                term = rest.astype(jnp.bfloat16).astype(jnp.float32)
                terms[SPLITS * j + split, k] = term
                rest = rest - term

    near_rows = halves + 2
    next_rows = halves * blocks
    row_wide = lax.broadcasted_iota(jnp.int32, (blocks, own), 0) ^ here
    for k in range(4):
        number = index[k]
        block_of, half = number // own, number // LANES % halves
        near = jnp.where(block_of == ((row_wide - 1) ^ here), 0, 1 + half)
        near = jnp.where(block_of == ((row_wide + 1) ^ here), 1 + halves, near)
        codes[0, k] = (number % LANES).astype(jnp.float32)
        codes[1, k] = jnp.where(block_of < blocks, near, -1).astype(jnp.float32)
        codes[2, k] = jnp.where(block_of < blocks, -1, half * blocks + block_of - blocks).astype(jnp.float32)

    values = 3 * SPLITS
    per_tile = 16 // near_rows
    near_tiles = -(-values // per_tile)
    iota = lax.broadcasted_iota(jnp.int32, (16, own), 0)
    near_iota = (iota % near_rows).astype(jnp.float32).astype(jnp.bfloat16)
    value_iota = (iota // near_rows).astype(jnp.float32).astype(jnp.bfloat16)
    value_masks = [value_iota == jnp.full((16, own), float(at), jnp.bfloat16) for at in range(per_tile)]
    iota = iota.astype(jnp.float32)
    low_iota = [(iota + float(16 * g)).astype(jnp.bfloat16) for g in range(LANES // 16)]
    next_iota = [(iota + float(16 * g)).astype(jnp.bfloat16) for g in range(next_rows // 16)]
    one = jnp.ones((16, own), jnp.bfloat16)
    zero = jnp.zeros((16, own), jnp.bfloat16)

    def spread_row(value):
        return jnp.broadcast_to(value, (16, own)).astype(jnp.bfloat16)

    def add_group(group, first, total):
        for block in range(8):
            part = None
            for k in range(4):
                low_row, near_row, next_row = (
                    spread_row(codes[at, k, group, :][block : block + 1]) for at in range(3)
                )
                rows = [spread_row(terms[at, k, group, :][block : block + 1]) for at in range(values)]
                spread = jnp.concatenate([jnp.where(low_row == value, one, zero) for value in low_iota], axis=0)
                mask = near_row == near_iota
                weights = []
                for tile in range(near_tiles):
                    inside = rows[tile * per_tile : (tile + 1) * per_tile]
                    value = inside[-1]
                    for at in range(len(inside) - 1):
                        value = jnp.where(value_masks[at], inside[at], value)
                    weights.append(jnp.where(mask, value, zero))
                masks = [next_row == value for value in next_iota]
                weights += [jnp.where(mask, row, zero) for row in rows for mask in masks]
                product = lax.dot_general(
                    jnp.concatenate(weights, axis=0),
                    spread,
                    (((1,), (1,)), ((), ())),
                    preferred_element_type=jnp.float32,
                )
                part = product if part is None else part + product
            start = (first + block) * 16 * near_tiles
            if not isinstance(start, int):
                start = pl.multiple_of(start, 16)
            nearby[pl.ds(start, 16 * near_tiles), :] = part[: 16 * near_tiles]
            total += part[16 * near_tiles :]
        return total

    total = repeat(blocks, add_group, jnp.zeros((values * next_rows, LANES), jnp.float32))

    def near_force(j, row):
        return sum(
            nearby[pl.ds((SPLITS * j + split) * near_rows + row, blocks, stride=16 * near_tiles), :]
            for split in range(SPLITS)
        )

    force_own, force_next = [], []
    for j in range(3):
        halves_own = [near_force(j, 1 + h) for h in range(halves)]
        to_left, to_right = near_force(j, 0), near_force(j, 1 + halves)
        from_right = from_left = jnp.zeros((blocks, LANES), jnp.float32)
        for block in range(blocks):
            wide_left = jnp.broadcast_to(to_left[block : block + 1], (blocks, LANES))
            wide_right = jnp.broadcast_to(to_right[block : block + 1], (blocks, LANES))
            from_right = jnp.where(right_block == block, wide_left, from_right)
            from_left = jnp.where(left_block == block, wide_right, from_left)
        halves_own[-1] = halves_own[-1] + from_right
        halves_own[0] = halves_own[0] + from_left
        force_own.append(jnp.concatenate(halves_own, axis=1))
        whole = sum(
            total[(SPLITS * j + split) * next_rows : (SPLITS * j + split + 1) * next_rows] for split in range(SPLITS)
        )
        force_next.append(jnp.concatenate([whole[h * blocks : (h + 1) * blocks] for h in range(halves)], axis=1))
    return dual_next, force_own, force_next


def stack_block(piece, slot, rows, stack):
    held = min(rows, piece.shape[0])
    for h in range(stack.shape[0]):
        stack[h, slot * rows : slot * rows + held, :] = piece[:held, h * LANES : (h + 1) * LANES]


def across(stack, row, rows):
    blocks = stack.shape[1] // rows
    return jnp.concatenate(
        [stack[h, pl.ds(row, blocks, stride=rows), :] for h in range(stack.shape[0])], axis=1
    )


def first_kernel(order, *refs):
    blocks = len(order)
    pieces = refs[:blocks]
    state, index, to_near, to_far, stack = refs[blocks : blocks + 5]
    work = refs[blocks + 5 :]
    table = work[0]
    own = index.shape[2]
    for piece, slot in zip(pieces, order):
        stack_block(piece, slot, ROWS, stack)
    flip = lax.axis_index("dom") * own
    even = lax.axis_index("sector") % 2 == 0
    for k in range(4):
        index[k] = across(stack, INDEX + k, ROWS).astype(jnp.int32) ^ flip
    for row in range(36):
        state[row] = across(stack, STRAIN + row, ROWS)
    step = across(stack, STEP, ROWS)
    state[STEP] = step
    state[KEPT_NEXT_STEP] = across(stack, NEXT_STEP, ROWS)
    for j in range(3):
        state[KEPT_LOAD + j] = across(stack, LOAD + j, ROWS)
        table[j] = across(stack, SPEED + j, ROWS)
        table[3 + j] = across(stack, NEXT_SPEED + j, ROWS)
    dual = [across(stack, DUAL + c, ROWS) for c in range(3)]
    dual, force_own, force_next = sweep(lambda row: state[row], index, work, dual)
    for c in range(3):
        state[DUAL + c] = dual[c]
        mine = table[c] - step * (force_own[c] - state[KEPT_LOAD + c])
        to_near[c] = jnp.where(even, force_next[c], mine)
        to_far[c] = jnp.where(even, mine, force_next[c])


def second_kernel(state, index, to_near, to_far, from_far, from_near, vectors, keep, *work):
    table = work[0]
    even = lax.axis_index("sector") % 2 == 0
    step, next_step = state[STEP], state[KEPT_NEXT_STEP]
    for j in range(3):
        near, far = to_near[j], to_far[j]
        near_in, far_in = from_near[j], from_far[j]
        table[j] = jnp.where(even, far, near) - step * jnp.where(even, far_in, near_in)
        table[3 + j] = jnp.where(even, near_in, far_in) - next_step * jnp.where(even, near, far)
    dual = [state[DUAL + c] for c in range(3)]
    dual_next, force_own, force_next = sweep(lambda row: state[row], index, work, dual)
    for c in range(3):
        after = table[c] - step * (force_own[c] - state[KEPT_LOAD + c])
        vectors[c] = after - table[c]
        vectors[3 + c] = -(next_step * force_next[c])
        keep[c] = dual_next[c]
        keep[3 + c] = dual_next[c] - dual[c]
        keep[6 + c] = after


def pairs(depth):
    return [(i, l) for i in range(depth) for l in range(i, depth + 1)]


def gram_kernel(depth, slots, vectors, keep, left, right, message, stack, rows_sum):
    blocks, own = keep.shape[1:]
    halves = own // LANES
    rows = 9 * depth
    for piece, own_slots in zip((left, right), slots):
        for at, slot in enumerate(own_slots):
            for kind in range(9):
                for h in range(halves):
                    start = slot * rows + kind * depth
                    stack[h, start : start + depth, :] = piece[at, kind, :, h * LANES : (h + 1) * LANES]
    for row in range(6):
        message[row] = vectors[row]
    message[6] = jnp.zeros((blocks, own), jnp.float32)
    sums, pushed, pushed_twice = {}, [0.0] * (depth + 1), 0.0
    for c, h, top in itertools.product(range(3), range(halves), range(0, blocks, 8)):
        lanes, group = slice(h * LANES, (h + 1) * LANES), slice(top, top + 8)

        def gap(kind, i):
            return stack[h, pl.ds(top * rows + depth * (3 * kind + c) + i, 8, stride=rows), :]

        for kind, moved in enumerate((keep[3 + c, group, lanes], vectors[c, group, lanes])):
            gaps = [moved - gap(kind, i) for i in range(depth)] + [moved]
            for i, l in pairs(depth):
                term = gaps[i] * gaps[l]
                sums[i, l] = sums[i, l] + term if (i, l) in sums else term
        push = vectors[3 + c, group, lanes]
        for i in range(depth):
            pushed[i] = pushed[i] + gap(2, i) * push
        pushed_twice = pushed_twice + push * push
    for at, (i, l) in enumerate(pairs(depth)):
        value = sums[i, l] + pushed_twice - pushed[i] - pushed[l]
        rows_sum[at : at + 1, :] = jnp.sum(value, axis=0, keepdims=True)
    count = len(pairs(depth))
    if rows_sum.shape[0] > count:
        rows_sum[count:, :] = jnp.zeros((rows_sum.shape[0] - count, LANES), jnp.float32)
    whole = jnp.broadcast_to(jnp.sum(rows_sum[...], axis=1, keepdims=True), rows_sum.shape)
    lane = lax.broadcasted_iota(jnp.int32, (8, LANES), 1)
    out = whole[0:8]
    for group in range(1, rows_sum.shape[0] // 8):
        out = jnp.where(lane == group, whole[8 * group : 8 * group + 8], out)
    message[6, 0:8, 0:LANES] = out


def solve_kernel(depth, square, *refs):
    parts = refs[:-8]
    keep, past_w, gap_w, past_u, gap_u, new_u, new_w, total = refs[-8:]
    own = new_u.shape[1]
    tile = parts[0][6, 0:8, 0:LANES]
    for other in parts[1:]:
        tile = tile + other[6, 0:8, 0:LANES]
    even = lax.axis_index("sector") % 2 == 0

    def ahead(by, row):
        if square and by in (1, 3):
            return jnp.where(even, parts[by][row], parts[4 - by][row])
        return parts[by][row]

    sectors = len(parts)
    pushes = [[ahead(by, 3 + j) for j in range(3)] for by in range(sectors)]
    cross = sum(ahead(by, j) * pushes[by - 1][j] for by in range(sectors) for j in range(3))
    cross = jnp.sum(jnp.sum(cross, axis=0, keepdims=True), axis=1, keepdims=True)
    last = [keep[6 + j, 0:1] + pushes[-1][j][0:1] for j in range(3)] + [keep[c, 0:1] for c in range(3)]
    for group in range(total.shape[0] // 8):
        total[8 * group : 8 * group + 8, :] = jnp.broadcast_to(tile[:, group : group + 1], (8, LANES))
    matrix = {
        pair: jnp.broadcast_to(total[at : at + 1, :], (depth, LANES)) + 2.0 * cross
        for at, pair in enumerate(pairs(depth))
    }
    ridge = 0.0001 * sum(matrix[i, i] for i in range(depth)) / depth
    for i in range(depth):
        matrix[i, i] = matrix[i, i] + ridge
    inverse = []
    for step in range(depth):
        inverse.append(1.0 / matrix[step, step])
        for i in range(step + 1, depth):
            factor = matrix[step, i] * inverse[step]
            for l in range(i, depth + 1):
                matrix[i, l] = matrix[i, l] - factor * matrix[step, l]
    weights = [None] * depth
    for i in reversed(range(depth)):
        value = matrix[i, depth]
        for l in range(i + 1, depth):
            value = value - matrix[i, l] * weights[l]
        weights[i] = value * inverse[i]
    row = lax.broadcasted_iota(jnp.int32, (depth, LANES), 0)
    weight = weights[0]
    for i in range(1, depth):
        weight = jnp.where(row == i, weights[i], weight)
    for start in range(0, own, LANES):
        lanes = slice(start, start + LANES)
        for at, (past, gap, out) in enumerate(((past_u, gap_u, new_u), (past_w, gap_w, new_w))):
            for c in range(3):
                value = jnp.broadcast_to(last[3 * at + c][:, lanes], (depth, LANES))
                change = weight * (value - past[c, :, lanes] - gap[c, :, lanes])
                out[c : c + 1, lanes] = value[0:1] - jnp.sum(change, axis=0, keepdims=True)


def per_device(
    strain_map,
    corner_nodes,
    counts,
    seam_nodes,
    velocity,
    dual_state,
    nodal_load,
    mobility,
    past_dual,
    past_dual_gap,
    past_velocity,
    past_velocity_gap,
):
    own = velocity.shape[1]
    halves = own // LANES
    blocks = lax.axis_size("dom")
    sectors = lax.axis_size("sector")
    depth = past_dual.shape[0]
    seam_rows = seam_nodes.shape[1] // own
    mobility = mobility.reshape(1, own)
    past_dual, past_dual_gap, past_velocity, past_velocity_gap = (
        value.transpose(1, 0, 2) for value in (past_dual, past_dual_gap, past_velocity, past_velocity_gap)
    )

    def send(value, target):
        return lax.ppermute(value, "sector", [(i, target(i) % sectors) for i in range(sectors)])

    def swap(value, bits):
        return lax.ppermute(value, "dom", [(i, i ^ bits) for i in range(blocks)])

    nodes = (velocity, mobility, seam_nodes)
    ahead = call(
        nodes_kernel,
        f32(8 + seam_rows + 3 * depth, own),
        in_hbm(*nodes, past_velocity_gap),
        loose=len(nodes) + 1,
        scratch=[pltpu.VMEM(value.shape, value.dtype) for value in nodes]
        + [pltpu.SemaphoreType.DMA((len(nodes) + 3,))],
    )
    held = (strain_map, dual_state, velocity, nodal_load, mobility, corner_nodes)
    base = call(
        base_kernel,
        f32(INDEX + 4, own),
        (counts, ahead, *in_hbm(*held)),
        scalars=1,
        loose=len(held) + 1,
        scratch=[pltpu.VMEM(value.shape, value.dtype) for value in held] + [pltpu.SemaphoreType.DMA((len(held),))],
    )
    ahead = send(ahead, lambda i: i - 1)
    history = call(
        history_kernel,
        f32(6, depth, own),
        (base, *in_hbm(past_dual_gap, past_velocity_gap)),
        loose=3,
        scratch=[pltpu.SemaphoreType.DMA((2,))],
    )
    partners = sorted(range(2, blocks, 2), reverse=True)
    lengths = [max(INDEX + 4, ROWS - place) for place in range(len(partners))]
    messages = call(
        functools.partial(message_kernel, own * blocks, depth),
        tuple(f32(rows, own) for rows in sorted(set(lengths), reverse=True)),
        (history, ahead, base),
        loose=1,
    )
    pieces = {0: messages[0]}
    for bits, rows in zip(partners, lengths):
        pieces[bits] = swap(next(value for value in messages if value.shape[0] == rows), bits)
    for even in range(0, blocks, 2):
        pieces[even + 1] = swap(pieces[even], 1)
    history = call(gaps_kernel, f32(1, 9, depth, own), (messages[0], history, ahead), loose=1)
    slots = [0]
    apart, after = 2, [pieces[bits] for bits in partners]
    history_in = swap(history, apart)
    sector = f32(3, blocks, own)
    order = tuple(reversed(range(blocks)))
    work = [
        pltpu.VMEM((6, blocks, own), jnp.float32),
        pltpu.VMEM((3 * SPLITS, 4, blocks, own), jnp.float32),
        pltpu.VMEM((3, 4, blocks, own), jnp.float32),
        pltpu.VMEM((blocks * 16 * -(-3 * SPLITS * (halves + 2) // 16), LANES), jnp.float32),
    ]
    state, index, to_near, to_far = call(
        functools.partial(first_kernel, order),
        (f32(KEPT, blocks, own), jax.ShapeDtypeStruct((4, blocks, own), jnp.int32), sector, sector),
        tuple(pieces[block] for block in order),
        scratch=[pltpu.VMEM((halves, blocks * ROWS, LANES), jnp.float32), *work],
    )
    from_far = send(to_far, lambda i: i + 1 if i % 2 else i - 1)
    from_near = send(to_near, lambda i: i ^ 1)
    while 2 * apart < blocks:
        history = call(join_kernel, f32(2 * history.shape[0], 9, depth, own), (*after, history, history_in), loose=len(after))
        slots += [slot ^ apart for slot in slots]
        apart, after = 2 * apart, [to_near]
        history_in = swap(history, apart)
    history = call(
        join_kernel, f32(2 * history.shape[0], 9, depth, own), (from_near, from_far, history, history_in), loose=2
    )
    slots += [slot ^ apart for slot in slots]
    history_in = swap(history, 1)
    vectors, keep = call(
        second_kernel,
        (f32(6, blocks, own), f32(9, blocks, own)),
        (state, index, to_near, to_far, from_far, from_near),
        scratch=work,
    )
    count = -(-len(pairs(depth)) // 8) * 8
    message = call(
        functools.partial(gram_kernel, depth, (tuple(slots), tuple(slot ^ 1 for slot in slots))),
        f32(7, blocks, own),
        (vectors, keep, history, history_in),
        scratch=[
            pltpu.VMEM((halves, blocks * 9 * depth, LANES), jnp.float32),
            pltpu.VMEM((count, LANES), jnp.float32),
        ],
    )
    square = sectors == 4
    parts = [message] + [None] * (sectors - 1)
    for by in sorted(range(1, sectors), reverse=True):
        parts[by] = send(message, (lambda i: i ^ by) if square else (lambda i: i - by))
    return call(
        functools.partial(solve_kernel, depth, square),
        (f32(3, own), f32(3, own)),
        (*parts, keep, past_dual, past_dual_gap, past_velocity, past_velocity_gap),
        scratch=[pltpu.VMEM((count, LANES), jnp.float32)],
    )


def solution(mesh):
    in_specs = (
        P(None, ("sector", "dom")),
        P(None, ("sector", "dom")),
        P(("sector", "dom")),
        P("sector", None),
        P(None, ("sector", "dom")),
        P(None, ("sector", "dom")),
        P(None, ("sector", "dom")),
        P(("sector", "dom")),
        P(None, None, ("sector", "dom")),
        P(None, None, ("sector", "dom")),
        P(None, None, ("sector", "dom")),
        P(None, None, ("sector", "dom")),
    )
    out_specs = (P(None, ("sector", "dom")), P(None, ("sector", "dom")))
    return jax.shard_map(
        per_device, mesh=mesh, in_specs=in_specs, out_specs=out_specs, check_vma=False
    )
```

```python
import functools
import itertools

import jax
import jax.numpy as jnp
from jax import lax
from jax.experimental import pallas as pl
from jax.experimental.pallas import tpu as pltpu
from jax.sharding import PartitionSpec as P

LANES = 128
VMEM_LIMIT = 24 * 1024 * 1024

STRAIN, DUAL, STEP, SPEED, LOAD, NEXT_STEP, NEXT_SPEED, INDEX, ROWS = 0, 36, 39, 40, 43, 46, 47, 50, 56
KEPT_NEXT_STEP, KEPT_LOAD, KEPT = 40, 41, 44
SPLITS = 2


def vmem():
    return pl.BlockSpec(memory_space=pltpu.VMEM)


def smem():
    return pl.BlockSpec(memory_space=pltpu.SMEM)


def call(kernel, outs, args, scalars=0, loose=0, scratch=()):
    return pl.pallas_call(
        kernel,
        out_shape=outs,
        in_specs=[smem()] * scalars
        + [pl.BlockSpec(memory_space=pl.ANY)] * loose
        + [vmem()] * (len(args) - scalars - loose),
        out_specs=jax.tree.map(lambda _: vmem(), outs),
        scratch_shapes=list(scratch),
        compiler_params=pltpu.CompilerParams(vmem_limit_bytes=VMEM_LIMIT),
    )(*args)


def f32(*shape):
    return jax.ShapeDtypeStruct(shape, jnp.float32)


def repeat(blocks, body, init):
    if blocks == 8:
        return body(slice(0, 8), 0, init)
    return lax.fori_loop(
        0, blocks // 8, lambda step, carry: body(pl.ds(pl.multiple_of(8 * step, 8), 8), 8 * step, carry), init
    )


def project_cone(trial):
    center = 0.5 * (trial[0] + trial[1])
    spread = 0.5 * (trial[0] - trial[1])
    shear = trial[2]
    radius = jnp.sqrt(spread * spread + shear * shear)
    upper = center + radius
    lower = center - radius
    iso_part = 0.5 * (jnp.maximum(upper, 0.0) + jnp.maximum(lower, 0.0))
    factor = jnp.clip((center + radius) / (2.0 * jnp.maximum(radius, 0.05)), 0.0, 1.0)
    return (iso_part + factor * spread, iso_part - factor * spread, factor * shear)


def fetch(pairs, sems):
    copies = [pltpu.make_async_copy(source, target, sems.at[at]) for at, (source, target) in enumerate(pairs)]
    for copy in copies:
        copy.start()
    for copy in copies:
        copy.wait()


def in_hbm(*values):
    return tuple(pltpu.with_memory_space_constraint(value, pltpu.HBM) for value in values)


def nodes_kernel(speed_in, mobility_in, seam_in, gap_u, ahead, speed, mobility, seam, sems):
    depth = gap_u.shape[1]
    start = ahead.shape[0] - 3 * depth
    gaps = [(gap_u.at[c], ahead.at[pl.ds(start + depth * c, depth)]) for c in range(3)]
    fetch(((speed_in, speed), (mobility_in, mobility), (seam_in, seam), *gaps), sems)
    own = speed.shape[1]
    ahead[0:3, :] = speed[...]
    ahead[3:4, :] = mobility[...]
    ahead[4:8, :] = jnp.zeros((4, own), jnp.float32)
    for row in range(8, start):
        ahead[row : row + 1, :] = seam[:, (row - 8) * own : (row - 7) * own].astype(jnp.float32)


def base_kernel(counts, after, *refs):
    count = (len(refs) - 2) // 2
    sources, base, held, sems = refs[:count], refs[count], refs[count + 1 : -1], refs[-1]
    fetch(zip(sources, held), sems)
    strain, dual, speed, load, mobility, corners = held
    own = speed.shape[1]
    slot = lax.broadcasted_iota(jnp.int32, (1, own), 1)
    alive = (slot < counts[0]).astype(jnp.float32)
    base[STRAIN:DUAL, :] = strain[...] * alive
    base[DUAL : DUAL + 3, :] = dual[...] * alive
    base[STEP : STEP + 1, :] = mobility[...]
    base[SPEED : SPEED + 3, :] = speed[...]
    base[LOAD : LOAD + 3, :] = load[...]
    base[NEXT_STEP:INDEX, :] = jnp.zeros((INDEX - NEXT_STEP, own), jnp.float32)
    base[INDEX : INDEX + 4, :] = corners[...].astype(jnp.float32)


def message_kernel(sector_nodes, depth, after, ahead, base, message, *shorter):
    own = message.shape[1]
    halves = own // LANES
    message[:NEXT_STEP, :] = base[:NEXT_STEP, :]
    message[NEXT_STEP : NEXT_STEP + 1, :] = ahead[3:4, :]
    message[NEXT_SPEED : NEXT_SPEED + 3, :] = ahead[0:3, :]
    message[INDEX + 4 :, :] = jnp.zeros((ROWS - INDEX - 4, own), jnp.float32)
    corners = base[INDEX : INDEX + 4, :].astype(jnp.int32)
    corner = jnp.concatenate([corners[:, h * LANES : (h + 1) * LANES] for h in range(halves)], axis=0)
    seam_rows = ahead.shape[0] - 8 - 3 * depth
    place = jnp.clip(corner - sector_nodes, 0, seam_rows * own - 1)
    high, low = place // LANES, place % LANES
    found = jnp.zeros(corner.shape, jnp.float32)
    for row in range(seam_rows):
        for h in range(halves):
            table = jnp.broadcast_to(ahead[8 + row : 9 + row, h * LANES : (h + 1) * LANES], corner.shape)
            value = jnp.take_along_axis(table, low, axis=1, mode="promise_in_bounds")
            found = jnp.where(high == row * halves + h, value, found)
    node = jnp.where(corner < sector_nodes, corner.astype(jnp.float32), found + float(sector_nodes))
    for h in range(halves):
        message[INDEX : INDEX + 4, h * LANES : (h + 1) * LANES] = node[4 * h : 4 * h + 4]
    for other in shorter:
        other[...] = message[: other.shape[0], :]


def history_kernel(after, gap_w, gap_u, history, sems):
    fetch(((gap_w, history.at[0:3]), (gap_u, history.at[3:6])), sems)


def wide_kernel(message, gaps, ahead, wide):
    depth = gaps.shape[1]
    start = ahead.shape[0] - 3 * depth
    wide[:ROWS, :] = message[...]
    for kind in range(6):
        wide[ROWS + depth * kind : ROWS + depth * (kind + 1), :] = gaps[kind]
    wide[ROWS + 6 * depth :, :] = ahead[start:, :]


def pair_kernel(*refs):
    left, right, joined = refs[-3:]
    joined[0] = left[ROWS:, :]
    joined[1] = right[ROWS:, :]


def copy_kernel(*refs):
    value, copied = refs[-2:]
    copied[...] = value[...]


def join_kernel(*refs):
    left, right, joined = refs[-3:]
    count = left.shape[0]
    joined[:count] = left[...]
    joined[count:] = right[...]


def sweep(strain_row, index, work, dual):
    table, terms, codes, nearby = work
    blocks, own = index.shape[1:]
    halves = own // LANES
    here = lax.axis_index("dom")
    row = lax.broadcasted_iota(jnp.int32, (blocks, LANES), 0)
    left_block = ((row ^ here) - 1) ^ here
    right_block = ((row ^ here) + 1) ^ here

    def wide(j, group, block, part):
        piece = table[j, group, part * LANES : (part + 1) * LANES][block : block + 1]
        return jnp.broadcast_to(piece, (blocks, LANES))

    def take_sides(group, first, sides):
        left, right = (list(side) for side in sides)
        for block in range(8):
            for j in range(3):
                left[j] = jnp.where(left_block == first + block, wide(j, group, block, halves - 1), left[j])
                right[j] = jnp.where(right_block == first + block, wide(j, group, block, 0), right[j])
        return tuple(left), tuple(right)

    blank = tuple(jnp.zeros((blocks, LANES), jnp.float32) for _ in range(3))
    left, right = repeat(blocks, take_sides, (blank, blank))
    speed = []
    for k in range(4):
        parts = []
        for h in range(halves):
            number = index[k, :, h * LANES : (h + 1) * LANES]
            high, low = number // LANES, number % LANES

            def take(value):
                return jnp.take_along_axis(value, low, axis=1, mode="promise_in_bounds")

            found = [take(table[j, :, 0:LANES]) for j in range(3)]
            for part in range(1, halves):
                mask = high % halves == part
                found = [
                    jnp.where(mask, take(table[j, :, part * LANES : (part + 1) * LANES]), found[j]) for j in range(3)
                ]
            mask = number // own == left_block
            found = [jnp.where(mask, take(left[j]), found[j]) for j in range(3)]
            mask = number // own == right_block
            found = [jnp.where(mask, take(right[j]), found[j]) for j in range(3)]

            def take_group(group, first, found):
                for part, block in itertools.product(range(halves), range(8)):
                    mask = high == (blocks + first + block) * halves + part
                    found = [jnp.where(mask, take(wide(3 + j, group, block, part)), found[j]) for j in range(3)]
                return tuple(found)

            parts.append(repeat(blocks, take_group, tuple(found)))
        speed.append([jnp.concatenate([found[j] for found in parts], axis=1) for j in range(3)])
    rate = []
    for c in range(3):
        total = None
        for k in range(4):
            for j in range(3):
                term = strain_row(12 * c + 3 * k + j) * speed[k][j]
                total = term if total is None else total + term
        rate.append(total)
    trial = [rate[c] + dual[c] for c in range(3)]
    cone = project_cone(trial)
    dual_next = [trial[c] - cone[c] for c in range(3)]
    misfit = [rate[c] - cone[c] + dual_next[c] for c in range(3)]
    for k in range(4):
        for j in range(3):
            rest = sum(strain_row(12 * c + 3 * k + j) * misfit[c] for c in range(3))
            for split in range(SPLITS):
                term = rest.astype(jnp.bfloat16).astype(jnp.float32)
                terms[SPLITS * j + split, k] = term
                rest = rest - term

    near_rows = halves + 2
    next_rows = halves * blocks
    row_wide = lax.broadcasted_iota(jnp.int32, (blocks, own), 0) ^ here
    for k in range(4):
        number = index[k]
        block_of, half = number // own, number // LANES % halves
        near = jnp.where(block_of == ((row_wide - 1) ^ here), 0, 1 + half)
        near = jnp.where(block_of == ((row_wide + 1) ^ here), 1 + halves, near)
        codes[0, k] = (number % LANES).astype(jnp.float32)
        codes[1, k] = jnp.where(block_of < blocks, near, -1).astype(jnp.float32)
        codes[2, k] = jnp.where(block_of < blocks, -1, half * blocks + block_of - blocks).astype(jnp.float32)

    values = 3 * SPLITS
    per_tile = 16 // near_rows
    near_tiles = -(-values // per_tile)
    iota = lax.broadcasted_iota(jnp.int32, (16, own), 0)
    near_iota = (iota % near_rows).astype(jnp.float32).astype(jnp.bfloat16)
    value_iota = (iota // near_rows).astype(jnp.float32).astype(jnp.bfloat16)
    value_masks = [value_iota == jnp.full((16, own), float(at), jnp.bfloat16) for at in range(per_tile)]
    iota = iota.astype(jnp.float32)
    low_iota = [(iota + float(16 * g)).astype(jnp.bfloat16) for g in range(LANES // 16)]
    next_iota = [(iota + float(16 * g)).astype(jnp.bfloat16) for g in range(next_rows // 16)]
    one = jnp.ones((16, own), jnp.bfloat16)
    zero = jnp.zeros((16, own), jnp.bfloat16)

    def spread_row(value):
        return jnp.broadcast_to(value, (16, own)).astype(jnp.bfloat16)

    def add_group(group, first, total):
        for block in range(8):
            part = None
            for k in range(4):
                low_row, near_row, next_row = (
                    spread_row(codes[at, k, group, :][block : block + 1]) for at in range(3)
                )
                rows = [spread_row(terms[at, k, group, :][block : block + 1]) for at in range(values)]
                spread = jnp.concatenate([jnp.where(low_row == value, one, zero) for value in low_iota], axis=0)
                mask = near_row == near_iota
                weights = []
                for tile in range(near_tiles):
                    inside = rows[tile * per_tile : (tile + 1) * per_tile]
                    value = inside[-1]
                    for at in range(len(inside) - 1):
                        value = jnp.where(value_masks[at], inside[at], value)
                    weights.append(jnp.where(mask, value, zero))
                masks = [next_row == value for value in next_iota]
                weights += [jnp.where(mask, row, zero) for row in rows for mask in masks]
                product = lax.dot_general(
                    jnp.concatenate(weights, axis=0),
                    spread,
                    (((1,), (1,)), ((), ())),
                    preferred_element_type=jnp.float32,
                )
                part = product if part is None else part + product
            start = (first + block) * 16 * near_tiles
            if not isinstance(start, int):
                start = pl.multiple_of(start, 16)
            nearby[pl.ds(start, 16 * near_tiles), :] = part[: 16 * near_tiles]
            total += part[16 * near_tiles :]
        return total

    total = repeat(blocks, add_group, jnp.zeros((values * next_rows, LANES), jnp.float32))

    def near_force(j, row):
        return sum(
            nearby[pl.ds((SPLITS * j + split) * near_rows + row, blocks, stride=16 * near_tiles), :]
            for split in range(SPLITS)
        )

    force_own, force_next = [], []
    for j in range(3):
        halves_own = [near_force(j, 1 + h) for h in range(halves)]
        to_left, to_right = near_force(j, 0), near_force(j, 1 + halves)
        from_right = from_left = jnp.zeros((blocks, LANES), jnp.float32)
        for block in range(blocks):
            wide_left = jnp.broadcast_to(to_left[block : block + 1], (blocks, LANES))
            wide_right = jnp.broadcast_to(to_right[block : block + 1], (blocks, LANES))
            from_right = jnp.where(right_block == block, wide_left, from_right)
            from_left = jnp.where(left_block == block, wide_right, from_left)
        halves_own[-1] = halves_own[-1] + from_right
        halves_own[0] = halves_own[0] + from_left
        force_own.append(jnp.concatenate(halves_own, axis=1))
        whole = sum(
            total[(SPLITS * j + split) * next_rows : (SPLITS * j + split + 1) * next_rows] for split in range(SPLITS)
        )
        force_next.append(jnp.concatenate([whole[h * blocks : (h + 1) * blocks] for h in range(halves)], axis=1))
    return dual_next, force_own, force_next


def stack_block(piece, slot, rows, stack):
    held = min(rows, piece.shape[0])
    for h in range(stack.shape[0]):
        stack[h, slot * rows : slot * rows + held, :] = piece[:held, h * LANES : (h + 1) * LANES]


def across(stack, row, rows):
    blocks = stack.shape[1] // rows
    return jnp.concatenate(
        [stack[h, pl.ds(row, blocks, stride=rows), :] for h in range(stack.shape[0])], axis=1
    )


def first_kernel(order, *refs):
    blocks = len(order)
    pieces = refs[:blocks]
    state, index, to_near, to_far, stack = refs[blocks : blocks + 5]
    work = refs[blocks + 5 :]
    table = work[0]
    own = index.shape[2]
    for piece, slot in zip(pieces, order):
        stack_block(piece, slot, ROWS, stack)
    flip = lax.axis_index("dom") * own
    even = lax.axis_index("sector") % 2 == 0
    for k in range(4):
        index[k] = across(stack, INDEX + k, ROWS).astype(jnp.int32) ^ flip
    for row in range(36):
        state[row] = across(stack, STRAIN + row, ROWS)
    step = across(stack, STEP, ROWS)
    state[STEP] = step
    state[KEPT_NEXT_STEP] = across(stack, NEXT_STEP, ROWS)
    for j in range(3):
        state[KEPT_LOAD + j] = across(stack, LOAD + j, ROWS)
        table[j] = across(stack, SPEED + j, ROWS)
        table[3 + j] = across(stack, NEXT_SPEED + j, ROWS)
    dual = [across(stack, DUAL + c, ROWS) for c in range(3)]
    dual, force_own, force_next = sweep(lambda row: state[row], index, work, dual)
    for c in range(3):
        state[DUAL + c] = dual[c]
        mine = table[c] - step * (force_own[c] - state[KEPT_LOAD + c])
        to_near[c] = jnp.where(even, force_next[c], mine)
        to_far[c] = jnp.where(even, mine, force_next[c])


def second_kernel(state, index, to_near, to_far, from_far, from_near, vectors, keep, *work):
    table = work[0]
    even = lax.axis_index("sector") % 2 == 0
    step, next_step = state[STEP], state[KEPT_NEXT_STEP]
    for j in range(3):
        near, far = to_near[j], to_far[j]
        near_in, far_in = from_near[j], from_far[j]
        table[j] = jnp.where(even, far, near) - step * jnp.where(even, far_in, near_in)
        table[3 + j] = jnp.where(even, near_in, far_in) - next_step * jnp.where(even, near, far)
    dual = [state[DUAL + c] for c in range(3)]
    dual_next, force_own, force_next = sweep(lambda row: state[row], index, work, dual)
    for c in range(3):
        after = table[c] - step * (force_own[c] - state[KEPT_LOAD + c])
        vectors[c] = after - table[c]
        vectors[3 + c] = -(next_step * force_next[c])
        keep[c] = dual_next[c]
        keep[3 + c] = dual_next[c] - dual[c]
        keep[6 + c] = after


def pairs(depth):
    return [(i, l) for i in range(depth) for l in range(i, depth + 1)]


def gram_kernel(depth, slots, vectors, keep, *refs):
    blocks, own = keep.shape[1:]
    halves = own // LANES
    rows = 9 * depth
    message, stack, rows_sum = refs[len(slots) :]
    for piece, own_slots in zip(refs, slots):
        for at, slot in enumerate(own_slots):
            stack_block(piece.at[at] if len(piece.shape) == 3 else piece.at[ROWS:], slot, rows, stack)
    for row in range(6):
        message[row] = vectors[row]
    message[6] = jnp.zeros((blocks, own), jnp.float32)
    sums, pushed, pushed_twice = {}, [0.0] * (depth + 1), 0.0
    for c, h, top in itertools.product(range(3), range(halves), range(0, blocks, 8)):
        lanes, group = slice(h * LANES, (h + 1) * LANES), slice(top, top + 8)

        def gap(kind, i):
            return stack[h, pl.ds(top * rows + depth * (3 * kind + c) + i, 8, stride=rows), :]

        for kind, moved in enumerate((keep[3 + c, group, lanes], vectors[c, group, lanes])):
            gaps = [moved - gap(kind, i) for i in range(depth)] + [moved]
            for i, l in pairs(depth):
                term = gaps[i] * gaps[l]
                sums[i, l] = sums[i, l] + term if (i, l) in sums else term
        push = vectors[3 + c, group, lanes]
        for i in range(depth):
            pushed[i] = pushed[i] + gap(2, i) * push
        pushed_twice = pushed_twice + push * push
    for at, (i, l) in enumerate(pairs(depth)):
        value = sums[i, l] + pushed_twice - pushed[i] - pushed[l]
        rows_sum[at : at + 1, :] = jnp.sum(value, axis=0, keepdims=True)
    count = len(pairs(depth))
    if rows_sum.shape[0] > count:
        rows_sum[count:, :] = jnp.zeros((rows_sum.shape[0] - count, LANES), jnp.float32)
    whole = jnp.broadcast_to(jnp.sum(rows_sum[...], axis=1, keepdims=True), rows_sum.shape)
    lane = lax.broadcasted_iota(jnp.int32, (8, LANES), 1)
    out = whole[0:8]
    for group in range(1, rows_sum.shape[0] // 8):
        out = jnp.where(lane == group, whole[8 * group : 8 * group + 8], out)
    message[6, 0:8, 0:LANES] = out


def solve_kernel(depth, square, *refs):
    parts = refs[:-8]
    keep, past_w, gap_w, past_u, gap_u, new_u, new_w, total = refs[-8:]
    own = new_u.shape[1]
    tile = parts[0][6, 0:8, 0:LANES]
    for other in parts[1:]:
        tile = tile + other[6, 0:8, 0:LANES]
    even = lax.axis_index("sector") % 2 == 0

    def ahead(by, row):
        if square and by in (1, 3):
            return jnp.where(even, parts[by][row], parts[4 - by][row])
        return parts[by][row]

    sectors = len(parts)
    pushes = [[ahead(by, 3 + j) for j in range(3)] for by in range(sectors)]
    cross = sum(ahead(by, j) * pushes[by - 1][j] for by in range(sectors) for j in range(3))
    cross = jnp.sum(jnp.sum(cross, axis=0, keepdims=True), axis=1, keepdims=True)
    last = [keep[6 + j, 0:1] + pushes[-1][j][0:1] for j in range(3)] + [keep[c, 0:1] for c in range(3)]
    for group in range(total.shape[0] // 8):
        total[8 * group : 8 * group + 8, :] = jnp.broadcast_to(tile[:, group : group + 1], (8, LANES))
    matrix = {
        pair: jnp.broadcast_to(total[at : at + 1, :], (depth, LANES)) + 2.0 * cross
        for at, pair in enumerate(pairs(depth))
    }
    ridge = 0.0001 * sum(matrix[i, i] for i in range(depth)) / depth
    for i in range(depth):
        matrix[i, i] = matrix[i, i] + ridge
    inverse = []
    for step in range(depth):
        inverse.append(1.0 / matrix[step, step])
        for i in range(step + 1, depth):
            factor = matrix[step, i] * inverse[step]
            for l in range(i, depth + 1):
                matrix[i, l] = matrix[i, l] - factor * matrix[step, l]
    weights = [None] * depth
    for i in reversed(range(depth)):
        value = matrix[i, depth]
        for l in range(i + 1, depth):
            value = value - matrix[i, l] * weights[l]
        weights[i] = value * inverse[i]
    row = lax.broadcasted_iota(jnp.int32, (depth, LANES), 0)
    weight = weights[0]
    for i in range(1, depth):
        weight = jnp.where(row == i, weights[i], weight)
    for start in range(0, own, LANES):
        lanes = slice(start, start + LANES)
        for at, (past, gap, out) in enumerate(((past_u, gap_u, new_u), (past_w, gap_w, new_w))):
            for c in range(3):
                value = jnp.broadcast_to(last[3 * at + c][:, lanes], (depth, LANES))
                change = weight * (value - past[c, :, lanes] - gap[c, :, lanes])
                out[c : c + 1, lanes] = value[0:1] - jnp.sum(change, axis=0, keepdims=True)


def per_device(
    strain_map,
    corner_nodes,
    counts,
    seam_nodes,
    velocity,
    dual_state,
    nodal_load,
    mobility,
    past_dual,
    past_dual_gap,
    past_velocity,
    past_velocity_gap,
):
    own = velocity.shape[1]
    halves = own // LANES
    blocks = lax.axis_size("dom")
    sectors = lax.axis_size("sector")
    depth = past_dual.shape[0]
    seam_rows = seam_nodes.shape[1] // own
    mobility = mobility.reshape(1, own)
    past_dual, past_dual_gap, past_velocity, past_velocity_gap = (
        value.transpose(1, 0, 2) for value in (past_dual, past_dual_gap, past_velocity, past_velocity_gap)
    )

    def send(value, target):
        return lax.ppermute(value, "sector", [(i, target(i) % sectors) for i in range(sectors)])

    def swap(value, bits):
        return lax.ppermute(value, "dom", [(i, i ^ bits) for i in range(blocks)])

    nodes = (velocity, mobility, seam_nodes)
    ahead = call(
        nodes_kernel,
        f32(8 + seam_rows + 3 * depth, own),
        in_hbm(*nodes, past_velocity_gap),
        loose=len(nodes) + 1,
        scratch=[pltpu.VMEM(value.shape, value.dtype) for value in nodes]
        + [pltpu.SemaphoreType.DMA((len(nodes) + 3,))],
    )
    held = (strain_map, dual_state, velocity, nodal_load, mobility, corner_nodes)
    base = call(
        base_kernel,
        f32(INDEX + 4, own),
        (counts, ahead, *in_hbm(*held)),
        scalars=1,
        loose=len(held) + 1,
        scratch=[pltpu.VMEM(value.shape, value.dtype) for value in held] + [pltpu.SemaphoreType.DMA((len(held),))],
    )
    ahead = send(ahead, lambda i: i - 1)
    history = call(
        history_kernel,
        f32(6, depth, own),
        (base, *in_hbm(past_dual_gap, past_velocity_gap)),
        loose=3,
        scratch=[pltpu.SemaphoreType.DMA((2,))],
    )
    partners = sorted(range(2, blocks, 2), reverse=True)
    lengths = [max(INDEX + 4, ROWS - place) for place in range(len(partners))]
    messages = call(
        functools.partial(message_kernel, own * blocks, depth),
        tuple(f32(rows, own) for rows in sorted(set(lengths), reverse=True)),
        (history, ahead, base),
        loose=1,
    )
    wide = call(wide_kernel, f32(ROWS + 9 * depth, own), (messages[0], history, ahead))
    pieces = {0: wide}
    for bits, rows in zip(partners, lengths):
        pieces[bits] = swap(wide if bits == 2 else next(value for value in messages if value.shape[0] == rows), bits)
    for even in range(0, blocks, 2):
        pieces[even + 1] = swap(pieces[even], 1)
    histories, slots = [pieces[block] for block in range(4)], [(block,) for block in range(4)]
    far_ones = [bits for bits in partners if bits > 2]
    history = call(
        pair_kernel, f32(2, 9 * depth, own), (*(pieces[bits] for bits in far_ones), wide, pieces[2]), loose=len(far_ones)
    )
    known, apart, later = (0, 2), 4, []
    while apart < blocks:
        other = swap(history, apart)
        later.append((other, tuple(slot ^ apart for slot in known)))
        known += later[-1][1]
        apart *= 2
        if apart < blocks:
            history = call(join_kernel, f32(2 * history.shape[0], 9 * depth, own), (history, other))
    order = tuple(reversed(range(blocks)))
    sector = f32(3, blocks, own)
    work = [
        pltpu.VMEM((6, blocks, own), jnp.float32),
        pltpu.VMEM((3 * SPLITS, 4, blocks, own), jnp.float32),
        pltpu.VMEM((3, 4, blocks, own), jnp.float32),
        pltpu.VMEM((blocks * 16 * -(-3 * SPLITS * (halves + 2) // 16), LANES), jnp.float32),
    ]
    state, index, to_near, to_far = call(
        functools.partial(first_kernel, order),
        (f32(KEPT, blocks, own), jax.ShapeDtypeStruct((4, blocks, own), jnp.int32), sector, sector),
        tuple(pieces[block] for block in order),
        scratch=[pltpu.VMEM((halves, blocks * ROWS, LANES), jnp.float32), *work],
    )
    from_far = send(to_far, lambda i: i + 1 if i % 2 else i - 1)
    from_near = send(to_near, lambda i: i ^ 1)
    for other, far in later:
        held_back = call(copy_kernel, f32(*other.shape), (from_near, from_far, other), loose=2)
        histories += [other, swap(held_back, 1)]
        slots += [far, tuple(slot ^ 1 for slot in far)]
    vectors, keep = call(
        second_kernel,
        (f32(6, blocks, own), f32(9, blocks, own)),
        (state, index, to_near, to_far, from_far, from_near),
        scratch=work,
    )
    count = -(-len(pairs(depth)) // 8) * 8
    message = call(
        functools.partial(gram_kernel, depth, tuple(slots)),
        f32(7, blocks, own),
        (vectors, keep, *histories),
        scratch=[
            pltpu.VMEM((halves, blocks * 9 * depth, LANES), jnp.float32),
            pltpu.VMEM((count, LANES), jnp.float32),
        ],
    )
    square = sectors == 4
    parts = [message] + [None] * (sectors - 1)
    for by in sorted(range(1, sectors), reverse=True):
        parts[by] = send(message, (lambda i: i ^ by) if square else (lambda i: i - by))
    return call(
        functools.partial(solve_kernel, depth, square),
        (f32(3, own), f32(3, own)),
        (*parts, keep, past_dual, past_dual_gap, past_velocity, past_velocity_gap),
        scratch=[pltpu.VMEM((count, LANES), jnp.float32)],
    )


def solution(mesh):
    in_specs = (
        P(None, ("sector", "dom")),
        P(None, ("sector", "dom")),
        P(("sector", "dom")),
        P("sector", None),
        P(None, ("sector", "dom")),
        P(None, ("sector", "dom")),
        P(None, ("sector", "dom")),
        P(("sector", "dom")),
        P(None, None, ("sector", "dom")),
        P(None, None, ("sector", "dom")),
        P(None, None, ("sector", "dom")),
        P(None, None, ("sector", "dom")),
    )
    out_specs = (P(None, ("sector", "dom")), P(None, ("sector", "dom")))
    return jax.shard_map(
        per_device, mesh=mesh, in_specs=in_specs, out_specs=out_specs, check_vma=False
    )
```

```python
import functools
import itertools

import jax
import jax.numpy as jnp
from jax import lax
from jax.experimental import pallas as pl
from jax.experimental.pallas import tpu as pltpu
from jax.sharding import PartitionSpec as P

LANES = 128
VMEM_LIMIT = 24 * 1024 * 1024

STRAIN, DUAL, STEP, SPEED, LOAD, NEXT_STEP, NEXT_SPEED, INDEX, ROWS = 0, 36, 39, 40, 43, 46, 47, 50, 56
KEPT_NEXT_STEP, KEPT_LOAD, KEPT = 40, 41, 44
SPLITS = 2


def vmem():
    return pl.BlockSpec(memory_space=pltpu.VMEM)


def smem():
    return pl.BlockSpec(memory_space=pltpu.SMEM)


def call(kernel, outs, args, scalars=0, loose=0, scratch=()):
    return pl.pallas_call(
        kernel,
        out_shape=outs,
        in_specs=[smem()] * scalars
        + [pl.BlockSpec(memory_space=pl.ANY)] * loose
        + [vmem()] * (len(args) - scalars - loose),
        out_specs=jax.tree.map(lambda _: vmem(), outs),
        scratch_shapes=list(scratch),
        compiler_params=pltpu.CompilerParams(vmem_limit_bytes=VMEM_LIMIT),
    )(*args)


def f32(*shape):
    return jax.ShapeDtypeStruct(shape, jnp.float32)


def repeat(blocks, body, init):
    if blocks == 8:
        return body(slice(0, 8), 0, init)
    return lax.fori_loop(
        0, blocks // 8, lambda step, carry: body(pl.ds(pl.multiple_of(8 * step, 8), 8), 8 * step, carry), init
    )


def project_cone(trial):
    center = 0.5 * (trial[0] + trial[1])
    spread = 0.5 * (trial[0] - trial[1])
    shear = trial[2]
    radius = jnp.sqrt(spread * spread + shear * shear)
    upper = center + radius
    lower = center - radius
    iso_part = 0.5 * (jnp.maximum(upper, 0.0) + jnp.maximum(lower, 0.0))
    factor = jnp.clip((center + radius) / (2.0 * jnp.maximum(radius, 0.05)), 0.0, 1.0)
    return (iso_part + factor * spread, iso_part - factor * spread, factor * shear)


def fetch(pairs, sems):
    copies = [pltpu.make_async_copy(source, target, sems.at[at]) for at, (source, target) in enumerate(pairs)]
    for copy in copies:
        copy.start()
    for copy in copies:
        copy.wait()


def in_hbm(*values):
    return tuple(pltpu.with_memory_space_constraint(value, pltpu.HBM) for value in values)


def nodes_kernel(speed_in, mobility_in, seam_in, gap_u, ahead, speed, mobility, seam, sems):
    depth = gap_u.shape[1]
    start = ahead.shape[0] - 8 - 3 * depth
    gaps = [(gap_u.at[c], ahead.at[pl.ds(start + depth * c, depth)]) for c in range(3)]
    fetch(((speed_in, speed), (mobility_in, mobility), (seam_in, seam), *gaps), sems)
    own = speed.shape[1]
    ahead[0:3, :] = speed[...]
    ahead[3:4, :] = mobility[...]
    ahead[4:8, :] = jnp.zeros((4, own), jnp.float32)
    ahead[start + 3 * depth :, :] = jnp.zeros((8, own), jnp.float32)
    for row in range(8, start):
        ahead[row : row + 1, :] = seam[:, (row - 8) * own : (row - 7) * own].astype(jnp.float32)


def base_kernel(counts, after, *refs):
    count = (len(refs) - 3) // 2
    sources, base, first, held, sems = refs[:count], refs[count], refs[count + 1], refs[count + 2 : -1], refs[-1]
    fetch(zip(sources, held), sems)
    strain, dual, speed, load, mobility, corners = held
    own = speed.shape[1]
    slot = lax.broadcasted_iota(jnp.int32, (1, own), 1)
    alive = (slot < counts[0]).astype(jnp.float32)
    base[STRAIN:DUAL, :] = strain[...] * alive
    base[DUAL : DUAL + 3, :] = dual[...] * alive
    base[STEP : STEP + 1, :] = mobility[...]
    base[SPEED : SPEED + 3, :] = speed[...]
    base[LOAD : LOAD + 3, :] = load[...]
    base[NEXT_STEP:INDEX, :] = jnp.zeros((INDEX - NEXT_STEP, own), jnp.float32)
    base[INDEX : INDEX + 4, :] = corners[...].astype(jnp.float32)
    first[...] = base[:NEXT_STEP, :]


def message_kernel(sector_nodes, depth, after, ahead, base, message, second):
    own = message.shape[1]
    halves = own // LANES
    message[:NEXT_STEP, :] = base[:NEXT_STEP, :]
    message[NEXT_STEP : NEXT_STEP + 1, :] = ahead[3:4, :]
    message[NEXT_SPEED : NEXT_SPEED + 3, :] = ahead[0:3, :]
    message[INDEX + 4 :, :] = jnp.zeros((ROWS - INDEX - 4, own), jnp.float32)
    corners = base[INDEX : INDEX + 4, :].astype(jnp.int32)
    corner = jnp.concatenate([corners[:, h * LANES : (h + 1) * LANES] for h in range(halves)], axis=0)
    seam_rows = ahead.shape[0] - 16 - 3 * depth
    place = jnp.clip(corner - sector_nodes, 0, seam_rows * own - 1)
    high, low = place // LANES, place % LANES
    found = jnp.zeros(corner.shape, jnp.float32)
    for row in range(seam_rows):
        for h in range(halves):
            table = jnp.broadcast_to(ahead[8 + row : 9 + row, h * LANES : (h + 1) * LANES], corner.shape)
            value = jnp.take_along_axis(table, low, axis=1, mode="promise_in_bounds")
            found = jnp.where(high == row * halves + h, value, found)
    node = jnp.where(corner < sector_nodes, corner.astype(jnp.float32), found + float(sector_nodes))
    for h in range(halves):
        message[INDEX : INDEX + 4, h * LANES : (h + 1) * LANES] = node[4 * h : 4 * h + 4]
    second[...] = message[NEXT_STEP : NEXT_STEP + 8, :]


def history_kernel(after, gap_w, gap_u, history, sems):
    fetch(((gap_w, history.at[0:3]), (gap_u, history.at[3:6])), sems)


def wide_kernel(*refs):
    message, gaps, ahead, wide = refs[-4:]
    depth = gaps.shape[1]
    start = ahead.shape[0] - 8 - 3 * depth
    wide[:ROWS, :] = message[...]
    for kind in range(6):
        wide[ROWS + depth * kind : ROWS + depth * (kind + 1), :] = gaps[kind]
    wide[ROWS + 6 * depth :, :] = ahead[start : start + 3 * depth, :]


def pair_kernel(*refs):
    left, right, joined = refs[-3:]
    joined[0] = left[ROWS:, :]
    joined[1] = right[ROWS:, :]


def copy_kernel(*refs):
    value, copied = refs[-2:]
    copied[...] = value[...]


def join_kernel(*refs):
    left, right, joined = refs[-3:]
    count = left.shape[0]
    joined[:count] = left[...]
    joined[count:] = right[...]


def sweep(strain_row, index, work, dual):
    table, terms, codes, nearby = work
    blocks, own = index.shape[1:]
    halves = own // LANES
    here = lax.axis_index("dom")
    row = lax.broadcasted_iota(jnp.int32, (blocks, LANES), 0)
    left_block = ((row ^ here) - 1) ^ here
    right_block = ((row ^ here) + 1) ^ here

    def wide(j, group, block, part):
        piece = table[j, group, part * LANES : (part + 1) * LANES][block : block + 1]
        return jnp.broadcast_to(piece, (blocks, LANES))

    def take_sides(group, first, sides):
        left, right = (list(side) for side in sides)
        for block in range(8):
            for j in range(3):
                left[j] = jnp.where(left_block == first + block, wide(j, group, block, halves - 1), left[j])
                right[j] = jnp.where(right_block == first + block, wide(j, group, block, 0), right[j])
        return tuple(left), tuple(right)

    blank = tuple(jnp.zeros((blocks, LANES), jnp.float32) for _ in range(3))
    left, right = repeat(blocks, take_sides, (blank, blank))
    speed = []
    for k in range(4):
        parts = []
        for h in range(halves):
            number = index[k, :, h * LANES : (h + 1) * LANES]
            high, low = number // LANES, number % LANES

            def take(value):
                return jnp.take_along_axis(value, low, axis=1, mode="promise_in_bounds")

            found = [take(table[j, :, 0:LANES]) for j in range(3)]
            for part in range(1, halves):
                mask = high % halves == part
                found = [
                    jnp.where(mask, take(table[j, :, part * LANES : (part + 1) * LANES]), found[j]) for j in range(3)
                ]
            mask = number // own == left_block
            found = [jnp.where(mask, take(left[j]), found[j]) for j in range(3)]
            mask = number // own == right_block
            found = [jnp.where(mask, take(right[j]), found[j]) for j in range(3)]

            def take_group(group, first, found):
                for part, block in itertools.product(range(halves), range(8)):
                    mask = high == (blocks + first + block) * halves + part
                    found = [jnp.where(mask, take(wide(3 + j, group, block, part)), found[j]) for j in range(3)]
                return tuple(found)

            parts.append(repeat(blocks, take_group, tuple(found)))
        speed.append([jnp.concatenate([found[j] for found in parts], axis=1) for j in range(3)])
    rate = []
    for c in range(3):
        total = None
        for k in range(4):
            for j in range(3):
                term = strain_row(12 * c + 3 * k + j) * speed[k][j]
                total = term if total is None else total + term
        rate.append(total)
    trial = [rate[c] + dual[c] for c in range(3)]
    cone = project_cone(trial)
    dual_next = [trial[c] - cone[c] for c in range(3)]
    misfit = [rate[c] - cone[c] + dual_next[c] for c in range(3)]
    for k in range(4):
        for j in range(3):
            rest = sum(strain_row(12 * c + 3 * k + j) * misfit[c] for c in range(3))
            for split in range(SPLITS):
                term = rest.astype(jnp.bfloat16).astype(jnp.float32)
                terms[SPLITS * j + split, k] = term
                rest = rest - term

    near_rows = halves + 2
    next_rows = halves * blocks
    row_wide = lax.broadcasted_iota(jnp.int32, (blocks, own), 0) ^ here
    for k in range(4):
        number = index[k]
        block_of, half = number // own, number // LANES % halves
        near = jnp.where(block_of == ((row_wide - 1) ^ here), 0, 1 + half)
        near = jnp.where(block_of == ((row_wide + 1) ^ here), 1 + halves, near)
        codes[0, k] = (number % LANES).astype(jnp.float32)
        codes[1, k] = jnp.where(block_of < blocks, near, -1).astype(jnp.float32)
        codes[2, k] = jnp.where(block_of < blocks, -1, half * blocks + block_of - blocks).astype(jnp.float32)

    values = 3 * SPLITS
    per_tile = 16 // near_rows
    near_tiles = -(-values // per_tile)
    iota = lax.broadcasted_iota(jnp.int32, (16, own), 0)
    near_iota = (iota % near_rows).astype(jnp.float32).astype(jnp.bfloat16)
    value_iota = (iota // near_rows).astype(jnp.float32).astype(jnp.bfloat16)
    value_masks = [value_iota == jnp.full((16, own), float(at), jnp.bfloat16) for at in range(per_tile)]
    iota = iota.astype(jnp.float32)
    low_iota = [(iota + float(16 * g)).astype(jnp.bfloat16) for g in range(LANES // 16)]
    next_iota = [(iota + float(16 * g)).astype(jnp.bfloat16) for g in range(next_rows // 16)]
    one = jnp.ones((16, own), jnp.bfloat16)
    zero = jnp.zeros((16, own), jnp.bfloat16)

    def spread_row(value):
        return jnp.broadcast_to(value, (16, own)).astype(jnp.bfloat16)

    def add_group(group, first, total):
        for block in range(8):
            part = None
            for k in range(4):
                low_row, near_row, next_row = (
                    spread_row(codes[at, k, group, :][block : block + 1]) for at in range(3)
                )
                rows = [spread_row(terms[at, k, group, :][block : block + 1]) for at in range(values)]
                spread = jnp.concatenate([jnp.where(low_row == value, one, zero) for value in low_iota], axis=0)
                mask = near_row == near_iota
                weights = []
                for tile in range(near_tiles):
                    inside = rows[tile * per_tile : (tile + 1) * per_tile]
                    value = inside[-1]
                    for at in range(len(inside) - 1):
                        value = jnp.where(value_masks[at], inside[at], value)
                    weights.append(jnp.where(mask, value, zero))
                masks = [next_row == value for value in next_iota]
                weights += [jnp.where(mask, row, zero) for row in rows for mask in masks]
                product = lax.dot_general(
                    jnp.concatenate(weights, axis=0),
                    spread,
                    (((1,), (1,)), ((), ())),
                    preferred_element_type=jnp.float32,
                )
                part = product if part is None else part + product
            start = (first + block) * 16 * near_tiles
            if not isinstance(start, int):
                start = pl.multiple_of(start, 16)
            nearby[pl.ds(start, 16 * near_tiles), :] = part[: 16 * near_tiles]
            total += part[16 * near_tiles :]
        return total

    total = repeat(blocks, add_group, jnp.zeros((values * next_rows, LANES), jnp.float32))

    def near_force(j, row):
        return sum(
            nearby[pl.ds((SPLITS * j + split) * near_rows + row, blocks, stride=16 * near_tiles), :]
            for split in range(SPLITS)
        )

    force_own, force_next = [], []
    for j in range(3):
        halves_own = [near_force(j, 1 + h) for h in range(halves)]
        to_left, to_right = near_force(j, 0), near_force(j, 1 + halves)
        from_right = from_left = jnp.zeros((blocks, LANES), jnp.float32)
        for block in range(blocks):
            wide_left = jnp.broadcast_to(to_left[block : block + 1], (blocks, LANES))
            wide_right = jnp.broadcast_to(to_right[block : block + 1], (blocks, LANES))
            from_right = jnp.where(right_block == block, wide_left, from_right)
            from_left = jnp.where(left_block == block, wide_right, from_left)
        halves_own[-1] = halves_own[-1] + from_right
        halves_own[0] = halves_own[0] + from_left
        force_own.append(jnp.concatenate(halves_own, axis=1))
        whole = sum(
            total[(SPLITS * j + split) * next_rows : (SPLITS * j + split + 1) * next_rows] for split in range(SPLITS)
        )
        force_next.append(jnp.concatenate([whole[h * blocks : (h + 1) * blocks] for h in range(halves)], axis=1))
    return dual_next, force_own, force_next


def stack_block(piece, slot, rows, stack, start=0):
    held, start = min(rows, piece.shape[0]), slot * rows + start
    for h in range(stack.shape[0]):
        stack[h, start : start + held, :] = piece[:held, h * LANES : (h + 1) * LANES]


def across(stack, row, rows):
    blocks = stack.shape[1] // rows
    return jnp.concatenate(
        [stack[h, pl.ds(row, blocks, stride=rows), :] for h in range(stack.shape[0])], axis=1
    )


def first_kernel(blocks, order, *refs):
    pieces = refs[: len(order)]
    state, index, to_near, to_far, stack = refs[len(order) : len(order) + 5]
    work = refs[len(order) + 5 :]
    table = work[0]
    own = index.shape[2]
    for piece, (slot, at) in zip(pieces, order):
        stack_block(piece, slot, ROWS, stack, NEXT_STEP * at)
    flip = lax.axis_index("dom") * own
    even = lax.axis_index("sector") % 2 == 0
    for k in range(4):
        index[k] = across(stack, INDEX + k, ROWS).astype(jnp.int32) ^ flip
    for row in range(36):
        state[row] = across(stack, STRAIN + row, ROWS)
    step = across(stack, STEP, ROWS)
    state[STEP] = step
    state[KEPT_NEXT_STEP] = across(stack, NEXT_STEP, ROWS)
    for j in range(3):
        state[KEPT_LOAD + j] = across(stack, LOAD + j, ROWS)
        table[j] = across(stack, SPEED + j, ROWS)
        table[3 + j] = across(stack, NEXT_SPEED + j, ROWS)
    dual = [across(stack, DUAL + c, ROWS) for c in range(3)]
    dual, force_own, force_next = sweep(lambda row: state[row], index, work, dual)
    for c in range(3):
        state[DUAL + c] = dual[c]
        mine = table[c] - step * (force_own[c] - state[KEPT_LOAD + c])
        to_near[c] = jnp.where(even, force_next[c], mine)
        to_far[c] = jnp.where(even, mine, force_next[c])


def second_kernel(state, index, to_near, to_far, from_far, from_near, vectors, keep, *work):
    table = work[0]
    even = lax.axis_index("sector") % 2 == 0
    step, next_step = state[STEP], state[KEPT_NEXT_STEP]
    for j in range(3):
        near, far = to_near[j], to_far[j]
        near_in, far_in = from_near[j], from_far[j]
        table[j] = jnp.where(even, far, near) - step * jnp.where(even, far_in, near_in)
        table[3 + j] = jnp.where(even, near_in, far_in) - next_step * jnp.where(even, near, far)
    dual = [state[DUAL + c] for c in range(3)]
    dual_next, force_own, force_next = sweep(lambda row: state[row], index, work, dual)
    for c in range(3):
        after = table[c] - step * (force_own[c] - state[KEPT_LOAD + c])
        vectors[c] = after - table[c]
        vectors[3 + c] = -(next_step * force_next[c])
        keep[c] = dual_next[c]
        keep[3 + c] = dual_next[c] - dual[c]
        keep[6 + c] = after


def pairs(depth):
    return [(i, l) for i in range(depth) for l in range(i, depth + 1)]


def gram_kernel(depth, slots, vectors, keep, *refs):
    blocks, own = keep.shape[1:]
    halves = own // LANES
    rows = 9 * depth
    message, stack, rows_sum = refs[len(slots) :]
    for piece, own_slots in zip(refs, slots):
        for at, slot in enumerate(own_slots):
            stack_block(piece.at[at] if len(piece.shape) == 3 else piece.at[ROWS:], slot, rows, stack)
    for row in range(6):
        message[row] = vectors[row]
    message[6] = jnp.zeros((blocks, own), jnp.float32)
    sums, pushed, pushed_twice = {}, [0.0] * (depth + 1), 0.0
    for c, h, top in itertools.product(range(3), range(halves), range(0, blocks, 8)):
        lanes, group = slice(h * LANES, (h + 1) * LANES), slice(top, top + 8)

        def gap(kind, i):
            return stack[h, pl.ds(top * rows + depth * (3 * kind + c) + i, 8, stride=rows), :]

        for kind, moved in enumerate((keep[3 + c, group, lanes], vectors[c, group, lanes])):
            gaps = [moved - gap(kind, i) for i in range(depth)] + [moved]
            for i, l in pairs(depth):
                term = gaps[i] * gaps[l]
                sums[i, l] = sums[i, l] + term if (i, l) in sums else term
        push = vectors[3 + c, group, lanes]
        for i in range(depth):
            pushed[i] = pushed[i] + gap(2, i) * push
        pushed_twice = pushed_twice + push * push
    for at, (i, l) in enumerate(pairs(depth)):
        value = sums[i, l] + pushed_twice - pushed[i] - pushed[l]
        rows_sum[at : at + 1, :] = jnp.sum(value, axis=0, keepdims=True)
    count = len(pairs(depth))
    if rows_sum.shape[0] > count:
        rows_sum[count:, :] = jnp.zeros((rows_sum.shape[0] - count, LANES), jnp.float32)
    whole = jnp.broadcast_to(jnp.sum(rows_sum[...], axis=1, keepdims=True), rows_sum.shape)
    lane = lax.broadcasted_iota(jnp.int32, (8, LANES), 1)
    out = whole[0:8]
    for group in range(1, rows_sum.shape[0] // 8):
        out = jnp.where(lane == group, whole[8 * group : 8 * group + 8], out)
    message[6, 0:8, 0:LANES] = out


def solve_kernel(depth, square, *refs):
    parts = refs[:-8]
    keep, past_w, gap_w, past_u, gap_u, new_u, new_w, total = refs[-8:]
    own = new_u.shape[1]
    tile = parts[0][6, 0:8, 0:LANES]
    for other in parts[1:]:
        tile = tile + other[6, 0:8, 0:LANES]
    even = lax.axis_index("sector") % 2 == 0

    def ahead(by, row):
        if square and by in (1, 3):
            return jnp.where(even, parts[by][row], parts[4 - by][row])
        return parts[by][row]

    sectors = len(parts)
    pushes = [[ahead(by, 3 + j) for j in range(3)] for by in range(sectors)]
    cross = sum(ahead(by, j) * pushes[by - 1][j] for by in range(sectors) for j in range(3))
    cross = jnp.sum(jnp.sum(cross, axis=0, keepdims=True), axis=1, keepdims=True)
    last = [keep[6 + j, 0:1] + pushes[-1][j][0:1] for j in range(3)] + [keep[c, 0:1] for c in range(3)]
    for group in range(total.shape[0] // 8):
        total[8 * group : 8 * group + 8, :] = jnp.broadcast_to(tile[:, group : group + 1], (8, LANES))
    matrix = {
        pair: jnp.broadcast_to(total[at : at + 1, :], (depth, LANES)) + 2.0 * cross
        for at, pair in enumerate(pairs(depth))
    }
    ridge = 0.0001 * sum(matrix[i, i] for i in range(depth)) / depth
    for i in range(depth):
        matrix[i, i] = matrix[i, i] + ridge
    inverse = []
    for step in range(depth):
        inverse.append(1.0 / matrix[step, step])
        for i in range(step + 1, depth):
            factor = matrix[step, i] * inverse[step]
            for l in range(i, depth + 1):
                matrix[i, l] = matrix[i, l] - factor * matrix[step, l]
    weights = [None] * depth
    for i in reversed(range(depth)):
        value = matrix[i, depth]
        for l in range(i + 1, depth):
            value = value - matrix[i, l] * weights[l]
        weights[i] = value * inverse[i]
    row = lax.broadcasted_iota(jnp.int32, (depth, LANES), 0)
    weight = weights[0]
    for i in range(1, depth):
        weight = jnp.where(row == i, weights[i], weight)
    for start in range(0, own, LANES):
        lanes = slice(start, start + LANES)
        for at, (past, gap, out) in enumerate(((past_u, gap_u, new_u), (past_w, gap_w, new_w))):
            for c in range(3):
                value = jnp.broadcast_to(last[3 * at + c][:, lanes], (depth, LANES))
                change = weight * (value - past[c, :, lanes] - gap[c, :, lanes])
                out[c : c + 1, lanes] = value[0:1] - jnp.sum(change, axis=0, keepdims=True)


def per_device(
    strain_map,
    corner_nodes,
    counts,
    seam_nodes,
    velocity,
    dual_state,
    nodal_load,
    mobility,
    past_dual,
    past_dual_gap,
    past_velocity,
    past_velocity_gap,
):
    own = velocity.shape[1]
    halves = own // LANES
    blocks = lax.axis_size("dom")
    sectors = lax.axis_size("sector")
    depth = past_dual.shape[0]
    seam_rows = seam_nodes.shape[1] // own
    mobility = mobility.reshape(1, own)
    past_dual, past_dual_gap, past_velocity, past_velocity_gap = (
        value.transpose(1, 0, 2) for value in (past_dual, past_dual_gap, past_velocity, past_velocity_gap)
    )

    def send(value, target):
        return lax.ppermute(value, "sector", [(i, target(i) % sectors) for i in range(sectors)])

    def swap(value, bits):
        return lax.ppermute(value, "dom", [(i, i ^ bits) for i in range(blocks)])

    nodes = (velocity, mobility, seam_nodes)
    ahead = call(
        nodes_kernel,
        f32(8 + seam_rows + 3 * depth + 8, own),
        in_hbm(*nodes, past_velocity_gap),
        loose=len(nodes) + 1,
        scratch=[pltpu.VMEM(value.shape, value.dtype) for value in nodes]
        + [pltpu.SemaphoreType.DMA((len(nodes) + 3,))],
    )
    held = (strain_map, dual_state, velocity, nodal_load, mobility, corner_nodes)
    base, first = call(
        base_kernel,
        (f32(INDEX + 4, own), f32(NEXT_STEP, own)),
        (counts, ahead, *in_hbm(*held)),
        scalars=1,
        loose=len(held) + 1,
        scratch=[pltpu.VMEM(value.shape, value.dtype) for value in held] + [pltpu.SemaphoreType.DMA((len(held),))],
    )
    ahead = send(ahead, lambda i: i - 1)
    history = call(
        history_kernel,
        f32(6, depth, own),
        (base, *in_hbm(past_dual_gap, past_velocity_gap)),
        loose=3,
        scratch=[pltpu.SemaphoreType.DMA((2,))],
    )
    message, second = call(
        functools.partial(message_kernel, own * blocks, depth),
        (f32(ROWS, own), f32(8, own)),
        (history, ahead, base),
        loose=1,
    )
    far_ones = list(range(4, blocks, 2))
    firsts = {bits: swap(first, bits) for bits in reversed(far_ones)}
    early = [firsts[bits] for bits in far_ones]
    wide = call(wide_kernel, f32(ROWS + 9 * depth, own), (*early, message, history, ahead), loose=len(early))
    pieces = {0: (wide,), 2: (swap(wide, 2),)}
    crossed = {bits: swap(firsts[bits], 1) for bits in reversed(far_ones)}
    held_back = call(copy_kernel, f32(8, own), (*crossed.values(), second), loose=len(crossed))
    for bits in reversed(far_ones):
        piece = swap(held_back, bits)
        pieces[bits], pieces[bits + 1] = (firsts[bits], piece), (crossed[bits], swap(piece, 1))
    for even in (0, 2):
        pieces[even + 1] = (swap(pieces[even][0], 1),)
    histories, slots = [pieces[block][0] for block in range(4)], [(block,) for block in range(4)]
    waited = [piece for bits in far_ones for piece in pieces[bits]]
    history = call(
        pair_kernel, f32(2, 9 * depth, own), (*waited, wide, pieces[2][0]), loose=len(waited)
    )
    known, apart, later = (0, 2), 4, []
    while apart < blocks:
        other = swap(history, apart)
        later.append((other, tuple(slot ^ apart for slot in known)))
        known += later[-1][1]
        apart *= 2
        if apart < blocks:
            history = call(join_kernel, f32(2 * history.shape[0], 9 * depth, own), (history, other))
    order = [(block, at) for block in reversed(range(blocks)) for at in range(len(pieces[block]))]
    sector = f32(3, blocks, own)
    work = [
        pltpu.VMEM((6, blocks, own), jnp.float32),
        pltpu.VMEM((3 * SPLITS, 4, blocks, own), jnp.float32),
        pltpu.VMEM((3, 4, blocks, own), jnp.float32),
        pltpu.VMEM((blocks * 16 * -(-3 * SPLITS * (halves + 2) // 16), LANES), jnp.float32),
    ]
    state, index, to_near, to_far = call(
        functools.partial(first_kernel, blocks, order),
        (f32(KEPT, blocks, own), jax.ShapeDtypeStruct((4, blocks, own), jnp.int32), sector, sector),
        tuple(pieces[block][at] for block, at in order),
        scratch=[pltpu.VMEM((halves, blocks * ROWS, LANES), jnp.float32), *work],
    )
    from_far = send(to_far, lambda i: i + 1 if i % 2 else i - 1)
    from_near = send(to_near, lambda i: i ^ 1)
    for other, far in later:
        held_back = call(copy_kernel, f32(*other.shape), (from_near, from_far, other), loose=2)
        histories += [other, swap(held_back, 1)]
        slots += [far, tuple(slot ^ 1 for slot in far)]
    vectors, keep = call(
        second_kernel,
        (f32(6, blocks, own), f32(9, blocks, own)),
        (state, index, to_near, to_far, from_far, from_near),
        scratch=work,
    )
    count = -(-len(pairs(depth)) // 8) * 8
    message = call(
        functools.partial(gram_kernel, depth, tuple(slots)),
        f32(7, blocks, own),
        (vectors, keep, *histories),
        scratch=[
            pltpu.VMEM((halves, blocks * 9 * depth, LANES), jnp.float32),
            pltpu.VMEM((count, LANES), jnp.float32),
        ],
    )
    square = sectors == 4
    parts = [message] + [None] * (sectors - 1)
    for by in sorted(range(1, sectors), reverse=True):
        parts[by] = send(message, (lambda i: i ^ by) if square else (lambda i: i - by))
    return call(
        functools.partial(solve_kernel, depth, square),
        (f32(3, own), f32(3, own)),
        (*parts, keep, past_dual, past_dual_gap, past_velocity, past_velocity_gap),
        scratch=[pltpu.VMEM((count, LANES), jnp.float32)],
    )


def solution(mesh):
    in_specs = (
        P(None, ("sector", "dom")),
        P(None, ("sector", "dom")),
        P(("sector", "dom")),
        P("sector", None),
        P(None, ("sector", "dom")),
        P(None, ("sector", "dom")),
        P(None, ("sector", "dom")),
        P(("sector", "dom")),
        P(None, None, ("sector", "dom")),
        P(None, None, ("sector", "dom")),
        P(None, None, ("sector", "dom")),
        P(None, None, ("sector", "dom")),
    )
    out_specs = (P(None, ("sector", "dom")), P(None, ("sector", "dom")))
    return jax.shard_map(
        per_device, mesh=mesh, in_specs=in_specs, out_specs=out_specs, check_vma=False
    )
```

```python
import functools
import itertools

import jax
import jax.numpy as jnp
from jax import lax
from jax.experimental import pallas as pl
from jax.experimental.pallas import tpu as pltpu
from jax.sharding import PartitionSpec as P

LANES = 128
VMEM_LIMIT = 24 * 1024 * 1024

STRAIN, DUAL, STEP, SPEED, LOAD, NEXT_STEP, NEXT_SPEED, INDEX, ROWS = 0, 36, 39, 40, 43, 46, 47, 50, 56
KEPT_NEXT_STEP, KEPT_LOAD, KEPT = 40, 41, 44
SPLITS = 2


def vmem():
    return pl.BlockSpec(memory_space=pltpu.VMEM)


def smem():
    return pl.BlockSpec(memory_space=pltpu.SMEM)


def call(kernel, outs, args, scalars=0, loose=0, scratch=()):
    return pl.pallas_call(
        kernel,
        out_shape=outs,
        in_specs=[smem()] * scalars
        + [pl.BlockSpec(memory_space=pl.ANY)] * loose
        + [vmem()] * (len(args) - scalars - loose),
        out_specs=jax.tree.map(lambda _: vmem(), outs),
        scratch_shapes=list(scratch),
        compiler_params=pltpu.CompilerParams(vmem_limit_bytes=VMEM_LIMIT),
    )(*args)


def f32(*shape):
    return jax.ShapeDtypeStruct(shape, jnp.float32)


def repeat(blocks, body, init):
    if blocks == 8:
        return body(slice(0, 8), 0, init)
    return lax.fori_loop(
        0, blocks // 8, lambda step, carry: body(pl.ds(pl.multiple_of(8 * step, 8), 8), 8 * step, carry), init
    )


def project_cone(trial):
    center = 0.5 * (trial[0] + trial[1])
    spread = 0.5 * (trial[0] - trial[1])
    shear = trial[2]
    radius = jnp.sqrt(spread * spread + shear * shear)
    upper = center + radius
    lower = center - radius
    iso_part = 0.5 * (jnp.maximum(upper, 0.0) + jnp.maximum(lower, 0.0))
    factor = jnp.clip((center + radius) / (2.0 * jnp.maximum(radius, 0.05)), 0.0, 1.0)
    return (iso_part + factor * spread, iso_part - factor * spread, factor * shear)


def fetch(pairs, sems):
    copies = [pltpu.make_async_copy(source, target, sems.at[at]) for at, (source, target) in enumerate(pairs)]
    for copy in copies:
        copy.start()
    for copy in copies:
        copy.wait()


def in_hbm(*values):
    return tuple(pltpu.with_memory_space_constraint(value, pltpu.HBM) for value in values)


def nodes_kernel(speed_in, mobility_in, seam_in, gap_u, ahead, speed, mobility, seam, sems):
    depth = gap_u.shape[1]
    start = ahead.shape[0] - 3 * depth
    gaps = [(gap_u.at[c], ahead.at[pl.ds(start + depth * c, depth)]) for c in range(3)]
    fetch(((speed_in, speed), (mobility_in, mobility), (seam_in, seam), *gaps), sems)
    own = speed.shape[1]
    ahead[0:3, :] = speed[...]
    ahead[3:4, :] = mobility[...]
    ahead[4:8, :] = jnp.zeros((4, own), jnp.float32)
    for row in range(8, start):
        ahead[row : row + 1, :] = seam[:, (row - 8) * own : (row - 7) * own].astype(jnp.float32)


def base_kernel(counts, after, *refs):
    count = (len(refs) - 2) // 2
    sources, base, held, sems = refs[:count], refs[count], refs[count + 1 : -1], refs[-1]
    fetch(zip(sources, held), sems)
    strain, dual, speed, load, mobility, corners = held
    own = speed.shape[1]
    slot = lax.broadcasted_iota(jnp.int32, (1, own), 1)
    alive = (slot < counts[0]).astype(jnp.float32)
    base[STRAIN:DUAL, :] = strain[...] * alive
    base[DUAL : DUAL + 3, :] = dual[...] * alive
    base[STEP : STEP + 1, :] = mobility[...]
    base[SPEED : SPEED + 3, :] = speed[...]
    base[LOAD : LOAD + 3, :] = load[...]
    base[NEXT_STEP:INDEX, :] = jnp.zeros((INDEX - NEXT_STEP, own), jnp.float32)
    base[INDEX : INDEX + 4, :] = corners[...].astype(jnp.float32)


def message_kernel(sector_nodes, depth, after, ahead, base, message, *shorter):
    own = message.shape[1]
    halves = own // LANES
    message[:NEXT_STEP, :] = base[:NEXT_STEP, :]
    message[NEXT_STEP : NEXT_STEP + 1, :] = ahead[3:4, :]
    message[NEXT_SPEED : NEXT_SPEED + 3, :] = ahead[0:3, :]
    message[INDEX + 4 :, :] = jnp.zeros((ROWS - INDEX - 4, own), jnp.float32)
    corners = base[INDEX : INDEX + 4, :].astype(jnp.int32)
    corner = jnp.concatenate([corners[:, h * LANES : (h + 1) * LANES] for h in range(halves)], axis=0)
    seam_rows = ahead.shape[0] - 8 - 3 * depth
    place = jnp.clip(corner - sector_nodes, 0, seam_rows * own - 1)
    high, low = place // LANES, place % LANES
    found = jnp.zeros(corner.shape, jnp.float32)
    for row in range(seam_rows):
        for h in range(halves):
            table = jnp.broadcast_to(ahead[8 + row : 9 + row, h * LANES : (h + 1) * LANES], corner.shape)
            value = jnp.take_along_axis(table, low, axis=1, mode="promise_in_bounds")
            found = jnp.where(high == row * halves + h, value, found)
    node = jnp.where(corner < sector_nodes, corner.astype(jnp.float32), found + float(sector_nodes))
    for h in range(halves):
        message[INDEX : INDEX + 4, h * LANES : (h + 1) * LANES] = node[4 * h : 4 * h + 4]
    for other in shorter:
        other[...] = message[: other.shape[0], :]


def history_kernel(after, gap_w, gap_u, history, sems):
    fetch(((gap_w, history.at[0:3]), (gap_u, history.at[3:6])), sems)


def wide_kernel(message, gaps, ahead, wide):
    depth = gaps.shape[1]
    start = ahead.shape[0] - 3 * depth
    wide[:ROWS, :] = message[...]
    for kind in range(6):
        wide[ROWS + depth * kind : ROWS + depth * (kind + 1), :] = gaps[kind]
    wide[ROWS + 6 * depth :, :] = ahead[start:, :]


def stack_kernel(*refs):
    stacked = refs[-1]
    for at, piece in enumerate(refs[:-1]):
        stacked[at * ROWS : at * ROWS + piece.shape[0], :] = piece[...]
        if piece.shape[0] < ROWS:
            start = at * ROWS + piece.shape[0]
            stacked[start : (at + 1) * ROWS, :] = jnp.zeros(((at + 1) * ROWS - start, piece.shape[1]), jnp.float32)


def pair_kernel(*refs):
    left, right, joined = refs[-3:]
    joined[0] = left[ROWS:, :]
    joined[1] = right[ROWS:, :]


def copy_kernel(*refs):
    value, copied = refs[-2:]
    copied[...] = value[...]


def join_kernel(*refs):
    left, right, joined = refs[-3:]
    count = left.shape[0]
    joined[:count] = left[...]
    joined[count:] = right[...]


def sweep(strain_row, index, work, dual):
    table, terms, codes, nearby = work
    blocks, own = index.shape[1:]
    halves = own // LANES
    here = lax.axis_index("dom")
    row = lax.broadcasted_iota(jnp.int32, (blocks, LANES), 0)
    left_block = ((row ^ here) - 1) ^ here
    right_block = ((row ^ here) + 1) ^ here

    def wide(j, group, block, part):
        piece = table[j, group, part * LANES : (part + 1) * LANES][block : block + 1]
        return jnp.broadcast_to(piece, (blocks, LANES))

    def take_sides(group, first, sides):
        left, right = (list(side) for side in sides)
        for block in range(8):
            for j in range(3):
                left[j] = jnp.where(left_block == first + block, wide(j, group, block, halves - 1), left[j])
                right[j] = jnp.where(right_block == first + block, wide(j, group, block, 0), right[j])
        return tuple(left), tuple(right)

    blank = tuple(jnp.zeros((blocks, LANES), jnp.float32) for _ in range(3))
    left, right = repeat(blocks, take_sides, (blank, blank))
    speed = []
    for k in range(4):
        parts = []
        for h in range(halves):
            number = index[k, :, h * LANES : (h + 1) * LANES]
            high, low = number // LANES, number % LANES

            def take(value):
                return jnp.take_along_axis(value, low, axis=1, mode="promise_in_bounds")

            found = [take(table[j, :, 0:LANES]) for j in range(3)]
            for part in range(1, halves):
                mask = high % halves == part
                found = [
                    jnp.where(mask, take(table[j, :, part * LANES : (part + 1) * LANES]), found[j]) for j in range(3)
                ]
            mask = number // own == left_block
            found = [jnp.where(mask, take(left[j]), found[j]) for j in range(3)]
            mask = number // own == right_block
            found = [jnp.where(mask, take(right[j]), found[j]) for j in range(3)]

            def take_group(group, first, found):
                for part, block in itertools.product(range(halves), range(8)):
                    mask = high == (blocks + first + block) * halves + part
                    found = [jnp.where(mask, take(wide(3 + j, group, block, part)), found[j]) for j in range(3)]
                return tuple(found)

            parts.append(repeat(blocks, take_group, tuple(found)))
        speed.append([jnp.concatenate([found[j] for found in parts], axis=1) for j in range(3)])
    rate = []
    for c in range(3):
        total = None
        for k in range(4):
            for j in range(3):
                term = strain_row(12 * c + 3 * k + j) * speed[k][j]
                total = term if total is None else total + term
        rate.append(total)
    trial = [rate[c] + dual[c] for c in range(3)]
    cone = project_cone(trial)
    dual_next = [trial[c] - cone[c] for c in range(3)]
    misfit = [rate[c] - cone[c] + dual_next[c] for c in range(3)]
    for k in range(4):
        for j in range(3):
            rest = sum(strain_row(12 * c + 3 * k + j) * misfit[c] for c in range(3))
            for split in range(SPLITS):
                term = rest.astype(jnp.bfloat16).astype(jnp.float32)
                terms[SPLITS * j + split, k] = term
                rest = rest - term

    near_rows = halves + 2
    next_rows = halves * blocks
    row_wide = lax.broadcasted_iota(jnp.int32, (blocks, own), 0) ^ here
    for k in range(4):
        number = index[k]
        block_of, half = number // own, number // LANES % halves
        near = jnp.where(block_of == ((row_wide - 1) ^ here), 0, 1 + half)
        near = jnp.where(block_of == ((row_wide + 1) ^ here), 1 + halves, near)
        codes[0, k] = (number % LANES).astype(jnp.float32)
        codes[1, k] = jnp.where(block_of < blocks, near, -1).astype(jnp.float32)
        codes[2, k] = jnp.where(block_of < blocks, -1, half * blocks + block_of - blocks).astype(jnp.float32)

    values = 3 * SPLITS
    per_tile = 16 // near_rows
    near_tiles = -(-values // per_tile)
    iota = lax.broadcasted_iota(jnp.int32, (16, own), 0)
    near_iota = (iota % near_rows).astype(jnp.float32).astype(jnp.bfloat16)
    value_iota = (iota // near_rows).astype(jnp.float32).astype(jnp.bfloat16)
    value_masks = [value_iota == jnp.full((16, own), float(at), jnp.bfloat16) for at in range(per_tile)]
    iota = iota.astype(jnp.float32)
    low_iota = [(iota + float(16 * g)).astype(jnp.bfloat16) for g in range(LANES // 16)]
    next_iota = [(iota + float(16 * g)).astype(jnp.bfloat16) for g in range(next_rows // 16)]
    one = jnp.ones((16, own), jnp.bfloat16)
    zero = jnp.zeros((16, own), jnp.bfloat16)

    def spread_row(value):
        return jnp.broadcast_to(value, (16, own)).astype(jnp.bfloat16)

    def add_group(group, first, total):
        for block in range(8):
            part = None
            for k in range(4):
                low_row, near_row, next_row = (
                    spread_row(codes[at, k, group, :][block : block + 1]) for at in range(3)
                )
                rows = [spread_row(terms[at, k, group, :][block : block + 1]) for at in range(values)]
                spread = jnp.concatenate([jnp.where(low_row == value, one, zero) for value in low_iota], axis=0)
                mask = near_row == near_iota
                weights = []
                for tile in range(near_tiles):
                    inside = rows[tile * per_tile : (tile + 1) * per_tile]
                    value = inside[-1]
                    for at in range(len(inside) - 1):
                        value = jnp.where(value_masks[at], inside[at], value)
                    weights.append(jnp.where(mask, value, zero))
                masks = [next_row == value for value in next_iota]
                weights += [jnp.where(mask, row, zero) for row in rows for mask in masks]
                product = lax.dot_general(
                    jnp.concatenate(weights, axis=0),
                    spread,
                    (((1,), (1,)), ((), ())),
                    preferred_element_type=jnp.float32,
                )
                part = product if part is None else part + product
            start = (first + block) * 16 * near_tiles
            if not isinstance(start, int):
                start = pl.multiple_of(start, 16)
            nearby[pl.ds(start, 16 * near_tiles), :] = part[: 16 * near_tiles]
            total += part[16 * near_tiles :]
        return total

    total = repeat(blocks, add_group, jnp.zeros((values * next_rows, LANES), jnp.float32))

    def near_force(j, row):
        return sum(
            nearby[pl.ds((SPLITS * j + split) * near_rows + row, blocks, stride=16 * near_tiles), :]
            for split in range(SPLITS)
        )

    force_own, force_next = [], []
    for j in range(3):
        halves_own = [near_force(j, 1 + h) for h in range(halves)]
        to_left, to_right = near_force(j, 0), near_force(j, 1 + halves)
        from_right = from_left = jnp.zeros((blocks, LANES), jnp.float32)
        for block in range(blocks):
            wide_left = jnp.broadcast_to(to_left[block : block + 1], (blocks, LANES))
            wide_right = jnp.broadcast_to(to_right[block : block + 1], (blocks, LANES))
            from_right = jnp.where(right_block == block, wide_left, from_right)
            from_left = jnp.where(left_block == block, wide_right, from_left)
        halves_own[-1] = halves_own[-1] + from_right
        halves_own[0] = halves_own[0] + from_left
        force_own.append(jnp.concatenate(halves_own, axis=1))
        whole = sum(
            total[(SPLITS * j + split) * next_rows : (SPLITS * j + split + 1) * next_rows] for split in range(SPLITS)
        )
        force_next.append(jnp.concatenate([whole[h * blocks : (h + 1) * blocks] for h in range(halves)], axis=1))
    return dual_next, force_own, force_next


def stack_block(piece, slot, rows, stack):
    held = min(rows, piece.shape[0])
    for h in range(stack.shape[0]):
        stack[h, slot * rows : slot * rows + held, :] = piece[:held, h * LANES : (h + 1) * LANES]


def across(stack, row, rows):
    blocks = stack.shape[1] // rows
    return jnp.concatenate(
        [stack[h, pl.ds(row, blocks, stride=rows), :] for h in range(stack.shape[0])], axis=1
    )


def first_kernel(blocks, order, *refs):
    pieces = refs[: len(order)]
    state, index, to_near, to_far, stack = refs[blocks : blocks + 5]
    work = refs[blocks + 5 :]
    table = work[0]
    own = index.shape[2]
    for piece, (start, slot) in zip(pieces, order):
        stack_block(piece.at[start : min(start + ROWS, piece.shape[0])], slot, ROWS, stack)
    flip = lax.axis_index("dom") * own
    even = lax.axis_index("sector") % 2 == 0
    for k in range(4):
        index[k] = across(stack, INDEX + k, ROWS).astype(jnp.int32) ^ flip
    for row in range(36):
        state[row] = across(stack, STRAIN + row, ROWS)
    step = across(stack, STEP, ROWS)
    state[STEP] = step
    state[KEPT_NEXT_STEP] = across(stack, NEXT_STEP, ROWS)
    for j in range(3):
        state[KEPT_LOAD + j] = across(stack, LOAD + j, ROWS)
        table[j] = across(stack, SPEED + j, ROWS)
        table[3 + j] = across(stack, NEXT_SPEED + j, ROWS)
    dual = [across(stack, DUAL + c, ROWS) for c in range(3)]
    dual, force_own, force_next = sweep(lambda row: state[row], index, work, dual)
    for c in range(3):
        state[DUAL + c] = dual[c]
        mine = table[c] - step * (force_own[c] - state[KEPT_LOAD + c])
        to_near[c] = jnp.where(even, force_next[c], mine)
        to_far[c] = jnp.where(even, mine, force_next[c])


def second_kernel(state, index, to_near, to_far, from_far, from_near, vectors, keep, *work):
    table = work[0]
    even = lax.axis_index("sector") % 2 == 0
    step, next_step = state[STEP], state[KEPT_NEXT_STEP]
    for j in range(3):
        near, far = to_near[j], to_far[j]
        near_in, far_in = from_near[j], from_far[j]
        table[j] = jnp.where(even, far, near) - step * jnp.where(even, far_in, near_in)
        table[3 + j] = jnp.where(even, near_in, far_in) - next_step * jnp.where(even, near, far)
    dual = [state[DUAL + c] for c in range(3)]
    dual_next, force_own, force_next = sweep(lambda row: state[row], index, work, dual)
    for c in range(3):
        after = table[c] - step * (force_own[c] - state[KEPT_LOAD + c])
        vectors[c] = after - table[c]
        vectors[3 + c] = -(next_step * force_next[c])
        keep[c] = dual_next[c]
        keep[3 + c] = dual_next[c] - dual[c]
        keep[6 + c] = after


def pairs(depth):
    return [(i, l) for i in range(depth) for l in range(i, depth + 1)]


def gram_kernel(depth, slots, vectors, keep, *refs):
    blocks, own = keep.shape[1:]
    halves = own // LANES
    rows = 9 * depth
    message, stack, rows_sum = refs[len(slots) :]
    for piece, own_slots in zip(refs, slots):
        for at, slot in enumerate(own_slots):
            stack_block(piece.at[at] if len(piece.shape) == 3 else piece.at[ROWS:], slot, rows, stack)
    for row in range(6):
        message[row] = vectors[row]
    message[6] = jnp.zeros((blocks, own), jnp.float32)
    sums, pushed, pushed_twice = {}, [0.0] * (depth + 1), 0.0
    for c, h, top in itertools.product(range(3), range(halves), range(0, blocks, 8)):
        lanes, group = slice(h * LANES, (h + 1) * LANES), slice(top, top + 8)

        def gap(kind, i):
            return stack[h, pl.ds(top * rows + depth * (3 * kind + c) + i, 8, stride=rows), :]

        for kind, moved in enumerate((keep[3 + c, group, lanes], vectors[c, group, lanes])):
            gaps = [moved - gap(kind, i) for i in range(depth)] + [moved]
            for i, l in pairs(depth):
                term = gaps[i] * gaps[l]
                sums[i, l] = sums[i, l] + term if (i, l) in sums else term
        push = vectors[3 + c, group, lanes]
        for i in range(depth):
            pushed[i] = pushed[i] + gap(2, i) * push
        pushed_twice = pushed_twice + push * push
    for at, (i, l) in enumerate(pairs(depth)):
        value = sums[i, l] + pushed_twice - pushed[i] - pushed[l]
        rows_sum[at : at + 1, :] = jnp.sum(value, axis=0, keepdims=True)
    count = len(pairs(depth))
    if rows_sum.shape[0] > count:
        rows_sum[count:, :] = jnp.zeros((rows_sum.shape[0] - count, LANES), jnp.float32)
    whole = jnp.broadcast_to(jnp.sum(rows_sum[...], axis=1, keepdims=True), rows_sum.shape)
    lane = lax.broadcasted_iota(jnp.int32, (8, LANES), 1)
    out = whole[0:8]
    for group in range(1, rows_sum.shape[0] // 8):
        out = jnp.where(lane == group, whole[8 * group : 8 * group + 8], out)
    message[6, 0:8, 0:LANES] = out


def solve_kernel(depth, square, *refs):
    parts = refs[:-8]
    keep, past_w, gap_w, past_u, gap_u, new_u, new_w, total = refs[-8:]
    own = new_u.shape[1]
    tile = parts[0][6, 0:8, 0:LANES]
    for other in parts[1:]:
        tile = tile + other[6, 0:8, 0:LANES]
    even = lax.axis_index("sector") % 2 == 0

    def ahead(by, row):
        if square and by in (1, 3):
            return jnp.where(even, parts[by][row], parts[4 - by][row])
        return parts[by][row]

    sectors = len(parts)
    pushes = [[ahead(by, 3 + j) for j in range(3)] for by in range(sectors)]
    cross = sum(ahead(by, j) * pushes[by - 1][j] for by in range(sectors) for j in range(3))
    cross = jnp.sum(jnp.sum(cross, axis=0, keepdims=True), axis=1, keepdims=True)
    last = [keep[6 + j, 0:1] + pushes[-1][j][0:1] for j in range(3)] + [keep[c, 0:1] for c in range(3)]
    for group in range(total.shape[0] // 8):
        total[8 * group : 8 * group + 8, :] = jnp.broadcast_to(tile[:, group : group + 1], (8, LANES))
    matrix = {
        pair: jnp.broadcast_to(total[at : at + 1, :], (depth, LANES)) + 2.0 * cross
        for at, pair in enumerate(pairs(depth))
    }
    ridge = 0.0001 * sum(matrix[i, i] for i in range(depth)) / depth
    for i in range(depth):
        matrix[i, i] = matrix[i, i] + ridge
    inverse = []
    for step in range(depth):
        inverse.append(1.0 / matrix[step, step])
        for i in range(step + 1, depth):
            factor = matrix[step, i] * inverse[step]
            for l in range(i, depth + 1):
                matrix[i, l] = matrix[i, l] - factor * matrix[step, l]
    weights = [None] * depth
    for i in reversed(range(depth)):
        value = matrix[i, depth]
        for l in range(i + 1, depth):
            value = value - matrix[i, l] * weights[l]
        weights[i] = value * inverse[i]
    row = lax.broadcasted_iota(jnp.int32, (depth, LANES), 0)
    weight = weights[0]
    for i in range(1, depth):
        weight = jnp.where(row == i, weights[i], weight)
    for start in range(0, own, LANES):
        lanes = slice(start, start + LANES)
        for at, (past, gap, out) in enumerate(((past_u, gap_u, new_u), (past_w, gap_w, new_w))):
            for c in range(3):
                value = jnp.broadcast_to(last[3 * at + c][:, lanes], (depth, LANES))
                change = weight * (value - past[c, :, lanes] - gap[c, :, lanes])
                out[c : c + 1, lanes] = value[0:1] - jnp.sum(change, axis=0, keepdims=True)


def per_device(
    strain_map,
    corner_nodes,
    counts,
    seam_nodes,
    velocity,
    dual_state,
    nodal_load,
    mobility,
    past_dual,
    past_dual_gap,
    past_velocity,
    past_velocity_gap,
):
    own = velocity.shape[1]
    halves = own // LANES
    blocks = lax.axis_size("dom")
    sectors = lax.axis_size("sector")
    depth = past_dual.shape[0]
    seam_rows = seam_nodes.shape[1] // own
    mobility = mobility.reshape(1, own)
    past_dual, past_dual_gap, past_velocity, past_velocity_gap = (
        value.transpose(1, 0, 2) for value in (past_dual, past_dual_gap, past_velocity, past_velocity_gap)
    )

    def send(value, target):
        return lax.ppermute(value, "sector", [(i, target(i) % sectors) for i in range(sectors)])

    def swap(value, bits):
        return lax.ppermute(value, "dom", [(i, i ^ bits) for i in range(blocks)])

    nodes = (velocity, mobility, seam_nodes)
    ahead = call(
        nodes_kernel,
        f32(8 + seam_rows + 3 * depth, own),
        in_hbm(*nodes, past_velocity_gap),
        loose=len(nodes) + 1,
        scratch=[pltpu.VMEM(value.shape, value.dtype) for value in nodes]
        + [pltpu.SemaphoreType.DMA((len(nodes) + 3,))],
    )
    held = (strain_map, dual_state, velocity, nodal_load, mobility, corner_nodes)
    base = call(
        base_kernel,
        f32(INDEX + 4, own),
        (counts, ahead, *in_hbm(*held)),
        scalars=1,
        loose=len(held) + 1,
        scratch=[pltpu.VMEM(value.shape, value.dtype) for value in held] + [pltpu.SemaphoreType.DMA((len(held),))],
    )
    ahead = send(ahead, lambda i: i - 1)
    history = call(
        history_kernel,
        f32(6, depth, own),
        (base, *in_hbm(past_dual_gap, past_velocity_gap)),
        loose=3,
        scratch=[pltpu.SemaphoreType.DMA((2,))],
    )
    far_ones = list(range(blocks - 2, 2, -2))
    lengths = [max(INDEX + 4, ROWS - place) for place in range(len(far_ones))]
    messages = call(
        functools.partial(message_kernel, own * blocks, depth),
        tuple(f32(rows, own) for rows in sorted(set(lengths), reverse=True)),
        (history, ahead, base),
        loose=1,
    )
    wide = call(wide_kernel, f32(ROWS + 9 * depth, own), (messages[0], history, ahead))
    pieces = {0: wide}
    for bits, rows in zip(far_ones, lengths):
        pieces[bits] = swap(next(value for value in messages if value.shape[0] == rows), bits)
    pieces[2] = swap(wide, 2)
    for even in (0, 2):
        pieces[even + 1] = swap(pieces[even], 1)
    count = len(far_ones)
    crossed = swap(
        call(stack_kernel, f32(count * ROWS, own), tuple(pieces[bits] for bits in far_ones)), 1
    )
    histories, slots = [pieces[block] for block in range(4)], [(block,) for block in range(4)]
    history = call(
        pair_kernel, f32(2, 9 * depth, own), (*(pieces[bits] for bits in far_ones), wide, pieces[2]), loose=len(far_ones)
    )
    known, apart, later = (0, 2), 4, []
    while apart < blocks:
        other = swap(history, apart)
        later.append((other, tuple(slot ^ apart for slot in known)))
        known += later[-1][1]
        apart *= 2
        if apart < blocks:
            history = call(join_kernel, f32(2 * history.shape[0], 9 * depth, own), (history, other))
    order = [(at * ROWS, bits + 1) for at, bits in enumerate(far_ones)]
    order += [(0, block) for block in reversed(range(blocks)) if block in pieces]
    sector = f32(3, blocks, own)
    work = [
        pltpu.VMEM((6, blocks, own), jnp.float32),
        pltpu.VMEM((3 * SPLITS, 4, blocks, own), jnp.float32),
        pltpu.VMEM((3, 4, blocks, own), jnp.float32),
        pltpu.VMEM((blocks * 16 * -(-3 * SPLITS * (halves + 2) // 16), LANES), jnp.float32),
    ]
    state, index, to_near, to_far = call(
        functools.partial(first_kernel, blocks, order),
        (f32(KEPT, blocks, own), jax.ShapeDtypeStruct((4, blocks, own), jnp.int32), sector, sector),
        (*([crossed] * count), *(pieces[block] for _, block in order[count:])),
        scratch=[pltpu.VMEM((halves, blocks * ROWS, LANES), jnp.float32), *work],
    )
    from_far = send(to_far, lambda i: i + 1 if i % 2 else i - 1)
    from_near = send(to_near, lambda i: i ^ 1)
    for other, far in later:
        held_back = call(copy_kernel, f32(*other.shape), (from_near, from_far, other), loose=2)
        histories += [other, swap(held_back, 1)]
        slots += [far, tuple(slot ^ 1 for slot in far)]
    vectors, keep = call(
        second_kernel,
        (f32(6, blocks, own), f32(9, blocks, own)),
        (state, index, to_near, to_far, from_far, from_near),
        scratch=work,
    )
    count = -(-len(pairs(depth)) // 8) * 8
    message = call(
        functools.partial(gram_kernel, depth, tuple(slots)),
        f32(7, blocks, own),
        (vectors, keep, *histories),
        scratch=[
            pltpu.VMEM((halves, blocks * 9 * depth, LANES), jnp.float32),
            pltpu.VMEM((count, LANES), jnp.float32),
        ],
    )
    square = sectors == 4
    parts = [message] + [None] * (sectors - 1)
    for by in sorted(range(1, sectors), reverse=True):
        parts[by] = send(message, (lambda i: i ^ by) if square else (lambda i: i - by))
    return call(
        functools.partial(solve_kernel, depth, square),
        (f32(3, own), f32(3, own)),
        (*parts, keep, past_dual, past_dual_gap, past_velocity, past_velocity_gap),
        scratch=[pltpu.VMEM((count, LANES), jnp.float32)],
    )


def solution(mesh):
    in_specs = (
        P(None, ("sector", "dom")),
        P(None, ("sector", "dom")),
        P(("sector", "dom")),
        P("sector", None),
        P(None, ("sector", "dom")),
        P(None, ("sector", "dom")),
        P(None, ("sector", "dom")),
        P(("sector", "dom")),
        P(None, None, ("sector", "dom")),
        P(None, None, ("sector", "dom")),
        P(None, None, ("sector", "dom")),
        P(None, None, ("sector", "dom")),
    )
    out_specs = (P(None, ("sector", "dom")), P(None, ("sector", "dom")))
    return jax.shard_map(
        per_device, mesh=mesh, in_specs=in_specs, out_specs=out_specs, check_vma=False
    )
```

```python
import functools
import itertools

import jax
import jax.numpy as jnp
from jax import lax
from jax.experimental import pallas as pl
from jax.experimental.pallas import tpu as pltpu
from jax.sharding import PartitionSpec as P

LANES = 128
VMEM_LIMIT = 24 * 1024 * 1024

STRAIN, DUAL, STEP, SPEED, LOAD, NEXT_STEP, NEXT_SPEED, INDEX, ROWS = 0, 36, 39, 40, 43, 46, 47, 50, 56
KEPT_NEXT_STEP, KEPT_LOAD, KEPT = 40, 41, 44
SPLITS = 2


def vmem():
    return pl.BlockSpec(memory_space=pltpu.VMEM)


def smem():
    return pl.BlockSpec(memory_space=pltpu.SMEM)


def call(kernel, outs, args, scalars=0, loose=0, scratch=()):
    return pl.pallas_call(
        kernel,
        out_shape=outs,
        in_specs=[smem()] * scalars
        + [pl.BlockSpec(memory_space=pl.ANY)] * loose
        + [vmem()] * (len(args) - scalars - loose),
        out_specs=jax.tree.map(lambda _: vmem(), outs),
        scratch_shapes=list(scratch),
        compiler_params=pltpu.CompilerParams(vmem_limit_bytes=VMEM_LIMIT),
    )(*args)


def f32(*shape):
    return jax.ShapeDtypeStruct(shape, jnp.float32)


def repeat(blocks, body, init):
    if blocks == 8:
        return body(slice(0, 8), 0, init)
    return lax.fori_loop(
        0, blocks // 8, lambda step, carry: body(pl.ds(pl.multiple_of(8 * step, 8), 8), 8 * step, carry), init
    )


def project_cone(trial):
    center = 0.5 * (trial[0] + trial[1])
    spread = 0.5 * (trial[0] - trial[1])
    shear = trial[2]
    radius = jnp.sqrt(spread * spread + shear * shear)
    upper = center + radius
    lower = center - radius
    iso_part = 0.5 * (jnp.maximum(upper, 0.0) + jnp.maximum(lower, 0.0))
    factor = jnp.clip((center + radius) / (2.0 * jnp.maximum(radius, 0.05)), 0.0, 1.0)
    return (iso_part + factor * spread, iso_part - factor * spread, factor * shear)


def fetch(pairs, sems):
    copies = [pltpu.make_async_copy(source, target, sems.at[at]) for at, (source, target) in enumerate(pairs)]
    for copy in copies:
        copy.start()
    for copy in copies:
        copy.wait()


def in_hbm(*values):
    return tuple(pltpu.with_memory_space_constraint(value, pltpu.HBM) for value in values)


def nodes_kernel(speed_in, mobility_in, seam_in, gap_u, ahead, speed, mobility, seam, sems):
    depth = gap_u.shape[1]
    start = ahead.shape[0] - 3 * depth
    gaps = [(gap_u.at[c], ahead.at[pl.ds(start + depth * c, depth)]) for c in range(3)]
    fetch(((speed_in, speed), (mobility_in, mobility), (seam_in, seam), *gaps), sems)
    own = speed.shape[1]
    ahead[0:3, :] = speed[...]
    ahead[3:4, :] = mobility[...]
    ahead[4:8, :] = jnp.zeros((4, own), jnp.float32)
    for row in range(8, start):
        ahead[row : row + 1, :] = seam[:, (row - 8) * own : (row - 7) * own].astype(jnp.float32)


def base_kernel(counts, after, *refs):
    count = (len(refs) - 2) // 2
    sources, base, held, sems = refs[:count], refs[count], refs[count + 1 : -1], refs[-1]
    fetch(zip(sources, held), sems)
    strain, dual, speed, load, mobility, corners = held
    own = speed.shape[1]
    slot = lax.broadcasted_iota(jnp.int32, (1, own), 1)
    alive = (slot < counts[0]).astype(jnp.float32)
    base[STRAIN:DUAL, :] = strain[...] * alive
    base[DUAL : DUAL + 3, :] = dual[...] * alive
    base[STEP : STEP + 1, :] = mobility[...]
    base[SPEED : SPEED + 3, :] = speed[...]
    base[LOAD : LOAD + 3, :] = load[...]
    base[NEXT_STEP:INDEX, :] = jnp.zeros((INDEX - NEXT_STEP, own), jnp.float32)
    base[INDEX : INDEX + 4, :] = corners[...].astype(jnp.float32)


def message_kernel(sector_nodes, depth, after, ahead, base, message, *shorter):
    own = message.shape[1]
    halves = own // LANES
    message[:NEXT_STEP, :] = base[:NEXT_STEP, :]
    message[NEXT_STEP : NEXT_STEP + 1, :] = ahead[3:4, :]
    message[NEXT_SPEED : NEXT_SPEED + 3, :] = ahead[0:3, :]
    message[INDEX + 4 :, :] = jnp.zeros((ROWS - INDEX - 4, own), jnp.float32)
    corners = base[INDEX : INDEX + 4, :].astype(jnp.int32)
    corner = jnp.concatenate([corners[:, h * LANES : (h + 1) * LANES] for h in range(halves)], axis=0)
    seam_rows = ahead.shape[0] - 8 - 3 * depth
    place = jnp.clip(corner - sector_nodes, 0, seam_rows * own - 1)
    high, low = place // LANES, place % LANES
    found = jnp.zeros(corner.shape, jnp.float32)
    for row in range(seam_rows):
        for h in range(halves):
            table = jnp.broadcast_to(ahead[8 + row : 9 + row, h * LANES : (h + 1) * LANES], corner.shape)
            value = jnp.take_along_axis(table, low, axis=1, mode="promise_in_bounds")
            found = jnp.where(high == row * halves + h, value, found)
    node = jnp.where(corner < sector_nodes, corner.astype(jnp.float32), found + float(sector_nodes))
    for h in range(halves):
        message[INDEX : INDEX + 4, h * LANES : (h + 1) * LANES] = node[4 * h : 4 * h + 4]
    for other in shorter:
        other[...] = message[: other.shape[0], :]


def history_kernel(after, gap_w, gap_u, history, sems):
    fetch(((gap_w, history.at[0:3]), (gap_u, history.at[3:6])), sems)


def wide_kernel(message, gaps, ahead, wide):
    depth = gaps.shape[1]
    start = ahead.shape[0] - 3 * depth
    wide[:ROWS, :] = message[...]
    for kind in range(6):
        wide[ROWS + depth * kind : ROWS + depth * (kind + 1), :] = gaps[kind]
    wide[ROWS + 6 * depth :, :] = ahead[start:, :]


def stack_kernel(*refs):
    stacked = refs[-1]
    for at, piece in enumerate(refs[:-1]):
        stacked[at * ROWS : at * ROWS + piece.shape[0], :] = piece[...]
        if piece.shape[0] < ROWS:
            start = at * ROWS + piece.shape[0]
            stacked[start : (at + 1) * ROWS, :] = jnp.zeros(((at + 1) * ROWS - start, piece.shape[1]), jnp.float32)


def pair_kernel(*refs):
    left, right, joined = refs[-3:]
    joined[0] = left[ROWS:, :]
    joined[1] = right[ROWS:, :]


def copy_kernel(*refs):
    value, copied = refs[-2:]
    copied[...] = value[...]


def join_kernel(*refs):
    left, right, joined = refs[-3:]
    count = left.shape[0]
    joined[:count] = left[...]
    joined[count:] = right[...]


def sweep(strain_row, index, work, dual):
    table, terms, codes, nearby = work
    blocks, own = index.shape[1:]
    halves = own // LANES
    here = lax.axis_index("dom")
    row = lax.broadcasted_iota(jnp.int32, (blocks, LANES), 0)
    left_block = ((row ^ here) - 1) ^ here
    right_block = ((row ^ here) + 1) ^ here

    def wide(j, group, block, part):
        piece = table[j, group, part * LANES : (part + 1) * LANES][block : block + 1]
        return jnp.broadcast_to(piece, (blocks, LANES))

    def take_sides(group, first, sides):
        left, right = (list(side) for side in sides)
        for block in range(8):
            for j in range(3):
                left[j] = jnp.where(left_block == first + block, wide(j, group, block, halves - 1), left[j])
                right[j] = jnp.where(right_block == first + block, wide(j, group, block, 0), right[j])
        return tuple(left), tuple(right)

    blank = tuple(jnp.zeros((blocks, LANES), jnp.float32) for _ in range(3))
    left, right = repeat(blocks, take_sides, (blank, blank))
    speed = []
    for k in range(4):
        parts = []
        for h in range(halves):
            number = index[k, :, h * LANES : (h + 1) * LANES]
            high, low = number // LANES, number % LANES

            def take(value):
                return jnp.take_along_axis(value, low, axis=1, mode="promise_in_bounds")

            found = [take(table[j, :, 0:LANES]) for j in range(3)]
            for part in range(1, halves):
                mask = high % halves == part
                found = [
                    jnp.where(mask, take(table[j, :, part * LANES : (part + 1) * LANES]), found[j]) for j in range(3)
                ]
            mask = number // own == left_block
            found = [jnp.where(mask, take(left[j]), found[j]) for j in range(3)]
            mask = number // own == right_block
            found = [jnp.where(mask, take(right[j]), found[j]) for j in range(3)]

            def take_group(group, first, found):
                for part, block in itertools.product(range(halves), range(8)):
                    mask = high == (blocks + first + block) * halves + part
                    found = [jnp.where(mask, take(wide(3 + j, group, block, part)), found[j]) for j in range(3)]
                return tuple(found)

            parts.append(repeat(blocks, take_group, tuple(found)))
        speed.append([jnp.concatenate([found[j] for found in parts], axis=1) for j in range(3)])
    rate = []
    for c in range(3):
        total = None
        for k in range(4):
            for j in range(3):
                term = strain_row(12 * c + 3 * k + j) * speed[k][j]
                total = term if total is None else total + term
        rate.append(total)
    trial = [rate[c] + dual[c] for c in range(3)]
    cone = project_cone(trial)
    dual_next = [trial[c] - cone[c] for c in range(3)]
    misfit = [rate[c] - cone[c] + dual_next[c] for c in range(3)]
    for k in range(4):
        for j in range(3):
            rest = sum(strain_row(12 * c + 3 * k + j) * misfit[c] for c in range(3))
            for split in range(SPLITS):
                term = rest.astype(jnp.bfloat16).astype(jnp.float32)
                terms[SPLITS * j + split, k] = term
                rest = rest - term

    near_rows = halves + 2
    next_rows = halves * blocks
    row_wide = lax.broadcasted_iota(jnp.int32, (blocks, own), 0) ^ here
    for k in range(4):
        number = index[k]
        block_of, half = number // own, number // LANES % halves
        near = jnp.where(block_of == ((row_wide - 1) ^ here), 0, 1 + half)
        near = jnp.where(block_of == ((row_wide + 1) ^ here), 1 + halves, near)
        codes[0, k] = (number % LANES).astype(jnp.float32)
        codes[1, k] = jnp.where(block_of < blocks, near, -1).astype(jnp.float32)
        codes[2, k] = jnp.where(block_of < blocks, -1, half * blocks + block_of - blocks).astype(jnp.float32)

    values = 3 * SPLITS
    per_tile = 16 // near_rows
    near_tiles = -(-values // per_tile)
    iota = lax.broadcasted_iota(jnp.int32, (16, own), 0)
    near_iota = (iota % near_rows).astype(jnp.float32).astype(jnp.bfloat16)
    value_iota = (iota // near_rows).astype(jnp.float32).astype(jnp.bfloat16)
    value_masks = [value_iota == jnp.full((16, own), float(at), jnp.bfloat16) for at in range(per_tile)]
    iota = iota.astype(jnp.float32)
    low_iota = [(iota + float(16 * g)).astype(jnp.bfloat16) for g in range(LANES // 16)]
    next_iota = [(iota + float(16 * g)).astype(jnp.bfloat16) for g in range(next_rows // 16)]
    one = jnp.ones((16, own), jnp.bfloat16)
    zero = jnp.zeros((16, own), jnp.bfloat16)

    def spread_row(value):
        return jnp.broadcast_to(value, (16, own)).astype(jnp.bfloat16)

    def add_group(group, first, total):
        for block in range(8):
            part = None
            for k in range(4):
                low_row, near_row, next_row = (
                    spread_row(codes[at, k, group, :][block : block + 1]) for at in range(3)
                )
                rows = [spread_row(terms[at, k, group, :][block : block + 1]) for at in range(values)]
                spread = jnp.concatenate([jnp.where(low_row == value, one, zero) for value in low_iota], axis=0)
                mask = near_row == near_iota
                weights = []
                for tile in range(near_tiles):
                    inside = rows[tile * per_tile : (tile + 1) * per_tile]
                    value = inside[-1]
                    for at in range(len(inside) - 1):
                        value = jnp.where(value_masks[at], inside[at], value)
                    weights.append(jnp.where(mask, value, zero))
                masks = [next_row == value for value in next_iota]
                weights += [jnp.where(mask, row, zero) for row in rows for mask in masks]
                product = lax.dot_general(
                    jnp.concatenate(weights, axis=0),
                    spread,
                    (((1,), (1,)), ((), ())),
                    preferred_element_type=jnp.float32,
                )
                part = product if part is None else part + product
            start = (first + block) * 16 * near_tiles
            if not isinstance(start, int):
                start = pl.multiple_of(start, 16)
            nearby[pl.ds(start, 16 * near_tiles), :] = part[: 16 * near_tiles]
            total += part[16 * near_tiles :]
        return total

    total = repeat(blocks, add_group, jnp.zeros((values * next_rows, LANES), jnp.float32))

    def near_force(j, row):
        return sum(
            nearby[pl.ds((SPLITS * j + split) * near_rows + row, blocks, stride=16 * near_tiles), :]
            for split in range(SPLITS)
        )

    force_own, force_next = [], []
    for j in range(3):
        halves_own = [near_force(j, 1 + h) for h in range(halves)]
        to_left, to_right = near_force(j, 0), near_force(j, 1 + halves)
        from_right = from_left = jnp.zeros((blocks, LANES), jnp.float32)
        for block in range(blocks):
            wide_left = jnp.broadcast_to(to_left[block : block + 1], (blocks, LANES))
            wide_right = jnp.broadcast_to(to_right[block : block + 1], (blocks, LANES))
            from_right = jnp.where(right_block == block, wide_left, from_right)
            from_left = jnp.where(left_block == block, wide_right, from_left)
        halves_own[-1] = halves_own[-1] + from_right
        halves_own[0] = halves_own[0] + from_left
        force_own.append(jnp.concatenate(halves_own, axis=1))
        whole = sum(
            total[(SPLITS * j + split) * next_rows : (SPLITS * j + split + 1) * next_rows] for split in range(SPLITS)
        )
        force_next.append(jnp.concatenate([whole[h * blocks : (h + 1) * blocks] for h in range(halves)], axis=1))
    return dual_next, force_own, force_next


def stack_block(piece, slot, rows, stack):
    held = min(rows, piece.shape[0])
    for h in range(stack.shape[0]):
        stack[h, slot * rows : slot * rows + held, :] = piece[:held, h * LANES : (h + 1) * LANES]


def across(stack, row, rows):
    blocks = stack.shape[1] // rows
    return jnp.concatenate(
        [stack[h, pl.ds(row, blocks, stride=rows), :] for h in range(stack.shape[0])], axis=1
    )


def first_kernel(blocks, order, *refs):
    pieces = refs[: len(order)]
    state, index, to_near, to_far, stack = refs[blocks : blocks + 5]
    work = refs[blocks + 5 :]
    table = work[0]
    own = index.shape[2]
    for piece, (start, slot) in zip(pieces, order):
        stack_block(piece.at[start : min(start + ROWS, piece.shape[0])], slot, ROWS, stack)
    flip = lax.axis_index("dom") * own
    even = lax.axis_index("sector") % 2 == 0
    for k in range(4):
        index[k] = across(stack, INDEX + k, ROWS).astype(jnp.int32) ^ flip
    for row in range(36):
        state[row] = across(stack, STRAIN + row, ROWS)
    step = across(stack, STEP, ROWS)
    state[STEP] = step
    state[KEPT_NEXT_STEP] = across(stack, NEXT_STEP, ROWS)
    for j in range(3):
        state[KEPT_LOAD + j] = across(stack, LOAD + j, ROWS)
        table[j] = across(stack, SPEED + j, ROWS)
        table[3 + j] = across(stack, NEXT_SPEED + j, ROWS)
    dual = [across(stack, DUAL + c, ROWS) for c in range(3)]
    dual, force_own, force_next = sweep(lambda row: state[row], index, work, dual)
    for c in range(3):
        state[DUAL + c] = dual[c]
        mine = table[c] - step * (force_own[c] - state[KEPT_LOAD + c])
        to_near[c] = jnp.where(even, force_next[c], mine)
        to_far[c] = jnp.where(even, mine, force_next[c])


def second_kernel(state, index, to_near, to_far, from_near, from_far, vectors, keep, *work):
    table = work[0]
    even = lax.axis_index("sector") % 2 == 0
    step, next_step = state[STEP], state[KEPT_NEXT_STEP]
    for j in range(3):
        near, far = to_near[j], to_far[j]
        near_in, far_in = from_near[j], from_far[j]
        table[j] = jnp.where(even, far, near) - step * jnp.where(even, far_in, near_in)
        table[3 + j] = jnp.where(even, near_in, far_in) - next_step * jnp.where(even, near, far)
    dual = [state[DUAL + c] for c in range(3)]
    dual_next, force_own, force_next = sweep(lambda row: state[row], index, work, dual)
    for c in range(3):
        after = table[c] - step * (force_own[c] - state[KEPT_LOAD + c])
        vectors[c] = after - table[c]
        vectors[3 + c] = -(next_step * force_next[c])
        keep[c] = dual_next[c]
        keep[3 + c] = dual_next[c] - dual[c]
        keep[6 + c] = after


def pairs(depth):
    return [(i, l) for i in range(depth) for l in range(i, depth + 1)]


def gram_kernel(depth, slots, vectors, keep, *refs):
    blocks, own = keep.shape[1:]
    halves = own // LANES
    rows = 9 * depth
    message, stack, rows_sum = refs[len(slots) :]
    for piece, own_slots in zip(refs, slots):
        for at, slot in enumerate(own_slots):
            stack_block(piece.at[at] if len(piece.shape) == 3 else piece.at[ROWS:], slot, rows, stack)
    for row in range(6):
        message[row] = vectors[row]
    message[6] = jnp.zeros((blocks, own), jnp.float32)
    sums, pushed, pushed_twice = {}, [0.0] * (depth + 1), 0.0
    for c, h, top in itertools.product(range(3), range(halves), range(0, blocks, 8)):
        lanes, group = slice(h * LANES, (h + 1) * LANES), slice(top, top + 8)

        def gap(kind, i):
            return stack[h, pl.ds(top * rows + depth * (3 * kind + c) + i, 8, stride=rows), :]

        for kind, moved in enumerate((keep[3 + c, group, lanes], vectors[c, group, lanes])):
            gaps = [moved - gap(kind, i) for i in range(depth)] + [moved]
            for i, l in pairs(depth):
                term = gaps[i] * gaps[l]
                sums[i, l] = sums[i, l] + term if (i, l) in sums else term
        push = vectors[3 + c, group, lanes]
        for i in range(depth):
            pushed[i] = pushed[i] + gap(2, i) * push
        pushed_twice = pushed_twice + push * push
    for at, (i, l) in enumerate(pairs(depth)):
        value = sums[i, l] + pushed_twice - pushed[i] - pushed[l]
        rows_sum[at : at + 1, :] = jnp.sum(value, axis=0, keepdims=True)
    count = len(pairs(depth))
    if rows_sum.shape[0] > count:
        rows_sum[count:, :] = jnp.zeros((rows_sum.shape[0] - count, LANES), jnp.float32)
    whole = jnp.broadcast_to(jnp.sum(rows_sum[...], axis=1, keepdims=True), rows_sum.shape)
    lane = lax.broadcasted_iota(jnp.int32, (8, LANES), 1)
    out = whole[0:8]
    for group in range(1, rows_sum.shape[0] // 8):
        out = jnp.where(lane == group, whole[8 * group : 8 * group + 8], out)
    message[6, 0:8, 0:LANES] = out


def solve_kernel(depth, square, *refs):
    parts = refs[:-8]
    keep, past_w, gap_w, past_u, gap_u, new_u, new_w, total = refs[-8:]
    own = new_u.shape[1]
    tile = parts[0][6, 0:8, 0:LANES]
    for other in parts[1:]:
        tile = tile + other[6, 0:8, 0:LANES]
    even = lax.axis_index("sector") % 2 == 0

    def ahead(by, row):
        if square and by in (1, 3):
            return jnp.where(even, parts[by][row], parts[4 - by][row])
        return parts[by][row]

    sectors = len(parts)
    pushes = [[ahead(by, 3 + j) for j in range(3)] for by in range(sectors)]
    cross = sum(ahead(by, j) * pushes[by - 1][j] for by in range(sectors) for j in range(3))
    cross = jnp.sum(jnp.sum(cross, axis=0, keepdims=True), axis=1, keepdims=True)
    last = [keep[6 + j, 0:1] + pushes[-1][j][0:1] for j in range(3)] + [keep[c, 0:1] for c in range(3)]
    for group in range(total.shape[0] // 8):
        total[8 * group : 8 * group + 8, :] = jnp.broadcast_to(tile[:, group : group + 1], (8, LANES))
    matrix = {
        pair: jnp.broadcast_to(total[at : at + 1, :], (depth, LANES)) + 2.0 * cross
        for at, pair in enumerate(pairs(depth))
    }
    ridge = 0.0001 * sum(matrix[i, i] for i in range(depth)) / depth
    for i in range(depth):
        matrix[i, i] = matrix[i, i] + ridge
    inverse = []
    for step in range(depth):
        inverse.append(1.0 / matrix[step, step])
        for i in range(step + 1, depth):
            factor = matrix[step, i] * inverse[step]
            for l in range(i, depth + 1):
                matrix[i, l] = matrix[i, l] - factor * matrix[step, l]
    weights = [None] * depth
    for i in reversed(range(depth)):
        value = matrix[i, depth]
        for l in range(i + 1, depth):
            value = value - matrix[i, l] * weights[l]
        weights[i] = value * inverse[i]
    row = lax.broadcasted_iota(jnp.int32, (depth, LANES), 0)
    weight = weights[0]
    for i in range(1, depth):
        weight = jnp.where(row == i, weights[i], weight)
    for start in range(0, own, LANES):
        lanes = slice(start, start + LANES)
        for at, (past, gap, out) in enumerate(((past_u, gap_u, new_u), (past_w, gap_w, new_w))):
            for c in range(3):
                value = jnp.broadcast_to(last[3 * at + c][:, lanes], (depth, LANES))
                change = weight * (value - past[c, :, lanes] - gap[c, :, lanes])
                out[c : c + 1, lanes] = value[0:1] - jnp.sum(change, axis=0, keepdims=True)


def per_device(
    strain_map,
    corner_nodes,
    counts,
    seam_nodes,
    velocity,
    dual_state,
    nodal_load,
    mobility,
    past_dual,
    past_dual_gap,
    past_velocity,
    past_velocity_gap,
):
    own = velocity.shape[1]
    halves = own // LANES
    blocks = lax.axis_size("dom")
    sectors = lax.axis_size("sector")
    depth = past_dual.shape[0]
    seam_rows = seam_nodes.shape[1] // own
    mobility = mobility.reshape(1, own)
    past_dual, past_dual_gap, past_velocity, past_velocity_gap = (
        value.transpose(1, 0, 2) for value in (past_dual, past_dual_gap, past_velocity, past_velocity_gap)
    )

    def send(value, target):
        return lax.ppermute(value, "sector", [(i, target(i) % sectors) for i in range(sectors)])

    def swap(value, bits):
        return lax.ppermute(value, "dom", [(i, i ^ bits) for i in range(blocks)])

    nodes = (velocity, mobility, seam_nodes)
    ahead = call(
        nodes_kernel,
        f32(8 + seam_rows + 3 * depth, own),
        in_hbm(*nodes, past_velocity_gap),
        loose=len(nodes) + 1,
        scratch=[pltpu.VMEM(value.shape, value.dtype) for value in nodes]
        + [pltpu.SemaphoreType.DMA((len(nodes) + 3,))],
    )
    held = (strain_map, dual_state, velocity, nodal_load, mobility, corner_nodes)
    base = call(
        base_kernel,
        f32(INDEX + 4, own),
        (counts, ahead, *in_hbm(*held)),
        scalars=1,
        loose=len(held) + 1,
        scratch=[pltpu.VMEM(value.shape, value.dtype) for value in held] + [pltpu.SemaphoreType.DMA((len(held),))],
    )
    ahead = send(ahead, lambda i: i - 1)
    history = call(
        history_kernel,
        f32(6, depth, own),
        (base, *in_hbm(past_dual_gap, past_velocity_gap)),
        loose=3,
        scratch=[pltpu.SemaphoreType.DMA((2,))],
    )
    far_ones = list(range(blocks - 2, 2, -2))
    lengths = [max(INDEX + 4, ROWS - place) for place in range(len(far_ones))]
    messages = call(
        functools.partial(message_kernel, own * blocks, depth),
        tuple(f32(rows, own) for rows in sorted(set(lengths), reverse=True)),
        (history, ahead, base),
        loose=1,
    )
    wide = call(wide_kernel, f32(ROWS + 9 * depth, own), (messages[0], history, ahead))
    pieces = {0: wide}
    for bits, rows in zip(far_ones, lengths):
        pieces[bits] = swap(next(value for value in messages if value.shape[0] == rows), bits)
    pieces[2] = swap(wide, 2)
    for even in (0, 2):
        pieces[even + 1] = swap(pieces[even], 1)
    count = len(far_ones)
    crossed = swap(
        call(stack_kernel, f32(count * ROWS, own), tuple(pieces[bits] for bits in far_ones)), 1
    )
    histories, slots = [pieces[block] for block in range(4)], [(block,) for block in range(4)]
    history = call(
        pair_kernel, f32(2, 9 * depth, own), (*(pieces[bits] for bits in far_ones), wide, pieces[2]), loose=len(far_ones)
    )
    known, apart, later = (0, 2), 4, []
    while apart < blocks:
        other = swap(history, apart)
        later.append((other, tuple(slot ^ apart for slot in known)))
        known += later[-1][1]
        apart *= 2
        if apart < blocks:
            history = call(join_kernel, f32(2 * history.shape[0], 9 * depth, own), (history, other))
    order = [(at * ROWS, bits + 1) for at, bits in enumerate(far_ones)]
    order += [(0, block) for block in reversed(range(blocks)) if block in pieces]
    sector = f32(3, blocks, own)
    work = [
        pltpu.VMEM((6, blocks, own), jnp.float32),
        pltpu.VMEM((3 * SPLITS, 4, blocks, own), jnp.float32),
        pltpu.VMEM((3, 4, blocks, own), jnp.float32),
        pltpu.VMEM((blocks * 16 * -(-3 * SPLITS * (halves + 2) // 16), LANES), jnp.float32),
    ]
    state, index, to_near, to_far = call(
        functools.partial(first_kernel, blocks, order),
        (f32(KEPT, blocks, own), jax.ShapeDtypeStruct((4, blocks, own), jnp.int32), sector, sector),
        (*([crossed] * count), *(pieces[block] for _, block in order[count:])),
        scratch=[pltpu.VMEM((halves, blocks * ROWS, LANES), jnp.float32), *work],
    )
    from_far = send(to_far, lambda i: i + 1 if i % 2 else i - 1)
    from_near = send(to_near, lambda i: i ^ 1)
    for other, far in later:
        held_back = call(copy_kernel, f32(*other.shape), (from_near, from_far, other), loose=2)
        histories += [other, swap(held_back, 1)]
        slots += [far, tuple(slot ^ 1 for slot in far)]
    vectors, keep = call(
        second_kernel,
        (f32(6, blocks, own), f32(9, blocks, own)),
        (state, index, to_near, to_far, from_near, from_far),
        scratch=work,
    )
    count = -(-len(pairs(depth)) // 8) * 8
    message = call(
        functools.partial(gram_kernel, depth, tuple(slots)),
        f32(7, blocks, own),
        (vectors, keep, *histories),
        scratch=[
            pltpu.VMEM((halves, blocks * 9 * depth, LANES), jnp.float32),
            pltpu.VMEM((count, LANES), jnp.float32),
        ],
    )
    square = sectors == 4
    parts = [message] + [None] * (sectors - 1)
    for by in range(1, sectors):
        parts[by] = send(message, (lambda i: i ^ by) if square else (lambda i: i - by))
    return call(
        functools.partial(solve_kernel, depth, square),
        (f32(3, own), f32(3, own)),
        (*parts, keep, past_dual, past_dual_gap, past_velocity, past_velocity_gap),
        scratch=[pltpu.VMEM((count, LANES), jnp.float32)],
    )


def solution(mesh):
    in_specs = (
        P(None, ("sector", "dom")),
        P(None, ("sector", "dom")),
        P(("sector", "dom")),
        P("sector", None),
        P(None, ("sector", "dom")),
        P(None, ("sector", "dom")),
        P(None, ("sector", "dom")),
        P(("sector", "dom")),
        P(None, None, ("sector", "dom")),
        P(None, None, ("sector", "dom")),
        P(None, None, ("sector", "dom")),
        P(None, None, ("sector", "dom")),
    )
    out_specs = (P(None, ("sector", "dom")), P(None, ("sector", "dom")))
    return jax.shard_map(
        per_device, mesh=mesh, in_specs=in_specs, out_specs=out_specs, check_vma=False
    )
```

```python
import functools
import itertools

import jax
import jax.numpy as jnp
from jax import lax
from jax.experimental import pallas as pl
from jax.experimental.pallas import tpu as pltpu
from jax.sharding import PartitionSpec as P

LANES = 128
VMEM_LIMIT = 24 * 1024 * 1024

STRAIN, DUAL, STEP, SPEED, LOAD, NEXT_STEP, NEXT_SPEED, INDEX, ROWS = 0, 36, 39, 40, 43, 46, 47, 50, 56
KEPT_NEXT_STEP, KEPT_LOAD, KEPT = 40, 41, 44
SPLITS = 2


def vmem():
    return pl.BlockSpec(memory_space=pltpu.VMEM)


def smem():
    return pl.BlockSpec(memory_space=pltpu.SMEM)


def call(kernel, outs, args, scalars=0, loose=0, scratch=()):
    return pl.pallas_call(
        kernel,
        out_shape=outs,
        in_specs=[smem()] * scalars
        + [pl.BlockSpec(memory_space=pl.ANY)] * loose
        + [vmem()] * (len(args) - scalars - loose),
        out_specs=jax.tree.map(lambda _: vmem(), outs),
        scratch_shapes=list(scratch),
        compiler_params=pltpu.CompilerParams(vmem_limit_bytes=VMEM_LIMIT),
    )(*args)


def f32(*shape):
    return jax.ShapeDtypeStruct(shape, jnp.float32)


def repeat(blocks, body, init):
    if blocks == 8:
        return body(slice(0, 8), 0, init)
    return lax.fori_loop(
        0, blocks // 8, lambda step, carry: body(pl.ds(pl.multiple_of(8 * step, 8), 8), 8 * step, carry), init
    )


def one_row(ref, lead, group, first, row, lanes=slice(None)):
    if isinstance(first, int):
        return ref[(*lead, slice(first + row, first + row + 1), lanes)]
    return ref[(*lead, group, lanes)][row : row + 1]


def project_cone(trial):
    center = 0.5 * (trial[0] + trial[1])
    spread = 0.5 * (trial[0] - trial[1])
    shear = trial[2]
    radius = jnp.sqrt(spread * spread + shear * shear)
    upper = center + radius
    lower = center - radius
    iso_part = 0.5 * (jnp.maximum(upper, 0.0) + jnp.maximum(lower, 0.0))
    factor = jnp.clip((center + radius) / (2.0 * jnp.maximum(radius, 0.05)), 0.0, 1.0)
    return (iso_part + factor * spread, iso_part - factor * spread, factor * shear)


def fetch(pairs, sems):
    copies = [pltpu.make_async_copy(source, target, sems.at[at]) for at, (source, target) in enumerate(pairs)]
    for copy in copies:
        copy.start()
    for copy in copies:
        copy.wait()


def in_hbm(*values):
    return tuple(pltpu.with_memory_space_constraint(value, pltpu.HBM) for value in values)


def nodes_kernel(speed_in, mobility_in, seam_in, gap_u, ahead, speed, mobility, seam, sems):
    depth = gap_u.shape[1]
    start = ahead.shape[0] - 3 * depth
    gaps = [(gap_u.at[c], ahead.at[pl.ds(start + depth * c, depth)]) for c in range(3)]
    fetch(((speed_in, speed), (mobility_in, mobility), (seam_in, seam), *gaps), sems)
    own = speed.shape[1]
    ahead[0:3, :] = speed[...]
    ahead[3:4, :] = mobility[...]
    ahead[4:8, :] = jnp.zeros((4, own), jnp.float32)
    for row in range(8, start):
        ahead[row : row + 1, :] = seam[:, (row - 8) * own : (row - 7) * own].astype(jnp.float32)


def base_kernel(counts, after, *refs):
    count = (len(refs) - 2) // 2
    sources, base, held, sems = refs[:count], refs[count], refs[count + 1 : -1], refs[-1]
    fetch(zip(sources, held), sems)
    strain, dual, speed, load, mobility, corners = held
    own = speed.shape[1]
    slot = lax.broadcasted_iota(jnp.int32, (1, own), 1)
    alive = (slot < counts[0]).astype(jnp.float32)
    base[STRAIN:DUAL, :] = strain[...] * alive
    base[DUAL : DUAL + 3, :] = dual[...] * alive
    base[STEP : STEP + 1, :] = mobility[...]
    base[SPEED : SPEED + 3, :] = speed[...]
    base[LOAD : LOAD + 3, :] = load[...]
    base[NEXT_STEP:INDEX, :] = jnp.zeros((INDEX - NEXT_STEP, own), jnp.float32)
    base[INDEX : INDEX + 4, :] = corners[...].astype(jnp.float32)


def message_kernel(sector_nodes, depth, after, ahead, base, message, *shorter):
    own = message.shape[1]
    halves = own // LANES
    message[:NEXT_STEP, :] = base[:NEXT_STEP, :]
    message[NEXT_STEP : NEXT_STEP + 1, :] = ahead[3:4, :]
    message[NEXT_SPEED : NEXT_SPEED + 3, :] = ahead[0:3, :]
    message[INDEX + 4 :, :] = jnp.zeros((ROWS - INDEX - 4, own), jnp.float32)
    corners = base[INDEX : INDEX + 4, :].astype(jnp.int32)
    corner = jnp.concatenate([corners[:, h * LANES : (h + 1) * LANES] for h in range(halves)], axis=0)
    seam_rows = ahead.shape[0] - 8 - 3 * depth
    place = jnp.clip(corner - sector_nodes, 0, seam_rows * own - 1)
    high, low = place // LANES, place % LANES
    found = jnp.zeros(corner.shape, jnp.float32)
    for row in range(seam_rows):
        for h in range(halves):
            table = jnp.broadcast_to(ahead[8 + row : 9 + row, h * LANES : (h + 1) * LANES], corner.shape)
            value = jnp.take_along_axis(table, low, axis=1, mode="promise_in_bounds")
            found = jnp.where(high == row * halves + h, value, found)
    node = jnp.where(corner < sector_nodes, corner.astype(jnp.float32), found + float(sector_nodes))
    for h in range(halves):
        message[INDEX : INDEX + 4, h * LANES : (h + 1) * LANES] = node[4 * h : 4 * h + 4]
    for other in shorter:
        other[...] = message[: other.shape[0], :]


def history_kernel(after, gap_w, gap_u, history, sems):
    fetch(((gap_w, history.at[0:3]), (gap_u, history.at[3:6])), sems)


def wide_kernel(message, gaps, ahead, wide):
    depth = gaps.shape[1]
    start = ahead.shape[0] - 3 * depth
    wide[:ROWS, :] = message[...]
    for kind in range(6):
        wide[ROWS + depth * kind : ROWS + depth * (kind + 1), :] = gaps[kind]
    wide[ROWS + 6 * depth :, :] = ahead[start:, :]


def stack_kernel(*refs):
    stacked = refs[-1]
    for at, piece in enumerate(refs[:-1]):
        stacked[at * ROWS : at * ROWS + piece.shape[0], :] = piece[...]
        if piece.shape[0] < ROWS:
            start = at * ROWS + piece.shape[0]
            stacked[start : (at + 1) * ROWS, :] = jnp.zeros(((at + 1) * ROWS - start, piece.shape[1]), jnp.float32)


def pair_kernel(*refs):
    left, right, joined = refs[-3:]
    joined[0] = left[ROWS:, :]
    joined[1] = right[ROWS:, :]


def copy_kernel(*refs):
    value, copied = refs[-2:]
    copied[...] = value[...]


def join_kernel(*refs):
    left, right, joined = refs[-3:]
    count = left.shape[0]
    joined[:count] = left[...]
    joined[count:] = right[...]


def sweep(strain_row, index, work, dual):
    table, terms, codes, nearby = work
    blocks, own = index.shape[1:]
    halves = own // LANES
    here = lax.axis_index("dom")
    row = lax.broadcasted_iota(jnp.int32, (blocks, LANES), 0)
    left_block = ((row ^ here) - 1) ^ here
    right_block = ((row ^ here) + 1) ^ here

    def wide(j, group, first, block, part):
        piece = one_row(table, (j,), group, first, block, slice(part * LANES, (part + 1) * LANES))
        return jnp.broadcast_to(piece, (blocks, LANES))

    def take_sides(group, first, sides):
        left, right = (list(side) for side in sides)
        for block in range(8):
            for j in range(3):
                left[j] = jnp.where(left_block == first + block, wide(j, group, first, block, halves - 1), left[j])
                right[j] = jnp.where(right_block == first + block, wide(j, group, first, block, 0), right[j])
        return tuple(left), tuple(right)

    blank = tuple(jnp.zeros((blocks, LANES), jnp.float32) for _ in range(3))
    left, right = repeat(blocks, take_sides, (blank, blank))
    speed = []
    for k in range(4):
        parts = []
        for h in range(halves):
            number = index[k, :, h * LANES : (h + 1) * LANES]
            high, low = number // LANES, number % LANES

            def take(value):
                return jnp.take_along_axis(value, low, axis=1, mode="promise_in_bounds")

            found = [take(table[j, :, 0:LANES]) for j in range(3)]
            for part in range(1, halves):
                mask = high % halves == part
                found = [
                    jnp.where(mask, take(table[j, :, part * LANES : (part + 1) * LANES]), found[j]) for j in range(3)
                ]
            mask = number // own == left_block
            found = [jnp.where(mask, take(left[j]), found[j]) for j in range(3)]
            mask = number // own == right_block
            found = [jnp.where(mask, take(right[j]), found[j]) for j in range(3)]

            def take_group(group, first, found):
                for part, block in itertools.product(range(halves), range(8)):
                    mask = high == (blocks + first + block) * halves + part
                    found = [jnp.where(mask, take(wide(3 + j, group, first, block, part)), found[j]) for j in range(3)]
                return tuple(found)

            parts.append(repeat(blocks, take_group, tuple(found)))
        speed.append([jnp.concatenate([found[j] for found in parts], axis=1) for j in range(3)])
    rate = []
    for c in range(3):
        total = None
        for k in range(4):
            for j in range(3):
                term = strain_row(12 * c + 3 * k + j) * speed[k][j]
                total = term if total is None else total + term
        rate.append(total)
    trial = [rate[c] + dual[c] for c in range(3)]
    cone = project_cone(trial)
    dual_next = [trial[c] - cone[c] for c in range(3)]
    misfit = [rate[c] - cone[c] + dual_next[c] for c in range(3)]
    for k in range(4):
        for j in range(3):
            rest = sum(strain_row(12 * c + 3 * k + j) * misfit[c] for c in range(3))
            for split in range(SPLITS):
                term = rest.astype(jnp.bfloat16).astype(jnp.float32)
                terms[SPLITS * j + split, k] = term
                rest = rest - term

    near_rows = halves + 2
    next_rows = halves * blocks
    row_wide = lax.broadcasted_iota(jnp.int32, (blocks, own), 0) ^ here
    for k in range(4):
        number = index[k]
        block_of, half = number // own, number // LANES % halves
        near = jnp.where(block_of == ((row_wide - 1) ^ here), 0, 1 + half)
        near = jnp.where(block_of == ((row_wide + 1) ^ here), 1 + halves, near)
        codes[0, k] = (number % LANES).astype(jnp.float32)
        codes[1, k] = jnp.where(block_of < blocks, near, -1).astype(jnp.float32)
        codes[2, k] = jnp.where(block_of < blocks, -1, half * blocks + block_of - blocks).astype(jnp.float32)

    values = 3 * SPLITS
    per_tile = 16 // near_rows
    near_tiles = -(-values // per_tile)
    iota = lax.broadcasted_iota(jnp.int32, (16, own), 0)
    near_iota = (iota % near_rows).astype(jnp.float32).astype(jnp.bfloat16)
    value_iota = (iota // near_rows).astype(jnp.float32).astype(jnp.bfloat16)
    value_masks = [value_iota == jnp.full((16, own), float(at), jnp.bfloat16) for at in range(per_tile)]
    iota = iota.astype(jnp.float32)
    low_iota = [(iota + float(16 * g)).astype(jnp.bfloat16) for g in range(LANES // 16)]
    next_iota = [(iota + float(16 * g)).astype(jnp.bfloat16) for g in range(next_rows // 16)]
    one = jnp.ones((16, own), jnp.bfloat16)
    zero = jnp.zeros((16, own), jnp.bfloat16)

    def spread_row(value):
        return jnp.broadcast_to(value, (16, own)).astype(jnp.bfloat16)

    def add_group(group, first, total):
        for block in range(8):
            part = None
            for k in range(4):
                low_row, near_row, next_row = (
                    spread_row(one_row(codes, (at, k), group, first, block)) for at in range(3)
                )
                rows = [spread_row(one_row(terms, (at, k), group, first, block)) for at in range(values)]
                spread = jnp.concatenate([jnp.where(low_row == value, one, zero) for value in low_iota], axis=0)
                mask = near_row == near_iota
                weights = []
                for tile in range(near_tiles):
                    inside = rows[tile * per_tile : (tile + 1) * per_tile]
                    value = inside[-1]
                    for at in range(len(inside) - 1):
                        value = jnp.where(value_masks[at], inside[at], value)
                    weights.append(jnp.where(mask, value, zero))
                masks = [next_row == value for value in next_iota]
                weights += [jnp.where(mask, row, zero) for row in rows for mask in masks]
                product = lax.dot_general(
                    jnp.concatenate(weights, axis=0),
                    spread,
                    (((1,), (1,)), ((), ())),
                    preferred_element_type=jnp.float32,
                )
                part = product if part is None else part + product
            start = (first + block) * 16 * near_tiles
            if not isinstance(start, int):
                start = pl.multiple_of(start, 16)
            nearby[pl.ds(start, 16 * near_tiles), :] = part[: 16 * near_tiles]
            total += part[16 * near_tiles :]
        return total

    total = repeat(blocks, add_group, jnp.zeros((values * next_rows, LANES), jnp.float32))

    def near_force(j, row):
        return sum(
            nearby[pl.ds((SPLITS * j + split) * near_rows + row, blocks, stride=16 * near_tiles), :]
            for split in range(SPLITS)
        )

    force_own, force_next = [], []
    for j in range(3):
        halves_own = [near_force(j, 1 + h) for h in range(halves)]
        to_left, to_right = near_force(j, 0), near_force(j, 1 + halves)
        from_right = from_left = jnp.zeros((blocks, LANES), jnp.float32)
        for block in range(blocks):
            wide_left = jnp.broadcast_to(to_left[block : block + 1], (blocks, LANES))
            wide_right = jnp.broadcast_to(to_right[block : block + 1], (blocks, LANES))
            from_right = jnp.where(right_block == block, wide_left, from_right)
            from_left = jnp.where(left_block == block, wide_right, from_left)
        halves_own[-1] = halves_own[-1] + from_right
        halves_own[0] = halves_own[0] + from_left
        force_own.append(jnp.concatenate(halves_own, axis=1))
        whole = sum(
            total[(SPLITS * j + split) * next_rows : (SPLITS * j + split + 1) * next_rows] for split in range(SPLITS)
        )
        force_next.append(jnp.concatenate([whole[h * blocks : (h + 1) * blocks] for h in range(halves)], axis=1))
    return dual_next, force_own, force_next


def stack_block(piece, slot, rows, stack):
    held = min(rows, piece.shape[0])
    for h in range(stack.shape[0]):
        stack[h, slot * rows : slot * rows + held, :] = piece[:held, h * LANES : (h + 1) * LANES]


def across(stack, row, rows):
    blocks = stack.shape[1] // rows
    return jnp.concatenate(
        [stack[h, pl.ds(row, blocks, stride=rows), :] for h in range(stack.shape[0])], axis=1
    )


def first_kernel(blocks, order, *refs):
    pieces = refs[: len(order)]
    state, index, to_near, to_far, stack = refs[blocks : blocks + 5]
    work = refs[blocks + 5 :]
    table = work[0]
    own = index.shape[2]
    for piece, (start, slot) in zip(pieces, order):
        stack_block(piece.at[start : min(start + ROWS, piece.shape[0])], slot, ROWS, stack)
    flip = lax.axis_index("dom") * own
    even = lax.axis_index("sector") % 2 == 0
    for k in range(4):
        index[k] = across(stack, INDEX + k, ROWS).astype(jnp.int32) ^ flip
    for row in range(36):
        state[row] = across(stack, STRAIN + row, ROWS)
    step = across(stack, STEP, ROWS)
    state[STEP] = step
    state[KEPT_NEXT_STEP] = across(stack, NEXT_STEP, ROWS)
    for j in range(3):
        state[KEPT_LOAD + j] = across(stack, LOAD + j, ROWS)
        table[j] = across(stack, SPEED + j, ROWS)
        table[3 + j] = across(stack, NEXT_SPEED + j, ROWS)
    dual = [across(stack, DUAL + c, ROWS) for c in range(3)]
    dual, force_own, force_next = sweep(lambda row: state[row], index, work, dual)
    for c in range(3):
        state[DUAL + c] = dual[c]
        mine = table[c] - step * (force_own[c] - state[KEPT_LOAD + c])
        to_near[c] = jnp.where(even, force_next[c], mine)
        to_far[c] = jnp.where(even, mine, force_next[c])


def second_kernel(state, index, to_near, to_far, from_far, from_near, vectors, keep, *work):
    table = work[0]
    even = lax.axis_index("sector") % 2 == 0
    step, next_step = state[STEP], state[KEPT_NEXT_STEP]
    for j in range(3):
        near, far = to_near[j], to_far[j]
        near_in, far_in = from_near[j], from_far[j]
        table[j] = jnp.where(even, far, near) - step * jnp.where(even, far_in, near_in)
        table[3 + j] = jnp.where(even, near_in, far_in) - next_step * jnp.where(even, near, far)
    dual = [state[DUAL + c] for c in range(3)]
    dual_next, force_own, force_next = sweep(lambda row: state[row], index, work, dual)
    for c in range(3):
        after = table[c] - step * (force_own[c] - state[KEPT_LOAD + c])
        vectors[c] = after - table[c]
        vectors[3 + c] = -(next_step * force_next[c])
        keep[c] = dual_next[c]
        keep[3 + c] = dual_next[c] - dual[c]
        keep[6 + c] = after


def pairs(depth):
    return [(i, l) for i in range(depth) for l in range(i, depth + 1)]


def gram_kernel(depth, slots, vectors, keep, *refs):
    blocks, own = keep.shape[1:]
    halves = own // LANES
    rows = 9 * depth
    message, stack, rows_sum = refs[len(slots) :]
    for piece, own_slots in zip(refs, slots):
        for at, slot in enumerate(own_slots):
            stack_block(piece.at[at] if len(piece.shape) == 3 else piece.at[ROWS:], slot, rows, stack)
    for row in range(6):
        message[row] = vectors[row]
    message[6] = jnp.zeros((blocks, own), jnp.float32)
    sums, pushed, pushed_twice = {}, [0.0] * (depth + 1), 0.0
    for c, h, top in itertools.product(range(3), range(halves), range(0, blocks, 8)):
        lanes, group = slice(h * LANES, (h + 1) * LANES), slice(top, top + 8)

        def gap(kind, i):
            return stack[h, pl.ds(top * rows + depth * (3 * kind + c) + i, 8, stride=rows), :]

        for kind, moved in enumerate((keep[3 + c, group, lanes], vectors[c, group, lanes])):
            gaps = [moved - gap(kind, i) for i in range(depth)] + [moved]
            for i, l in pairs(depth):
                term = gaps[i] * gaps[l]
                sums[i, l] = sums[i, l] + term if (i, l) in sums else term
        push = vectors[3 + c, group, lanes]
        for i in range(depth):
            pushed[i] = pushed[i] + gap(2, i) * push
        pushed_twice = pushed_twice + push * push
    for at, (i, l) in enumerate(pairs(depth)):
        value = sums[i, l] + pushed_twice - pushed[i] - pushed[l]
        rows_sum[at : at + 1, :] = jnp.sum(value, axis=0, keepdims=True)
    count = len(pairs(depth))
    if rows_sum.shape[0] > count:
        rows_sum[count:, :] = jnp.zeros((rows_sum.shape[0] - count, LANES), jnp.float32)
    whole = jnp.broadcast_to(jnp.sum(rows_sum[...], axis=1, keepdims=True), rows_sum.shape)
    lane = lax.broadcasted_iota(jnp.int32, (8, LANES), 1)
    out = whole[0:8]
    for group in range(1, rows_sum.shape[0] // 8):
        out = jnp.where(lane == group, whole[8 * group : 8 * group + 8], out)
    message[6, 0:8, 0:LANES] = out


def solve_kernel(depth, square, *refs):
    parts = refs[:-8]
    keep, past_w, gap_w, past_u, gap_u, new_u, new_w, total = refs[-8:]
    own = new_u.shape[1]
    tile = parts[0][6, 0:8, 0:LANES]
    for other in parts[1:]:
        tile = tile + other[6, 0:8, 0:LANES]
    even = lax.axis_index("sector") % 2 == 0

    def ahead(by, row):
        if square and by in (1, 3):
            return jnp.where(even, parts[by][row], parts[4 - by][row])
        return parts[by][row]

    sectors = len(parts)
    pushes = [[ahead(by, 3 + j) for j in range(3)] for by in range(sectors)]
    cross = sum(ahead(by, j) * pushes[by - 1][j] for by in range(sectors) for j in range(3))
    cross = jnp.sum(jnp.sum(cross, axis=0, keepdims=True), axis=1, keepdims=True)
    last = [keep[6 + j, 0:1] + pushes[-1][j][0:1] for j in range(3)] + [keep[c, 0:1] for c in range(3)]
    for group in range(total.shape[0] // 8):
        total[8 * group : 8 * group + 8, :] = jnp.broadcast_to(tile[:, group : group + 1], (8, LANES))
    matrix = {
        pair: jnp.broadcast_to(total[at : at + 1, :], (depth, LANES)) + 2.0 * cross
        for at, pair in enumerate(pairs(depth))
    }
    ridge = 0.0001 * sum(matrix[i, i] for i in range(depth)) / depth
    for i in range(depth):
        matrix[i, i] = matrix[i, i] + ridge
    inverse = []
    for step in range(depth):
        inverse.append(1.0 / matrix[step, step])
        for i in range(step + 1, depth):
            factor = matrix[step, i] * inverse[step]
            for l in range(i, depth + 1):
                matrix[i, l] = matrix[i, l] - factor * matrix[step, l]
    weights = [None] * depth
    for i in reversed(range(depth)):
        value = matrix[i, depth]
        for l in range(i + 1, depth):
            value = value - matrix[i, l] * weights[l]
        weights[i] = value * inverse[i]
    row = lax.broadcasted_iota(jnp.int32, (depth, LANES), 0)
    weight = weights[0]
    for i in range(1, depth):
        weight = jnp.where(row == i, weights[i], weight)
    for start in range(0, own, LANES):
        lanes = slice(start, start + LANES)
        for at, (past, gap, out) in enumerate(((past_u, gap_u, new_u), (past_w, gap_w, new_w))):
            for c in range(3):
                value = jnp.broadcast_to(last[3 * at + c][:, lanes], (depth, LANES))
                change = weight * (value - past[c, :, lanes] - gap[c, :, lanes])
                out[c : c + 1, lanes] = value[0:1] - jnp.sum(change, axis=0, keepdims=True)


def per_device(
    strain_map,
    corner_nodes,
    counts,
    seam_nodes,
    velocity,
    dual_state,
    nodal_load,
    mobility,
    past_dual,
    past_dual_gap,
    past_velocity,
    past_velocity_gap,
):
    own = velocity.shape[1]
    halves = own // LANES
    blocks = lax.axis_size("dom")
    sectors = lax.axis_size("sector")
    depth = past_dual.shape[0]
    seam_rows = seam_nodes.shape[1] // own
    mobility = mobility.reshape(1, own)
    past_dual, past_dual_gap, past_velocity, past_velocity_gap = (
        value.transpose(1, 0, 2) for value in (past_dual, past_dual_gap, past_velocity, past_velocity_gap)
    )

    def send(value, target):
        return lax.ppermute(value, "sector", [(i, target(i) % sectors) for i in range(sectors)])

    def swap(value, bits):
        return lax.ppermute(value, "dom", [(i, i ^ bits) for i in range(blocks)])

    nodes = (velocity, mobility, seam_nodes)
    ahead = call(
        nodes_kernel,
        f32(8 + seam_rows + 3 * depth, own),
        in_hbm(*nodes, past_velocity_gap),
        loose=len(nodes) + 1,
        scratch=[pltpu.VMEM(value.shape, value.dtype) for value in nodes]
        + [pltpu.SemaphoreType.DMA((len(nodes) + 3,))],
    )
    held = (strain_map, dual_state, velocity, nodal_load, mobility, corner_nodes)
    base = call(
        base_kernel,
        f32(INDEX + 4, own),
        (counts, ahead, *in_hbm(*held)),
        scalars=1,
        loose=len(held) + 1,
        scratch=[pltpu.VMEM(value.shape, value.dtype) for value in held] + [pltpu.SemaphoreType.DMA((len(held),))],
    )
    ahead = send(ahead, lambda i: i - 1)
    history = call(
        history_kernel,
        f32(6, depth, own),
        (base, *in_hbm(past_dual_gap, past_velocity_gap)),
        loose=3,
        scratch=[pltpu.SemaphoreType.DMA((2,))],
    )
    far_ones = list(range(blocks - 2, 2, -2))
    lengths = [max(INDEX + 4, ROWS - place) for place in range(len(far_ones))]
    messages = call(
        functools.partial(message_kernel, own * blocks, depth),
        tuple(f32(rows, own) for rows in sorted(set(lengths), reverse=True)),
        (history, ahead, base),
        loose=1,
    )
    wide = call(wide_kernel, f32(ROWS + 9 * depth, own), (messages[0], history, ahead))
    pieces = {0: wide}
    for bits, rows in zip(far_ones, lengths):
        pieces[bits] = swap(next(value for value in messages if value.shape[0] == rows), bits)
    pieces[2] = swap(wide, 2)
    for even in (0, 2):
        pieces[even + 1] = swap(pieces[even], 1)
    count = len(far_ones)
    crossed = swap(
        call(stack_kernel, f32(count * ROWS, own), tuple(pieces[bits] for bits in far_ones)), 1
    )
    histories, slots = [pieces[block] for block in range(4)], [(block,) for block in range(4)]
    history = call(
        pair_kernel, f32(2, 9 * depth, own), (*(pieces[bits] for bits in far_ones), wide, pieces[2]), loose=len(far_ones)
    )
    known, apart, later = (0, 2), 4, []
    while apart < blocks:
        other = swap(history, apart)
        later.append((other, tuple(slot ^ apart for slot in known)))
        known += later[-1][1]
        apart *= 2
        if apart < blocks:
            history = call(join_kernel, f32(2 * history.shape[0], 9 * depth, own), (history, other))
    order = [(at * ROWS, bits + 1) for at, bits in enumerate(far_ones)]
    order += [(0, block) for block in reversed(range(blocks)) if block in pieces]
    sector = f32(3, blocks, own)
    work = [
        pltpu.VMEM((6, blocks, own), jnp.float32),
        pltpu.VMEM((3 * SPLITS, 4, blocks, own), jnp.float32),
        pltpu.VMEM((3, 4, blocks, own), jnp.float32),
        pltpu.VMEM((blocks * 16 * -(-3 * SPLITS * (halves + 2) // 16), LANES), jnp.float32),
    ]
    state, index, to_near, to_far = call(
        functools.partial(first_kernel, blocks, order),
        (f32(KEPT, blocks, own), jax.ShapeDtypeStruct((4, blocks, own), jnp.int32), sector, sector),
        (*([crossed] * count), *(pieces[block] for _, block in order[count:])),
        scratch=[pltpu.VMEM((halves, blocks * ROWS, LANES), jnp.float32), *work],
    )
    from_far = send(to_far, lambda i: i + 1 if i % 2 else i - 1)
    from_near = send(to_near, lambda i: i ^ 1)
    for other, far in later:
        held_back = call(copy_kernel, f32(*other.shape), (from_near, from_far, other), loose=2)
        histories += [other, swap(held_back, 1)]
        slots += [far, tuple(slot ^ 1 for slot in far)]
    vectors, keep = call(
        second_kernel,
        (f32(6, blocks, own), f32(9, blocks, own)),
        (state, index, to_near, to_far, from_far, from_near),
        scratch=work,
    )
    count = -(-len(pairs(depth)) // 8) * 8
    message = call(
        functools.partial(gram_kernel, depth, tuple(slots)),
        f32(7, blocks, own),
        (vectors, keep, *histories),
        scratch=[
            pltpu.VMEM((halves, blocks * 9 * depth, LANES), jnp.float32),
            pltpu.VMEM((count, LANES), jnp.float32),
        ],
    )
    square = sectors == 4
    parts = [message] + [None] * (sectors - 1)
    for by in sorted(range(1, sectors), reverse=True):
        parts[by] = send(message, (lambda i: i ^ by) if square else (lambda i: i - by))
    return call(
        functools.partial(solve_kernel, depth, square),
        (f32(3, own), f32(3, own)),
        (*parts, keep, past_dual, past_dual_gap, past_velocity, past_velocity_gap),
        scratch=[pltpu.VMEM((count, LANES), jnp.float32)],
    )


def solution(mesh):
    in_specs = (
        P(None, ("sector", "dom")),
        P(None, ("sector", "dom")),
        P(("sector", "dom")),
        P("sector", None),
        P(None, ("sector", "dom")),
        P(None, ("sector", "dom")),
        P(None, ("sector", "dom")),
        P(("sector", "dom")),
        P(None, None, ("sector", "dom")),
        P(None, None, ("sector", "dom")),
        P(None, None, ("sector", "dom")),
        P(None, None, ("sector", "dom")),
    )
    out_specs = (P(None, ("sector", "dom")), P(None, ("sector", "dom")))
    return jax.shard_map(
        per_device, mesh=mesh, in_specs=in_specs, out_specs=out_specs, check_vma=False
    )
```

```python
import functools
import itertools

import jax
import jax.numpy as jnp
from jax import lax
from jax.experimental import pallas as pl
from jax.experimental.pallas import tpu as pltpu
from jax.sharding import PartitionSpec as P

LANES = 128
VMEM_LIMIT = 24 * 1024 * 1024

STRAIN, DUAL, STEP, SPEED, LOAD, NEXT_STEP, NEXT_SPEED, INDEX, ROWS = 0, 36, 39, 40, 43, 46, 47, 50, 56
KEPT_NEXT_STEP, KEPT_LOAD, KEPT = 40, 41, 44
SPLITS = 2


def vmem():
    return pl.BlockSpec(memory_space=pltpu.VMEM)


def smem():
    return pl.BlockSpec(memory_space=pltpu.SMEM)


def call(kernel, outs, args, scalars=0, loose=0, scratch=()):
    return pl.pallas_call(
        kernel,
        out_shape=outs,
        in_specs=[smem()] * scalars
        + [pl.BlockSpec(memory_space=pl.ANY)] * loose
        + [vmem()] * (len(args) - scalars - loose),
        out_specs=jax.tree.map(lambda _: vmem(), outs),
        scratch_shapes=list(scratch),
        compiler_params=pltpu.CompilerParams(vmem_limit_bytes=VMEM_LIMIT),
    )(*args)


def f32(*shape):
    return jax.ShapeDtypeStruct(shape, jnp.float32)


def repeat(blocks, body, init):
    if blocks == 8:
        return body(slice(0, 8), 0, init)
    return lax.fori_loop(
        0, blocks // 8, lambda step, carry: body(pl.ds(pl.multiple_of(8 * step, 8), 8), 8 * step, carry), init
    )


def one_row(ref, lead, group, first, row, lanes=slice(None)):
    if isinstance(first, int):
        return ref[(*lead, slice(first + row, first + row + 1), lanes)]
    return ref[(*lead, group, lanes)][row : row + 1]


def project_cone(trial):
    center = 0.5 * (trial[0] + trial[1])
    spread = 0.5 * (trial[0] - trial[1])
    shear = trial[2]
    radius = jnp.sqrt(spread * spread + shear * shear)
    upper = center + radius
    lower = center - radius
    iso_part = 0.5 * (jnp.maximum(upper, 0.0) + jnp.maximum(lower, 0.0))
    factor = jnp.clip((center + radius) / (2.0 * jnp.maximum(radius, 0.05)), 0.0, 1.0)
    return (iso_part + factor * spread, iso_part - factor * spread, factor * shear)


def fetch(pairs, sems):
    copies = [pltpu.make_async_copy(source, target, sems.at[at]) for at, (source, target) in enumerate(pairs)]
    for copy in copies:
        copy.start()
    for copy in copies:
        copy.wait()


def in_hbm(*values):
    return tuple(pltpu.with_memory_space_constraint(value, pltpu.HBM) for value in values)


def nodes_kernel(speed_in, mobility_in, seam_in, gap_u, ahead, speed, mobility, seam, sems):
    depth = gap_u.shape[1]
    start = ahead.shape[0] - 3 * depth
    gaps = [(gap_u.at[c], ahead.at[pl.ds(start + depth * c, depth)]) for c in range(3)]
    fetch(((speed_in, speed), (mobility_in, mobility), (seam_in, seam), *gaps), sems)
    own = speed.shape[1]
    ahead[0:3, :] = speed[...]
    ahead[3:4, :] = mobility[...]
    ahead[4:8, :] = jnp.zeros((4, own), jnp.float32)
    for row in range(8, start):
        ahead[row : row + 1, :] = seam[:, (row - 8) * own : (row - 7) * own].astype(jnp.float32)


def base_kernel(counts, after, *refs):
    count = (len(refs) - 2) // 2
    sources, base, held, sems = refs[:count], refs[count], refs[count + 1 : -1], refs[-1]
    fetch(zip(sources, held), sems)
    strain, dual, speed, load, mobility, corners = held
    own = speed.shape[1]
    slot = lax.broadcasted_iota(jnp.int32, (1, own), 1)
    alive = (slot < counts[0]).astype(jnp.float32)
    base[STRAIN:DUAL, :] = strain[...] * alive
    base[DUAL : DUAL + 3, :] = dual[...] * alive
    base[STEP : STEP + 1, :] = mobility[...]
    base[SPEED : SPEED + 3, :] = speed[...]
    base[LOAD : LOAD + 3, :] = load[...]
    base[NEXT_STEP:INDEX, :] = jnp.zeros((INDEX - NEXT_STEP, own), jnp.float32)
    base[INDEX : INDEX + 4, :] = corners[...].astype(jnp.float32)


def message_kernel(sector_nodes, depth, after, ahead, base, message, *shorter):
    own = message.shape[1]
    halves = own // LANES
    message[:NEXT_STEP, :] = base[:NEXT_STEP, :]
    message[NEXT_STEP : NEXT_STEP + 1, :] = ahead[3:4, :]
    message[NEXT_SPEED : NEXT_SPEED + 3, :] = ahead[0:3, :]
    message[INDEX + 4 :, :] = jnp.zeros((ROWS - INDEX - 4, own), jnp.float32)
    corners = base[INDEX : INDEX + 4, :].astype(jnp.int32)
    corner = jnp.concatenate([corners[:, h * LANES : (h + 1) * LANES] for h in range(halves)], axis=0)
    seam_rows = ahead.shape[0] - 8 - 3 * depth
    place = jnp.clip(corner - sector_nodes, 0, seam_rows * own - 1)
    high, low = place // LANES, place % LANES
    found = jnp.zeros(corner.shape, jnp.float32)
    for row in range(seam_rows):
        for h in range(halves):
            table = jnp.broadcast_to(ahead[8 + row : 9 + row, h * LANES : (h + 1) * LANES], corner.shape)
            value = jnp.take_along_axis(table, low, axis=1, mode="promise_in_bounds")
            found = jnp.where(high == row * halves + h, value, found)
    node = jnp.where(corner < sector_nodes, corner.astype(jnp.float32), found + float(sector_nodes))
    for h in range(halves):
        message[INDEX : INDEX + 4, h * LANES : (h + 1) * LANES] = node[4 * h : 4 * h + 4]
    for other in shorter:
        other[...] = message[: other.shape[0], :]


def history_kernel(after, gap_w, gap_u, history, sems):
    fetch(((gap_w, history.at[0:3]), (gap_u, history.at[3:6])), sems)


def wide_kernel(message, gaps, ahead, wide):
    depth = gaps.shape[1]
    start = ahead.shape[0] - 3 * depth
    wide[:ROWS, :] = message[...]
    for kind in range(6):
        wide[ROWS + depth * kind : ROWS + depth * (kind + 1), :] = gaps[kind]
    wide[ROWS + 6 * depth :, :] = ahead[start:, :]


def stack_kernel(*refs):
    stacked = refs[-1]
    for at, piece in enumerate(refs[:-1]):
        stacked[at * ROWS : at * ROWS + piece.shape[0], :] = piece[...]
        if piece.shape[0] < ROWS:
            start = at * ROWS + piece.shape[0]
            stacked[start : (at + 1) * ROWS, :] = jnp.zeros(((at + 1) * ROWS - start, piece.shape[1]), jnp.float32)


def pair_kernel(*refs):
    left, right, joined = refs[-3:]
    joined[0] = left[ROWS:, :]
    joined[1] = right[ROWS:, :]


def copy_kernel(*refs):
    value, copied = refs[-2:]
    copied[...] = value[...]


def join_kernel(*refs):
    left, right, joined = refs[-3:]
    count = left.shape[0]
    joined[:count] = left[...]
    joined[count:] = right[...]


def sweep(strain_row, index, work, dual):
    table, terms, codes, nearby = work
    blocks, own = index.shape[1:]
    halves = own // LANES
    here = lax.axis_index("dom")
    row = lax.broadcasted_iota(jnp.int32, (blocks, LANES), 0)
    left_block = ((row ^ here) - 1) ^ here
    right_block = ((row ^ here) + 1) ^ here

    def wide(j, group, first, block, part):
        piece = one_row(table, (j,), group, first, block, slice(part * LANES, (part + 1) * LANES))
        return jnp.broadcast_to(piece, (blocks, LANES))

    def take_sides(group, first, sides):
        left, right = (list(side) for side in sides)
        for block in range(8):
            for j in range(3):
                left[j] = jnp.where(left_block == first + block, wide(j, group, first, block, halves - 1), left[j])
                right[j] = jnp.where(right_block == first + block, wide(j, group, first, block, 0), right[j])
        return tuple(left), tuple(right)

    blank = tuple(jnp.zeros((blocks, LANES), jnp.float32) for _ in range(3))
    left, right = repeat(blocks, take_sides, (blank, blank))
    speed = []
    for k in range(4):
        parts = []
        for h in range(halves):
            number = index[k, :, h * LANES : (h + 1) * LANES]
            high, low = number // LANES, number % LANES

            def take(value):
                return jnp.take_along_axis(value, low, axis=1, mode="promise_in_bounds")

            found = [take(table[j, :, 0:LANES]) for j in range(3)]
            for part in range(1, halves):
                mask = high % halves == part
                found = [
                    jnp.where(mask, take(table[j, :, part * LANES : (part + 1) * LANES]), found[j]) for j in range(3)
                ]
            mask = number // own == left_block
            found = [jnp.where(mask, take(left[j]), found[j]) for j in range(3)]
            mask = number // own == right_block
            found = [jnp.where(mask, take(right[j]), found[j]) for j in range(3)]

            def take_group(group, first, found):
                for part, block in itertools.product(range(halves), range(8)):
                    mask = high == (blocks + first + block) * halves + part
                    found = [jnp.where(mask, take(wide(3 + j, group, first, block, part)), found[j]) for j in range(3)]
                return tuple(found)

            parts.append(repeat(blocks, take_group, tuple(found)))
        speed.append([jnp.concatenate([found[j] for found in parts], axis=1) for j in range(3)])
    rate = []
    for c in range(3):
        total = None
        for k in range(4):
            for j in range(3):
                term = strain_row(12 * c + 3 * k + j) * speed[k][j]
                total = term if total is None else total + term
        rate.append(total)
    trial = [rate[c] + dual[c] for c in range(3)]
    cone = project_cone(trial)
    dual_next = [trial[c] - cone[c] for c in range(3)]
    misfit = [rate[c] - cone[c] + dual_next[c] for c in range(3)]
    for k in range(4):
        for j in range(3):
            rest = sum(strain_row(12 * c + 3 * k + j) * misfit[c] for c in range(3))
            for split in range(SPLITS):
                term = rest.astype(jnp.bfloat16).astype(jnp.float32)
                terms[SPLITS * j + split, k] = term
                rest = rest - term

    near_rows = halves + 2
    next_rows = halves * blocks
    row_wide = lax.broadcasted_iota(jnp.int32, (blocks, own), 0) ^ here
    for k in range(4):
        number = index[k]
        block_of, half = number // own, number // LANES % halves
        near = jnp.where(block_of == ((row_wide - 1) ^ here), 0, 1 + half)
        near = jnp.where(block_of == ((row_wide + 1) ^ here), 1 + halves, near)
        codes[0, k] = (number % LANES).astype(jnp.float32)
        codes[1, k] = jnp.where(block_of < blocks, near, -1).astype(jnp.float32)
        codes[2, k] = jnp.where(block_of < blocks, -1, half * blocks + block_of - blocks).astype(jnp.float32)

    values = 3 * SPLITS
    per_tile = 16 // near_rows
    near_tiles = -(-values // per_tile)
    iota = lax.broadcasted_iota(jnp.int32, (16, own), 0)
    near_iota = (iota % near_rows).astype(jnp.float32).astype(jnp.bfloat16)
    value_iota = (iota // near_rows).astype(jnp.float32).astype(jnp.bfloat16)
    value_masks = [value_iota == jnp.full((16, own), float(at), jnp.bfloat16) for at in range(per_tile)]
    iota = iota.astype(jnp.float32)
    low_iota = [(iota + float(16 * g)).astype(jnp.bfloat16) for g in range(LANES // 16)]
    next_iota = [(iota + float(16 * g)).astype(jnp.bfloat16) for g in range(next_rows // 16)]
    one = jnp.ones((16, own), jnp.bfloat16)
    zero = jnp.zeros((16, own), jnp.bfloat16)

    def spread_row(value):
        return jnp.broadcast_to(value, (16, own)).astype(jnp.bfloat16)

    def add_group(group, first, total):
        for block in range(8):
            columns = []
            for k in range(4):
                low_row, near_row, next_row = (
                    spread_row(one_row(codes, (at, k), group, first, block)) for at in range(3)
                )
                rows = [spread_row(one_row(terms, (at, k), group, first, block)) for at in range(values)]
                spread = jnp.concatenate([jnp.where(low_row == value, one, zero) for value in low_iota], axis=0)
                mask = near_row == near_iota
                weights = []
                for tile in range(near_tiles):
                    inside = rows[tile * per_tile : (tile + 1) * per_tile]
                    value = inside[-1]
                    for at in range(len(inside) - 1):
                        value = jnp.where(value_masks[at], inside[at], value)
                    weights.append(jnp.where(mask, value, zero))
                masks = [next_row == value for value in next_iota]
                weights += [jnp.where(mask, row, zero) for row in rows for mask in masks]
                columns.append((jnp.concatenate(weights, axis=0), spread))
            part = lax.dot_general(
                jnp.concatenate([weights for weights, _ in columns], axis=1),
                jnp.concatenate([spread for _, spread in columns], axis=1),
                (((1,), (1,)), ((), ())),
                preferred_element_type=jnp.float32,
            )
            start = (first + block) * 16 * near_tiles
            if not isinstance(start, int):
                start = pl.multiple_of(start, 16)
            nearby[pl.ds(start, 16 * near_tiles), :] = part[: 16 * near_tiles]
            total += part[16 * near_tiles :]
        return total

    total = repeat(blocks, add_group, jnp.zeros((values * next_rows, LANES), jnp.float32))

    def near_force(j, row):
        return sum(
            nearby[pl.ds((SPLITS * j + split) * near_rows + row, blocks, stride=16 * near_tiles), :]
            for split in range(SPLITS)
        )

    force_own, force_next = [], []
    for j in range(3):
        halves_own = [near_force(j, 1 + h) for h in range(halves)]
        to_left, to_right = near_force(j, 0), near_force(j, 1 + halves)
        from_right = from_left = jnp.zeros((blocks, LANES), jnp.float32)
        for block in range(blocks):
            wide_left = jnp.broadcast_to(to_left[block : block + 1], (blocks, LANES))
            wide_right = jnp.broadcast_to(to_right[block : block + 1], (blocks, LANES))
            from_right = jnp.where(right_block == block, wide_left, from_right)
            from_left = jnp.where(left_block == block, wide_right, from_left)
        halves_own[-1] = halves_own[-1] + from_right
        halves_own[0] = halves_own[0] + from_left
        force_own.append(jnp.concatenate(halves_own, axis=1))
        whole = sum(
            total[(SPLITS * j + split) * next_rows : (SPLITS * j + split + 1) * next_rows] for split in range(SPLITS)
        )
        force_next.append(jnp.concatenate([whole[h * blocks : (h + 1) * blocks] for h in range(halves)], axis=1))
    return dual_next, force_own, force_next


def stack_block(piece, slot, rows, stack):
    held = min(rows, piece.shape[0])
    for h in range(stack.shape[0]):
        stack[h, slot * rows : slot * rows + held, :] = piece[:held, h * LANES : (h + 1) * LANES]


def across(stack, row, rows):
    blocks = stack.shape[1] // rows
    return jnp.concatenate(
        [stack[h, pl.ds(row, blocks, stride=rows), :] for h in range(stack.shape[0])], axis=1
    )


def first_kernel(blocks, order, *refs):
    pieces = refs[: len(order)]
    state, index, to_near, to_far, stack = refs[blocks : blocks + 5]
    work = refs[blocks + 5 :]
    table = work[0]
    own = index.shape[2]
    for piece, (start, slot) in zip(pieces, order):
        stack_block(piece.at[start : min(start + ROWS, piece.shape[0])], slot, ROWS, stack)
    flip = lax.axis_index("dom") * own
    even = lax.axis_index("sector") % 2 == 0
    for k in range(4):
        index[k] = across(stack, INDEX + k, ROWS).astype(jnp.int32) ^ flip
    for row in range(36):
        state[row] = across(stack, STRAIN + row, ROWS)
    step = across(stack, STEP, ROWS)
    state[STEP] = step
    state[KEPT_NEXT_STEP] = across(stack, NEXT_STEP, ROWS)
    for j in range(3):
        state[KEPT_LOAD + j] = across(stack, LOAD + j, ROWS)
        table[j] = across(stack, SPEED + j, ROWS)
        table[3 + j] = across(stack, NEXT_SPEED + j, ROWS)
    dual = [across(stack, DUAL + c, ROWS) for c in range(3)]
    dual, force_own, force_next = sweep(lambda row: state[row], index, work, dual)
    for c in range(3):
        state[DUAL + c] = dual[c]
        mine = table[c] - step * (force_own[c] - state[KEPT_LOAD + c])
        to_near[c] = jnp.where(even, force_next[c], mine)
        to_far[c] = jnp.where(even, mine, force_next[c])


def second_kernel(state, index, to_near, to_far, from_far, from_near, vectors, keep, *work):
    table = work[0]
    even = lax.axis_index("sector") % 2 == 0
    step, next_step = state[STEP], state[KEPT_NEXT_STEP]
    for j in range(3):
        near, far = to_near[j], to_far[j]
        near_in, far_in = from_near[j], from_far[j]
        table[j] = jnp.where(even, far, near) - step * jnp.where(even, far_in, near_in)
        table[3 + j] = jnp.where(even, near_in, far_in) - next_step * jnp.where(even, near, far)
    dual = [state[DUAL + c] for c in range(3)]
    dual_next, force_own, force_next = sweep(lambda row: state[row], index, work, dual)
    for c in range(3):
        after = table[c] - step * (force_own[c] - state[KEPT_LOAD + c])
        vectors[c] = after - table[c]
        vectors[3 + c] = -(next_step * force_next[c])
        keep[c] = dual_next[c]
        keep[3 + c] = dual_next[c] - dual[c]
        keep[6 + c] = after


def pairs(depth):
    return [(i, l) for i in range(depth) for l in range(i, depth + 1)]


def gram_kernel(depth, slots, vectors, keep, *refs):
    blocks, own = keep.shape[1:]
    halves = own // LANES
    rows = 9 * depth
    message, stack, rows_sum = refs[len(slots) :]
    for piece, own_slots in zip(refs, slots):
        for at, slot in enumerate(own_slots):
            stack_block(piece.at[at] if len(piece.shape) == 3 else piece.at[ROWS:], slot, rows, stack)
    for row in range(6):
        message[row] = vectors[row]
    message[6] = jnp.zeros((blocks, own), jnp.float32)
    sums, pushed, pushed_twice = {}, [0.0] * (depth + 1), 0.0
    for c, h, top in itertools.product(range(3), range(halves), range(0, blocks, 8)):
        lanes, group = slice(h * LANES, (h + 1) * LANES), slice(top, top + 8)

        def gap(kind, i):
            return stack[h, pl.ds(top * rows + depth * (3 * kind + c) + i, 8, stride=rows), :]

        for kind, moved in enumerate((keep[3 + c, group, lanes], vectors[c, group, lanes])):
            gaps = [moved - gap(kind, i) for i in range(depth)] + [moved]
            for i, l in pairs(depth):
                term = gaps[i] * gaps[l]
                sums[i, l] = sums[i, l] + term if (i, l) in sums else term
        push = vectors[3 + c, group, lanes]
        for i in range(depth):
            pushed[i] = pushed[i] + gap(2, i) * push
        pushed_twice = pushed_twice + push * push
    for at, (i, l) in enumerate(pairs(depth)):
        value = sums[i, l] + pushed_twice - pushed[i] - pushed[l]
        rows_sum[at : at + 1, :] = jnp.sum(value, axis=0, keepdims=True)
    count = len(pairs(depth))
    if rows_sum.shape[0] > count:
        rows_sum[count:, :] = jnp.zeros((rows_sum.shape[0] - count, LANES), jnp.float32)
    whole = jnp.broadcast_to(jnp.sum(rows_sum[...], axis=1, keepdims=True), rows_sum.shape)
    lane = lax.broadcasted_iota(jnp.int32, (8, LANES), 1)
    out = whole[0:8]
    for group in range(1, rows_sum.shape[0] // 8):
        out = jnp.where(lane == group, whole[8 * group : 8 * group + 8], out)
    message[6, 0:8, 0:LANES] = out


def solve_kernel(depth, square, *refs):
    parts = refs[:-8]
    keep, past_w, gap_w, past_u, gap_u, new_u, new_w, total = refs[-8:]
    own = new_u.shape[1]
    tile = parts[0][6, 0:8, 0:LANES]
    for other in parts[1:]:
        tile = tile + other[6, 0:8, 0:LANES]
    even = lax.axis_index("sector") % 2 == 0

    def ahead(by, row):
        if square and by in (1, 3):
            return jnp.where(even, parts[by][row], parts[4 - by][row])
        return parts[by][row]

    sectors = len(parts)
    pushes = [[ahead(by, 3 + j) for j in range(3)] for by in range(sectors)]
    cross = sum(ahead(by, j) * pushes[by - 1][j] for by in range(sectors) for j in range(3))
    cross = jnp.sum(jnp.sum(cross, axis=0, keepdims=True), axis=1, keepdims=True)
    last = [keep[6 + j, 0:1] + pushes[-1][j][0:1] for j in range(3)] + [keep[c, 0:1] for c in range(3)]
    for group in range(total.shape[0] // 8):
        total[8 * group : 8 * group + 8, :] = jnp.broadcast_to(tile[:, group : group + 1], (8, LANES))
    matrix = {
        pair: jnp.broadcast_to(total[at : at + 1, :], (depth, LANES)) + 2.0 * cross
        for at, pair in enumerate(pairs(depth))
    }
    ridge = 0.0001 * sum(matrix[i, i] for i in range(depth)) / depth
    for i in range(depth):
        matrix[i, i] = matrix[i, i] + ridge
    inverse = []
    for step in range(depth):
        inverse.append(1.0 / matrix[step, step])
        for i in range(step + 1, depth):
            factor = matrix[step, i] * inverse[step]
            for l in range(i, depth + 1):
                matrix[i, l] = matrix[i, l] - factor * matrix[step, l]
    weights = [None] * depth
    for i in reversed(range(depth)):
        value = matrix[i, depth]
        for l in range(i + 1, depth):
            value = value - matrix[i, l] * weights[l]
        weights[i] = value * inverse[i]
    row = lax.broadcasted_iota(jnp.int32, (depth, LANES), 0)
    weight = weights[0]
    for i in range(1, depth):
        weight = jnp.where(row == i, weights[i], weight)
    for start in range(0, own, LANES):
        lanes = slice(start, start + LANES)
        for at, (past, gap, out) in enumerate(((past_u, gap_u, new_u), (past_w, gap_w, new_w))):
            for c in range(3):
                value = jnp.broadcast_to(last[3 * at + c][:, lanes], (depth, LANES))
                change = weight * (value - past[c, :, lanes] - gap[c, :, lanes])
                out[c : c + 1, lanes] = value[0:1] - jnp.sum(change, axis=0, keepdims=True)


def per_device(
    strain_map,
    corner_nodes,
    counts,
    seam_nodes,
    velocity,
    dual_state,
    nodal_load,
    mobility,
    past_dual,
    past_dual_gap,
    past_velocity,
    past_velocity_gap,
):
    own = velocity.shape[1]
    halves = own // LANES
    blocks = lax.axis_size("dom")
    sectors = lax.axis_size("sector")
    depth = past_dual.shape[0]
    seam_rows = seam_nodes.shape[1] // own
    mobility = mobility.reshape(1, own)
    past_dual, past_dual_gap, past_velocity, past_velocity_gap = (
        value.transpose(1, 0, 2) for value in (past_dual, past_dual_gap, past_velocity, past_velocity_gap)
    )

    def send(value, target):
        return lax.ppermute(value, "sector", [(i, target(i) % sectors) for i in range(sectors)])

    def swap(value, bits):
        return lax.ppermute(value, "dom", [(i, i ^ bits) for i in range(blocks)])

    nodes = (velocity, mobility, seam_nodes)
    ahead = call(
        nodes_kernel,
        f32(8 + seam_rows + 3 * depth, own),
        in_hbm(*nodes, past_velocity_gap),
        loose=len(nodes) + 1,
        scratch=[pltpu.VMEM(value.shape, value.dtype) for value in nodes]
        + [pltpu.SemaphoreType.DMA((len(nodes) + 3,))],
    )
    held = (strain_map, dual_state, velocity, nodal_load, mobility, corner_nodes)
    base = call(
        base_kernel,
        f32(INDEX + 4, own),
        (counts, ahead, *in_hbm(*held)),
        scalars=1,
        loose=len(held) + 1,
        scratch=[pltpu.VMEM(value.shape, value.dtype) for value in held] + [pltpu.SemaphoreType.DMA((len(held),))],
    )
    ahead = send(ahead, lambda i: i - 1)
    history = call(
        history_kernel,
        f32(6, depth, own),
        (base, *in_hbm(past_dual_gap, past_velocity_gap)),
        loose=3,
        scratch=[pltpu.SemaphoreType.DMA((2,))],
    )
    far_ones = list(range(blocks - 2, 2, -2))
    lengths = [max(INDEX + 4, ROWS - place) for place in range(len(far_ones))]
    messages = call(
        functools.partial(message_kernel, own * blocks, depth),
        tuple(f32(rows, own) for rows in sorted(set(lengths), reverse=True)),
        (history, ahead, base),
        loose=1,
    )
    wide = call(wide_kernel, f32(ROWS + 9 * depth, own), (messages[0], history, ahead))
    pieces = {0: wide}
    for bits, rows in zip(far_ones, lengths):
        pieces[bits] = swap(next(value for value in messages if value.shape[0] == rows), bits)
    pieces[2] = swap(wide, 2)
    for even in (0, 2):
        pieces[even + 1] = swap(pieces[even], 1)
    count = len(far_ones)
    crossed = swap(
        call(stack_kernel, f32(count * ROWS, own), tuple(pieces[bits] for bits in far_ones)), 1
    )
    histories, slots = [pieces[block] for block in range(4)], [(block,) for block in range(4)]
    history = call(
        pair_kernel, f32(2, 9 * depth, own), (*(pieces[bits] for bits in far_ones), wide, pieces[2]), loose=len(far_ones)
    )
    known, apart, later = (0, 2), 4, []
    while apart < blocks:
        other = swap(history, apart)
        later.append((other, tuple(slot ^ apart for slot in known)))
        known += later[-1][1]
        apart *= 2
        if apart < blocks:
            history = call(join_kernel, f32(2 * history.shape[0], 9 * depth, own), (history, other))
    order = [(at * ROWS, bits + 1) for at, bits in enumerate(far_ones)]
    order += [(0, block) for block in reversed(range(blocks)) if block in pieces]
    sector = f32(3, blocks, own)
    work = [
        pltpu.VMEM((6, blocks, own), jnp.float32),
        pltpu.VMEM((3 * SPLITS, 4, blocks, own), jnp.float32),
        pltpu.VMEM((3, 4, blocks, own), jnp.float32),
        pltpu.VMEM((blocks * 16 * -(-3 * SPLITS * (halves + 2) // 16), LANES), jnp.float32),
    ]
    state, index, to_near, to_far = call(
        functools.partial(first_kernel, blocks, order),
        (f32(KEPT, blocks, own), jax.ShapeDtypeStruct((4, blocks, own), jnp.int32), sector, sector),
        (*([crossed] * count), *(pieces[block] for _, block in order[count:])),
        scratch=[pltpu.VMEM((halves, blocks * ROWS, LANES), jnp.float32), *work],
    )
    from_far = send(to_far, lambda i: i + 1 if i % 2 else i - 1)
    from_near = send(to_near, lambda i: i ^ 1)
    for other, far in later:
        held_back = call(copy_kernel, f32(*other.shape), (from_near, from_far, other), loose=2)
        histories += [other, swap(held_back, 1)]
        slots += [far, tuple(slot ^ 1 for slot in far)]
    vectors, keep = call(
        second_kernel,
        (f32(6, blocks, own), f32(9, blocks, own)),
        (state, index, to_near, to_far, from_far, from_near),
        scratch=work,
    )
    count = -(-len(pairs(depth)) // 8) * 8
    message = call(
        functools.partial(gram_kernel, depth, tuple(slots)),
        f32(7, blocks, own),
        (vectors, keep, *histories),
        scratch=[
            pltpu.VMEM((halves, blocks * 9 * depth, LANES), jnp.float32),
            pltpu.VMEM((count, LANES), jnp.float32),
        ],
    )
    square = sectors == 4
    parts = [message] + [None] * (sectors - 1)
    for by in sorted(range(1, sectors), reverse=True):
        parts[by] = send(message, (lambda i: i ^ by) if square else (lambda i: i - by))
    return call(
        functools.partial(solve_kernel, depth, square),
        (f32(3, own), f32(3, own)),
        (*parts, keep, past_dual, past_dual_gap, past_velocity, past_velocity_gap),
        scratch=[pltpu.VMEM((count, LANES), jnp.float32)],
    )


def solution(mesh):
    in_specs = (
        P(None, ("sector", "dom")),
        P(None, ("sector", "dom")),
        P(("sector", "dom")),
        P("sector", None),
        P(None, ("sector", "dom")),
        P(None, ("sector", "dom")),
        P(None, ("sector", "dom")),
        P(("sector", "dom")),
        P(None, None, ("sector", "dom")),
        P(None, None, ("sector", "dom")),
        P(None, None, ("sector", "dom")),
        P(None, None, ("sector", "dom")),
    )
    out_specs = (P(None, ("sector", "dom")), P(None, ("sector", "dom")))
    return jax.shard_map(
        per_device, mesh=mesh, in_specs=in_specs, out_specs=out_specs, check_vma=False
    )
```

```python
import functools
import itertools

import jax
import jax.numpy as jnp
from jax import lax
from jax.experimental import pallas as pl
from jax.experimental.pallas import tpu as pltpu
from jax.sharding import PartitionSpec as P

LANES = 128
VMEM_LIMIT = 24 * 1024 * 1024

STRAIN, DUAL, STEP, SPEED, LOAD, NEXT_STEP, NEXT_SPEED, INDEX, ROWS = 0, 36, 39, 40, 43, 46, 47, 50, 56
KEPT_NEXT_STEP, KEPT_LOAD, KEPT = 40, 41, 44
SPLITS = 2


def vmem():
    return pl.BlockSpec(memory_space=pltpu.VMEM)


def smem():
    return pl.BlockSpec(memory_space=pltpu.SMEM)


def call(kernel, outs, args, scalars=0, loose=0, scratch=()):
    return pl.pallas_call(
        kernel,
        out_shape=outs,
        in_specs=[smem()] * scalars
        + [pl.BlockSpec(memory_space=pl.ANY)] * loose
        + [vmem()] * (len(args) - scalars - loose),
        out_specs=jax.tree.map(lambda _: vmem(), outs),
        scratch_shapes=list(scratch),
        compiler_params=pltpu.CompilerParams(vmem_limit_bytes=VMEM_LIMIT),
    )(*args)


def f32(*shape):
    return jax.ShapeDtypeStruct(shape, jnp.float32)


def repeat(blocks, body, init):
    if blocks == 8:
        return body(slice(0, 8), 0, init)
    return lax.fori_loop(
        0, blocks // 8, lambda step, carry: body(pl.ds(pl.multiple_of(8 * step, 8), 8), 8 * step, carry), init
    )


def one_row(ref, lead, group, first, row, lanes=slice(None)):
    if isinstance(first, int):
        return ref[(*lead, slice(first + row, first + row + 1), lanes)]
    return ref[(*lead, group, lanes)][row : row + 1]


def project_cone(trial):
    center = 0.5 * (trial[0] + trial[1])
    spread = 0.5 * (trial[0] - trial[1])
    shear = trial[2]
    radius = jnp.sqrt(spread * spread + shear * shear)
    upper = center + radius
    lower = center - radius
    iso_part = 0.5 * (jnp.maximum(upper, 0.0) + jnp.maximum(lower, 0.0))
    factor = jnp.clip((center + radius) / (2.0 * jnp.maximum(radius, 0.05)), 0.0, 1.0)
    return (iso_part + factor * spread, iso_part - factor * spread, factor * shear)


def fetch(pairs, sems):
    copies = [pltpu.make_async_copy(source, target, sems.at[at]) for at, (source, target) in enumerate(pairs)]
    for copy in copies:
        copy.start()
    for copy in copies:
        copy.wait()


def in_hbm(*values):
    return tuple(pltpu.with_memory_space_constraint(value, pltpu.HBM) for value in values)


def nodes_kernel(speed_in, mobility_in, seam_in, gap_u, ahead, speed, mobility, seam, sems):
    depth = gap_u.shape[1]
    start = ahead.shape[0] - 3 * depth
    gaps = [(gap_u.at[c], ahead.at[pl.ds(start + depth * c, depth)]) for c in range(3)]
    fetch(((speed_in, speed), (mobility_in, mobility), (seam_in, seam), *gaps), sems)
    own = speed.shape[1]
    ahead[0:3, :] = speed[...]
    ahead[3:4, :] = mobility[...]
    ahead[4:8, :] = jnp.zeros((4, own), jnp.float32)
    for row in range(8, start):
        ahead[row : row + 1, :] = seam[:, (row - 8) * own : (row - 7) * own].astype(jnp.float32)


def base_kernel(counts, after, *refs):
    count = (len(refs) - 2) // 2
    sources, base, held, sems = refs[:count], refs[count], refs[count + 1 : -1], refs[-1]
    fetch(zip(sources, held), sems)
    strain, dual, speed, load, mobility, corners = held
    own = speed.shape[1]
    slot = lax.broadcasted_iota(jnp.int32, (1, own), 1)
    alive = (slot < counts[0]).astype(jnp.float32)
    base[STRAIN:DUAL, :] = strain[...] * alive
    base[DUAL : DUAL + 3, :] = dual[...] * alive
    base[STEP : STEP + 1, :] = mobility[...]
    base[SPEED : SPEED + 3, :] = speed[...]
    base[LOAD : LOAD + 3, :] = load[...]
    base[NEXT_STEP:INDEX, :] = jnp.zeros((INDEX - NEXT_STEP, own), jnp.float32)
    base[INDEX : INDEX + 4, :] = corners[...].astype(jnp.float32)


def message_kernel(sector_nodes, depth, after, ahead, base, message, *shorter):
    own = message.shape[1]
    halves = own // LANES
    message[:NEXT_STEP, :] = base[:NEXT_STEP, :]
    message[NEXT_STEP : NEXT_STEP + 1, :] = ahead[3:4, :]
    message[NEXT_SPEED : NEXT_SPEED + 3, :] = ahead[0:3, :]
    message[INDEX + 4 :, :] = jnp.zeros((ROWS - INDEX - 4, own), jnp.float32)
    corners = base[INDEX : INDEX + 4, :].astype(jnp.int32)
    corner = jnp.concatenate([corners[:, h * LANES : (h + 1) * LANES] for h in range(halves)], axis=0)
    seam_rows = ahead.shape[0] - 8 - 3 * depth
    place = jnp.clip(corner - sector_nodes, 0, seam_rows * own - 1)
    high, low = place // LANES, place % LANES
    found = jnp.zeros(corner.shape, jnp.float32)
    for row in range(seam_rows):
        for h in range(halves):
            table = jnp.broadcast_to(ahead[8 + row : 9 + row, h * LANES : (h + 1) * LANES], corner.shape)
            value = jnp.take_along_axis(table, low, axis=1, mode="promise_in_bounds")
            found = jnp.where(high == row * halves + h, value, found)
    node = jnp.where(corner < sector_nodes, corner.astype(jnp.float32), found + float(sector_nodes))
    for h in range(halves):
        message[INDEX : INDEX + 4, h * LANES : (h + 1) * LANES] = node[4 * h : 4 * h + 4]
    for other in shorter:
        other[...] = message[: other.shape[0], :]


def history_kernel(after, gap_w, gap_u, history, sems):
    fetch(((gap_w, history.at[0:3]), (gap_u, history.at[3:6])), sems)


def wide_kernel(message, gaps, ahead, wide):
    depth = gaps.shape[1]
    start = ahead.shape[0] - 3 * depth
    wide[:ROWS, :] = message[...]
    for kind in range(6):
        wide[ROWS + depth * kind : ROWS + depth * (kind + 1), :] = gaps[kind]
    wide[ROWS + 6 * depth :, :] = ahead[start:, :]


def stack_kernel(*refs):
    stacked = refs[-1]
    for at, piece in enumerate(refs[:-1]):
        stacked[at * ROWS : at * ROWS + piece.shape[0], :] = piece[...]
        if piece.shape[0] < ROWS:
            start = at * ROWS + piece.shape[0]
            stacked[start : (at + 1) * ROWS, :] = jnp.zeros(((at + 1) * ROWS - start, piece.shape[1]), jnp.float32)


def pair_kernel(*refs):
    left, right, joined = refs[-3:]
    joined[0] = left[ROWS:, :]
    joined[1] = right[ROWS:, :]


def copy_kernel(*refs):
    value, copied = refs[-2:]
    copied[...] = value[...]


def join_kernel(*refs):
    left, right, joined = refs[-3:]
    count = left.shape[0]
    joined[:count] = left[...]
    joined[count:] = right[...]


def sweep(strain_row, index, codes, spreads, work, dual, fresh):
    table, terms, nearby = work
    blocks, own = index.shape[1:]
    halves = own // LANES
    here = lax.axis_index("dom")
    row = lax.broadcasted_iota(jnp.int32, (blocks, LANES), 0)
    left_block = ((row ^ here) - 1) ^ here
    right_block = ((row ^ here) + 1) ^ here

    def wide(j, group, first, block, part):
        piece = one_row(table, (j,), group, first, block, slice(part * LANES, (part + 1) * LANES))
        return jnp.broadcast_to(piece, (blocks, LANES))

    def take_sides(group, first, sides):
        left, right = (list(side) for side in sides)
        for block in range(8):
            for j in range(3):
                left[j] = jnp.where(left_block == first + block, wide(j, group, first, block, halves - 1), left[j])
                right[j] = jnp.where(right_block == first + block, wide(j, group, first, block, 0), right[j])
        return tuple(left), tuple(right)

    blank = tuple(jnp.zeros((blocks, LANES), jnp.float32) for _ in range(3))
    left, right = repeat(blocks, take_sides, (blank, blank))
    speed = []
    for k in range(4):
        parts = []
        for h in range(halves):
            number = index[k, :, h * LANES : (h + 1) * LANES]
            high, low = number // LANES, number % LANES

            def take(value):
                return jnp.take_along_axis(value, low, axis=1, mode="promise_in_bounds")

            found = [take(table[j, :, 0:LANES]) for j in range(3)]
            for part in range(1, halves):
                mask = high % halves == part
                found = [
                    jnp.where(mask, take(table[j, :, part * LANES : (part + 1) * LANES]), found[j]) for j in range(3)
                ]
            mask = number // own == left_block
            found = [jnp.where(mask, take(left[j]), found[j]) for j in range(3)]
            mask = number // own == right_block
            found = [jnp.where(mask, take(right[j]), found[j]) for j in range(3)]

            def take_group(group, first, found):
                for part, block in itertools.product(range(halves), range(8)):
                    mask = high == (blocks + first + block) * halves + part
                    found = [jnp.where(mask, take(wide(3 + j, group, first, block, part)), found[j]) for j in range(3)]
                return tuple(found)

            parts.append(repeat(blocks, take_group, tuple(found)))
        speed.append([jnp.concatenate([found[j] for found in parts], axis=1) for j in range(3)])
    rate = []
    for c in range(3):
        total = None
        for k in range(4):
            for j in range(3):
                term = strain_row(12 * c + 3 * k + j) * speed[k][j]
                total = term if total is None else total + term
        rate.append(total)
    trial = [rate[c] + dual[c] for c in range(3)]
    cone = project_cone(trial)
    dual_next = [trial[c] - cone[c] for c in range(3)]
    misfit = [rate[c] - cone[c] + dual_next[c] for c in range(3)]
    for k in range(4):
        for j in range(3):
            rest = sum(strain_row(12 * c + 3 * k + j) * misfit[c] for c in range(3))
            for split in range(SPLITS):
                term = rest.astype(jnp.bfloat16).astype(jnp.float32)
                terms[SPLITS * j + split, k] = term
                rest = rest - term

    near_rows = halves + 2
    next_rows = halves * blocks
    row_wide = lax.broadcasted_iota(jnp.int32, (blocks, own), 0) ^ here
    for k in range(4) if fresh else ():
        number = index[k]
        block_of, half = number // own, number // LANES % halves
        near = jnp.where(block_of == ((row_wide - 1) ^ here), 0, 1 + half)
        near = jnp.where(block_of == ((row_wide + 1) ^ here), 1 + halves, near)
        codes[0, k] = (number % LANES).astype(jnp.float32)
        codes[1, k] = jnp.where(block_of < blocks, near, -1).astype(jnp.float32)
        codes[2, k] = jnp.where(block_of < blocks, -1, half * blocks + block_of - blocks).astype(jnp.float32)

    values = 3 * SPLITS
    per_tile = 16 // near_rows
    near_tiles = -(-values // per_tile)
    iota = lax.broadcasted_iota(jnp.int32, (16, own), 0)
    near_iota = (iota % near_rows).astype(jnp.float32).astype(jnp.bfloat16)
    value_iota = (iota // near_rows).astype(jnp.float32).astype(jnp.bfloat16)
    value_masks = [value_iota == jnp.full((16, own), float(at), jnp.bfloat16) for at in range(per_tile)]
    iota = iota.astype(jnp.float32)
    low_iota = [(iota + float(16 * g)).astype(jnp.bfloat16) for g in range(LANES // 16)]
    next_iota = [(iota + float(16 * g)).astype(jnp.bfloat16) for g in range(next_rows // 16)]
    one = jnp.ones((16, own), jnp.bfloat16)
    zero = jnp.zeros((16, own), jnp.bfloat16)

    def spread_row(value):
        return jnp.broadcast_to(value, (16, own)).astype(jnp.bfloat16)

    def add_group(group, first, total):
        for block in range(8):
            part = None
            for k in range(4):
                near_row, next_row = (spread_row(one_row(codes, (at, k), group, first, block)) for at in (1, 2))
                rows = [spread_row(one_row(terms, (at, k), group, first, block)) for at in range(values)]
                start = ((first + block) * 4 + k) * LANES
                if not isinstance(start, int):
                    start = pl.multiple_of(start, LANES)
                if fresh:
                    low_row = spread_row(one_row(codes, (0, k), group, first, block))
                    spread = jnp.concatenate([jnp.where(low_row == value, one, zero) for value in low_iota], axis=0)
                    spreads[pl.ds(start, LANES), :] = spread
                else:
                    spread = spreads[pl.ds(start, LANES), :]
                mask = near_row == near_iota
                weights = []
                for tile in range(near_tiles):
                    inside = rows[tile * per_tile : (tile + 1) * per_tile]
                    value = inside[-1]
                    for at in range(len(inside) - 1):
                        value = jnp.where(value_masks[at], inside[at], value)
                    weights.append(jnp.where(mask, value, zero))
                masks = [next_row == value for value in next_iota]
                weights += [jnp.where(mask, row, zero) for row in rows for mask in masks]
                product = lax.dot_general(
                    jnp.concatenate(weights, axis=0),
                    spread,
                    (((1,), (1,)), ((), ())),
                    preferred_element_type=jnp.float32,
                )
                part = product if part is None else part + product
            start = (first + block) * 16 * near_tiles
            if not isinstance(start, int):
                start = pl.multiple_of(start, 16)
            nearby[pl.ds(start, 16 * near_tiles), :] = part[: 16 * near_tiles]
            total += part[16 * near_tiles :]
        return total

    total = repeat(blocks, add_group, jnp.zeros((values * next_rows, LANES), jnp.float32))

    def near_force(j, row):
        return sum(
            nearby[pl.ds((SPLITS * j + split) * near_rows + row, blocks, stride=16 * near_tiles), :]
            for split in range(SPLITS)
        )

    force_own, force_next = [], []
    for j in range(3):
        halves_own = [near_force(j, 1 + h) for h in range(halves)]
        to_left, to_right = near_force(j, 0), near_force(j, 1 + halves)
        from_right = from_left = jnp.zeros((blocks, LANES), jnp.float32)
        for block in range(blocks):
            wide_left = jnp.broadcast_to(to_left[block : block + 1], (blocks, LANES))
            wide_right = jnp.broadcast_to(to_right[block : block + 1], (blocks, LANES))
            from_right = jnp.where(right_block == block, wide_left, from_right)
            from_left = jnp.where(left_block == block, wide_right, from_left)
        halves_own[-1] = halves_own[-1] + from_right
        halves_own[0] = halves_own[0] + from_left
        force_own.append(jnp.concatenate(halves_own, axis=1))
        whole = sum(
            total[(SPLITS * j + split) * next_rows : (SPLITS * j + split + 1) * next_rows] for split in range(SPLITS)
        )
        force_next.append(jnp.concatenate([whole[h * blocks : (h + 1) * blocks] for h in range(halves)], axis=1))
    return dual_next, force_own, force_next


def stack_block(piece, slot, rows, stack):
    held = min(rows, piece.shape[0])
    for h in range(stack.shape[0]):
        stack[h, slot * rows : slot * rows + held, :] = piece[:held, h * LANES : (h + 1) * LANES]


def across(stack, row, rows):
    blocks = stack.shape[1] // rows
    return jnp.concatenate(
        [stack[h, pl.ds(row, blocks, stride=rows), :] for h in range(stack.shape[0])], axis=1
    )


def first_kernel(blocks, order, *refs):
    pieces = refs[: len(order)]
    state, index, codes, spreads, to_near, to_far, stack = refs[blocks : blocks + 7]
    work = refs[blocks + 7 :]
    table = work[0]
    own = index.shape[2]
    for piece, (start, slot) in zip(pieces, order):
        stack_block(piece.at[start : min(start + ROWS, piece.shape[0])], slot, ROWS, stack)
    flip = lax.axis_index("dom") * own
    even = lax.axis_index("sector") % 2 == 0
    for k in range(4):
        index[k] = across(stack, INDEX + k, ROWS).astype(jnp.int32) ^ flip
    for row in range(36):
        state[row] = across(stack, STRAIN + row, ROWS)
    step = across(stack, STEP, ROWS)
    state[STEP] = step
    state[KEPT_NEXT_STEP] = across(stack, NEXT_STEP, ROWS)
    for j in range(3):
        state[KEPT_LOAD + j] = across(stack, LOAD + j, ROWS)
        table[j] = across(stack, SPEED + j, ROWS)
        table[3 + j] = across(stack, NEXT_SPEED + j, ROWS)
    dual = [across(stack, DUAL + c, ROWS) for c in range(3)]
    dual, force_own, force_next = sweep(lambda row: state[row], index, codes, spreads, work, dual, True)
    for c in range(3):
        state[DUAL + c] = dual[c]
        mine = table[c] - step * (force_own[c] - state[KEPT_LOAD + c])
        to_near[c] = jnp.where(even, force_next[c], mine)
        to_far[c] = jnp.where(even, mine, force_next[c])


def second_kernel(state, index, codes, spreads, to_near, to_far, from_far, from_near, vectors, keep, *work):
    table = work[0]
    even = lax.axis_index("sector") % 2 == 0
    step, next_step = state[STEP], state[KEPT_NEXT_STEP]
    for j in range(3):
        near, far = to_near[j], to_far[j]
        near_in, far_in = from_near[j], from_far[j]
        table[j] = jnp.where(even, far, near) - step * jnp.where(even, far_in, near_in)
        table[3 + j] = jnp.where(even, near_in, far_in) - next_step * jnp.where(even, near, far)
    dual = [state[DUAL + c] for c in range(3)]
    dual_next, force_own, force_next = sweep(lambda row: state[row], index, codes, spreads, work, dual, False)
    for c in range(3):
        after = table[c] - step * (force_own[c] - state[KEPT_LOAD + c])
        vectors[c] = after - table[c]
        vectors[3 + c] = -(next_step * force_next[c])
        keep[c] = dual_next[c]
        keep[3 + c] = dual_next[c] - dual[c]
        keep[6 + c] = after


def pairs(depth):
    return [(i, l) for i in range(depth) for l in range(i, depth + 1)]


def gram_kernel(depth, slots, vectors, keep, *refs):
    blocks, own = keep.shape[1:]
    halves = own // LANES
    rows = 9 * depth
    message, stack, rows_sum = refs[len(slots) :]
    for piece, own_slots in zip(refs, slots):
        for at, slot in enumerate(own_slots):
            stack_block(piece.at[at] if len(piece.shape) == 3 else piece.at[ROWS:], slot, rows, stack)
    for row in range(6):
        message[row] = vectors[row]
    message[6] = jnp.zeros((blocks, own), jnp.float32)
    sums, pushed, pushed_twice = {}, [0.0] * (depth + 1), 0.0
    for c, h, top in itertools.product(range(3), range(halves), range(0, blocks, 8)):
        lanes, group = slice(h * LANES, (h + 1) * LANES), slice(top, top + 8)

        def gap(kind, i):
            return stack[h, pl.ds(top * rows + depth * (3 * kind + c) + i, 8, stride=rows), :]

        for kind, moved in enumerate((keep[3 + c, group, lanes], vectors[c, group, lanes])):
            gaps = [moved - gap(kind, i) for i in range(depth)] + [moved]
            for i, l in pairs(depth):
                term = gaps[i] * gaps[l]
                sums[i, l] = sums[i, l] + term if (i, l) in sums else term
        push = vectors[3 + c, group, lanes]
        for i in range(depth):
            pushed[i] = pushed[i] + gap(2, i) * push
        pushed_twice = pushed_twice + push * push
    for at, (i, l) in enumerate(pairs(depth)):
        value = sums[i, l] + pushed_twice - pushed[i] - pushed[l]
        rows_sum[at : at + 1, :] = jnp.sum(value, axis=0, keepdims=True)
    count = len(pairs(depth))
    if rows_sum.shape[0] > count:
        rows_sum[count:, :] = jnp.zeros((rows_sum.shape[0] - count, LANES), jnp.float32)
    whole = jnp.broadcast_to(jnp.sum(rows_sum[...], axis=1, keepdims=True), rows_sum.shape)
    lane = lax.broadcasted_iota(jnp.int32, (8, LANES), 1)
    out = whole[0:8]
    for group in range(1, rows_sum.shape[0] // 8):
        out = jnp.where(lane == group, whole[8 * group : 8 * group + 8], out)
    message[6, 0:8, 0:LANES] = out


def solve_kernel(depth, square, *refs):
    parts = refs[:-8]
    keep, past_w, gap_w, past_u, gap_u, new_u, new_w, total = refs[-8:]
    own = new_u.shape[1]
    tile = parts[0][6, 0:8, 0:LANES]
    for other in parts[1:]:
        tile = tile + other[6, 0:8, 0:LANES]
    even = lax.axis_index("sector") % 2 == 0

    def ahead(by, row):
        if square and by in (1, 3):
            return jnp.where(even, parts[by][row], parts[4 - by][row])
        return parts[by][row]

    sectors = len(parts)
    pushes = [[ahead(by, 3 + j) for j in range(3)] for by in range(sectors)]
    cross = sum(ahead(by, j) * pushes[by - 1][j] for by in range(sectors) for j in range(3))
    cross = jnp.sum(jnp.sum(cross, axis=0, keepdims=True), axis=1, keepdims=True)
    last = [keep[6 + j, 0:1] + pushes[-1][j][0:1] for j in range(3)] + [keep[c, 0:1] for c in range(3)]
    for group in range(total.shape[0] // 8):
        total[8 * group : 8 * group + 8, :] = jnp.broadcast_to(tile[:, group : group + 1], (8, LANES))
    matrix = {
        pair: jnp.broadcast_to(total[at : at + 1, :], (depth, LANES)) + 2.0 * cross
        for at, pair in enumerate(pairs(depth))
    }
    ridge = 0.0001 * sum(matrix[i, i] for i in range(depth)) / depth
    for i in range(depth):
        matrix[i, i] = matrix[i, i] + ridge
    inverse = []
    for step in range(depth):
        inverse.append(1.0 / matrix[step, step])
        for i in range(step + 1, depth):
            factor = matrix[step, i] * inverse[step]
            for l in range(i, depth + 1):
                matrix[i, l] = matrix[i, l] - factor * matrix[step, l]
    weights = [None] * depth
    for i in reversed(range(depth)):
        value = matrix[i, depth]
        for l in range(i + 1, depth):
            value = value - matrix[i, l] * weights[l]
        weights[i] = value * inverse[i]
    row = lax.broadcasted_iota(jnp.int32, (depth, LANES), 0)
    weight = weights[0]
    for i in range(1, depth):
        weight = jnp.where(row == i, weights[i], weight)
    for start in range(0, own, LANES):
        lanes = slice(start, start + LANES)
        for at, (past, gap, out) in enumerate(((past_u, gap_u, new_u), (past_w, gap_w, new_w))):
            for c in range(3):
                value = jnp.broadcast_to(last[3 * at + c][:, lanes], (depth, LANES))
                change = weight * (value - past[c, :, lanes] - gap[c, :, lanes])
                out[c : c + 1, lanes] = value[0:1] - jnp.sum(change, axis=0, keepdims=True)


def per_device(
    strain_map,
    corner_nodes,
    counts,
    seam_nodes,
    velocity,
    dual_state,
    nodal_load,
    mobility,
    past_dual,
    past_dual_gap,
    past_velocity,
    past_velocity_gap,
):
    own = velocity.shape[1]
    halves = own // LANES
    blocks = lax.axis_size("dom")
    sectors = lax.axis_size("sector")
    depth = past_dual.shape[0]
    seam_rows = seam_nodes.shape[1] // own
    mobility = mobility.reshape(1, own)
    past_dual, past_dual_gap, past_velocity, past_velocity_gap = (
        value.transpose(1, 0, 2) for value in (past_dual, past_dual_gap, past_velocity, past_velocity_gap)
    )

    def send(value, target):
        return lax.ppermute(value, "sector", [(i, target(i) % sectors) for i in range(sectors)])

    def swap(value, bits):
        return lax.ppermute(value, "dom", [(i, i ^ bits) for i in range(blocks)])

    nodes = (velocity, mobility, seam_nodes)
    ahead = call(
        nodes_kernel,
        f32(8 + seam_rows + 3 * depth, own),
        in_hbm(*nodes, past_velocity_gap),
        loose=len(nodes) + 1,
        scratch=[pltpu.VMEM(value.shape, value.dtype) for value in nodes]
        + [pltpu.SemaphoreType.DMA((len(nodes) + 3,))],
    )
    held = (strain_map, dual_state, velocity, nodal_load, mobility, corner_nodes)
    base = call(
        base_kernel,
        f32(INDEX + 4, own),
        (counts, ahead, *in_hbm(*held)),
        scalars=1,
        loose=len(held) + 1,
        scratch=[pltpu.VMEM(value.shape, value.dtype) for value in held] + [pltpu.SemaphoreType.DMA((len(held),))],
    )
    ahead = send(ahead, lambda i: i - 1)
    history = call(
        history_kernel,
        f32(6, depth, own),
        (base, *in_hbm(past_dual_gap, past_velocity_gap)),
        loose=3,
        scratch=[pltpu.SemaphoreType.DMA((2,))],
    )
    far_ones = list(range(blocks - 2, 2, -2))
    lengths = [max(INDEX + 4, ROWS - place) for place in range(len(far_ones))]
    messages = call(
        functools.partial(message_kernel, own * blocks, depth),
        tuple(f32(rows, own) for rows in sorted(set(lengths), reverse=True)),
        (history, ahead, base),
        loose=1,
    )
    wide = call(wide_kernel, f32(ROWS + 9 * depth, own), (messages[0], history, ahead))
    pieces = {0: wide}
    for bits, rows in zip(far_ones, lengths):
        pieces[bits] = swap(next(value for value in messages if value.shape[0] == rows), bits)
    pieces[2] = swap(wide, 2)
    for even in (0, 2):
        pieces[even + 1] = swap(pieces[even], 1)
    count = len(far_ones)
    crossed = swap(
        call(stack_kernel, f32(count * ROWS, own), tuple(pieces[bits] for bits in far_ones)), 1
    )
    histories, slots = [pieces[block] for block in range(4)], [(block,) for block in range(4)]
    history = call(
        pair_kernel, f32(2, 9 * depth, own), (*(pieces[bits] for bits in far_ones), wide, pieces[2]), loose=len(far_ones)
    )
    known, apart, later = (0, 2), 4, []
    while apart < blocks:
        other = swap(history, apart)
        later.append((other, tuple(slot ^ apart for slot in known)))
        known += later[-1][1]
        apart *= 2
        if apart < blocks:
            history = call(join_kernel, f32(2 * history.shape[0], 9 * depth, own), (history, other))
    order = [(at * ROWS, bits + 1) for at, bits in enumerate(far_ones)]
    order += [(0, block) for block in reversed(range(blocks)) if block in pieces]
    sector = f32(3, blocks, own)
    work = [
        pltpu.VMEM((6, blocks, own), jnp.float32),
        pltpu.VMEM((3 * SPLITS, 4, blocks, own), jnp.float32),
        pltpu.VMEM((blocks * 16 * -(-3 * SPLITS * (halves + 2) // 16), LANES), jnp.float32),
    ]
    state, index, codes, spreads, to_near, to_far = call(
        functools.partial(first_kernel, blocks, order),
        (
            f32(KEPT, blocks, own),
            jax.ShapeDtypeStruct((4, blocks, own), jnp.int32),
            f32(3, 4, blocks, own),
            jax.ShapeDtypeStruct((4 * blocks * LANES, own), jnp.bfloat16),
            sector,
            sector,
        ),
        (*([crossed] * count), *(pieces[block] for _, block in order[count:])),
        scratch=[pltpu.VMEM((halves, blocks * ROWS, LANES), jnp.float32), *work],
    )
    from_far = send(to_far, lambda i: i + 1 if i % 2 else i - 1)
    from_near = send(to_near, lambda i: i ^ 1)
    for other, far in later:
        held_back = call(copy_kernel, f32(*other.shape), (from_near, from_far, other), loose=2)
        histories += [other, swap(held_back, 1)]
        slots += [far, tuple(slot ^ 1 for slot in far)]
    vectors, keep = call(
        second_kernel,
        (f32(6, blocks, own), f32(9, blocks, own)),
        (state, index, codes, spreads, to_near, to_far, from_far, from_near),
        scratch=work,
    )
    count = -(-len(pairs(depth)) // 8) * 8
    message = call(
        functools.partial(gram_kernel, depth, tuple(slots)),
        f32(7, blocks, own),
        (vectors, keep, *histories),
        scratch=[
            pltpu.VMEM((halves, blocks * 9 * depth, LANES), jnp.float32),
            pltpu.VMEM((count, LANES), jnp.float32),
        ],
    )
    square = sectors == 4
    parts = [message] + [None] * (sectors - 1)
    for by in sorted(range(1, sectors), reverse=True):
        parts[by] = send(message, (lambda i: i ^ by) if square else (lambda i: i - by))
    return call(
        functools.partial(solve_kernel, depth, square),
        (f32(3, own), f32(3, own)),
        (*parts, keep, past_dual, past_dual_gap, past_velocity, past_velocity_gap),
        scratch=[pltpu.VMEM((count, LANES), jnp.float32)],
    )


def solution(mesh):
    in_specs = (
        P(None, ("sector", "dom")),
        P(None, ("sector", "dom")),
        P(("sector", "dom")),
        P("sector", None),
        P(None, ("sector", "dom")),
        P(None, ("sector", "dom")),
        P(None, ("sector", "dom")),
        P(("sector", "dom")),
        P(None, None, ("sector", "dom")),
        P(None, None, ("sector", "dom")),
        P(None, None, ("sector", "dom")),
        P(None, None, ("sector", "dom")),
    )
    out_specs = (P(None, ("sector", "dom")), P(None, ("sector", "dom")))
    return jax.shard_map(
        per_device, mesh=mesh, in_specs=in_specs, out_specs=out_specs, check_vma=False
    )
```

```python
import functools
import itertools

import jax
import jax.numpy as jnp
from jax import lax
from jax.experimental import pallas as pl
from jax.experimental.pallas import tpu as pltpu
from jax.sharding import PartitionSpec as P

LANES = 128
VMEM_LIMIT = 24 * 1024 * 1024

STRAIN, DUAL, STEP, SPEED, LOAD, NEXT_STEP, NEXT_SPEED, INDEX, ROWS = 0, 36, 39, 40, 43, 46, 47, 50, 56
KEPT_NEXT_STEP, KEPT_LOAD, KEPT = 40, 41, 44
SPLITS = 2


def vmem():
    return pl.BlockSpec(memory_space=pltpu.VMEM)


def smem():
    return pl.BlockSpec(memory_space=pltpu.SMEM)


def call(kernel, outs, args, scalars=0, loose=0, scratch=()):
    return pl.pallas_call(
        kernel,
        out_shape=outs,
        in_specs=[smem()] * scalars
        + [pl.BlockSpec(memory_space=pl.ANY)] * loose
        + [vmem()] * (len(args) - scalars - loose),
        out_specs=jax.tree.map(lambda _: vmem(), outs),
        scratch_shapes=list(scratch),
        compiler_params=pltpu.CompilerParams(vmem_limit_bytes=VMEM_LIMIT),
    )(*args)


def f32(*shape):
    return jax.ShapeDtypeStruct(shape, jnp.float32)


def repeat(blocks, body, init):
    if blocks == 8:
        return body(slice(0, 8), 0, init)
    return lax.fori_loop(
        0, blocks // 8, lambda step, carry: body(pl.ds(pl.multiple_of(8 * step, 8), 8), 8 * step, carry), init
    )


def one_row(ref, lead, group, first, row, lanes=slice(None)):
    if isinstance(first, int):
        return ref[(*lead, slice(first + row, first + row + 1), lanes)]
    return ref[(*lead, group, lanes)][row : row + 1]


def project_cone(trial):
    center = 0.5 * (trial[0] + trial[1])
    spread = 0.5 * (trial[0] - trial[1])
    shear = trial[2]
    radius = jnp.sqrt(spread * spread + shear * shear)
    upper = center + radius
    lower = center - radius
    iso_part = 0.5 * (jnp.maximum(upper, 0.0) + jnp.maximum(lower, 0.0))
    factor = jnp.clip((center + radius) / (2.0 * jnp.maximum(radius, 0.05)), 0.0, 1.0)
    return (iso_part + factor * spread, iso_part - factor * spread, factor * shear)


def fetch(pairs, sems):
    copies = [pltpu.make_async_copy(source, target, sems.at[at]) for at, (source, target) in enumerate(pairs)]
    for copy in copies:
        copy.start()
    for copy in copies:
        copy.wait()


def in_hbm(*values):
    return tuple(pltpu.with_memory_space_constraint(value, pltpu.HBM) for value in values)


def nodes_kernel(speed_in, mobility_in, seam_in, gap_u, ahead, speed, mobility, seam, sems):
    depth = gap_u.shape[1]
    start = ahead.shape[0] - 3 * depth
    gaps = [(gap_u.at[c], ahead.at[pl.ds(start + depth * c, depth)]) for c in range(3)]
    fetch(((speed_in, speed), (mobility_in, mobility), (seam_in, seam), *gaps), sems)
    own = speed.shape[1]
    ahead[0:3, :] = speed[...]
    ahead[3:4, :] = mobility[...]
    ahead[4:8, :] = jnp.zeros((4, own), jnp.float32)
    for row in range(8, start):
        ahead[row : row + 1, :] = seam[:, (row - 8) * own : (row - 7) * own].astype(jnp.float32)


def base_kernel(counts, after, *refs):
    count = (len(refs) - 2) // 2
    sources, base, held, sems = refs[:count], refs[count], refs[count + 1 : -1], refs[-1]
    fetch(zip(sources, held), sems)
    strain, dual, speed, load, mobility, corners = held
    own = speed.shape[1]
    slot = lax.broadcasted_iota(jnp.int32, (1, own), 1)
    alive = (slot < counts[0]).astype(jnp.float32)
    base[STRAIN:DUAL, :] = strain[...] * alive
    base[DUAL : DUAL + 3, :] = dual[...] * alive
    base[STEP : STEP + 1, :] = mobility[...]
    base[SPEED : SPEED + 3, :] = speed[...]
    base[LOAD : LOAD + 3, :] = load[...]
    base[NEXT_STEP:INDEX, :] = jnp.zeros((INDEX - NEXT_STEP, own), jnp.float32)
    base[INDEX : INDEX + 4, :] = corners[...].astype(jnp.float32)


def message_kernel(sector_nodes, depth, after, ahead, base, message, *shorter):
    own = message.shape[1]
    halves = own // LANES
    message[:NEXT_STEP, :] = base[:NEXT_STEP, :]
    message[NEXT_STEP : NEXT_STEP + 1, :] = ahead[3:4, :]
    message[NEXT_SPEED : NEXT_SPEED + 3, :] = ahead[0:3, :]
    message[INDEX + 4 :, :] = jnp.zeros((ROWS - INDEX - 4, own), jnp.float32)
    corners = base[INDEX : INDEX + 4, :].astype(jnp.int32)
    corner = jnp.concatenate([corners[:, h * LANES : (h + 1) * LANES] for h in range(halves)], axis=0)
    seam_rows = ahead.shape[0] - 8 - 3 * depth
    place = jnp.clip(corner - sector_nodes, 0, seam_rows * own - 1)
    high, low = place // LANES, place % LANES
    found = jnp.zeros(corner.shape, jnp.float32)
    for row in range(seam_rows):
        for h in range(halves):
            table = jnp.broadcast_to(ahead[8 + row : 9 + row, h * LANES : (h + 1) * LANES], corner.shape)
            value = jnp.take_along_axis(table, low, axis=1, mode="promise_in_bounds")
            found = jnp.where(high == row * halves + h, value, found)
    node = jnp.where(corner < sector_nodes, corner.astype(jnp.float32), found + float(sector_nodes))
    for h in range(halves):
        message[INDEX : INDEX + 4, h * LANES : (h + 1) * LANES] = node[4 * h : 4 * h + 4]
    for other in shorter:
        other[...] = message[: other.shape[0], :]


def history_kernel(after, gap_w, gap_u, history, sems):
    fetch(((gap_w, history.at[0:3]), (gap_u, history.at[3:6])), sems)


def wide_kernel(message, gaps, ahead, wide):
    depth = gaps.shape[1]
    start = ahead.shape[0] - 3 * depth
    wide[:ROWS, :] = message[...]
    for kind in range(6):
        wide[ROWS + depth * kind : ROWS + depth * (kind + 1), :] = gaps[kind]
    wide[ROWS + 6 * depth :, :] = ahead[start:, :]


def stack_kernel(*refs):
    stacked = refs[-1]
    for at, piece in enumerate(refs[:-1]):
        stacked[at * ROWS : at * ROWS + piece.shape[0], :] = piece[...]
        if piece.shape[0] < ROWS:
            start = at * ROWS + piece.shape[0]
            stacked[start : (at + 1) * ROWS, :] = jnp.zeros(((at + 1) * ROWS - start, piece.shape[1]), jnp.float32)


def pair_kernel(*refs):
    left, right, joined = refs[-3:]
    joined[0] = left[ROWS:, :]
    joined[1] = right[ROWS:, :]


def copy_kernel(*refs):
    value, copied = refs[-2:]
    copied[...] = value[...]


def join_kernel(*refs):
    left, right, joined = refs[-3:]
    count = left.shape[0]
    joined[:count] = left[...]
    joined[count:] = right[...]


def sweep(strain_row, index, work, dual):
    table, terms, codes, nearby = work
    blocks, own = index.shape[1:]
    halves = own // LANES
    here = lax.axis_index("dom")
    row = lax.broadcasted_iota(jnp.int32, (blocks, LANES), 0)
    left_block = ((row ^ here) - 1) ^ here
    right_block = ((row ^ here) + 1) ^ here

    def wide(j, group, first, block, part):
        piece = one_row(table, (j,), group, first, block, slice(part * LANES, (part + 1) * LANES))
        return jnp.broadcast_to(piece, (blocks, LANES))

    def take_sides(group, first, sides):
        left, right = (list(side) for side in sides)
        for block in range(8):
            for j in range(3):
                left[j] = jnp.where(left_block == first + block, wide(j, group, first, block, halves - 1), left[j])
                right[j] = jnp.where(right_block == first + block, wide(j, group, first, block, 0), right[j])
        return tuple(left), tuple(right)

    blank = tuple(jnp.zeros((blocks, LANES), jnp.float32) for _ in range(3))
    left, right = repeat(blocks, take_sides, (blank, blank))

    def take_corner(k, carry):
        for h in range(halves):
            number = index[k, :, h * LANES : (h + 1) * LANES]
            high, low = number // LANES, number % LANES

            def take(value):
                return jnp.take_along_axis(value, low, axis=1, mode="promise_in_bounds")

            found = [take(table[j, :, 0:LANES]) for j in range(3)]
            for part in range(1, halves):
                mask = high % halves == part
                found = [
                    jnp.where(mask, take(table[j, :, part * LANES : (part + 1) * LANES]), found[j]) for j in range(3)
                ]
            mask = number // own == left_block
            found = [jnp.where(mask, take(left[j]), found[j]) for j in range(3)]
            mask = number // own == right_block
            found = [jnp.where(mask, take(right[j]), found[j]) for j in range(3)]

            def take_group(group, first, found):
                for part, block in itertools.product(range(halves), range(8)):
                    mask = high == (blocks + first + block) * halves + part
                    found = [jnp.where(mask, take(wide(3 + j, group, first, block, part)), found[j]) for j in range(3)]
                return tuple(found)

            found = repeat(blocks, take_group, tuple(found))
            for j in range(3):
                terms[j, k, :, h * LANES : (h + 1) * LANES] = found[j]
        return carry

    lax.fori_loop(0, 4, take_corner, 0)

    def add_rate(k, rate):
        return tuple(
            rate[c] + sum(strain_row(12 * c + 3 * k + j) * terms[j, k] for j in range(3)) for c in range(3)
        )

    flat = jnp.zeros((blocks, own), jnp.float32)
    rate = lax.fori_loop(0, 4, add_rate, (flat, flat, flat))
    trial = [rate[c] + dual[c] for c in range(3)]
    cone = project_cone(trial)
    dual_next = [trial[c] - cone[c] for c in range(3)]
    misfit = [rate[c] - cone[c] + dual_next[c] for c in range(3)]

    def split_corner(k, carry):
        for j in range(3):
            rest = sum(strain_row(12 * c + 3 * k + j) * misfit[c] for c in range(3))
            for split in range(SPLITS):
                term = rest.astype(jnp.bfloat16).astype(jnp.float32)
                terms[SPLITS * j + split, k] = term
                rest = rest - term
        return carry

    lax.fori_loop(0, 4, split_corner, 0)

    near_rows = halves + 2
    next_rows = halves * blocks
    row_wide = lax.broadcasted_iota(jnp.int32, (blocks, own), 0) ^ here
    for k in range(4):
        number = index[k]
        block_of, half = number // own, number // LANES % halves
        near = jnp.where(block_of == ((row_wide - 1) ^ here), 0, 1 + half)
        near = jnp.where(block_of == ((row_wide + 1) ^ here), 1 + halves, near)
        codes[0, k] = (number % LANES).astype(jnp.float32)
        codes[1, k] = jnp.where(block_of < blocks, near, -1).astype(jnp.float32)
        codes[2, k] = jnp.where(block_of < blocks, -1, half * blocks + block_of - blocks).astype(jnp.float32)

    values = 3 * SPLITS
    per_tile = 16 // near_rows
    near_tiles = -(-values // per_tile)
    iota = lax.broadcasted_iota(jnp.int32, (16, own), 0)
    near_iota = (iota % near_rows).astype(jnp.float32).astype(jnp.bfloat16)
    value_iota = (iota // near_rows).astype(jnp.float32).astype(jnp.bfloat16)
    value_masks = [value_iota == jnp.full((16, own), float(at), jnp.bfloat16) for at in range(per_tile)]
    iota = iota.astype(jnp.float32)
    low_iota = [(iota + float(16 * g)).astype(jnp.bfloat16) for g in range(LANES // 16)]
    next_iota = [(iota + float(16 * g)).astype(jnp.bfloat16) for g in range(next_rows // 16)]
    one = jnp.ones((16, own), jnp.bfloat16)
    zero = jnp.zeros((16, own), jnp.bfloat16)

    def spread_row(value):
        return jnp.broadcast_to(value, (16, own)).astype(jnp.bfloat16)

    def add_corner(k, total):
        def add_group(group, first, total):
            for block in range(8):
                low_row, near_row, next_row = (
                    spread_row(one_row(codes, (at, k), group, first, block)) for at in range(3)
                )
                rows = [spread_row(one_row(terms, (at, k), group, first, block)) for at in range(values)]
                spread = jnp.concatenate([jnp.where(low_row == value, one, zero) for value in low_iota], axis=0)
                mask = near_row == near_iota
                weights = []
                for tile in range(near_tiles):
                    inside = rows[tile * per_tile : (tile + 1) * per_tile]
                    value = inside[-1]
                    for at in range(len(inside) - 1):
                        value = jnp.where(value_masks[at], inside[at], value)
                    weights.append(jnp.where(mask, value, zero))
                masks = [next_row == value for value in next_iota]
                weights += [jnp.where(mask, row, zero) for row in rows for mask in masks]
                product = lax.dot_general(
                    jnp.concatenate(weights, axis=0),
                    spread,
                    (((1,), (1,)), ((), ())),
                    preferred_element_type=jnp.float32,
                )
                start = (first + block) * 16 * near_tiles
                if not isinstance(start, int):
                    start = pl.multiple_of(start, 16)
                nearby[pl.ds(start, 16 * near_tiles), :] += product[: 16 * near_tiles]
                total += product[16 * near_tiles :]
            return total

        return repeat(blocks, add_group, total)

    nearby[...] = jnp.zeros(nearby.shape, jnp.float32)
    total = lax.fori_loop(0, 4, add_corner, jnp.zeros((values * next_rows, LANES), jnp.float32))

    def near_force(j, row):
        return sum(
            nearby[pl.ds((SPLITS * j + split) * near_rows + row, blocks, stride=16 * near_tiles), :]
            for split in range(SPLITS)
        )

    force_own, force_next = [], []
    for j in range(3):
        halves_own = [near_force(j, 1 + h) for h in range(halves)]
        to_left, to_right = near_force(j, 0), near_force(j, 1 + halves)
        from_right = from_left = jnp.zeros((blocks, LANES), jnp.float32)
        for block in range(blocks):
            wide_left = jnp.broadcast_to(to_left[block : block + 1], (blocks, LANES))
            wide_right = jnp.broadcast_to(to_right[block : block + 1], (blocks, LANES))
            from_right = jnp.where(right_block == block, wide_left, from_right)
            from_left = jnp.where(left_block == block, wide_right, from_left)
        halves_own[-1] = halves_own[-1] + from_right
        halves_own[0] = halves_own[0] + from_left
        force_own.append(jnp.concatenate(halves_own, axis=1))
        whole = sum(
            total[(SPLITS * j + split) * next_rows : (SPLITS * j + split + 1) * next_rows] for split in range(SPLITS)
        )
        force_next.append(jnp.concatenate([whole[h * blocks : (h + 1) * blocks] for h in range(halves)], axis=1))
    return dual_next, force_own, force_next


def stack_block(piece, slot, rows, stack):
    held = min(rows, piece.shape[0])
    for h in range(stack.shape[0]):
        stack[h, slot * rows : slot * rows + held, :] = piece[:held, h * LANES : (h + 1) * LANES]


def across(stack, row, rows):
    blocks = stack.shape[1] // rows
    return jnp.concatenate(
        [stack[h, pl.ds(row, blocks, stride=rows), :] for h in range(stack.shape[0])], axis=1
    )


def first_kernel(blocks, order, *refs):
    pieces = refs[: len(order)]
    state, index, to_near, to_far, stack = refs[blocks : blocks + 5]
    work = refs[blocks + 5 :]
    table = work[0]
    own = index.shape[2]
    for piece, (start, slot) in zip(pieces, order):
        stack_block(piece.at[start : min(start + ROWS, piece.shape[0])], slot, ROWS, stack)
    flip = lax.axis_index("dom") * own
    even = lax.axis_index("sector") % 2 == 0
    for k in range(4):
        index[k] = across(stack, INDEX + k, ROWS).astype(jnp.int32) ^ flip
    for row in range(36):
        state[row] = across(stack, STRAIN + row, ROWS)
    step = across(stack, STEP, ROWS)
    state[STEP] = step
    state[KEPT_NEXT_STEP] = across(stack, NEXT_STEP, ROWS)
    for j in range(3):
        state[KEPT_LOAD + j] = across(stack, LOAD + j, ROWS)
        table[j] = across(stack, SPEED + j, ROWS)
        table[3 + j] = across(stack, NEXT_SPEED + j, ROWS)
    dual = [across(stack, DUAL + c, ROWS) for c in range(3)]
    dual, force_own, force_next = sweep(lambda row: state[row], index, work, dual)
    for c in range(3):
        state[DUAL + c] = dual[c]
        mine = table[c] - step * (force_own[c] - state[KEPT_LOAD + c])
        to_near[c] = jnp.where(even, force_next[c], mine)
        to_far[c] = jnp.where(even, mine, force_next[c])


def second_kernel(state, index, to_near, to_far, from_far, from_near, vectors, keep, *work):
    table = work[0]
    even = lax.axis_index("sector") % 2 == 0
    step, next_step = state[STEP], state[KEPT_NEXT_STEP]
    for j in range(3):
        near, far = to_near[j], to_far[j]
        near_in, far_in = from_near[j], from_far[j]
        table[j] = jnp.where(even, far, near) - step * jnp.where(even, far_in, near_in)
        table[3 + j] = jnp.where(even, near_in, far_in) - next_step * jnp.where(even, near, far)
    dual = [state[DUAL + c] for c in range(3)]
    dual_next, force_own, force_next = sweep(lambda row: state[row], index, work, dual)
    for c in range(3):
        after = table[c] - step * (force_own[c] - state[KEPT_LOAD + c])
        vectors[c] = after - table[c]
        vectors[3 + c] = -(next_step * force_next[c])
        keep[c] = dual_next[c]
        keep[3 + c] = dual_next[c] - dual[c]
        keep[6 + c] = after


def pairs(depth):
    return [(i, l) for i in range(depth) for l in range(i, depth + 1)]


def gram_kernel(depth, slots, vectors, keep, *refs):
    blocks, own = keep.shape[1:]
    halves = own // LANES
    rows = 9 * depth
    message, stack, rows_sum = refs[len(slots) :]
    for piece, own_slots in zip(refs, slots):
        for at, slot in enumerate(own_slots):
            stack_block(piece.at[at] if len(piece.shape) == 3 else piece.at[ROWS:], slot, rows, stack)
    for row in range(6):
        message[row] = vectors[row]
    message[6] = jnp.zeros((blocks, own), jnp.float32)
    sums, pushed, pushed_twice = {}, [0.0] * (depth + 1), 0.0
    for c, h, top in itertools.product(range(3), range(halves), range(0, blocks, 8)):
        lanes, group = slice(h * LANES, (h + 1) * LANES), slice(top, top + 8)

        def gap(kind, i):
            return stack[h, pl.ds(top * rows + depth * (3 * kind + c) + i, 8, stride=rows), :]

        for kind, moved in enumerate((keep[3 + c, group, lanes], vectors[c, group, lanes])):
            gaps = [moved - gap(kind, i) for i in range(depth)] + [moved]
            for i, l in pairs(depth):
                term = gaps[i] * gaps[l]
                sums[i, l] = sums[i, l] + term if (i, l) in sums else term
        push = vectors[3 + c, group, lanes]
        for i in range(depth):
            pushed[i] = pushed[i] + gap(2, i) * push
        pushed_twice = pushed_twice + push * push
    for at, (i, l) in enumerate(pairs(depth)):
        value = sums[i, l] + pushed_twice - pushed[i] - pushed[l]
        rows_sum[at : at + 1, :] = jnp.sum(value, axis=0, keepdims=True)
    count = len(pairs(depth))
    if rows_sum.shape[0] > count:
        rows_sum[count:, :] = jnp.zeros((rows_sum.shape[0] - count, LANES), jnp.float32)
    whole = jnp.broadcast_to(jnp.sum(rows_sum[...], axis=1, keepdims=True), rows_sum.shape)
    lane = lax.broadcasted_iota(jnp.int32, (8, LANES), 1)
    out = whole[0:8]
    for group in range(1, rows_sum.shape[0] // 8):
        out = jnp.where(lane == group, whole[8 * group : 8 * group + 8], out)
    message[6, 0:8, 0:LANES] = out


def solve_kernel(depth, square, *refs):
    parts = refs[:-8]
    keep, past_w, gap_w, past_u, gap_u, new_u, new_w, total = refs[-8:]
    own = new_u.shape[1]
    tile = parts[0][6, 0:8, 0:LANES]
    for other in parts[1:]:
        tile = tile + other[6, 0:8, 0:LANES]
    even = lax.axis_index("sector") % 2 == 0

    def ahead(by, row):
        if square and by in (1, 3):
            return jnp.where(even, parts[by][row], parts[4 - by][row])
        return parts[by][row]

    sectors = len(parts)
    pushes = [[ahead(by, 3 + j) for j in range(3)] for by in range(sectors)]
    cross = sum(ahead(by, j) * pushes[by - 1][j] for by in range(sectors) for j in range(3))
    cross = jnp.sum(jnp.sum(cross, axis=0, keepdims=True), axis=1, keepdims=True)
    last = [keep[6 + j, 0:1] + pushes[-1][j][0:1] for j in range(3)] + [keep[c, 0:1] for c in range(3)]
    for group in range(total.shape[0] // 8):
        total[8 * group : 8 * group + 8, :] = jnp.broadcast_to(tile[:, group : group + 1], (8, LANES))
    matrix = {
        pair: jnp.broadcast_to(total[at : at + 1, :], (depth, LANES)) + 2.0 * cross
        for at, pair in enumerate(pairs(depth))
    }
    ridge = 0.0001 * sum(matrix[i, i] for i in range(depth)) / depth
    for i in range(depth):
        matrix[i, i] = matrix[i, i] + ridge
    inverse = []
    for step in range(depth):
        inverse.append(1.0 / matrix[step, step])
        for i in range(step + 1, depth):
            factor = matrix[step, i] * inverse[step]
            for l in range(i, depth + 1):
                matrix[i, l] = matrix[i, l] - factor * matrix[step, l]
    weights = [None] * depth
    for i in reversed(range(depth)):
        value = matrix[i, depth]
        for l in range(i + 1, depth):
            value = value - matrix[i, l] * weights[l]
        weights[i] = value * inverse[i]
    row = lax.broadcasted_iota(jnp.int32, (depth, LANES), 0)
    weight = weights[0]
    for i in range(1, depth):
        weight = jnp.where(row == i, weights[i], weight)
    for start in range(0, own, LANES):
        lanes = slice(start, start + LANES)
        for at, (past, gap, out) in enumerate(((past_u, gap_u, new_u), (past_w, gap_w, new_w))):
            for c in range(3):
                value = jnp.broadcast_to(last[3 * at + c][:, lanes], (depth, LANES))
                change = weight * (value - past[c, :, lanes] - gap[c, :, lanes])
                out[c : c + 1, lanes] = value[0:1] - jnp.sum(change, axis=0, keepdims=True)


def per_device(
    strain_map,
    corner_nodes,
    counts,
    seam_nodes,
    velocity,
    dual_state,
    nodal_load,
    mobility,
    past_dual,
    past_dual_gap,
    past_velocity,
    past_velocity_gap,
):
    own = velocity.shape[1]
    halves = own // LANES
    blocks = lax.axis_size("dom")
    sectors = lax.axis_size("sector")
    depth = past_dual.shape[0]
    seam_rows = seam_nodes.shape[1] // own
    mobility = mobility.reshape(1, own)
    past_dual, past_dual_gap, past_velocity, past_velocity_gap = (
        value.transpose(1, 0, 2) for value in (past_dual, past_dual_gap, past_velocity, past_velocity_gap)
    )

    def send(value, target):
        return lax.ppermute(value, "sector", [(i, target(i) % sectors) for i in range(sectors)])

    def swap(value, bits):
        return lax.ppermute(value, "dom", [(i, i ^ bits) for i in range(blocks)])

    nodes = (velocity, mobility, seam_nodes)
    ahead = call(
        nodes_kernel,
        f32(8 + seam_rows + 3 * depth, own),
        in_hbm(*nodes, past_velocity_gap),
        loose=len(nodes) + 1,
        scratch=[pltpu.VMEM(value.shape, value.dtype) for value in nodes]
        + [pltpu.SemaphoreType.DMA((len(nodes) + 3,))],
    )
    held = (strain_map, dual_state, velocity, nodal_load, mobility, corner_nodes)
    base = call(
        base_kernel,
        f32(INDEX + 4, own),
        (counts, ahead, *in_hbm(*held)),
        scalars=1,
        loose=len(held) + 1,
        scratch=[pltpu.VMEM(value.shape, value.dtype) for value in held] + [pltpu.SemaphoreType.DMA((len(held),))],
    )
    ahead = send(ahead, lambda i: i - 1)
    history = call(
        history_kernel,
        f32(6, depth, own),
        (base, *in_hbm(past_dual_gap, past_velocity_gap)),
        loose=3,
        scratch=[pltpu.SemaphoreType.DMA((2,))],
    )
    far_ones = list(range(blocks - 2, 2, -2))
    lengths = [max(INDEX + 4, ROWS - place) for place in range(len(far_ones))]
    messages = call(
        functools.partial(message_kernel, own * blocks, depth),
        tuple(f32(rows, own) for rows in sorted(set(lengths), reverse=True)),
        (history, ahead, base),
        loose=1,
    )
    wide = call(wide_kernel, f32(ROWS + 9 * depth, own), (messages[0], history, ahead))
    pieces = {0: wide}
    for bits, rows in zip(far_ones, lengths):
        pieces[bits] = swap(next(value for value in messages if value.shape[0] == rows), bits)
    pieces[2] = swap(wide, 2)
    for even in (0, 2):
        pieces[even + 1] = swap(pieces[even], 1)
    count = len(far_ones)
    crossed = swap(
        call(stack_kernel, f32(count * ROWS, own), tuple(pieces[bits] for bits in far_ones)), 1
    )
    histories, slots = [pieces[block] for block in range(4)], [(block,) for block in range(4)]
    history = call(
        pair_kernel, f32(2, 9 * depth, own), (*(pieces[bits] for bits in far_ones), wide, pieces[2]), loose=len(far_ones)
    )
    known, apart, later = (0, 2), 4, []
    while apart < blocks:
        other = swap(history, apart)
        later.append((other, tuple(slot ^ apart for slot in known)))
        known += later[-1][1]
        apart *= 2
        if apart < blocks:
            history = call(join_kernel, f32(2 * history.shape[0], 9 * depth, own), (history, other))
    order = [(at * ROWS, bits + 1) for at, bits in enumerate(far_ones)]
    order += [(0, block) for block in reversed(range(blocks)) if block in pieces]
    sector = f32(3, blocks, own)
    work = [
        pltpu.VMEM((6, blocks, own), jnp.float32),
        pltpu.VMEM((3 * SPLITS, 4, blocks, own), jnp.float32),
        pltpu.VMEM((3, 4, blocks, own), jnp.float32),
        pltpu.VMEM((blocks * 16 * -(-3 * SPLITS * (halves + 2) // 16), LANES), jnp.float32),
    ]
    state, index, to_near, to_far = call(
        functools.partial(first_kernel, blocks, order),
        (f32(KEPT, blocks, own), jax.ShapeDtypeStruct((4, blocks, own), jnp.int32), sector, sector),
        (*([crossed] * count), *(pieces[block] for _, block in order[count:])),
        scratch=[pltpu.VMEM((halves, blocks * ROWS, LANES), jnp.float32), *work],
    )
    from_far = send(to_far, lambda i: i + 1 if i % 2 else i - 1)
    from_near = send(to_near, lambda i: i ^ 1)
    for other, far in later:
        held_back = call(copy_kernel, f32(*other.shape), (from_near, from_far, other), loose=2)
        histories += [other, swap(held_back, 1)]
        slots += [far, tuple(slot ^ 1 for slot in far)]
    vectors, keep = call(
        second_kernel,
        (f32(6, blocks, own), f32(9, blocks, own)),
        (state, index, to_near, to_far, from_far, from_near),
        scratch=work,
    )
    count = -(-len(pairs(depth)) // 8) * 8
    message = call(
        functools.partial(gram_kernel, depth, tuple(slots)),
        f32(7, blocks, own),
        (vectors, keep, *histories),
        scratch=[
            pltpu.VMEM((halves, blocks * 9 * depth, LANES), jnp.float32),
            pltpu.VMEM((count, LANES), jnp.float32),
        ],
    )
    square = sectors == 4
    parts = [message] + [None] * (sectors - 1)
    for by in sorted(range(1, sectors), reverse=True):
        parts[by] = send(message, (lambda i: i ^ by) if square else (lambda i: i - by))
    return call(
        functools.partial(solve_kernel, depth, square),
        (f32(3, own), f32(3, own)),
        (*parts, keep, past_dual, past_dual_gap, past_velocity, past_velocity_gap),
        scratch=[pltpu.VMEM((count, LANES), jnp.float32)],
    )


def solution(mesh):
    in_specs = (
        P(None, ("sector", "dom")),
        P(None, ("sector", "dom")),
        P(("sector", "dom")),
        P("sector", None),
        P(None, ("sector", "dom")),
        P(None, ("sector", "dom")),
        P(None, ("sector", "dom")),
        P(("sector", "dom")),
        P(None, None, ("sector", "dom")),
        P(None, None, ("sector", "dom")),
        P(None, None, ("sector", "dom")),
        P(None, None, ("sector", "dom")),
    )
    out_specs = (P(None, ("sector", "dom")), P(None, ("sector", "dom")))
    return jax.shard_map(
        per_device, mesh=mesh, in_specs=in_specs, out_specs=out_specs, check_vma=False
    )
```

```python
import functools
import itertools

import jax
import jax.numpy as jnp
from jax import lax
from jax.experimental import pallas as pl
from jax.experimental.pallas import tpu as pltpu
from jax.sharding import PartitionSpec as P

LANES = 128
VMEM_LIMIT = 24 * 1024 * 1024

STRAIN, DUAL, STEP, SPEED, LOAD, NEXT_STEP, NEXT_SPEED, INDEX, ROWS = 0, 36, 39, 40, 43, 46, 47, 50, 56
KEPT_NEXT_STEP, KEPT_LOAD, KEPT = 40, 41, 44
SPLITS = 2


def vmem():
    return pl.BlockSpec(memory_space=pltpu.VMEM)


def smem():
    return pl.BlockSpec(memory_space=pltpu.SMEM)


def call(kernel, outs, args, scalars=0, loose=0, scratch=()):
    return pl.pallas_call(
        kernel,
        out_shape=outs,
        in_specs=[smem()] * scalars
        + [pl.BlockSpec(memory_space=pl.ANY)] * loose
        + [vmem()] * (len(args) - scalars - loose),
        out_specs=jax.tree.map(lambda _: vmem(), outs),
        scratch_shapes=list(scratch),
        compiler_params=pltpu.CompilerParams(vmem_limit_bytes=VMEM_LIMIT),
    )(*args)


def f32(*shape):
    return jax.ShapeDtypeStruct(shape, jnp.float32)


def repeat(blocks, body, init):
    if blocks == 8:
        return body(slice(0, 8), 0, init)
    return lax.fori_loop(
        0, blocks // 8, lambda step, carry: body(pl.ds(pl.multiple_of(8 * step, 8), 8), 8 * step, carry), init
    )


def one_row(ref, lead, group, first, row, lanes=slice(None)):
    if isinstance(first, int):
        return ref[(*lead, slice(first + row, first + row + 1), lanes)]
    return ref[(*lead, group, lanes)][row : row + 1]


def project_cone(trial):
    center = 0.5 * (trial[0] + trial[1])
    spread = 0.5 * (trial[0] - trial[1])
    shear = trial[2]
    radius = jnp.sqrt(spread * spread + shear * shear)
    upper = center + radius
    lower = center - radius
    iso_part = 0.5 * (jnp.maximum(upper, 0.0) + jnp.maximum(lower, 0.0))
    factor = jnp.clip((center + radius) / (2.0 * jnp.maximum(radius, 0.05)), 0.0, 1.0)
    return (iso_part + factor * spread, iso_part - factor * spread, factor * shear)


def fetch(pairs, sems):
    copies = [pltpu.make_async_copy(source, target, sems.at[at]) for at, (source, target) in enumerate(pairs)]
    for copy in copies:
        copy.start()
    for copy in copies:
        copy.wait()


def in_hbm(*values):
    return tuple(pltpu.with_memory_space_constraint(value, pltpu.HBM) for value in values)


def nodes_kernel(speed_in, mobility_in, seam_in, gap_u, ahead, speed, mobility, seam, sems):
    depth = gap_u.shape[1]
    start = ahead.shape[0] - 3 * depth
    gaps = [(gap_u.at[c], ahead.at[pl.ds(start + depth * c, depth)]) for c in range(3)]
    fetch(((speed_in, speed), (mobility_in, mobility), (seam_in, seam), *gaps), sems)
    own = speed.shape[1]
    ahead[0:3, :] = speed[...]
    ahead[3:4, :] = mobility[...]
    ahead[4:8, :] = jnp.zeros((4, own), jnp.float32)
    for row in range(8, start):
        ahead[row : row + 1, :] = seam[:, (row - 8) * own : (row - 7) * own].astype(jnp.float32)


def base_kernel(counts, after, *refs):
    count = (len(refs) - 2) // 2
    sources, base, held, sems = refs[:count], refs[count], refs[count + 1 : -1], refs[-1]
    fetch(zip(sources, held), sems)
    strain, dual, speed, load, mobility, corners = held
    own = speed.shape[1]
    slot = lax.broadcasted_iota(jnp.int32, (1, own), 1)
    alive = (slot < counts[0]).astype(jnp.float32)
    base[STRAIN:DUAL, :] = strain[...] * alive
    base[DUAL : DUAL + 3, :] = dual[...] * alive
    base[STEP : STEP + 1, :] = mobility[...]
    base[SPEED : SPEED + 3, :] = speed[...]
    base[LOAD : LOAD + 3, :] = load[...]
    base[NEXT_STEP:INDEX, :] = jnp.zeros((INDEX - NEXT_STEP, own), jnp.float32)
    base[INDEX : INDEX + 4, :] = corners[...].astype(jnp.float32)


def message_kernel(sector_nodes, depth, after, ahead, base, message, *shorter):
    own = message.shape[1]
    halves = own // LANES
    message[:NEXT_STEP, :] = base[:NEXT_STEP, :]
    message[NEXT_STEP : NEXT_STEP + 1, :] = ahead[3:4, :]
    message[NEXT_SPEED : NEXT_SPEED + 3, :] = ahead[0:3, :]
    message[INDEX + 4 :, :] = jnp.zeros((ROWS - INDEX - 4, own), jnp.float32)
    corners = base[INDEX : INDEX + 4, :].astype(jnp.int32)
    corner = jnp.concatenate([corners[:, h * LANES : (h + 1) * LANES] for h in range(halves)], axis=0)
    seam_rows = ahead.shape[0] - 8 - 3 * depth
    place = jnp.clip(corner - sector_nodes, 0, seam_rows * own - 1)
    high, low = place // LANES, place % LANES
    found = jnp.zeros(corner.shape, jnp.float32)
    for row in range(seam_rows):
        for h in range(halves):
            table = jnp.broadcast_to(ahead[8 + row : 9 + row, h * LANES : (h + 1) * LANES], corner.shape)
            value = jnp.take_along_axis(table, low, axis=1, mode="promise_in_bounds")
            found = jnp.where(high == row * halves + h, value, found)
    node = jnp.where(corner < sector_nodes, corner.astype(jnp.float32), found + float(sector_nodes))
    for h in range(halves):
        message[INDEX : INDEX + 4, h * LANES : (h + 1) * LANES] = node[4 * h : 4 * h + 4]
    for other in shorter:
        other[...] = message[: other.shape[0], :]


def history_kernel(after, gap_w, gap_u, history, sems):
    fetch(((gap_w, history.at[0:3]), (gap_u, history.at[3:6])), sems)


def wide_kernel(message, gaps, ahead, wide):
    depth = gaps.shape[1]
    start = ahead.shape[0] - 3 * depth
    wide[:ROWS, :] = message[...]
    for kind in range(6):
        wide[ROWS + depth * kind : ROWS + depth * (kind + 1), :] = gaps[kind]
    wide[ROWS + 6 * depth :, :] = ahead[start:, :]


def stack_kernel(*refs):
    stacked = refs[-1]
    for at, piece in enumerate(refs[:-1]):
        stacked[at * ROWS : at * ROWS + piece.shape[0], :] = piece[...]
        if piece.shape[0] < ROWS:
            start = at * ROWS + piece.shape[0]
            stacked[start : (at + 1) * ROWS, :] = jnp.zeros(((at + 1) * ROWS - start, piece.shape[1]), jnp.float32)


def pair_kernel(*refs):
    left, right, joined = refs[-3:]
    joined[0] = left[ROWS:, :]
    joined[1] = right[ROWS:, :]


def copy_kernel(*refs):
    value, copied = refs[-2:]
    copied[...] = value[...]


def join_kernel(*refs):
    left, right, joined = refs[-3:]
    count = left.shape[0]
    joined[:count] = left[...]
    joined[count:] = right[...]


def sweep(strain_row, index, work, dual):
    table, terms, codes, nearby = work
    blocks, own = index.shape[1:]
    halves = own // LANES
    here = lax.axis_index("dom")
    row = lax.broadcasted_iota(jnp.int32, (blocks, LANES), 0)
    left_block = ((row ^ here) - 1) ^ here
    right_block = ((row ^ here) + 1) ^ here

    def wide(j, group, first, block, part):
        piece = one_row(table, (j,), group, first, block, slice(part * LANES, (part + 1) * LANES))
        return jnp.broadcast_to(piece, (blocks, LANES))

    def take_sides(group, first, sides):
        left, right = (list(side) for side in sides)
        for block in range(8):
            for j in range(3):
                left[j] = jnp.where(left_block == first + block, wide(j, group, first, block, halves - 1), left[j])
                right[j] = jnp.where(right_block == first + block, wide(j, group, first, block, 0), right[j])
        return tuple(left), tuple(right)

    blank = tuple(jnp.zeros((blocks, LANES), jnp.float32) for _ in range(3))
    left, right = repeat(blocks, take_sides, (blank, blank))
    speed = []
    for k in range(4):
        parts = []
        for h in range(halves):
            number = index[k, :, h * LANES : (h + 1) * LANES]
            high, low = number // LANES, number % LANES

            def take(value):
                return jnp.take_along_axis(value, low, axis=1, mode="promise_in_bounds")

            found = [take(table[j, :, 0:LANES]) for j in range(3)]
            for part in range(1, halves):
                mask = high % halves == part
                found = [
                    jnp.where(mask, take(table[j, :, part * LANES : (part + 1) * LANES]), found[j]) for j in range(3)
                ]
            mask = number // own == left_block
            found = [jnp.where(mask, take(left[j]), found[j]) for j in range(3)]
            mask = number // own == right_block
            found = [jnp.where(mask, take(right[j]), found[j]) for j in range(3)]

            def take_group(group, first, found):
                for part, block in itertools.product(range(halves), range(8)):
                    mask = high == (blocks + first + block) * halves + part
                    found = [jnp.where(mask, take(wide(3 + j, group, first, block, part)), found[j]) for j in range(3)]
                return tuple(found)

            parts.append(repeat(blocks, take_group, tuple(found)))
        speed.append([jnp.concatenate([found[j] for found in parts], axis=1) for j in range(3)])
    rate = []
    for c in range(3):
        total = None
        for k in range(4):
            for j in range(3):
                term = strain_row(12 * c + 3 * k + j) * speed[k][j]
                total = term if total is None else total + term
        rate.append(total)
    trial = [rate[c] + dual[c] for c in range(3)]
    cone = project_cone(trial)
    dual_next = [trial[c] - cone[c] for c in range(3)]
    misfit = [rate[c] - cone[c] + dual_next[c] for c in range(3)]
    for k in range(4):
        for j in range(3):
            rest = sum(strain_row(12 * c + 3 * k + j) * misfit[c] for c in range(3))
            for split in range(SPLITS):
                term = rest.astype(jnp.bfloat16).astype(jnp.float32)
                terms[SPLITS * j + split, k] = term
                rest = rest - term

    near_rows = halves + 2
    next_rows = halves * blocks
    row_wide = lax.broadcasted_iota(jnp.int32, (blocks, own), 0) ^ here
    for k in range(4):
        number = index[k]
        block_of, half = number // own, number // LANES % halves
        near = jnp.where(block_of == ((row_wide - 1) ^ here), 0, 1 + half)
        near = jnp.where(block_of == ((row_wide + 1) ^ here), 1 + halves, near)
        codes[0, k] = (number % LANES).astype(jnp.float32)
        codes[1, k] = jnp.where(block_of < blocks, near, -1).astype(jnp.float32)
        codes[2, k] = jnp.where(block_of < blocks, -1, half * blocks + block_of - blocks).astype(jnp.float32)

    values = 3 * SPLITS
    per_tile = 16 // near_rows
    near_tiles = -(-values // per_tile)
    iota = lax.broadcasted_iota(jnp.int32, (16, own), 0)
    near_iota = (iota % near_rows).astype(jnp.float32).astype(jnp.bfloat16)
    value_iota = (iota // near_rows).astype(jnp.float32).astype(jnp.bfloat16)
    value_masks = [value_iota == jnp.full((16, own), float(at), jnp.bfloat16) for at in range(per_tile)]
    iota = iota.astype(jnp.float32)
    low_iota = [(iota + float(16 * g)).astype(jnp.bfloat16) for g in range(LANES // 16)]
    next_iota = [(iota + float(16 * g)).astype(jnp.bfloat16) for g in range(next_rows // 16)]
    one = jnp.ones((16, own), jnp.bfloat16)
    zero = jnp.zeros((16, own), jnp.bfloat16)

    def spread_row(value):
        return jnp.broadcast_to(value, (16, own)).astype(jnp.bfloat16)

    def add_group(group, first, total):
        for block in range(8):
            part = None
            for k in range(4):
                low_row, near_row, next_row = (
                    spread_row(one_row(codes, (at, k), group, first, block)) for at in range(3)
                )
                rows = [spread_row(one_row(terms, (at, k), group, first, block)) for at in range(values)]
                spread = jnp.concatenate([jnp.where(low_row == value, one, zero) for value in low_iota], axis=0)
                mask = near_row == near_iota
                weights = []
                for tile in range(near_tiles):
                    inside = rows[tile * per_tile : (tile + 1) * per_tile]
                    value = inside[-1]
                    for at in range(len(inside) - 1):
                        value = jnp.where(value_masks[at], inside[at], value)
                    weights.append(jnp.where(mask, value, zero))
                masks = [next_row == value for value in next_iota]
                weights += [jnp.where(mask, row, zero) for row in rows for mask in masks]
                product = lax.dot_general(
                    jnp.concatenate(weights, axis=0),
                    spread,
                    (((1,), (1,)), ((), ())),
                    preferred_element_type=jnp.float32,
                )
                part = product if part is None else part + product
            start = (first + block) * 16 * near_tiles
            if not isinstance(start, int):
                start = pl.multiple_of(start, 16)
            nearby[pl.ds(start, 16 * near_tiles), :] = part[: 16 * near_tiles]
            total += part[16 * near_tiles :]
        return total

    total = repeat(blocks, add_group, jnp.zeros((values * next_rows, LANES), jnp.float32))

    def near_force(j, row):
        return sum(
            nearby[pl.ds((SPLITS * j + split) * near_rows + row, blocks, stride=16 * near_tiles), :]
            for split in range(SPLITS)
        )

    force_own, force_next = [], []
    for j in range(3):
        halves_own = [near_force(j, 1 + h) for h in range(halves)]
        to_left, to_right = near_force(j, 0), near_force(j, 1 + halves)
        from_right = from_left = jnp.zeros((blocks, LANES), jnp.float32)
        for block in range(blocks):
            wide_left = jnp.broadcast_to(to_left[block : block + 1], (blocks, LANES))
            wide_right = jnp.broadcast_to(to_right[block : block + 1], (blocks, LANES))
            from_right = jnp.where(right_block == block, wide_left, from_right)
            from_left = jnp.where(left_block == block, wide_right, from_left)
        halves_own[-1] = halves_own[-1] + from_right
        halves_own[0] = halves_own[0] + from_left
        force_own.append(jnp.concatenate(halves_own, axis=1))
        whole = sum(
            total[(SPLITS * j + split) * next_rows : (SPLITS * j + split + 1) * next_rows] for split in range(SPLITS)
        )
        force_next.append(jnp.concatenate([whole[h * blocks : (h + 1) * blocks] for h in range(halves)], axis=1))
    return dual_next, force_own, force_next


def stack_block(piece, slot, rows, stack):
    held = min(rows, piece.shape[0])
    for h in range(stack.shape[0]):
        stack[h, slot * rows : slot * rows + held, :] = piece[:held, h * LANES : (h + 1) * LANES]


def across(stack, row, rows):
    blocks = stack.shape[1] // rows
    return jnp.concatenate(
        [stack[h, pl.ds(row, blocks, stride=rows), :] for h in range(stack.shape[0])], axis=1
    )


def first_kernel(blocks, order, *refs):
    pieces = refs[: len(order)]
    state, index, to_near, to_far, stack = refs[blocks : blocks + 5]
    work = refs[blocks + 5 :]
    table = work[0]
    own = index.shape[2]
    for piece, (start, slot) in zip(pieces, order):
        stack_block(piece.at[start : min(start + ROWS, piece.shape[0])], slot, ROWS, stack)
    flip = lax.axis_index("dom") * own
    even = lax.axis_index("sector") % 2 == 0
    for k in range(4):
        index[k] = across(stack, INDEX + k, ROWS).astype(jnp.int32) ^ flip
    for row in range(36):
        state[row] = across(stack, STRAIN + row, ROWS)
    step = across(stack, STEP, ROWS)
    state[STEP] = step
    state[KEPT_NEXT_STEP] = across(stack, NEXT_STEP, ROWS)
    for j in range(3):
        state[KEPT_LOAD + j] = across(stack, LOAD + j, ROWS)
        table[j] = across(stack, SPEED + j, ROWS)
        table[3 + j] = across(stack, NEXT_SPEED + j, ROWS)
    dual = [across(stack, DUAL + c, ROWS) for c in range(3)]
    dual, force_own, force_next = sweep(lambda row: state[row], index, work, dual)
    for c in range(3):
        state[DUAL + c] = dual[c]
        mine = table[c] - step * (force_own[c] - state[KEPT_LOAD + c])
        to_near[c] = jnp.where(even, force_next[c], mine)
        to_far[c] = jnp.where(even, mine, force_next[c])


def second_kernel(state, index, to_near, to_far, from_far, from_near, vectors, keep, *work):
    table = work[0]
    even = lax.axis_index("sector") % 2 == 0
    step, next_step = state[STEP], state[KEPT_NEXT_STEP]
    for j in range(3):
        near, far = to_near[j], to_far[j]
        near_in, far_in = from_near[j], from_far[j]
        table[j] = jnp.where(even, far, near) - step * jnp.where(even, far_in, near_in)
        table[3 + j] = jnp.where(even, near_in, far_in) - next_step * jnp.where(even, near, far)
    dual = [state[DUAL + c] for c in range(3)]
    dual_next, force_own, force_next = sweep(lambda row: state[row], index, work, dual)
    for c in range(3):
        after = table[c] - step * (force_own[c] - state[KEPT_LOAD + c])
        vectors[c] = after - table[c]
        vectors[3 + c] = -(next_step * force_next[c])
        keep[c] = dual_next[c]
        keep[3 + c] = dual_next[c] - dual[c]
        keep[6 + c] = after


def pairs(depth):
    return [(i, l) for i in range(depth) for l in range(i, depth + 1)]


def gram_kernel(depth, slots, vectors, keep, *refs):
    blocks, own = keep.shape[1:]
    halves = own // LANES
    rows = 9 * depth
    message, stack, rows_sum = refs[len(slots) :]
    for piece, own_slots in zip(refs, slots):
        for at, slot in enumerate(own_slots):
            stack_block(piece.at[at] if len(piece.shape) == 3 else piece.at[ROWS:], slot, rows, stack)
    for row in range(6):
        message[row] = vectors[row]
    message[6] = jnp.zeros((blocks, own), jnp.float32)
    sums, pushed, pushed_twice = {}, [0.0] * (depth + 1), 0.0
    for c, h, top in itertools.product(range(3), range(halves), range(0, blocks, 8)):
        lanes, group = slice(h * LANES, (h + 1) * LANES), slice(top, top + 8)

        def gap(kind, i):
            return stack[h, pl.ds(top * rows + depth * (3 * kind + c) + i, 8, stride=rows), :]

        for kind, moved in enumerate((keep[3 + c, group, lanes], vectors[c, group, lanes])):
            gaps = [moved - gap(kind, i) for i in range(depth)] + [moved]
            for i, l in pairs(depth):
                term = gaps[i] * gaps[l]
                sums[i, l] = sums[i, l] + term if (i, l) in sums else term
        push = vectors[3 + c, group, lanes]
        for i in range(depth):
            pushed[i] = pushed[i] + gap(2, i) * push
        pushed_twice = pushed_twice + push * push
    for at, (i, l) in enumerate(pairs(depth)):
        value = sums[i, l] + pushed_twice - pushed[i] - pushed[l]
        rows_sum[at : at + 1, :] = jnp.sum(value, axis=0, keepdims=True)
    count = len(pairs(depth))
    if rows_sum.shape[0] > count:
        rows_sum[count:, :] = jnp.zeros((rows_sum.shape[0] - count, LANES), jnp.float32)
    whole = jnp.broadcast_to(jnp.sum(rows_sum[...], axis=1, keepdims=True), rows_sum.shape)
    lane = lax.broadcasted_iota(jnp.int32, (8, LANES), 1)
    out = whole[0:8]
    for group in range(1, rows_sum.shape[0] // 8):
        out = jnp.where(lane == group, whole[8 * group : 8 * group + 8], out)
    message[6, 0:8, 0:LANES] = out


def solve_kernel(depth, square, *refs):
    parts = refs[:-8]
    keep, past_w, gap_w, past_u, gap_u, new_u, new_w, total = refs[-8:]
    own = new_u.shape[1]
    tile = parts[0][6, 0:8, 0:LANES]
    for other in parts[1:]:
        tile = tile + other[6, 0:8, 0:LANES]
    even = lax.axis_index("sector") % 2 == 0

    def ahead(by, row):
        if square and by in (1, 3):
            return jnp.where(even, parts[by][row], parts[4 - by][row])
        return parts[by][row]

    sectors = len(parts)
    pushes = [[ahead(by, 3 + j) for j in range(3)] for by in range(sectors)]
    cross = sum(ahead(by, j) * pushes[by - 1][j] for by in range(sectors) for j in range(3))
    cross = jnp.sum(jnp.sum(cross, axis=0, keepdims=True), axis=1, keepdims=True)
    last = [keep[6 + j, 0:1] + pushes[-1][j][0:1] for j in range(3)] + [keep[c, 0:1] for c in range(3)]
    for group in range(total.shape[0] // 8):
        total[8 * group : 8 * group + 8, :] = jnp.broadcast_to(tile[:, group : group + 1], (8, LANES))
    matrix = {
        pair: jnp.broadcast_to(total[at : at + 1, :], (depth, LANES)) + 2.0 * cross
        for at, pair in enumerate(pairs(depth))
    }
    ridge = 0.0001 * sum(matrix[i, i] for i in range(depth)) / depth
    for i in range(depth):
        matrix[i, i] = matrix[i, i] + ridge
    inverse = []
    for step in range(depth):
        inverse.append(1.0 / matrix[step, step])
        for i in range(step + 1, depth):
            factor = matrix[step, i] * inverse[step]
            for l in range(i, depth + 1):
                matrix[i, l] = matrix[i, l] - factor * matrix[step, l]
    weights = [None] * depth
    for i in reversed(range(depth)):
        value = matrix[i, depth]
        for l in range(i + 1, depth):
            value = value - matrix[i, l] * weights[l]
        weights[i] = value * inverse[i]
    row = lax.broadcasted_iota(jnp.int32, (depth, LANES), 0)
    weight = weights[0]
    for i in range(1, depth):
        weight = jnp.where(row == i, weights[i], weight)
    for start in range(0, own, LANES):
        lanes = slice(start, start + LANES)
        for at, (past, gap, out) in enumerate(((past_u, gap_u, new_u), (past_w, gap_w, new_w))):
            for c in range(3):
                value = jnp.broadcast_to(last[3 * at + c][:, lanes], (depth, LANES))
                change = weight * (value - past[c, :, lanes] - gap[c, :, lanes])
                out[c : c + 1, lanes] = value[0:1] - jnp.sum(change, axis=0, keepdims=True)


def per_device(
    strain_map,
    corner_nodes,
    counts,
    seam_nodes,
    velocity,
    dual_state,
    nodal_load,
    mobility,
    past_dual,
    past_dual_gap,
    past_velocity,
    past_velocity_gap,
):
    own = velocity.shape[1]
    halves = own // LANES
    blocks = lax.axis_size("dom")
    sectors = lax.axis_size("sector")
    depth = past_dual.shape[0]
    seam_rows = seam_nodes.shape[1] // own
    mobility = mobility.reshape(1, own)
    past_dual, past_dual_gap, past_velocity, past_velocity_gap = (
        value.transpose(1, 0, 2) for value in (past_dual, past_dual_gap, past_velocity, past_velocity_gap)
    )

    def send(value, target):
        return lax.ppermute(value, "sector", [(i, target(i) % sectors) for i in range(sectors)])

    def swap(value, bits):
        return lax.ppermute(value, "dom", [(i, i ^ bits) for i in range(blocks)])

    nodes = (velocity, mobility, seam_nodes)
    ahead = call(
        nodes_kernel,
        f32(8 + seam_rows + 3 * depth, own),
        in_hbm(*nodes, past_velocity_gap),
        loose=len(nodes) + 1,
        scratch=[pltpu.VMEM(value.shape, value.dtype) for value in nodes]
        + [pltpu.SemaphoreType.DMA((len(nodes) + 3,))],
    )
    held = (strain_map, dual_state, velocity, nodal_load, mobility, corner_nodes)
    base = call(
        base_kernel,
        f32(INDEX + 4, own),
        (counts, ahead, *in_hbm(*held)),
        scalars=1,
        loose=len(held) + 1,
        scratch=[pltpu.VMEM(value.shape, value.dtype) for value in held] + [pltpu.SemaphoreType.DMA((len(held),))],
    )
    ahead = send(ahead, lambda i: i - 1)
    history = call(
        history_kernel,
        f32(6, depth, own),
        (base, *in_hbm(past_dual_gap, past_velocity_gap)),
        loose=3,
        scratch=[pltpu.SemaphoreType.DMA((2,))],
    )
    far_ones = list(range(4, blocks, 2))
    lengths = [max(INDEX + 4, ROWS - place) for place in range(len(far_ones))]
    messages = call(
        functools.partial(message_kernel, own * blocks, depth),
        tuple(f32(rows, own) for rows in sorted(set(lengths), reverse=True)),
        (history, ahead, base),
        loose=1,
    )
    wide = call(wide_kernel, f32(ROWS + 9 * depth, own), (messages[0], history, ahead))
    pieces = {0: wide}
    for bits, rows in zip(far_ones, lengths):
        pieces[bits] = swap(next(value for value in messages if value.shape[0] == rows), bits)
    pieces[2] = swap(wide, 2)
    for even in (0, 2):
        pieces[even + 1] = swap(pieces[even], 1)
    count = len(far_ones)
    crossed = swap(
        call(stack_kernel, f32(count * ROWS, own), tuple(pieces[bits] for bits in far_ones)), 1
    )
    histories, slots = [pieces[block] for block in range(4)], [(block,) for block in range(4)]
    history = call(
        pair_kernel, f32(2, 9 * depth, own), (*(pieces[bits] for bits in far_ones), wide, pieces[2]), loose=len(far_ones)
    )
    known, apart, later = (0, 2), 4, []
    while apart < blocks:
        other = swap(history, apart)
        later.append((other, tuple(slot ^ apart for slot in known)))
        known += later[-1][1]
        apart *= 2
        if apart < blocks:
            history = call(join_kernel, f32(2 * history.shape[0], 9 * depth, own), (history, other))
    order = [(at * ROWS, bits + 1) for at, bits in enumerate(far_ones)]
    order += [(0, block) for block in reversed(range(blocks)) if block in pieces]
    sector = f32(3, blocks, own)
    work = [
        pltpu.VMEM((6, blocks, own), jnp.float32),
        pltpu.VMEM((3 * SPLITS, 4, blocks, own), jnp.float32),
        pltpu.VMEM((3, 4, blocks, own), jnp.float32),
        pltpu.VMEM((blocks * 16 * -(-3 * SPLITS * (halves + 2) // 16), LANES), jnp.float32),
    ]
    state, index, to_near, to_far = call(
        functools.partial(first_kernel, blocks, order),
        (f32(KEPT, blocks, own), jax.ShapeDtypeStruct((4, blocks, own), jnp.int32), sector, sector),
        (*([crossed] * count), *(pieces[block] for _, block in order[count:])),
        scratch=[pltpu.VMEM((halves, blocks * ROWS, LANES), jnp.float32), *work],
    )
    from_far = send(to_far, lambda i: i + 1 if i % 2 else i - 1)
    from_near = send(to_near, lambda i: i ^ 1)
    for other, far in later:
        held_back = call(copy_kernel, f32(*other.shape), (from_near, from_far, other), loose=2)
        histories += [other, swap(held_back, 1)]
        slots += [far, tuple(slot ^ 1 for slot in far)]
    vectors, keep = call(
        second_kernel,
        (f32(6, blocks, own), f32(9, blocks, own)),
        (state, index, to_near, to_far, from_far, from_near),
        scratch=work,
    )
    count = -(-len(pairs(depth)) // 8) * 8
    message = call(
        functools.partial(gram_kernel, depth, tuple(slots)),
        f32(7, blocks, own),
        (vectors, keep, *histories),
        scratch=[
            pltpu.VMEM((halves, blocks * 9 * depth, LANES), jnp.float32),
            pltpu.VMEM((count, LANES), jnp.float32),
        ],
    )
    square = sectors == 4
    parts = [message] + [None] * (sectors - 1)
    for by in sorted(range(1, sectors), reverse=True):
        parts[by] = send(message, (lambda i: i ^ by) if square else (lambda i: i - by))
    return call(
        functools.partial(solve_kernel, depth, square),
        (f32(3, own), f32(3, own)),
        (*parts, keep, past_dual, past_dual_gap, past_velocity, past_velocity_gap),
        scratch=[pltpu.VMEM((count, LANES), jnp.float32)],
    )


def solution(mesh):
    in_specs = (
        P(None, ("sector", "dom")),
        P(None, ("sector", "dom")),
        P(("sector", "dom")),
        P("sector", None),
        P(None, ("sector", "dom")),
        P(None, ("sector", "dom")),
        P(None, ("sector", "dom")),
        P(("sector", "dom")),
        P(None, None, ("sector", "dom")),
        P(None, None, ("sector", "dom")),
        P(None, None, ("sector", "dom")),
        P(None, None, ("sector", "dom")),
    )
    out_specs = (P(None, ("sector", "dom")), P(None, ("sector", "dom")))
    return jax.shard_map(
        per_device, mesh=mesh, in_specs=in_specs, out_specs=out_specs, check_vma=False
    )
```

```python
import functools
import itertools

import jax
import jax.numpy as jnp
from jax import lax
from jax.experimental import pallas as pl
from jax.experimental.pallas import tpu as pltpu
from jax.sharding import PartitionSpec as P

LANES = 128
VMEM_LIMIT = 24 * 1024 * 1024

STRAIN, DUAL, STEP, SPEED, LOAD, NEXT_STEP, NEXT_SPEED, INDEX, ROWS = 0, 36, 39, 40, 43, 46, 47, 50, 56
KEPT_NEXT_STEP, KEPT_LOAD, KEPT = 40, 41, 44
SPLITS = 2


def vmem():
    return pl.BlockSpec(memory_space=pltpu.VMEM)


def smem():
    return pl.BlockSpec(memory_space=pltpu.SMEM)


def call(kernel, outs, args, scalars=0, loose=0, scratch=()):
    return pl.pallas_call(
        kernel,
        out_shape=outs,
        in_specs=[smem()] * scalars
        + [pl.BlockSpec(memory_space=pl.ANY)] * loose
        + [vmem()] * (len(args) - scalars - loose),
        out_specs=jax.tree.map(lambda _: vmem(), outs),
        scratch_shapes=list(scratch),
        compiler_params=pltpu.CompilerParams(vmem_limit_bytes=VMEM_LIMIT),
    )(*args)


def f32(*shape):
    return jax.ShapeDtypeStruct(shape, jnp.float32)


def repeat(blocks, body, init):
    if blocks == 8:
        return body(slice(0, 8), 0, init)
    return lax.fori_loop(
        0, blocks // 8, lambda step, carry: body(pl.ds(pl.multiple_of(8 * step, 8), 8), 8 * step, carry), init
    )


def one_row(ref, lead, group, first, row, lanes=slice(None)):
    if isinstance(first, int):
        return ref[(*lead, slice(first + row, first + row + 1), lanes)]
    return ref[(*lead, group, lanes)][row : row + 1]


def project_cone(trial):
    center = 0.5 * (trial[0] + trial[1])
    spread = 0.5 * (trial[0] - trial[1])
    shear = trial[2]
    radius = jnp.sqrt(spread * spread + shear * shear)
    upper = center + radius
    lower = center - radius
    iso_part = 0.5 * (jnp.maximum(upper, 0.0) + jnp.maximum(lower, 0.0))
    factor = jnp.clip((center + radius) / (2.0 * jnp.maximum(radius, 0.05)), 0.0, 1.0)
    return (iso_part + factor * spread, iso_part - factor * spread, factor * shear)


def fetch(pairs, sems):
    copies = [pltpu.make_async_copy(source, target, sems.at[at]) for at, (source, target) in enumerate(pairs)]
    for copy in copies:
        copy.start()
    for copy in copies:
        copy.wait()


def in_hbm(*values):
    return tuple(pltpu.with_memory_space_constraint(value, pltpu.HBM) for value in values)


def nodes_kernel(speed_in, mobility_in, seam_in, gap_u, ahead, speed, mobility, seam, sems):
    depth = gap_u.shape[1]
    start = ahead.shape[0] - 3 * depth
    gaps = [(gap_u.at[c], ahead.at[pl.ds(start + depth * c, depth)]) for c in range(3)]
    fetch(((speed_in, speed), (mobility_in, mobility), (seam_in, seam), *gaps), sems)
    own = speed.shape[1]
    ahead[0:3, :] = speed[...]
    ahead[3:4, :] = mobility[...]
    ahead[4:8, :] = jnp.zeros((4, own), jnp.float32)
    for row in range(8, start):
        ahead[row : row + 1, :] = seam[:, (row - 8) * own : (row - 7) * own].astype(jnp.float32)


def base_kernel(counts, after, *refs):
    count = (len(refs) - 2) // 2
    sources, base, held, sems = refs[:count], refs[count], refs[count + 1 : -1], refs[-1]
    fetch(zip(sources, held), sems)
    strain, dual, speed, load, mobility, corners = held
    own = speed.shape[1]
    slot = lax.broadcasted_iota(jnp.int32, (1, own), 1)
    alive = (slot < counts[0]).astype(jnp.float32)
    base[STRAIN:DUAL, :] = strain[...] * alive
    base[DUAL : DUAL + 3, :] = dual[...] * alive
    base[STEP : STEP + 1, :] = mobility[...]
    base[SPEED : SPEED + 3, :] = speed[...]
    base[LOAD : LOAD + 3, :] = load[...]
    base[NEXT_STEP:INDEX, :] = jnp.zeros((INDEX - NEXT_STEP, own), jnp.float32)
    base[INDEX : INDEX + 4, :] = corners[...].astype(jnp.float32)


def message_kernel(sector_nodes, depth, after, ahead, base, message, *shorter):
    own = message.shape[1]
    halves = own // LANES
    message[:NEXT_STEP, :] = base[:NEXT_STEP, :]
    message[NEXT_STEP : NEXT_STEP + 1, :] = ahead[3:4, :]
    message[NEXT_SPEED : NEXT_SPEED + 3, :] = ahead[0:3, :]
    message[INDEX + 4 :, :] = jnp.zeros((ROWS - INDEX - 4, own), jnp.float32)
    corners = base[INDEX : INDEX + 4, :].astype(jnp.int32)
    corner = jnp.concatenate([corners[:, h * LANES : (h + 1) * LANES] for h in range(halves)], axis=0)
    seam_rows = ahead.shape[0] - 8 - 3 * depth
    place = jnp.clip(corner - sector_nodes, 0, seam_rows * own - 1)
    high, low = place // LANES, place % LANES
    found = jnp.zeros(corner.shape, jnp.float32)
    for row in range(seam_rows):
        for h in range(halves):
            table = jnp.broadcast_to(ahead[8 + row : 9 + row, h * LANES : (h + 1) * LANES], corner.shape)
            value = jnp.take_along_axis(table, low, axis=1, mode="promise_in_bounds")
            found = jnp.where(high == row * halves + h, value, found)
    node = jnp.where(corner < sector_nodes, corner.astype(jnp.float32), found + float(sector_nodes))
    for h in range(halves):
        message[INDEX : INDEX + 4, h * LANES : (h + 1) * LANES] = node[4 * h : 4 * h + 4]
    for other in shorter:
        other[...] = message[: other.shape[0], :]


def history_kernel(after, gap_w, gap_u, history, sems):
    fetch(((gap_w, history.at[0:3]), (gap_u, history.at[3:6])), sems)


def wide_kernel(message, gaps, ahead, wide):
    depth = gaps.shape[1]
    start = ahead.shape[0] - 3 * depth
    wide[:ROWS, :] = message[...]
    for kind in range(6):
        wide[ROWS + depth * kind : ROWS + depth * (kind + 1), :] = gaps[kind]
    wide[ROWS + 6 * depth :, :] = ahead[start:, :]


def stack_kernel(*refs):
    stacked = refs[-1]
    for at, piece in enumerate(refs[:-1]):
        stacked[at * ROWS : at * ROWS + piece.shape[0], :] = piece[...]
        if piece.shape[0] < ROWS:
            start = at * ROWS + piece.shape[0]
            stacked[start : (at + 1) * ROWS, :] = jnp.zeros(((at + 1) * ROWS - start, piece.shape[1]), jnp.float32)


def pair_kernel(*refs):
    left, right, joined = refs[-3:]
    joined[0] = left[ROWS:, :]
    joined[1] = right[ROWS:, :]


def copy_kernel(*refs):
    value, copied = refs[-2:]
    copied[...] = value[...]


def join_kernel(*refs):
    left, right, joined = refs[-3:]
    count = left.shape[0]
    joined[:count] = left[...]
    joined[count:] = right[...]


def sweep(strain_row, index, work, dual):
    table, terms, codes, nearby = work
    blocks, own = index.shape[1:]
    halves = own // LANES
    here = lax.axis_index("dom")
    row = lax.broadcasted_iota(jnp.int32, (blocks, LANES), 0)
    left_block = ((row ^ here) - 1) ^ here
    right_block = ((row ^ here) + 1) ^ here

    def wide(j, group, first, block, part):
        piece = one_row(table, (j,), group, first, block, slice(part * LANES, (part + 1) * LANES))
        return jnp.broadcast_to(piece, (blocks, LANES))

    def take_sides(group, first, sides):
        left, right = (list(side) for side in sides)
        for block in range(8):
            for j in range(3):
                left[j] = jnp.where(left_block == first + block, wide(j, group, first, block, halves - 1), left[j])
                right[j] = jnp.where(right_block == first + block, wide(j, group, first, block, 0), right[j])
        return tuple(left), tuple(right)

    blank = tuple(jnp.zeros((blocks, LANES), jnp.float32) for _ in range(3))
    left, right = repeat(blocks, take_sides, (blank, blank))
    places = list(itertools.product(range(4), range(halves)))
    highs, lows, found = [], [], []
    for k, h in places:
        number = index[k, :, h * LANES : (h + 1) * LANES]
        highs.append(number // LANES)
        lows.append(number % LANES)

        def take(value):
            return jnp.take_along_axis(value, lows[-1], axis=1, mode="promise_in_bounds")

        near = [take(table[j, :, 0:LANES]) for j in range(3)]
        for part in range(1, halves):
            mask = highs[-1] % halves == part
            near = [jnp.where(mask, take(table[j, :, part * LANES : (part + 1) * LANES]), near[j]) for j in range(3)]
        mask = number // own == left_block
        near = [jnp.where(mask, take(left[j]), near[j]) for j in range(3)]
        mask = number // own == right_block
        found += [jnp.where(mask, take(right[j]), near[j]) for j in range(3)]

    def take_group(group, first, found):
        found = list(found)
        for part, block in itertools.product(range(halves), range(8)):
            rows = [wide(3 + j, group, first, block, part) for j in range(3)]
            for at in range(len(places)):
                mask = highs[at] == (blocks + first + block) * halves + part
                for j in range(3):
                    value = jnp.take_along_axis(rows[j], lows[at], axis=1, mode="promise_in_bounds")
                    found[3 * at + j] = jnp.where(mask, value, found[3 * at + j])
        return tuple(found)

    found = repeat(blocks, take_group, tuple(found))
    speed = [
        [jnp.concatenate([found[3 * (halves * k + h) + j] for h in range(halves)], axis=1) for j in range(3)]
        for k in range(4)
    ]
    rate = []
    for c in range(3):
        total = None
        for k in range(4):
            for j in range(3):
                term = strain_row(12 * c + 3 * k + j) * speed[k][j]
                total = term if total is None else total + term
        rate.append(total)
    trial = [rate[c] + dual[c] for c in range(3)]
    cone = project_cone(trial)
    dual_next = [trial[c] - cone[c] for c in range(3)]
    misfit = [rate[c] - cone[c] + dual_next[c] for c in range(3)]
    for k in range(4):
        for j in range(3):
            rest = sum(strain_row(12 * c + 3 * k + j) * misfit[c] for c in range(3))
            for split in range(SPLITS):
                term = rest.astype(jnp.bfloat16).astype(jnp.float32)
                terms[SPLITS * j + split, k] = term
                rest = rest - term

    near_rows = halves + 2
    next_rows = halves * blocks
    row_wide = lax.broadcasted_iota(jnp.int32, (blocks, own), 0) ^ here
    for k in range(4):
        number = index[k]
        block_of, half = number // own, number // LANES % halves
        near = jnp.where(block_of == ((row_wide - 1) ^ here), 0, 1 + half)
        near = jnp.where(block_of == ((row_wide + 1) ^ here), 1 + halves, near)
        codes[0, k] = (number % LANES).astype(jnp.float32)
        codes[1, k] = jnp.where(block_of < blocks, near, -1).astype(jnp.float32)
        codes[2, k] = jnp.where(block_of < blocks, -1, half * blocks + block_of - blocks).astype(jnp.float32)

    values = 3 * SPLITS
    per_tile = 16 // near_rows
    near_tiles = -(-values // per_tile)
    iota = lax.broadcasted_iota(jnp.int32, (16, own), 0)
    near_iota = (iota % near_rows).astype(jnp.float32).astype(jnp.bfloat16)
    value_iota = (iota // near_rows).astype(jnp.float32).astype(jnp.bfloat16)
    value_masks = [value_iota == jnp.full((16, own), float(at), jnp.bfloat16) for at in range(per_tile)]
    iota = iota.astype(jnp.float32)
    low_iota = [(iota + float(16 * g)).astype(jnp.bfloat16) for g in range(LANES // 16)]
    next_iota = [(iota + float(16 * g)).astype(jnp.bfloat16) for g in range(next_rows // 16)]
    one = jnp.ones((16, own), jnp.bfloat16)
    zero = jnp.zeros((16, own), jnp.bfloat16)

    def spread_row(value):
        return jnp.broadcast_to(value, (16, own)).astype(jnp.bfloat16)

    def add_group(group, first, total):
        for block in range(8):
            part = None
            for k in range(4):
                low_row, near_row, next_row = (
                    spread_row(one_row(codes, (at, k), group, first, block)) for at in range(3)
                )
                rows = [spread_row(one_row(terms, (at, k), group, first, block)) for at in range(values)]
                spread = jnp.concatenate([jnp.where(low_row == value, one, zero) for value in low_iota], axis=0)
                mask = near_row == near_iota
                weights = []
                for tile in range(near_tiles):
                    inside = rows[tile * per_tile : (tile + 1) * per_tile]
                    value = inside[-1]
                    for at in range(len(inside) - 1):
                        value = jnp.where(value_masks[at], inside[at], value)
                    weights.append(jnp.where(mask, value, zero))
                masks = [next_row == value for value in next_iota]
                weights += [jnp.where(mask, row, zero) for row in rows for mask in masks]
                product = lax.dot_general(
                    jnp.concatenate(weights, axis=0),
                    spread,
                    (((1,), (1,)), ((), ())),
                    preferred_element_type=jnp.float32,
                )
                part = product if part is None else part + product
            start = (first + block) * 16 * near_tiles
            if not isinstance(start, int):
                start = pl.multiple_of(start, 16)
            nearby[pl.ds(start, 16 * near_tiles), :] = part[: 16 * near_tiles]
            total += part[16 * near_tiles :]
        return total

    total = repeat(blocks, add_group, jnp.zeros((values * next_rows, LANES), jnp.float32))

    def near_force(j, row):
        return sum(
            nearby[pl.ds((SPLITS * j + split) * near_rows + row, blocks, stride=16 * near_tiles), :]
            for split in range(SPLITS)
        )

    force_own, force_next = [], []
    for j in range(3):
        halves_own = [near_force(j, 1 + h) for h in range(halves)]
        to_left, to_right = near_force(j, 0), near_force(j, 1 + halves)
        from_right = from_left = jnp.zeros((blocks, LANES), jnp.float32)
        for block in range(blocks):
            wide_left = jnp.broadcast_to(to_left[block : block + 1], (blocks, LANES))
            wide_right = jnp.broadcast_to(to_right[block : block + 1], (blocks, LANES))
            from_right = jnp.where(right_block == block, wide_left, from_right)
            from_left = jnp.where(left_block == block, wide_right, from_left)
        halves_own[-1] = halves_own[-1] + from_right
        halves_own[0] = halves_own[0] + from_left
        force_own.append(jnp.concatenate(halves_own, axis=1))
        whole = sum(
            total[(SPLITS * j + split) * next_rows : (SPLITS * j + split + 1) * next_rows] for split in range(SPLITS)
        )
        force_next.append(jnp.concatenate([whole[h * blocks : (h + 1) * blocks] for h in range(halves)], axis=1))
    return dual_next, force_own, force_next


def stack_block(piece, slot, rows, stack):
    held = min(rows, piece.shape[0])
    for h in range(stack.shape[0]):
        stack[h, slot * rows : slot * rows + held, :] = piece[:held, h * LANES : (h + 1) * LANES]


def across(stack, row, rows):
    blocks = stack.shape[1] // rows
    return jnp.concatenate(
        [stack[h, pl.ds(row, blocks, stride=rows), :] for h in range(stack.shape[0])], axis=1
    )


def first_kernel(blocks, order, *refs):
    pieces = refs[: len(order)]
    state, index, to_near, to_far, stack = refs[blocks : blocks + 5]
    work = refs[blocks + 5 :]
    table = work[0]
    own = index.shape[2]
    for piece, (start, slot) in zip(pieces, order):
        stack_block(piece.at[start : min(start + ROWS, piece.shape[0])], slot, ROWS, stack)
    flip = lax.axis_index("dom") * own
    even = lax.axis_index("sector") % 2 == 0
    for k in range(4):
        index[k] = across(stack, INDEX + k, ROWS).astype(jnp.int32) ^ flip
    for row in range(36):
        state[row] = across(stack, STRAIN + row, ROWS)
    step = across(stack, STEP, ROWS)
    state[STEP] = step
    state[KEPT_NEXT_STEP] = across(stack, NEXT_STEP, ROWS)
    for j in range(3):
        state[KEPT_LOAD + j] = across(stack, LOAD + j, ROWS)
        table[j] = across(stack, SPEED + j, ROWS)
        table[3 + j] = across(stack, NEXT_SPEED + j, ROWS)
    dual = [across(stack, DUAL + c, ROWS) for c in range(3)]
    dual, force_own, force_next = sweep(lambda row: state[row], index, work, dual)
    for c in range(3):
        state[DUAL + c] = dual[c]
        mine = table[c] - step * (force_own[c] - state[KEPT_LOAD + c])
        to_near[c] = jnp.where(even, force_next[c], mine)
        to_far[c] = jnp.where(even, mine, force_next[c])


def second_kernel(state, index, to_near, to_far, from_far, from_near, vectors, keep, *work):
    table = work[0]
    even = lax.axis_index("sector") % 2 == 0
    step, next_step = state[STEP], state[KEPT_NEXT_STEP]
    for j in range(3):
        near, far = to_near[j], to_far[j]
        near_in, far_in = from_near[j], from_far[j]
        table[j] = jnp.where(even, far, near) - step * jnp.where(even, far_in, near_in)
        table[3 + j] = jnp.where(even, near_in, far_in) - next_step * jnp.where(even, near, far)
    dual = [state[DUAL + c] for c in range(3)]
    dual_next, force_own, force_next = sweep(lambda row: state[row], index, work, dual)
    for c in range(3):
        after = table[c] - step * (force_own[c] - state[KEPT_LOAD + c])
        vectors[c] = after - table[c]
        vectors[3 + c] = -(next_step * force_next[c])
        keep[c] = dual_next[c]
        keep[3 + c] = dual_next[c] - dual[c]
        keep[6 + c] = after


def pairs(depth):
    return [(i, l) for i in range(depth) for l in range(i, depth + 1)]


def gram_kernel(depth, slots, vectors, keep, *refs):
    blocks, own = keep.shape[1:]
    halves = own // LANES
    rows = 9 * depth
    message, stack, rows_sum = refs[len(slots) :]
    for piece, own_slots in zip(refs, slots):
        for at, slot in enumerate(own_slots):
            stack_block(piece.at[at] if len(piece.shape) == 3 else piece.at[ROWS:], slot, rows, stack)
    for row in range(6):
        message[row] = vectors[row]
    message[6] = jnp.zeros((blocks, own), jnp.float32)
    sums, pushed, pushed_twice = {}, [0.0] * (depth + 1), 0.0
    for c, h, top in itertools.product(range(3), range(halves), range(0, blocks, 8)):
        lanes, group = slice(h * LANES, (h + 1) * LANES), slice(top, top + 8)

        def gap(kind, i):
            return stack[h, pl.ds(top * rows + depth * (3 * kind + c) + i, 8, stride=rows), :]

        for kind, moved in enumerate((keep[3 + c, group, lanes], vectors[c, group, lanes])):
            gaps = [moved - gap(kind, i) for i in range(depth)] + [moved]
            for i, l in pairs(depth):
                term = gaps[i] * gaps[l]
                sums[i, l] = sums[i, l] + term if (i, l) in sums else term
        push = vectors[3 + c, group, lanes]
        for i in range(depth):
            pushed[i] = pushed[i] + gap(2, i) * push
        pushed_twice = pushed_twice + push * push
    for at, (i, l) in enumerate(pairs(depth)):
        value = sums[i, l] + pushed_twice - pushed[i] - pushed[l]
        rows_sum[at : at + 1, :] = jnp.sum(value, axis=0, keepdims=True)
    count = len(pairs(depth))
    if rows_sum.shape[0] > count:
        rows_sum[count:, :] = jnp.zeros((rows_sum.shape[0] - count, LANES), jnp.float32)
    whole = jnp.broadcast_to(jnp.sum(rows_sum[...], axis=1, keepdims=True), rows_sum.shape)
    lane = lax.broadcasted_iota(jnp.int32, (8, LANES), 1)
    out = whole[0:8]
    for group in range(1, rows_sum.shape[0] // 8):
        out = jnp.where(lane == group, whole[8 * group : 8 * group + 8], out)
    message[6, 0:8, 0:LANES] = out


def solve_kernel(depth, square, *refs):
    parts = refs[:-8]
    keep, past_w, gap_w, past_u, gap_u, new_u, new_w, total = refs[-8:]
    own = new_u.shape[1]
    tile = parts[0][6, 0:8, 0:LANES]
    for other in parts[1:]:
        tile = tile + other[6, 0:8, 0:LANES]
    even = lax.axis_index("sector") % 2 == 0

    def ahead(by, row):
        if square and by in (1, 3):
            return jnp.where(even, parts[by][row], parts[4 - by][row])
        return parts[by][row]

    sectors = len(parts)
    pushes = [[ahead(by, 3 + j) for j in range(3)] for by in range(sectors)]
    cross = sum(ahead(by, j) * pushes[by - 1][j] for by in range(sectors) for j in range(3))
    cross = jnp.sum(jnp.sum(cross, axis=0, keepdims=True), axis=1, keepdims=True)
    last = [keep[6 + j, 0:1] + pushes[-1][j][0:1] for j in range(3)] + [keep[c, 0:1] for c in range(3)]
    for group in range(total.shape[0] // 8):
        total[8 * group : 8 * group + 8, :] = jnp.broadcast_to(tile[:, group : group + 1], (8, LANES))
    matrix = {
        pair: jnp.broadcast_to(total[at : at + 1, :], (depth, LANES)) + 2.0 * cross
        for at, pair in enumerate(pairs(depth))
    }
    ridge = 0.0001 * sum(matrix[i, i] for i in range(depth)) / depth
    for i in range(depth):
        matrix[i, i] = matrix[i, i] + ridge
    inverse = []
    for step in range(depth):
        inverse.append(1.0 / matrix[step, step])
        for i in range(step + 1, depth):
            factor = matrix[step, i] * inverse[step]
            for l in range(i, depth + 1):
                matrix[i, l] = matrix[i, l] - factor * matrix[step, l]
    weights = [None] * depth
    for i in reversed(range(depth)):
        value = matrix[i, depth]
        for l in range(i + 1, depth):
            value = value - matrix[i, l] * weights[l]
        weights[i] = value * inverse[i]
    row = lax.broadcasted_iota(jnp.int32, (depth, LANES), 0)
    weight = weights[0]
    for i in range(1, depth):
        weight = jnp.where(row == i, weights[i], weight)
    for start in range(0, own, LANES):
        lanes = slice(start, start + LANES)
        for at, (past, gap, out) in enumerate(((past_u, gap_u, new_u), (past_w, gap_w, new_w))):
            for c in range(3):
                value = jnp.broadcast_to(last[3 * at + c][:, lanes], (depth, LANES))
                change = weight * (value - past[c, :, lanes] - gap[c, :, lanes])
                out[c : c + 1, lanes] = value[0:1] - jnp.sum(change, axis=0, keepdims=True)


def per_device(
    strain_map,
    corner_nodes,
    counts,
    seam_nodes,
    velocity,
    dual_state,
    nodal_load,
    mobility,
    past_dual,
    past_dual_gap,
    past_velocity,
    past_velocity_gap,
):
    own = velocity.shape[1]
    halves = own // LANES
    blocks = lax.axis_size("dom")
    sectors = lax.axis_size("sector")
    depth = past_dual.shape[0]
    seam_rows = seam_nodes.shape[1] // own
    mobility = mobility.reshape(1, own)
    past_dual, past_dual_gap, past_velocity, past_velocity_gap = (
        value.transpose(1, 0, 2) for value in (past_dual, past_dual_gap, past_velocity, past_velocity_gap)
    )

    def send(value, target):
        return lax.ppermute(value, "sector", [(i, target(i) % sectors) for i in range(sectors)])

    def swap(value, bits):
        return lax.ppermute(value, "dom", [(i, i ^ bits) for i in range(blocks)])

    nodes = (velocity, mobility, seam_nodes)
    ahead = call(
        nodes_kernel,
        f32(8 + seam_rows + 3 * depth, own),
        in_hbm(*nodes, past_velocity_gap),
        loose=len(nodes) + 1,
        scratch=[pltpu.VMEM(value.shape, value.dtype) for value in nodes]
        + [pltpu.SemaphoreType.DMA((len(nodes) + 3,))],
    )
    held = (strain_map, dual_state, velocity, nodal_load, mobility, corner_nodes)
    base = call(
        base_kernel,
        f32(INDEX + 4, own),
        (counts, ahead, *in_hbm(*held)),
        scalars=1,
        loose=len(held) + 1,
        scratch=[pltpu.VMEM(value.shape, value.dtype) for value in held] + [pltpu.SemaphoreType.DMA((len(held),))],
    )
    ahead = send(ahead, lambda i: i - 1)
    history = call(
        history_kernel,
        f32(6, depth, own),
        (base, *in_hbm(past_dual_gap, past_velocity_gap)),
        loose=3,
        scratch=[pltpu.SemaphoreType.DMA((2,))],
    )
    far_ones = list(range(blocks - 2, 2, -2))
    lengths = [max(INDEX + 4, ROWS - place) for place in range(len(far_ones))]
    messages = call(
        functools.partial(message_kernel, own * blocks, depth),
        tuple(f32(rows, own) for rows in sorted(set(lengths), reverse=True)),
        (history, ahead, base),
        loose=1,
    )
    wide = call(wide_kernel, f32(ROWS + 9 * depth, own), (messages[0], history, ahead))
    pieces = {0: wide}
    for bits, rows in zip(far_ones, lengths):
        pieces[bits] = swap(next(value for value in messages if value.shape[0] == rows), bits)
    pieces[2] = swap(wide, 2)
    for even in (0, 2):
        pieces[even + 1] = swap(pieces[even], 1)
    count = len(far_ones)
    crossed = swap(
        call(stack_kernel, f32(count * ROWS, own), tuple(pieces[bits] for bits in far_ones)), 1
    )
    histories, slots = [pieces[block] for block in range(4)], [(block,) for block in range(4)]
    history = call(
        pair_kernel, f32(2, 9 * depth, own), (*(pieces[bits] for bits in far_ones), wide, pieces[2]), loose=len(far_ones)
    )
    known, apart, later = (0, 2), 4, []
    while apart < blocks:
        other = swap(history, apart)
        later.append((other, tuple(slot ^ apart for slot in known)))
        known += later[-1][1]
        apart *= 2
        if apart < blocks:
            history = call(join_kernel, f32(2 * history.shape[0], 9 * depth, own), (history, other))
    order = [(at * ROWS, bits + 1) for at, bits in enumerate(far_ones)]
    order += [(0, block) for block in reversed(range(blocks)) if block in pieces]
    sector = f32(3, blocks, own)
    work = [
        pltpu.VMEM((6, blocks, own), jnp.float32),
        pltpu.VMEM((3 * SPLITS, 4, blocks, own), jnp.float32),
        pltpu.VMEM((3, 4, blocks, own), jnp.float32),
        pltpu.VMEM((blocks * 16 * -(-3 * SPLITS * (halves + 2) // 16), LANES), jnp.float32),
    ]
    state, index, to_near, to_far = call(
        functools.partial(first_kernel, blocks, order),
        (f32(KEPT, blocks, own), jax.ShapeDtypeStruct((4, blocks, own), jnp.int32), sector, sector),
        (*([crossed] * count), *(pieces[block] for _, block in order[count:])),
        scratch=[pltpu.VMEM((halves, blocks * ROWS, LANES), jnp.float32), *work],
    )
    from_far = send(to_far, lambda i: i + 1 if i % 2 else i - 1)
    from_near = send(to_near, lambda i: i ^ 1)
    for other, far in later:
        held_back = call(copy_kernel, f32(*other.shape), (from_near, from_far, other), loose=2)
        histories += [other, swap(held_back, 1)]
        slots += [far, tuple(slot ^ 1 for slot in far)]
    vectors, keep = call(
        second_kernel,
        (f32(6, blocks, own), f32(9, blocks, own)),
        (state, index, to_near, to_far, from_far, from_near),
        scratch=work,
    )
    count = -(-len(pairs(depth)) // 8) * 8
    message = call(
        functools.partial(gram_kernel, depth, tuple(slots)),
        f32(7, blocks, own),
        (vectors, keep, *histories),
        scratch=[
            pltpu.VMEM((halves, blocks * 9 * depth, LANES), jnp.float32),
            pltpu.VMEM((count, LANES), jnp.float32),
        ],
    )
    square = sectors == 4
    parts = [message] + [None] * (sectors - 1)
    for by in sorted(range(1, sectors), reverse=True):
        parts[by] = send(message, (lambda i: i ^ by) if square else (lambda i: i - by))
    return call(
        functools.partial(solve_kernel, depth, square),
        (f32(3, own), f32(3, own)),
        (*parts, keep, past_dual, past_dual_gap, past_velocity, past_velocity_gap),
        scratch=[pltpu.VMEM((count, LANES), jnp.float32)],
    )


def solution(mesh):
    in_specs = (
        P(None, ("sector", "dom")),
        P(None, ("sector", "dom")),
        P(("sector", "dom")),
        P("sector", None),
        P(None, ("sector", "dom")),
        P(None, ("sector", "dom")),
        P(None, ("sector", "dom")),
        P(("sector", "dom")),
        P(None, None, ("sector", "dom")),
        P(None, None, ("sector", "dom")),
        P(None, None, ("sector", "dom")),
        P(None, None, ("sector", "dom")),
    )
    out_specs = (P(None, ("sector", "dom")), P(None, ("sector", "dom")))
    return jax.shard_map(
        per_device, mesh=mesh, in_specs=in_specs, out_specs=out_specs, check_vma=False
    )
```

```python
import functools
import itertools

import jax
import jax.numpy as jnp
from jax import lax
from jax.experimental import pallas as pl
from jax.experimental.pallas import tpu as pltpu
from jax.sharding import PartitionSpec as P

LANES = 128
VMEM_LIMIT = 24 * 1024 * 1024

STRAIN, DUAL, STEP, SPEED, LOAD, NEXT_STEP, NEXT_SPEED, INDEX, ROWS = 0, 36, 39, 40, 43, 46, 47, 50, 56
KEPT_NEXT_STEP, KEPT_LOAD, KEPT = 40, 41, 44
SPLITS = 2


def vmem():
    return pl.BlockSpec(memory_space=pltpu.VMEM)


def smem():
    return pl.BlockSpec(memory_space=pltpu.SMEM)


def call(kernel, outs, args, scalars=0, loose=0, scratch=()):
    return pl.pallas_call(
        kernel,
        out_shape=outs,
        in_specs=[smem()] * scalars
        + [pl.BlockSpec(memory_space=pl.ANY)] * loose
        + [vmem()] * (len(args) - scalars - loose),
        out_specs=jax.tree.map(lambda _: vmem(), outs),
        scratch_shapes=list(scratch),
        compiler_params=pltpu.CompilerParams(vmem_limit_bytes=VMEM_LIMIT),
    )(*args)


def f32(*shape):
    return jax.ShapeDtypeStruct(shape, jnp.float32)


def repeat(blocks, body, init):
    if blocks == 8:
        return body(slice(0, 8), 0, init)
    return lax.fori_loop(
        0, blocks // 8, lambda step, carry: body(pl.ds(pl.multiple_of(8 * step, 8), 8), 8 * step, carry), init
    )


def one_row(ref, lead, group, first, row, lanes=slice(None)):
    if isinstance(first, int):
        return ref[(*lead, slice(first + row, first + row + 1), lanes)]
    return ref[(*lead, group, lanes)][row : row + 1]


def project_cone(trial):
    center = 0.5 * (trial[0] + trial[1])
    spread = 0.5 * (trial[0] - trial[1])
    shear = trial[2]
    radius = jnp.sqrt(spread * spread + shear * shear)
    upper = center + radius
    lower = center - radius
    iso_part = 0.5 * (jnp.maximum(upper, 0.0) + jnp.maximum(lower, 0.0))
    factor = jnp.clip((center + radius) / (2.0 * jnp.maximum(radius, 0.05)), 0.0, 1.0)
    return (iso_part + factor * spread, iso_part - factor * spread, factor * shear)


def fetch(pairs, sems):
    copies = [pltpu.make_async_copy(source, target, sems.at[at]) for at, (source, target) in enumerate(pairs)]
    for copy in copies:
        copy.start()
    for copy in copies:
        copy.wait()


def in_hbm(*values):
    return tuple(pltpu.with_memory_space_constraint(value, pltpu.HBM) for value in values)


def nodes_kernel(speed_in, mobility_in, seam_in, gap_u, ahead, speed, mobility, seam, sems):
    depth = gap_u.shape[1]
    start = ahead.shape[0] - 3 * depth
    gaps = [(gap_u.at[c], ahead.at[pl.ds(start + depth * c, depth)]) for c in range(3)]
    fetch(((speed_in, speed), (mobility_in, mobility), (seam_in, seam), *gaps), sems)
    own = speed.shape[1]
    ahead[0:3, :] = speed[...]
    ahead[3:4, :] = mobility[...]
    ahead[4:8, :] = jnp.zeros((4, own), jnp.float32)
    for row in range(8, start):
        ahead[row : row + 1, :] = seam[:, (row - 8) * own : (row - 7) * own].astype(jnp.float32)


def base_kernel(counts, after, *refs):
    count = (len(refs) - 5) // 2
    sources, gaps = refs[:count], refs[count : count + 2]
    base, history, held, sems = refs[count + 2], refs[count + 3], refs[count + 4 : -1], refs[-1]
    fetch((*zip(sources, held), (gaps[0], history.at[0:3]), (gaps[1], history.at[3:6])), sems)
    strain, dual, speed, load, mobility, corners = held
    own = speed.shape[1]
    slot = lax.broadcasted_iota(jnp.int32, (1, own), 1)
    alive = (slot < counts[0]).astype(jnp.float32)
    base[STRAIN:DUAL, :] = strain[...] * alive
    base[DUAL : DUAL + 3, :] = dual[...] * alive
    base[STEP : STEP + 1, :] = mobility[...]
    base[SPEED : SPEED + 3, :] = speed[...]
    base[LOAD : LOAD + 3, :] = load[...]
    base[NEXT_STEP:INDEX, :] = jnp.zeros((INDEX - NEXT_STEP, own), jnp.float32)
    base[INDEX : INDEX + 4, :] = corners[...].astype(jnp.float32)


def message_kernel(sector_nodes, depth, after, ahead, base, message, *shorter):
    own = message.shape[1]
    halves = own // LANES
    message[:NEXT_STEP, :] = base[:NEXT_STEP, :]
    message[NEXT_STEP : NEXT_STEP + 1, :] = ahead[3:4, :]
    message[NEXT_SPEED : NEXT_SPEED + 3, :] = ahead[0:3, :]
    message[INDEX + 4 :, :] = jnp.zeros((ROWS - INDEX - 4, own), jnp.float32)
    corners = base[INDEX : INDEX + 4, :].astype(jnp.int32)
    corner = jnp.concatenate([corners[:, h * LANES : (h + 1) * LANES] for h in range(halves)], axis=0)
    seam_rows = ahead.shape[0] - 8 - 3 * depth
    place = jnp.clip(corner - sector_nodes, 0, seam_rows * own - 1)
    high, low = place // LANES, place % LANES
    found = jnp.zeros(corner.shape, jnp.float32)
    for row in range(seam_rows):
        for h in range(halves):
            table = jnp.broadcast_to(ahead[8 + row : 9 + row, h * LANES : (h + 1) * LANES], corner.shape)
            value = jnp.take_along_axis(table, low, axis=1, mode="promise_in_bounds")
            found = jnp.where(high == row * halves + h, value, found)
    node = jnp.where(corner < sector_nodes, corner.astype(jnp.float32), found + float(sector_nodes))
    for h in range(halves):
        message[INDEX : INDEX + 4, h * LANES : (h + 1) * LANES] = node[4 * h : 4 * h + 4]
    for other in shorter:
        other[...] = message[: other.shape[0], :]


def wide_kernel(message, gaps, ahead, wide):
    depth = gaps.shape[1]
    start = ahead.shape[0] - 3 * depth
    wide[:ROWS, :] = message[...]
    for kind in range(6):
        wide[ROWS + depth * kind : ROWS + depth * (kind + 1), :] = gaps[kind]
    wide[ROWS + 6 * depth :, :] = ahead[start:, :]


def stack_kernel(*refs):
    stacked = refs[-1]
    for at, piece in enumerate(refs[:-1]):
        stacked[at * ROWS : at * ROWS + piece.shape[0], :] = piece[...]
        if piece.shape[0] < ROWS:
            start = at * ROWS + piece.shape[0]
            stacked[start : (at + 1) * ROWS, :] = jnp.zeros(((at + 1) * ROWS - start, piece.shape[1]), jnp.float32)


def pair_kernel(*refs):
    left, right, joined = refs[-3:]
    joined[0] = left[ROWS:, :]
    joined[1] = right[ROWS:, :]


def copy_kernel(*refs):
    value, copied = refs[-2:]
    copied[...] = value[...]


def join_kernel(*refs):
    left, right, joined = refs[-3:]
    count = left.shape[0]
    joined[:count] = left[...]
    joined[count:] = right[...]


def sweep(strain_row, index, work, dual):
    table, terms, codes, nearby = work
    blocks, own = index.shape[1:]
    halves = own // LANES
    here = lax.axis_index("dom")
    row = lax.broadcasted_iota(jnp.int32, (blocks, LANES), 0)
    left_block = ((row ^ here) - 1) ^ here
    right_block = ((row ^ here) + 1) ^ here

    def wide(j, group, first, block, part):
        piece = one_row(table, (j,), group, first, block, slice(part * LANES, (part + 1) * LANES))
        return jnp.broadcast_to(piece, (blocks, LANES))

    def take_sides(group, first, sides):
        left, right = (list(side) for side in sides)
        for block in range(8):
            for j in range(3):
                left[j] = jnp.where(left_block == first + block, wide(j, group, first, block, halves - 1), left[j])
                right[j] = jnp.where(right_block == first + block, wide(j, group, first, block, 0), right[j])
        return tuple(left), tuple(right)

    blank = tuple(jnp.zeros((blocks, LANES), jnp.float32) for _ in range(3))
    left, right = repeat(blocks, take_sides, (blank, blank))
    speed = []
    for k in range(4):
        parts = []
        for h in range(halves):
            number = index[k, :, h * LANES : (h + 1) * LANES]
            high, low = number // LANES, number % LANES

            def take(value):
                return jnp.take_along_axis(value, low, axis=1, mode="promise_in_bounds")

            found = [take(table[j, :, 0:LANES]) for j in range(3)]
            for part in range(1, halves):
                mask = high % halves == part
                found = [
                    jnp.where(mask, take(table[j, :, part * LANES : (part + 1) * LANES]), found[j]) for j in range(3)
                ]
            mask = number // own == left_block
            found = [jnp.where(mask, take(left[j]), found[j]) for j in range(3)]
            mask = number // own == right_block
            found = [jnp.where(mask, take(right[j]), found[j]) for j in range(3)]

            def take_group(group, first, found):
                for part, block in itertools.product(range(halves), range(8)):
                    mask = high == (blocks + first + block) * halves + part
                    found = [jnp.where(mask, take(wide(3 + j, group, first, block, part)), found[j]) for j in range(3)]
                return tuple(found)

            parts.append(repeat(blocks, take_group, tuple(found)))
        speed.append([jnp.concatenate([found[j] for found in parts], axis=1) for j in range(3)])
    rate = []
    for c in range(3):
        total = None
        for k in range(4):
            for j in range(3):
                term = strain_row(12 * c + 3 * k + j) * speed[k][j]
                total = term if total is None else total + term
        rate.append(total)
    trial = [rate[c] + dual[c] for c in range(3)]
    cone = project_cone(trial)
    dual_next = [trial[c] - cone[c] for c in range(3)]
    misfit = [rate[c] - cone[c] + dual_next[c] for c in range(3)]
    for k in range(4):
        for j in range(3):
            rest = sum(strain_row(12 * c + 3 * k + j) * misfit[c] for c in range(3))
            for split in range(SPLITS):
                term = rest.astype(jnp.bfloat16).astype(jnp.float32)
                terms[SPLITS * j + split, k] = term
                rest = rest - term

    near_rows = halves + 2
    next_rows = halves * blocks
    row_wide = lax.broadcasted_iota(jnp.int32, (blocks, own), 0) ^ here
    for k in range(4):
        number = index[k]
        block_of, half = number // own, number // LANES % halves
        near = jnp.where(block_of == ((row_wide - 1) ^ here), 0, 1 + half)
        near = jnp.where(block_of == ((row_wide + 1) ^ here), 1 + halves, near)
        codes[0, k] = (number % LANES).astype(jnp.float32)
        codes[1, k] = jnp.where(block_of < blocks, near, -1).astype(jnp.float32)
        codes[2, k] = jnp.where(block_of < blocks, -1, half * blocks + block_of - blocks).astype(jnp.float32)

    values = 3 * SPLITS
    per_tile = 16 // near_rows
    near_tiles = -(-values // per_tile)
    iota = lax.broadcasted_iota(jnp.int32, (16, own), 0)
    near_iota = (iota % near_rows).astype(jnp.float32).astype(jnp.bfloat16)
    value_iota = (iota // near_rows).astype(jnp.float32).astype(jnp.bfloat16)
    value_masks = [value_iota == jnp.full((16, own), float(at), jnp.bfloat16) for at in range(per_tile)]
    iota = iota.astype(jnp.float32)
    low_iota = [(iota + float(16 * g)).astype(jnp.bfloat16) for g in range(LANES // 16)]
    next_iota = [(iota + float(16 * g)).astype(jnp.bfloat16) for g in range(next_rows // 16)]
    one = jnp.ones((16, own), jnp.bfloat16)
    zero = jnp.zeros((16, own), jnp.bfloat16)

    def spread_row(value):
        return jnp.broadcast_to(value, (16, own)).astype(jnp.bfloat16)

    def add_group(group, first, total):
        for block in range(8):
            part = None
            for k in range(4):
                low_row, near_row, next_row = (
                    spread_row(one_row(codes, (at, k), group, first, block)) for at in range(3)
                )
                rows = [spread_row(one_row(terms, (at, k), group, first, block)) for at in range(values)]
                spread = jnp.concatenate([jnp.where(low_row == value, one, zero) for value in low_iota], axis=0)
                mask = near_row == near_iota
                weights = []
                for tile in range(near_tiles):
                    inside = rows[tile * per_tile : (tile + 1) * per_tile]
                    value = inside[-1]
                    for at in range(len(inside) - 1):
                        value = jnp.where(value_masks[at], inside[at], value)
                    weights.append(jnp.where(mask, value, zero))
                masks = [next_row == value for value in next_iota]
                weights += [jnp.where(mask, row, zero) for row in rows for mask in masks]
                product = lax.dot_general(
                    jnp.concatenate(weights, axis=0),
                    spread,
                    (((1,), (1,)), ((), ())),
                    preferred_element_type=jnp.float32,
                )
                part = product if part is None else part + product
            start = (first + block) * 16 * near_tiles
            if not isinstance(start, int):
                start = pl.multiple_of(start, 16)
            nearby[pl.ds(start, 16 * near_tiles), :] = part[: 16 * near_tiles]
            total += part[16 * near_tiles :]
        return total

    total = repeat(blocks, add_group, jnp.zeros((values * next_rows, LANES), jnp.float32))

    def near_force(j, row):
        return sum(
            nearby[pl.ds((SPLITS * j + split) * near_rows + row, blocks, stride=16 * near_tiles), :]
            for split in range(SPLITS)
        )

    force_own, force_next = [], []
    for j in range(3):
        halves_own = [near_force(j, 1 + h) for h in range(halves)]
        to_left, to_right = near_force(j, 0), near_force(j, 1 + halves)
        from_right = from_left = jnp.zeros((blocks, LANES), jnp.float32)
        for block in range(blocks):
            wide_left = jnp.broadcast_to(to_left[block : block + 1], (blocks, LANES))
            wide_right = jnp.broadcast_to(to_right[block : block + 1], (blocks, LANES))
            from_right = jnp.where(right_block == block, wide_left, from_right)
            from_left = jnp.where(left_block == block, wide_right, from_left)
        halves_own[-1] = halves_own[-1] + from_right
        halves_own[0] = halves_own[0] + from_left
        force_own.append(jnp.concatenate(halves_own, axis=1))
        whole = sum(
            total[(SPLITS * j + split) * next_rows : (SPLITS * j + split + 1) * next_rows] for split in range(SPLITS)
        )
        force_next.append(jnp.concatenate([whole[h * blocks : (h + 1) * blocks] for h in range(halves)], axis=1))
    return dual_next, force_own, force_next


def stack_block(piece, slot, rows, stack):
    held = min(rows, piece.shape[0])
    for h in range(stack.shape[0]):
        stack[h, slot * rows : slot * rows + held, :] = piece[:held, h * LANES : (h + 1) * LANES]


def across(stack, row, rows):
    blocks = stack.shape[1] // rows
    return jnp.concatenate(
        [stack[h, pl.ds(row, blocks, stride=rows), :] for h in range(stack.shape[0])], axis=1
    )


def first_kernel(blocks, order, *refs):
    pieces = refs[: len(order)]
    state, index, to_near, to_far, stack = refs[blocks : blocks + 5]
    work = refs[blocks + 5 :]
    table = work[0]
    own = index.shape[2]
    for piece, (start, slot) in zip(pieces, order):
        stack_block(piece.at[start : min(start + ROWS, piece.shape[0])], slot, ROWS, stack)
    flip = lax.axis_index("dom") * own
    even = lax.axis_index("sector") % 2 == 0
    for k in range(4):
        index[k] = across(stack, INDEX + k, ROWS).astype(jnp.int32) ^ flip
    for row in range(36):
        state[row] = across(stack, STRAIN + row, ROWS)
    step = across(stack, STEP, ROWS)
    state[STEP] = step
    state[KEPT_NEXT_STEP] = across(stack, NEXT_STEP, ROWS)
    for j in range(3):
        state[KEPT_LOAD + j] = across(stack, LOAD + j, ROWS)
        table[j] = across(stack, SPEED + j, ROWS)
        table[3 + j] = across(stack, NEXT_SPEED + j, ROWS)
    dual = [across(stack, DUAL + c, ROWS) for c in range(3)]
    dual, force_own, force_next = sweep(lambda row: state[row], index, work, dual)
    for c in range(3):
        state[DUAL + c] = dual[c]
        mine = table[c] - step * (force_own[c] - state[KEPT_LOAD + c])
        to_near[c] = jnp.where(even, force_next[c], mine)
        to_far[c] = jnp.where(even, mine, force_next[c])


def second_kernel(state, index, to_near, to_far, from_far, from_near, vectors, keep, *work):
    table = work[0]
    even = lax.axis_index("sector") % 2 == 0
    step, next_step = state[STEP], state[KEPT_NEXT_STEP]
    for j in range(3):
        near, far = to_near[j], to_far[j]
        near_in, far_in = from_near[j], from_far[j]
        table[j] = jnp.where(even, far, near) - step * jnp.where(even, far_in, near_in)
        table[3 + j] = jnp.where(even, near_in, far_in) - next_step * jnp.where(even, near, far)
    dual = [state[DUAL + c] for c in range(3)]
    dual_next, force_own, force_next = sweep(lambda row: state[row], index, work, dual)
    for c in range(3):
        after = table[c] - step * (force_own[c] - state[KEPT_LOAD + c])
        vectors[c] = after - table[c]
        vectors[3 + c] = -(next_step * force_next[c])
        keep[c] = dual_next[c]
        keep[3 + c] = dual_next[c] - dual[c]
        keep[6 + c] = after


def pairs(depth):
    return [(i, l) for i in range(depth) for l in range(i, depth + 1)]


def gram_kernel(depth, slots, vectors, keep, *refs):
    blocks, own = keep.shape[1:]
    halves = own // LANES
    rows = 9 * depth
    message, stack, rows_sum = refs[len(slots) :]
    for piece, own_slots in zip(refs, slots):
        for at, slot in enumerate(own_slots):
            stack_block(piece.at[at] if len(piece.shape) == 3 else piece.at[ROWS:], slot, rows, stack)
    for row in range(6):
        message[row] = vectors[row]
    message[6] = jnp.zeros((blocks, own), jnp.float32)
    sums, pushed, pushed_twice = {}, [0.0] * (depth + 1), 0.0
    for c, h, top in itertools.product(range(3), range(halves), range(0, blocks, 8)):
        lanes, group = slice(h * LANES, (h + 1) * LANES), slice(top, top + 8)

        def gap(kind, i):
            return stack[h, pl.ds(top * rows + depth * (3 * kind + c) + i, 8, stride=rows), :]

        for kind, moved in enumerate((keep[3 + c, group, lanes], vectors[c, group, lanes])):
            gaps = [moved - gap(kind, i) for i in range(depth)] + [moved]
            for i, l in pairs(depth):
                term = gaps[i] * gaps[l]
                sums[i, l] = sums[i, l] + term if (i, l) in sums else term
        push = vectors[3 + c, group, lanes]
        for i in range(depth):
            pushed[i] = pushed[i] + gap(2, i) * push
        pushed_twice = pushed_twice + push * push
    for at, (i, l) in enumerate(pairs(depth)):
        value = sums[i, l] + pushed_twice - pushed[i] - pushed[l]
        rows_sum[at : at + 1, :] = jnp.sum(value, axis=0, keepdims=True)
    count = len(pairs(depth))
    if rows_sum.shape[0] > count:
        rows_sum[count:, :] = jnp.zeros((rows_sum.shape[0] - count, LANES), jnp.float32)
    whole = jnp.broadcast_to(jnp.sum(rows_sum[...], axis=1, keepdims=True), rows_sum.shape)
    lane = lax.broadcasted_iota(jnp.int32, (8, LANES), 1)
    out = whole[0:8]
    for group in range(1, rows_sum.shape[0] // 8):
        out = jnp.where(lane == group, whole[8 * group : 8 * group + 8], out)
    message[6, 0:8, 0:LANES] = out


def solve_kernel(depth, square, *refs):
    parts = refs[:-8]
    keep, past_w, gap_w, past_u, gap_u, new_u, new_w, total = refs[-8:]
    own = new_u.shape[1]
    tile = parts[0][6, 0:8, 0:LANES]
    for other in parts[1:]:
        tile = tile + other[6, 0:8, 0:LANES]
    even = lax.axis_index("sector") % 2 == 0

    def ahead(by, row):
        if square and by in (1, 3):
            return jnp.where(even, parts[by][row], parts[4 - by][row])
        return parts[by][row]

    sectors = len(parts)
    pushes = [[ahead(by, 3 + j) for j in range(3)] for by in range(sectors)]
    cross = sum(ahead(by, j) * pushes[by - 1][j] for by in range(sectors) for j in range(3))
    cross = jnp.sum(jnp.sum(cross, axis=0, keepdims=True), axis=1, keepdims=True)
    last = [keep[6 + j, 0:1] + pushes[-1][j][0:1] for j in range(3)] + [keep[c, 0:1] for c in range(3)]
    for group in range(total.shape[0] // 8):
        total[8 * group : 8 * group + 8, :] = jnp.broadcast_to(tile[:, group : group + 1], (8, LANES))
    matrix = {
        pair: jnp.broadcast_to(total[at : at + 1, :], (depth, LANES)) + 2.0 * cross
        for at, pair in enumerate(pairs(depth))
    }
    ridge = 0.0001 * sum(matrix[i, i] for i in range(depth)) / depth
    for i in range(depth):
        matrix[i, i] = matrix[i, i] + ridge
    inverse = []
    for step in range(depth):
        inverse.append(1.0 / matrix[step, step])
        for i in range(step + 1, depth):
            factor = matrix[step, i] * inverse[step]
            for l in range(i, depth + 1):
                matrix[i, l] = matrix[i, l] - factor * matrix[step, l]
    weights = [None] * depth
    for i in reversed(range(depth)):
        value = matrix[i, depth]
        for l in range(i + 1, depth):
            value = value - matrix[i, l] * weights[l]
        weights[i] = value * inverse[i]
    row = lax.broadcasted_iota(jnp.int32, (depth, LANES), 0)
    weight = weights[0]
    for i in range(1, depth):
        weight = jnp.where(row == i, weights[i], weight)
    for start in range(0, own, LANES):
        lanes = slice(start, start + LANES)
        for at, (past, gap, out) in enumerate(((past_u, gap_u, new_u), (past_w, gap_w, new_w))):
            for c in range(3):
                value = jnp.broadcast_to(last[3 * at + c][:, lanes], (depth, LANES))
                change = weight * (value - past[c, :, lanes] - gap[c, :, lanes])
                out[c : c + 1, lanes] = value[0:1] - jnp.sum(change, axis=0, keepdims=True)


def per_device(
    strain_map,
    corner_nodes,
    counts,
    seam_nodes,
    velocity,
    dual_state,
    nodal_load,
    mobility,
    past_dual,
    past_dual_gap,
    past_velocity,
    past_velocity_gap,
):
    own = velocity.shape[1]
    halves = own // LANES
    blocks = lax.axis_size("dom")
    sectors = lax.axis_size("sector")
    depth = past_dual.shape[0]
    seam_rows = seam_nodes.shape[1] // own
    mobility = mobility.reshape(1, own)
    past_dual, past_dual_gap, past_velocity, past_velocity_gap = (
        value.transpose(1, 0, 2) for value in (past_dual, past_dual_gap, past_velocity, past_velocity_gap)
    )

    def send(value, target):
        return lax.ppermute(value, "sector", [(i, target(i) % sectors) for i in range(sectors)])

    def swap(value, bits):
        return lax.ppermute(value, "dom", [(i, i ^ bits) for i in range(blocks)])

    nodes = (velocity, mobility, seam_nodes)
    ahead = call(
        nodes_kernel,
        f32(8 + seam_rows + 3 * depth, own),
        in_hbm(*nodes, past_velocity_gap),
        loose=len(nodes) + 1,
        scratch=[pltpu.VMEM(value.shape, value.dtype) for value in nodes]
        + [pltpu.SemaphoreType.DMA((len(nodes) + 3,))],
    )
    held = (strain_map, dual_state, velocity, nodal_load, mobility, corner_nodes)
    base, history = call(
        base_kernel,
        (f32(INDEX + 4, own), f32(6, depth, own)),
        (counts, ahead, *in_hbm(*held, past_dual_gap, past_velocity_gap)),
        scalars=1,
        loose=len(held) + 3,
        scratch=[pltpu.VMEM(value.shape, value.dtype) for value in held]
        + [pltpu.SemaphoreType.DMA((len(held) + 2,))],
    )
    ahead = send(ahead, lambda i: i - 1)
    far_ones = list(range(blocks - 2, 2, -2))
    lengths = [max(INDEX + 4, ROWS - place) for place in range(len(far_ones))]
    messages = call(
        functools.partial(message_kernel, own * blocks, depth),
        tuple(f32(rows, own) for rows in sorted(set(lengths), reverse=True)),
        (history, ahead, base),
        loose=1,
    )
    wide = call(wide_kernel, f32(ROWS + 9 * depth, own), (messages[0], history, ahead))
    pieces = {0: wide}
    for bits, rows in zip(far_ones, lengths):
        pieces[bits] = swap(next(value for value in messages if value.shape[0] == rows), bits)
    pieces[2] = swap(wide, 2)
    for even in (0, 2):
        pieces[even + 1] = swap(pieces[even], 1)
    count = len(far_ones)
    crossed = swap(
        call(stack_kernel, f32(count * ROWS, own), tuple(pieces[bits] for bits in far_ones)), 1
    )
    histories, slots = [pieces[block] for block in range(4)], [(block,) for block in range(4)]
    history = call(
        pair_kernel, f32(2, 9 * depth, own), (*(pieces[bits] for bits in far_ones), wide, pieces[2]), loose=len(far_ones)
    )
    known, apart, later = (0, 2), 4, []
    while apart < blocks:
        other = swap(history, apart)
        later.append((other, tuple(slot ^ apart for slot in known)))
        known += later[-1][1]
        apart *= 2
        if apart < blocks:
            history = call(join_kernel, f32(2 * history.shape[0], 9 * depth, own), (history, other))
    order = [(at * ROWS, bits + 1) for at, bits in enumerate(far_ones)]
    order += [(0, block) for block in reversed(range(blocks)) if block in pieces]
    sector = f32(3, blocks, own)
    work = [
        pltpu.VMEM((6, blocks, own), jnp.float32),
        pltpu.VMEM((3 * SPLITS, 4, blocks, own), jnp.float32),
        pltpu.VMEM((3, 4, blocks, own), jnp.float32),
        pltpu.VMEM((blocks * 16 * -(-3 * SPLITS * (halves + 2) // 16), LANES), jnp.float32),
    ]
    state, index, to_near, to_far = call(
        functools.partial(first_kernel, blocks, order),
        (f32(KEPT, blocks, own), jax.ShapeDtypeStruct((4, blocks, own), jnp.int32), sector, sector),
        (*([crossed] * count), *(pieces[block] for _, block in order[count:])),
        scratch=[pltpu.VMEM((halves, blocks * ROWS, LANES), jnp.float32), *work],
    )
    from_far = send(to_far, lambda i: i + 1 if i % 2 else i - 1)
    from_near = send(to_near, lambda i: i ^ 1)
    for other, far in later:
        held_back = call(copy_kernel, f32(*other.shape), (from_near, from_far, other), loose=2)
        histories += [other, swap(held_back, 1)]
        slots += [far, tuple(slot ^ 1 for slot in far)]
    vectors, keep = call(
        second_kernel,
        (f32(6, blocks, own), f32(9, blocks, own)),
        (state, index, to_near, to_far, from_far, from_near),
        scratch=work,
    )
    count = -(-len(pairs(depth)) // 8) * 8
    message = call(
        functools.partial(gram_kernel, depth, tuple(slots)),
        f32(7, blocks, own),
        (vectors, keep, *histories),
        scratch=[
            pltpu.VMEM((halves, blocks * 9 * depth, LANES), jnp.float32),
            pltpu.VMEM((count, LANES), jnp.float32),
        ],
    )
    square = sectors == 4
    parts = [message] + [None] * (sectors - 1)
    for by in sorted(range(1, sectors), reverse=True):
        parts[by] = send(message, (lambda i: i ^ by) if square else (lambda i: i - by))
    return call(
        functools.partial(solve_kernel, depth, square),
        (f32(3, own), f32(3, own)),
        (*parts, keep, past_dual, past_dual_gap, past_velocity, past_velocity_gap),
        scratch=[pltpu.VMEM((count, LANES), jnp.float32)],
    )


def solution(mesh):
    in_specs = (
        P(None, ("sector", "dom")),
        P(None, ("sector", "dom")),
        P(("sector", "dom")),
        P("sector", None),
        P(None, ("sector", "dom")),
        P(None, ("sector", "dom")),
        P(None, ("sector", "dom")),
        P(("sector", "dom")),
        P(None, None, ("sector", "dom")),
        P(None, None, ("sector", "dom")),
        P(None, None, ("sector", "dom")),
        P(None, None, ("sector", "dom")),
    )
    out_specs = (P(None, ("sector", "dom")), P(None, ("sector", "dom")))
    return jax.shard_map(
        per_device, mesh=mesh, in_specs=in_specs, out_specs=out_specs, check_vma=False
    )
```

```python
import functools
import itertools

import jax
import jax.numpy as jnp
from jax import lax
from jax.experimental import pallas as pl
from jax.experimental.pallas import tpu as pltpu
from jax.sharding import PartitionSpec as P

LANES = 128
VMEM_LIMIT = 24 * 1024 * 1024

STRAIN, DUAL, STEP, SPEED, LOAD, NEXT_STEP, NEXT_SPEED, INDEX, ROWS = 0, 36, 39, 40, 43, 46, 47, 50, 56
KEPT_NEXT_STEP, KEPT_LOAD, KEPT = 40, 41, 44
SPLITS = 2


def vmem():
    return pl.BlockSpec(memory_space=pltpu.VMEM)


def smem():
    return pl.BlockSpec(memory_space=pltpu.SMEM)


def call(kernel, outs, args, scalars=0, loose=0, scratch=()):
    return pl.pallas_call(
        kernel,
        out_shape=outs,
        in_specs=[smem()] * scalars
        + [pl.BlockSpec(memory_space=pl.ANY)] * loose
        + [vmem()] * (len(args) - scalars - loose),
        out_specs=jax.tree.map(lambda _: vmem(), outs),
        scratch_shapes=list(scratch),
        compiler_params=pltpu.CompilerParams(vmem_limit_bytes=VMEM_LIMIT),
    )(*args)


def f32(*shape):
    return jax.ShapeDtypeStruct(shape, jnp.float32)


def repeat(blocks, body, init):
    if blocks == 8:
        return body(slice(0, 8), 0, init)
    return lax.fori_loop(
        0, blocks // 8, lambda step, carry: body(pl.ds(pl.multiple_of(8 * step, 8), 8), 8 * step, carry), init
    )


def one_row(ref, lead, group, first, row, lanes=slice(None)):
    if isinstance(first, int):
        return ref[(*lead, slice(first + row, first + row + 1), lanes)]
    return ref[(*lead, group, lanes)][row : row + 1]


def project_cone(trial):
    center = 0.5 * (trial[0] + trial[1])
    spread = 0.5 * (trial[0] - trial[1])
    shear = trial[2]
    radius = jnp.sqrt(spread * spread + shear * shear)
    upper = center + radius
    lower = center - radius
    iso_part = 0.5 * (jnp.maximum(upper, 0.0) + jnp.maximum(lower, 0.0))
    factor = jnp.clip((center + radius) / (2.0 * jnp.maximum(radius, 0.05)), 0.0, 1.0)
    return (iso_part + factor * spread, iso_part - factor * spread, factor * shear)


def fetch(pairs, sems):
    copies = [pltpu.make_async_copy(source, target, sems.at[at]) for at, (source, target) in enumerate(pairs)]
    for copy in copies:
        copy.start()
    for copy in copies:
        copy.wait()


def in_hbm(*values):
    return tuple(pltpu.with_memory_space_constraint(value, pltpu.HBM) for value in values)


def nodes_kernel(speed_in, mobility_in, seam_in, gap_u, ahead, speed, mobility, seam, sems):
    depth = gap_u.shape[1]
    start = ahead.shape[0] - 3 * depth
    gaps = [(gap_u.at[c], ahead.at[pl.ds(start + depth * c, depth)]) for c in range(3)]
    fetch(((speed_in, speed), (mobility_in, mobility), (seam_in, seam), *gaps), sems)
    own = speed.shape[1]
    ahead[0:3, :] = speed[...]
    ahead[3:4, :] = mobility[...]
    ahead[4:8, :] = jnp.zeros((4, own), jnp.float32)
    for row in range(8, start):
        ahead[row : row + 1, :] = seam[:, (row - 8) * own : (row - 7) * own].astype(jnp.float32)


def base_kernel(counts, after, *refs):
    count = (len(refs) - 5) // 2
    sources, gaps = refs[:count], refs[count : count + 2]
    base, history, held, sems = refs[count + 2], refs[count + 3], refs[count + 4 : -1], refs[-1]
    fetch((*zip(sources, held), (gaps[0], history.at[0:3]), (gaps[1], history.at[3:6])), sems)
    strain, dual, speed, load, mobility, corners = held
    own = speed.shape[1]
    slot = lax.broadcasted_iota(jnp.int32, (1, own), 1)
    alive = (slot < counts[0]).astype(jnp.float32)
    base[STRAIN:DUAL, :] = strain[...] * alive
    base[DUAL : DUAL + 3, :] = dual[...] * alive
    base[STEP : STEP + 1, :] = mobility[...]
    base[SPEED : SPEED + 3, :] = speed[...]
    base[LOAD : LOAD + 3, :] = load[...]
    base[NEXT_STEP:INDEX, :] = jnp.zeros((INDEX - NEXT_STEP, own), jnp.float32)
    base[INDEX : INDEX + 4, :] = corners[...].astype(jnp.float32)


def message_kernel(sector_nodes, depth, after, ahead, base, message):
    own = message.shape[1]
    halves = own // LANES
    message[:NEXT_STEP, :] = base[:NEXT_STEP, :]
    message[NEXT_STEP : NEXT_STEP + 1, :] = ahead[3:4, :]
    message[NEXT_SPEED : NEXT_SPEED + 3, :] = ahead[0:3, :]
    message[INDEX + 4 :, :] = jnp.zeros((ROWS - INDEX - 4, own), jnp.float32)
    corners = base[INDEX : INDEX + 4, :].astype(jnp.int32)
    corner = jnp.concatenate([corners[:, h * LANES : (h + 1) * LANES] for h in range(halves)], axis=0)
    seam_rows = ahead.shape[0] - 8 - 3 * depth
    place = jnp.clip(corner - sector_nodes, 0, seam_rows * own - 1)
    high, low = place // LANES, place % LANES
    found = jnp.zeros(corner.shape, jnp.float32)
    for row in range(seam_rows):
        for h in range(halves):
            table = jnp.broadcast_to(ahead[8 + row : 9 + row, h * LANES : (h + 1) * LANES], corner.shape)
            value = jnp.take_along_axis(table, low, axis=1, mode="promise_in_bounds")
            found = jnp.where(high == row * halves + h, value, found)
    node = jnp.where(corner < sector_nodes, corner.astype(jnp.float32), found + float(sector_nodes))
    for h in range(halves):
        message[INDEX : INDEX + 4, h * LANES : (h + 1) * LANES] = node[4 * h : 4 * h + 4]


def wide_kernel(message, gaps, ahead, wide):
    depth = gaps.shape[1]
    start = ahead.shape[0] - 3 * depth
    wide[:ROWS, :] = message[...]
    for kind in range(6):
        wide[ROWS + depth * kind : ROWS + depth * (kind + 1), :] = gaps[kind]
    wide[ROWS + 6 * depth :, :] = ahead[start:, :]


def stack_kernel(*refs):
    stacked = refs[-1]
    for at, piece in enumerate(refs[:-1]):
        stacked[at * ROWS : at * ROWS + piece.shape[0], :] = piece[...]
        if piece.shape[0] < ROWS:
            start = at * ROWS + piece.shape[0]
            stacked[start : (at + 1) * ROWS, :] = jnp.zeros(((at + 1) * ROWS - start, piece.shape[1]), jnp.float32)


def pair_kernel(*refs):
    left, right, joined = refs[-3:]
    joined[0] = left[ROWS:, :]
    joined[1] = right[ROWS:, :]


def copy_kernel(*refs):
    value, copied = refs[-2:]
    copied[...] = value[...]


def join_kernel(*refs):
    left, right, joined = refs[-3:]
    count = left.shape[0]
    joined[:count] = left[...]
    joined[count:] = right[...]


def sweep(strain_row, index, work, dual):
    table, terms, codes, nearby = work
    blocks, own = index.shape[1:]
    halves = own // LANES
    here = lax.axis_index("dom")
    row = lax.broadcasted_iota(jnp.int32, (blocks, LANES), 0)
    left_block = ((row ^ here) - 1) ^ here
    right_block = ((row ^ here) + 1) ^ here

    def wide(j, group, first, block, part):
        piece = one_row(table, (j,), group, first, block, slice(part * LANES, (part + 1) * LANES))
        return jnp.broadcast_to(piece, (blocks, LANES))

    def take_sides(group, first, sides):
        left, right = (list(side) for side in sides)
        for block in range(8):
            for j in range(3):
                left[j] = jnp.where(left_block == first + block, wide(j, group, first, block, halves - 1), left[j])
                right[j] = jnp.where(right_block == first + block, wide(j, group, first, block, 0), right[j])
        return tuple(left), tuple(right)

    blank = tuple(jnp.zeros((blocks, LANES), jnp.float32) for _ in range(3))
    left, right = repeat(blocks, take_sides, (blank, blank))
    speed = []
    for k in range(4):
        parts = []
        for h in range(halves):
            number = index[k, :, h * LANES : (h + 1) * LANES]
            high, low = number // LANES, number % LANES

            def take(value):
                return jnp.take_along_axis(value, low, axis=1, mode="promise_in_bounds")

            found = [take(table[j, :, 0:LANES]) for j in range(3)]
            for part in range(1, halves):
                mask = high % halves == part
                found = [
                    jnp.where(mask, take(table[j, :, part * LANES : (part + 1) * LANES]), found[j]) for j in range(3)
                ]
            mask = number // own == left_block
            found = [jnp.where(mask, take(left[j]), found[j]) for j in range(3)]
            mask = number // own == right_block
            found = [jnp.where(mask, take(right[j]), found[j]) for j in range(3)]

            def take_group(group, first, found):
                for part, block in itertools.product(range(halves), range(8)):
                    mask = high == (blocks + first + block) * halves + part
                    found = [jnp.where(mask, take(wide(3 + j, group, first, block, part)), found[j]) for j in range(3)]
                return tuple(found)

            parts.append(repeat(blocks, take_group, tuple(found)))
        speed.append([jnp.concatenate([found[j] for found in parts], axis=1) for j in range(3)])
    rate = []
    for c in range(3):
        total = None
        for k in range(4):
            for j in range(3):
                term = strain_row(12 * c + 3 * k + j) * speed[k][j]
                total = term if total is None else total + term
        rate.append(total)
    trial = [rate[c] + dual[c] for c in range(3)]
    cone = project_cone(trial)
    dual_next = [trial[c] - cone[c] for c in range(3)]
    misfit = [rate[c] - cone[c] + dual_next[c] for c in range(3)]
    for k in range(4):
        for j in range(3):
            rest = sum(strain_row(12 * c + 3 * k + j) * misfit[c] for c in range(3))
            for split in range(SPLITS):
                term = rest.astype(jnp.bfloat16).astype(jnp.float32)
                terms[SPLITS * j + split, k] = term
                rest = rest - term

    near_rows = halves + 2
    next_rows = halves * blocks
    row_wide = lax.broadcasted_iota(jnp.int32, (blocks, own), 0) ^ here
    for k in range(4):
        number = index[k]
        block_of, half = number // own, number // LANES % halves
        near = jnp.where(block_of == ((row_wide - 1) ^ here), 0, 1 + half)
        near = jnp.where(block_of == ((row_wide + 1) ^ here), 1 + halves, near)
        codes[0, k] = (number % LANES).astype(jnp.float32)
        codes[1, k] = jnp.where(block_of < blocks, near, -1).astype(jnp.float32)
        codes[2, k] = jnp.where(block_of < blocks, -1, half * blocks + block_of - blocks).astype(jnp.float32)

    values = 3 * SPLITS
    per_tile = 16 // near_rows
    near_tiles = -(-values // per_tile)
    iota = lax.broadcasted_iota(jnp.int32, (16, own), 0)
    near_iota = (iota % near_rows).astype(jnp.float32).astype(jnp.bfloat16)
    value_iota = (iota // near_rows).astype(jnp.float32).astype(jnp.bfloat16)
    value_masks = [value_iota == jnp.full((16, own), float(at), jnp.bfloat16) for at in range(per_tile)]
    iota = iota.astype(jnp.float32)
    low_iota = [(iota + float(16 * g)).astype(jnp.bfloat16) for g in range(LANES // 16)]
    next_iota = [(iota + float(16 * g)).astype(jnp.bfloat16) for g in range(next_rows // 16)]
    one = jnp.ones((16, own), jnp.bfloat16)
    zero = jnp.zeros((16, own), jnp.bfloat16)

    def spread_row(value):
        return jnp.broadcast_to(value, (16, own)).astype(jnp.bfloat16)

    def add_group(group, first, total):
        for block in range(8):
            part = None
            for k in range(4):
                low_row, near_row, next_row = (
                    spread_row(one_row(codes, (at, k), group, first, block)) for at in range(3)
                )
                rows = [spread_row(one_row(terms, (at, k), group, first, block)) for at in range(values)]
                spread = jnp.concatenate([jnp.where(low_row == value, one, zero) for value in low_iota], axis=0)
                mask = near_row == near_iota
                weights = []
                for tile in range(near_tiles):
                    inside = rows[tile * per_tile : (tile + 1) * per_tile]
                    value = inside[-1]
                    for at in range(len(inside) - 1):
                        value = jnp.where(value_masks[at], inside[at], value)
                    weights.append(jnp.where(mask, value, zero))
                masks = [next_row == value for value in next_iota]
                weights += [jnp.where(mask, row, zero) for row in rows for mask in masks]
                product = lax.dot_general(
                    jnp.concatenate(weights, axis=0),
                    spread,
                    (((1,), (1,)), ((), ())),
                    preferred_element_type=jnp.float32,
                )
                part = product if part is None else part + product
            start = (first + block) * 16 * near_tiles
            if not isinstance(start, int):
                start = pl.multiple_of(start, 16)
            nearby[pl.ds(start, 16 * near_tiles), :] = part[: 16 * near_tiles]
            total += part[16 * near_tiles :]
        return total

    total = repeat(blocks, add_group, jnp.zeros((values * next_rows, LANES), jnp.float32))

    def near_force(j, row):
        return sum(
            nearby[pl.ds((SPLITS * j + split) * near_rows + row, blocks, stride=16 * near_tiles), :]
            for split in range(SPLITS)
        )

    force_own, force_next = [], []
    for j in range(3):
        halves_own = [near_force(j, 1 + h) for h in range(halves)]
        to_left, to_right = near_force(j, 0), near_force(j, 1 + halves)
        from_right = from_left = jnp.zeros((blocks, LANES), jnp.float32)
        for block in range(blocks):
            wide_left = jnp.broadcast_to(to_left[block : block + 1], (blocks, LANES))
            wide_right = jnp.broadcast_to(to_right[block : block + 1], (blocks, LANES))
            from_right = jnp.where(right_block == block, wide_left, from_right)
            from_left = jnp.where(left_block == block, wide_right, from_left)
        halves_own[-1] = halves_own[-1] + from_right
        halves_own[0] = halves_own[0] + from_left
        force_own.append(jnp.concatenate(halves_own, axis=1))
        whole = sum(
            total[(SPLITS * j + split) * next_rows : (SPLITS * j + split + 1) * next_rows] for split in range(SPLITS)
        )
        force_next.append(jnp.concatenate([whole[h * blocks : (h + 1) * blocks] for h in range(halves)], axis=1))
    return dual_next, force_own, force_next


def stack_block(piece, slot, rows, stack):
    held = min(rows, piece.shape[0])
    for h in range(stack.shape[0]):
        stack[h, slot * rows : slot * rows + held, :] = piece[:held, h * LANES : (h + 1) * LANES]


def across(stack, row, rows):
    blocks = stack.shape[1] // rows
    return jnp.concatenate(
        [stack[h, pl.ds(row, blocks, stride=rows), :] for h in range(stack.shape[0])], axis=1
    )


def first_kernel(blocks, order, *refs):
    pieces = refs[: len(order)]
    state, index, to_near, to_far, stack = refs[blocks : blocks + 5]
    work = refs[blocks + 5 :]
    table = work[0]
    own = index.shape[2]
    for piece, (start, slot) in zip(pieces, order):
        stack_block(piece.at[start : min(start + ROWS, piece.shape[0])], slot, ROWS, stack)
    flip = lax.axis_index("dom") * own
    even = lax.axis_index("sector") % 2 == 0
    for k in range(4):
        index[k] = across(stack, INDEX + k, ROWS).astype(jnp.int32) ^ flip
    for row in range(36):
        state[row] = across(stack, STRAIN + row, ROWS)
    step = across(stack, STEP, ROWS)
    state[STEP] = step
    state[KEPT_NEXT_STEP] = across(stack, NEXT_STEP, ROWS)
    for j in range(3):
        state[KEPT_LOAD + j] = across(stack, LOAD + j, ROWS)
        table[j] = across(stack, SPEED + j, ROWS)
        table[3 + j] = across(stack, NEXT_SPEED + j, ROWS)
    dual = [across(stack, DUAL + c, ROWS) for c in range(3)]
    dual, force_own, force_next = sweep(lambda row: state[row], index, work, dual)
    for c in range(3):
        state[DUAL + c] = dual[c]
        mine = table[c] - step * (force_own[c] - state[KEPT_LOAD + c])
        to_near[c] = jnp.where(even, force_next[c], mine)
        to_far[c] = jnp.where(even, mine, force_next[c])


def second_kernel(state, index, to_near, to_far, from_far, from_near, vectors, keep, *work):
    table = work[0]
    even = lax.axis_index("sector") % 2 == 0
    step, next_step = state[STEP], state[KEPT_NEXT_STEP]
    for j in range(3):
        near, far = to_near[j], to_far[j]
        near_in, far_in = from_near[j], from_far[j]
        table[j] = jnp.where(even, far, near) - step * jnp.where(even, far_in, near_in)
        table[3 + j] = jnp.where(even, near_in, far_in) - next_step * jnp.where(even, near, far)
    dual = [state[DUAL + c] for c in range(3)]
    dual_next, force_own, force_next = sweep(lambda row: state[row], index, work, dual)
    for c in range(3):
        after = table[c] - step * (force_own[c] - state[KEPT_LOAD + c])
        vectors[c] = after - table[c]
        vectors[3 + c] = -(next_step * force_next[c])
        keep[c] = dual_next[c]
        keep[3 + c] = dual_next[c] - dual[c]
        keep[6 + c] = after


def pairs(depth):
    return [(i, l) for i in range(depth) for l in range(i, depth + 1)]


def gram_kernel(depth, slots, vectors, keep, *refs):
    blocks, own = keep.shape[1:]
    halves = own // LANES
    rows = 9 * depth
    message, stack, rows_sum = refs[len(slots) :]
    for piece, own_slots in zip(refs, slots):
        for at, slot in enumerate(own_slots):
            stack_block(piece.at[at] if len(piece.shape) == 3 else piece.at[ROWS:], slot, rows, stack)
    for row in range(6):
        message[row] = vectors[row]
    message[6] = jnp.zeros((blocks, own), jnp.float32)
    sums, pushed, pushed_twice = {}, [0.0] * (depth + 1), 0.0
    for c, h, top in itertools.product(range(3), range(halves), range(0, blocks, 8)):
        lanes, group = slice(h * LANES, (h + 1) * LANES), slice(top, top + 8)

        def gap(kind, i):
            return stack[h, pl.ds(top * rows + depth * (3 * kind + c) + i, 8, stride=rows), :]

        for kind, moved in enumerate((keep[3 + c, group, lanes], vectors[c, group, lanes])):
            gaps = [moved - gap(kind, i) for i in range(depth)] + [moved]
            for i, l in pairs(depth):
                term = gaps[i] * gaps[l]
                sums[i, l] = sums[i, l] + term if (i, l) in sums else term
        push = vectors[3 + c, group, lanes]
        for i in range(depth):
            pushed[i] = pushed[i] + gap(2, i) * push
        pushed_twice = pushed_twice + push * push
    for at, (i, l) in enumerate(pairs(depth)):
        value = sums[i, l] + pushed_twice - pushed[i] - pushed[l]
        rows_sum[at : at + 1, :] = jnp.sum(value, axis=0, keepdims=True)
    count = len(pairs(depth))
    if rows_sum.shape[0] > count:
        rows_sum[count:, :] = jnp.zeros((rows_sum.shape[0] - count, LANES), jnp.float32)
    whole = jnp.broadcast_to(jnp.sum(rows_sum[...], axis=1, keepdims=True), rows_sum.shape)
    lane = lax.broadcasted_iota(jnp.int32, (8, LANES), 1)
    out = whole[0:8]
    for group in range(1, rows_sum.shape[0] // 8):
        out = jnp.where(lane == group, whole[8 * group : 8 * group + 8], out)
    message[6, 0:8, 0:LANES] = out


def solve_kernel(depth, square, *refs):
    parts = refs[:-8]
    keep, past_w, gap_w, past_u, gap_u, new_u, new_w, total = refs[-8:]
    own = new_u.shape[1]
    tile = parts[0][6, 0:8, 0:LANES]
    for other in parts[1:]:
        tile = tile + other[6, 0:8, 0:LANES]
    even = lax.axis_index("sector") % 2 == 0

    def ahead(by, row):
        if square and by in (1, 3):
            return jnp.where(even, parts[by][row], parts[4 - by][row])
        return parts[by][row]

    sectors = len(parts)
    pushes = [[ahead(by, 3 + j) for j in range(3)] for by in range(sectors)]
    cross = sum(ahead(by, j) * pushes[by - 1][j] for by in range(sectors) for j in range(3))
    cross = jnp.sum(jnp.sum(cross, axis=0, keepdims=True), axis=1, keepdims=True)
    last = [keep[6 + j, 0:1] + pushes[-1][j][0:1] for j in range(3)] + [keep[c, 0:1] for c in range(3)]
    for group in range(total.shape[0] // 8):
        total[8 * group : 8 * group + 8, :] = jnp.broadcast_to(tile[:, group : group + 1], (8, LANES))
    matrix = {
        pair: jnp.broadcast_to(total[at : at + 1, :], (depth, LANES)) + 2.0 * cross
        for at, pair in enumerate(pairs(depth))
    }
    ridge = 0.0001 * sum(matrix[i, i] for i in range(depth)) / depth
    for i in range(depth):
        matrix[i, i] = matrix[i, i] + ridge
    inverse = []
    for step in range(depth):
        inverse.append(1.0 / matrix[step, step])
        for i in range(step + 1, depth):
            factor = matrix[step, i] * inverse[step]
            for l in range(i, depth + 1):
                matrix[i, l] = matrix[i, l] - factor * matrix[step, l]
    weights = [None] * depth
    for i in reversed(range(depth)):
        value = matrix[i, depth]
        for l in range(i + 1, depth):
            value = value - matrix[i, l] * weights[l]
        weights[i] = value * inverse[i]
    row = lax.broadcasted_iota(jnp.int32, (depth, LANES), 0)
    weight = weights[0]
    for i in range(1, depth):
        weight = jnp.where(row == i, weights[i], weight)
    for start in range(0, own, LANES):
        lanes = slice(start, start + LANES)
        for at, (past, gap, out) in enumerate(((past_u, gap_u, new_u), (past_w, gap_w, new_w))):
            for c in range(3):
                value = jnp.broadcast_to(last[3 * at + c][:, lanes], (depth, LANES))
                change = weight * (value - past[c, :, lanes] - gap[c, :, lanes])
                out[c : c + 1, lanes] = value[0:1] - jnp.sum(change, axis=0, keepdims=True)


def per_device(
    strain_map,
    corner_nodes,
    counts,
    seam_nodes,
    velocity,
    dual_state,
    nodal_load,
    mobility,
    past_dual,
    past_dual_gap,
    past_velocity,
    past_velocity_gap,
):
    own = velocity.shape[1]
    halves = own // LANES
    blocks = lax.axis_size("dom")
    sectors = lax.axis_size("sector")
    depth = past_dual.shape[0]
    seam_rows = seam_nodes.shape[1] // own
    mobility = mobility.reshape(1, own)
    past_dual, past_dual_gap, past_velocity, past_velocity_gap = (
        value.transpose(1, 0, 2) for value in (past_dual, past_dual_gap, past_velocity, past_velocity_gap)
    )

    def send(value, target):
        return lax.ppermute(value, "sector", [(i, target(i) % sectors) for i in range(sectors)])

    def swap(value, bits):
        return lax.ppermute(value, "dom", [(i, i ^ bits) for i in range(blocks)])

    nodes = (velocity, mobility, seam_nodes)
    ahead = call(
        nodes_kernel,
        f32(8 + seam_rows + 3 * depth, own),
        in_hbm(*nodes, past_velocity_gap),
        loose=len(nodes) + 1,
        scratch=[pltpu.VMEM(value.shape, value.dtype) for value in nodes]
        + [pltpu.SemaphoreType.DMA((len(nodes) + 3,))],
    )
    held = (strain_map, dual_state, velocity, nodal_load, mobility, corner_nodes)
    base, history = call(
        base_kernel,
        (f32(INDEX + 4, own), f32(6, depth, own)),
        (counts, ahead, *in_hbm(*held, past_dual_gap, past_velocity_gap)),
        scalars=1,
        loose=len(held) + 3,
        scratch=[pltpu.VMEM(value.shape, value.dtype) for value in held]
        + [pltpu.SemaphoreType.DMA((len(held) + 2,))],
    )
    ahead = send(ahead, lambda i: i - 1)
    far_ones = list(range(4, blocks, 2))
    message = call(
        functools.partial(message_kernel, own * blocks, depth), f32(ROWS, own), (history, ahead, base), loose=1
    )
    wide = call(wide_kernel, f32(ROWS + 9 * depth, own), (message, history, ahead))
    pieces = {0: wide}
    for bits in far_ones:
        pieces[bits] = swap(pieces[bits - 2], 2) if bits % 4 else swap(message, bits)
    pieces[2] = swap(wide, 2)
    for even in (0, 2):
        pieces[even + 1] = swap(pieces[even], 1)
    count = len(far_ones)
    crossed = swap(
        call(stack_kernel, f32(count * ROWS, own), tuple(pieces[bits] for bits in far_ones)), 1
    )
    histories, slots = [pieces[block] for block in range(4)], [(block,) for block in range(4)]
    history = call(
        pair_kernel, f32(2, 9 * depth, own), (*(pieces[bits] for bits in far_ones), wide, pieces[2]), loose=len(far_ones)
    )
    known, apart, later = (0, 2), 4, []
    while apart < blocks:
        other = swap(history, apart)
        later.append((other, tuple(slot ^ apart for slot in known)))
        known += later[-1][1]
        apart *= 2
        if apart < blocks:
            history = call(join_kernel, f32(2 * history.shape[0], 9 * depth, own), (history, other))
    order = [(at * ROWS, bits + 1) for at, bits in enumerate(far_ones)]
    order += [(0, block) for block in reversed(range(blocks)) if block in pieces]
    sector = f32(3, blocks, own)
    work = [
        pltpu.VMEM((6, blocks, own), jnp.float32),
        pltpu.VMEM((3 * SPLITS, 4, blocks, own), jnp.float32),
        pltpu.VMEM((3, 4, blocks, own), jnp.float32),
        pltpu.VMEM((blocks * 16 * -(-3 * SPLITS * (halves + 2) // 16), LANES), jnp.float32),
    ]
    state, index, to_near, to_far = call(
        functools.partial(first_kernel, blocks, order),
        (f32(KEPT, blocks, own), jax.ShapeDtypeStruct((4, blocks, own), jnp.int32), sector, sector),
        (*([crossed] * count), *(pieces[block] for _, block in order[count:])),
        scratch=[pltpu.VMEM((halves, blocks * ROWS, LANES), jnp.float32), *work],
    )
    from_far = send(to_far, lambda i: i + 1 if i % 2 else i - 1)
    from_near = send(to_near, lambda i: i ^ 1)
    for other, far in later:
        held_back = call(copy_kernel, f32(*other.shape), (from_near, from_far, other), loose=2)
        histories += [other, swap(held_back, 1)]
        slots += [far, tuple(slot ^ 1 for slot in far)]
    vectors, keep = call(
        second_kernel,
        (f32(6, blocks, own), f32(9, blocks, own)),
        (state, index, to_near, to_far, from_far, from_near),
        scratch=work,
    )
    count = -(-len(pairs(depth)) // 8) * 8
    message = call(
        functools.partial(gram_kernel, depth, tuple(slots)),
        f32(7, blocks, own),
        (vectors, keep, *histories),
        scratch=[
            pltpu.VMEM((halves, blocks * 9 * depth, LANES), jnp.float32),
            pltpu.VMEM((count, LANES), jnp.float32),
        ],
    )
    square = sectors == 4
    parts = [message] + [None] * (sectors - 1)
    for by in sorted(range(1, sectors), reverse=True):
        parts[by] = send(message, (lambda i: i ^ by) if square else (lambda i: i - by))
    return call(
        functools.partial(solve_kernel, depth, square),
        (f32(3, own), f32(3, own)),
        (*parts, keep, past_dual, past_dual_gap, past_velocity, past_velocity_gap),
        scratch=[pltpu.VMEM((count, LANES), jnp.float32)],
    )


def solution(mesh):
    in_specs = (
        P(None, ("sector", "dom")),
        P(None, ("sector", "dom")),
        P(("sector", "dom")),
        P("sector", None),
        P(None, ("sector", "dom")),
        P(None, ("sector", "dom")),
        P(None, ("sector", "dom")),
        P(("sector", "dom")),
        P(None, None, ("sector", "dom")),
        P(None, None, ("sector", "dom")),
        P(None, None, ("sector", "dom")),
        P(None, None, ("sector", "dom")),
    )
    out_specs = (P(None, ("sector", "dom")), P(None, ("sector", "dom")))
    return jax.shard_map(
        per_device, mesh=mesh, in_specs=in_specs, out_specs=out_specs, check_vma=False
    )
```

```python
import functools
import itertools

import jax
import jax.numpy as jnp
from jax import lax
from jax.experimental import pallas as pl
from jax.experimental.pallas import tpu as pltpu
from jax.sharding import PartitionSpec as P

LANES = 128
VMEM_LIMIT = 24 * 1024 * 1024

STRAIN, DUAL, STEP, SPEED, LOAD, NEXT_STEP, NEXT_SPEED, INDEX, ROWS = 0, 36, 39, 40, 43, 46, 47, 50, 56
KEPT_NEXT_STEP, KEPT_LOAD, KEPT = 40, 41, 44
SPLITS = 2


def vmem():
    return pl.BlockSpec(memory_space=pltpu.VMEM)


def smem():
    return pl.BlockSpec(memory_space=pltpu.SMEM)


def call(kernel, outs, args, scalars=0, loose=0, scratch=()):
    return pl.pallas_call(
        kernel,
        out_shape=outs,
        in_specs=[smem()] * scalars
        + [pl.BlockSpec(memory_space=pl.ANY)] * loose
        + [vmem()] * (len(args) - scalars - loose),
        out_specs=jax.tree.map(lambda _: vmem(), outs),
        scratch_shapes=list(scratch),
        compiler_params=pltpu.CompilerParams(vmem_limit_bytes=VMEM_LIMIT),
    )(*args)


def f32(*shape):
    return jax.ShapeDtypeStruct(shape, jnp.float32)


def repeat(blocks, body, init):
    if blocks == 8:
        return body(slice(0, 8), 0, init)
    return lax.fori_loop(
        0, blocks // 8, lambda step, carry: body(pl.ds(pl.multiple_of(8 * step, 8), 8), 8 * step, carry), init
    )


def one_row(ref, lead, group, first, row, lanes=slice(None)):
    if isinstance(first, int):
        return ref[(*lead, slice(first + row, first + row + 1), lanes)]
    return ref[(*lead, group, lanes)][row : row + 1]


def project_cone(trial):
    center = 0.5 * (trial[0] + trial[1])
    spread = 0.5 * (trial[0] - trial[1])
    shear = trial[2]
    radius = jnp.sqrt(spread * spread + shear * shear)
    upper = center + radius
    lower = center - radius
    iso_part = 0.5 * (jnp.maximum(upper, 0.0) + jnp.maximum(lower, 0.0))
    factor = jnp.clip((center + radius) / (2.0 * jnp.maximum(radius, 0.05)), 0.0, 1.0)
    return (iso_part + factor * spread, iso_part - factor * spread, factor * shear)


def fetch(pairs, sems):
    copies = [pltpu.make_async_copy(source, target, sems.at[at]) for at, (source, target) in enumerate(pairs)]
    for copy in copies:
        copy.start()
    for copy in copies:
        copy.wait()


def in_hbm(*values):
    return tuple(pltpu.with_memory_space_constraint(value, pltpu.HBM) for value in values)


def nodes_kernel(speed_in, mobility_in, seam_in, gap_u, ahead, speed, mobility, seam, sems):
    depth = gap_u.shape[1]
    start = ahead.shape[0] - 3 * depth
    gaps = [(gap_u.at[c], ahead.at[pl.ds(start + depth * c, depth)]) for c in range(3)]
    fetch(((speed_in, speed), (mobility_in, mobility), (seam_in, seam), *gaps), sems)
    own = speed.shape[1]
    ahead[0:3, :] = speed[...]
    ahead[3:4, :] = mobility[...]
    ahead[4:8, :] = jnp.zeros((4, own), jnp.float32)
    for row in range(8, start):
        ahead[row : row + 1, :] = seam[:, (row - 8) * own : (row - 7) * own].astype(jnp.float32)


def base_kernel(counts, after, *refs):
    count = (len(refs) - 5) // 2
    sources, gaps = refs[:count], refs[count : count + 2]
    base, history, held, sems = refs[count + 2], refs[count + 3], refs[count + 4 : -1], refs[-1]
    fetch((*zip(sources, held), (gaps[0], history.at[0:3]), (gaps[1], history.at[3:6])), sems)
    strain, dual, speed, load, mobility, corners = held
    own = speed.shape[1]
    slot = lax.broadcasted_iota(jnp.int32, (1, own), 1)
    alive = (slot < counts[0]).astype(jnp.float32)
    base[STRAIN:DUAL, :] = strain[...] * alive
    base[DUAL : DUAL + 3, :] = dual[...] * alive
    base[STEP : STEP + 1, :] = mobility[...]
    base[SPEED : SPEED + 3, :] = speed[...]
    base[LOAD : LOAD + 3, :] = load[...]
    base[NEXT_STEP:INDEX, :] = jnp.zeros((INDEX - NEXT_STEP, own), jnp.float32)
    base[INDEX : INDEX + 4, :] = corners[...].astype(jnp.float32)


def message_kernel(sector_nodes, depth, after, ahead, base, message, *shorter):
    own = message.shape[1]
    halves = own // LANES
    message[:NEXT_STEP, :] = base[:NEXT_STEP, :]
    message[NEXT_STEP : NEXT_STEP + 1, :] = ahead[3:4, :]
    message[NEXT_SPEED : NEXT_SPEED + 3, :] = ahead[0:3, :]
    message[INDEX + 4 :, :] = jnp.zeros((ROWS - INDEX - 4, own), jnp.float32)
    corners = base[INDEX : INDEX + 4, :].astype(jnp.int32)
    corner = jnp.concatenate([corners[:, h * LANES : (h + 1) * LANES] for h in range(halves)], axis=0)
    seam_rows = ahead.shape[0] - 8 - 3 * depth
    place = jnp.clip(corner - sector_nodes, 0, seam_rows * own - 1)
    high, low = place // LANES, place % LANES
    found = jnp.zeros(corner.shape, jnp.float32)
    for row in range(seam_rows):
        for h in range(halves):
            table = jnp.broadcast_to(ahead[8 + row : 9 + row, h * LANES : (h + 1) * LANES], corner.shape)
            value = jnp.take_along_axis(table, low, axis=1, mode="promise_in_bounds")
            found = jnp.where(high == row * halves + h, value, found)
    node = jnp.where(corner < sector_nodes, corner.astype(jnp.float32), found + float(sector_nodes))
    for h in range(halves):
        message[INDEX : INDEX + 4, h * LANES : (h + 1) * LANES] = node[4 * h : 4 * h + 4]
    for other in shorter:
        other[...] = message[: other.shape[0], :]


def wide_kernel(message, gaps, ahead, wide):
    depth = gaps.shape[1]
    start = ahead.shape[0] - 3 * depth
    wide[:ROWS, :] = message[...]
    for kind in range(6):
        wide[ROWS + depth * kind : ROWS + depth * (kind + 1), :] = gaps[kind]
    wide[ROWS + 6 * depth :, :] = ahead[start:, :]


def stack_kernel(*refs):
    stacked = refs[-1]
    for at, piece in enumerate(refs[:-1]):
        stacked[at * ROWS : at * ROWS + piece.shape[0], :] = piece[...]
        if piece.shape[0] < ROWS:
            start = at * ROWS + piece.shape[0]
            stacked[start : (at + 1) * ROWS, :] = jnp.zeros(((at + 1) * ROWS - start, piece.shape[1]), jnp.float32)


def pair_kernel(*refs):
    left, right, joined = refs[-3:]
    joined[0] = left[ROWS:, :]
    joined[1] = right[ROWS:, :]


def copy_kernel(*refs):
    value, copied = refs[-2:]
    copied[...] = value[...]


def join_kernel(*refs):
    left, right, joined = refs[-3:]
    count = left.shape[0]
    joined[:count] = left[...]
    joined[count:] = right[...]


def sweep(strain_row, index, work, dual):
    table, terms, codes, nearby = work
    blocks, own = index.shape[1:]
    halves = own // LANES
    here = lax.axis_index("dom")
    row = lax.broadcasted_iota(jnp.int32, (blocks, LANES), 0)
    left_block = ((row ^ here) - 1) ^ here
    right_block = ((row ^ here) + 1) ^ here

    def wide(j, group, first, block, part):
        piece = one_row(table, (j,), group, first, block, slice(part * LANES, (part + 1) * LANES))
        return jnp.broadcast_to(piece, (blocks, LANES))

    def take_sides(group, first, sides):
        left, right = (list(side) for side in sides)
        for block in range(8):
            for j in range(3):
                left[j] = jnp.where(left_block == first + block, wide(j, group, first, block, halves - 1), left[j])
                right[j] = jnp.where(right_block == first + block, wide(j, group, first, block, 0), right[j])
        return tuple(left), tuple(right)

    blank = tuple(jnp.zeros((blocks, LANES), jnp.float32) for _ in range(3))
    left, right = repeat(blocks, take_sides, (blank, blank))
    speed = []
    for k in range(4):
        parts = []
        for h in range(halves):
            number = index[k, :, h * LANES : (h + 1) * LANES]
            high, low = number // LANES, number % LANES

            def take(value):
                return jnp.take_along_axis(value, low, axis=1, mode="promise_in_bounds")

            found = [take(table[j, :, 0:LANES]) for j in range(3)]
            for part in range(1, halves):
                mask = high % halves == part
                found = [
                    jnp.where(mask, take(table[j, :, part * LANES : (part + 1) * LANES]), found[j]) for j in range(3)
                ]
            mask = number // own == left_block
            found = [jnp.where(mask, take(left[j]), found[j]) for j in range(3)]
            mask = number // own == right_block
            found = [jnp.where(mask, take(right[j]), found[j]) for j in range(3)]

            def take_group(group, first, found):
                for part, block in itertools.product(range(halves), range(8)):
                    mask = high == (blocks + first + block) * halves + part
                    found = [jnp.where(mask, take(wide(3 + j, group, first, block, part)), found[j]) for j in range(3)]
                return tuple(found)

            parts.append(repeat(blocks, take_group, tuple(found)))
        speed.append([jnp.concatenate([found[j] for found in parts], axis=1) for j in range(3)])
    rate = []
    for c in range(3):
        total = None
        for k in range(4):
            for j in range(3):
                term = strain_row(12 * c + 3 * k + j) * speed[k][j]
                total = term if total is None else total + term
        rate.append(total)
    trial = [rate[c] + dual[c] for c in range(3)]
    cone = project_cone(trial)
    dual_next = [trial[c] - cone[c] for c in range(3)]
    misfit = [rate[c] - cone[c] + dual_next[c] for c in range(3)]
    for k in range(4):
        for j in range(3):
            rest = sum(strain_row(12 * c + 3 * k + j) * misfit[c] for c in range(3))
            for split in range(SPLITS):
                term = rest.astype(jnp.bfloat16).astype(jnp.float32)
                terms[SPLITS * j + split, k] = term
                rest = rest - term

    near_rows = halves + 2
    next_rows = halves * blocks
    row_wide = lax.broadcasted_iota(jnp.int32, (blocks, own), 0) ^ here
    for k in range(4):
        number = index[k]
        block_of, half = number // own, number // LANES % halves
        near = jnp.where(block_of == ((row_wide - 1) ^ here), 0, 1 + half)
        near = jnp.where(block_of == ((row_wide + 1) ^ here), 1 + halves, near)
        codes[0, k] = (number % LANES).astype(jnp.float32)
        codes[1, k] = jnp.where(block_of < blocks, near, -1).astype(jnp.float32)
        codes[2, k] = jnp.where(block_of < blocks, -1, half * blocks + block_of - blocks).astype(jnp.float32)

    values = 3 * SPLITS
    per_tile = 16 // near_rows
    near_tiles = -(-values // per_tile)
    iota = lax.broadcasted_iota(jnp.int32, (16, own), 0)
    near_iota = (iota % near_rows).astype(jnp.float32).astype(jnp.bfloat16)
    value_iota = (iota // near_rows).astype(jnp.float32).astype(jnp.bfloat16)
    value_masks = [value_iota == jnp.full((16, own), float(at), jnp.bfloat16) for at in range(per_tile)]
    iota = iota.astype(jnp.float32)
    low_iota = [(iota + float(16 * g)).astype(jnp.bfloat16) for g in range(LANES // 16)]
    next_iota = [(iota + float(16 * g)).astype(jnp.bfloat16) for g in range(next_rows // 16)]
    one = jnp.ones((16, own), jnp.bfloat16)
    zero = jnp.zeros((16, own), jnp.bfloat16)

    def spread_row(value):
        return jnp.broadcast_to(value, (16, own)).astype(jnp.bfloat16)

    def add_group(group, first, total):
        for block in range(8):
            part = None
            for k in range(4):
                low_row, near_row, next_row = (
                    spread_row(one_row(codes, (at, k), group, first, block)) for at in range(3)
                )
                rows = [spread_row(one_row(terms, (at, k), group, first, block)) for at in range(values)]
                spread = jnp.concatenate([jnp.where(low_row == value, one, zero) for value in low_iota], axis=0)
                mask = near_row == near_iota
                weights = []
                for tile in range(near_tiles):
                    inside = rows[tile * per_tile : (tile + 1) * per_tile]
                    value = inside[-1]
                    for at in range(len(inside) - 1):
                        value = jnp.where(value_masks[at], inside[at], value)
                    weights.append(jnp.where(mask, value, zero))
                masks = [next_row == value for value in next_iota]
                weights += [jnp.where(mask, row, zero) for row in rows for mask in masks]
                product = lax.dot_general(
                    jnp.concatenate(weights, axis=0),
                    spread,
                    (((1,), (1,)), ((), ())),
                    preferred_element_type=jnp.float32,
                )
                part = product if part is None else part + product
            start = (first + block) * 16 * near_tiles
            if not isinstance(start, int):
                start = pl.multiple_of(start, 16)
            nearby[pl.ds(start, 16 * near_tiles), :] = part[: 16 * near_tiles]
            total += part[16 * near_tiles :]
        return total

    total = repeat(blocks, add_group, jnp.zeros((values * next_rows, LANES), jnp.float32))

    def near_force(j, row):
        return sum(
            nearby[pl.ds((SPLITS * j + split) * near_rows + row, blocks, stride=16 * near_tiles), :]
            for split in range(SPLITS)
        )

    force_own, force_next = [], []
    for j in range(3):
        halves_own = [near_force(j, 1 + h) for h in range(halves)]
        to_left, to_right = near_force(j, 0), near_force(j, 1 + halves)
        from_right = from_left = jnp.zeros((blocks, LANES), jnp.float32)
        for block in range(blocks):
            wide_left = jnp.broadcast_to(to_left[block : block + 1], (blocks, LANES))
            wide_right = jnp.broadcast_to(to_right[block : block + 1], (blocks, LANES))
            from_right = jnp.where(right_block == block, wide_left, from_right)
            from_left = jnp.where(left_block == block, wide_right, from_left)
        halves_own[-1] = halves_own[-1] + from_right
        halves_own[0] = halves_own[0] + from_left
        force_own.append(jnp.concatenate(halves_own, axis=1))
        whole = sum(
            total[(SPLITS * j + split) * next_rows : (SPLITS * j + split + 1) * next_rows] for split in range(SPLITS)
        )
        force_next.append(jnp.concatenate([whole[h * blocks : (h + 1) * blocks] for h in range(halves)], axis=1))
    return dual_next, force_own, force_next


def stack_block(piece, slot, rows, stack):
    held = min(rows, piece.shape[0])
    for h in range(stack.shape[0]):
        stack[h, slot * rows : slot * rows + held, :] = piece[:held, h * LANES : (h + 1) * LANES]


def across(stack, row, rows):
    blocks = stack.shape[1] // rows
    return jnp.concatenate(
        [stack[h, pl.ds(row, blocks, stride=rows), :] for h in range(stack.shape[0])], axis=1
    )


def first_kernel(blocks, order, *refs):
    pieces = refs[: len(order)]
    state, index, to_near, to_far, stack = refs[blocks : blocks + 5]
    work = refs[blocks + 5 :]
    table = work[0]
    own = index.shape[2]
    for piece, (start, slot) in zip(pieces, order):
        stack_block(piece.at[start : min(start + ROWS, piece.shape[0])], slot, ROWS, stack)
    flip = lax.axis_index("dom") * own
    even = lax.axis_index("sector") % 2 == 0
    for k in range(4):
        index[k] = across(stack, INDEX + k, ROWS).astype(jnp.int32) ^ flip
    for row in range(36):
        state[row] = across(stack, STRAIN + row, ROWS)
    step = across(stack, STEP, ROWS)
    state[STEP] = step
    state[KEPT_NEXT_STEP] = across(stack, NEXT_STEP, ROWS)
    for j in range(3):
        state[KEPT_LOAD + j] = across(stack, LOAD + j, ROWS)
        table[j] = across(stack, SPEED + j, ROWS)
        table[3 + j] = across(stack, NEXT_SPEED + j, ROWS)
    dual = [across(stack, DUAL + c, ROWS) for c in range(3)]
    dual, force_own, force_next = sweep(lambda row: state[row], index, work, dual)
    for c in range(3):
        state[DUAL + c] = dual[c]
        mine = table[c] - step * (force_own[c] - state[KEPT_LOAD + c])
        to_near[c] = jnp.where(even, force_next[c], mine)
        to_far[c] = jnp.where(even, mine, force_next[c])


def second_kernel(state, index, to_near, to_far, from_far, from_near, vectors, keep, *work):
    table = work[0]
    even = lax.axis_index("sector") % 2 == 0
    step, next_step = state[STEP], state[KEPT_NEXT_STEP]
    for j in range(3):
        near, far = to_near[j], to_far[j]
        near_in, far_in = from_near[j], from_far[j]
        table[j] = jnp.where(even, far, near) - step * jnp.where(even, far_in, near_in)
        table[3 + j] = jnp.where(even, near_in, far_in) - next_step * jnp.where(even, near, far)
    dual = [state[DUAL + c] for c in range(3)]
    dual_next, force_own, force_next = sweep(lambda row: state[row], index, work, dual)
    for c in range(3):
        after = table[c] - step * (force_own[c] - state[KEPT_LOAD + c])
        vectors[c] = after - table[c]
        vectors[3 + c] = -(next_step * force_next[c])
        keep[c] = dual_next[c]
        keep[3 + c] = dual_next[c] - dual[c]
        keep[6 + c] = after


def pairs(depth):
    return [(i, l) for i in range(depth) for l in range(i, depth + 1)]


def gram_kernel(depth, slots, vectors, keep, *refs):
    blocks, own = keep.shape[1:]
    halves = own // LANES
    rows = 9 * depth
    message, stack, rows_sum = refs[len(slots) :]
    for piece, own_slots in zip(refs, slots):
        for at, slot in enumerate(own_slots):
            stack_block(piece.at[at] if len(piece.shape) == 3 else piece.at[ROWS:], slot, rows, stack)
    for row in range(6):
        message[row] = vectors[row]
    message[6] = jnp.zeros((blocks, own), jnp.float32)
    sums, pushed, pushed_twice = {}, [0.0] * (depth + 1), 0.0
    for c, h, top in itertools.product(range(3), range(halves), range(0, blocks, 8)):
        lanes, group = slice(h * LANES, (h + 1) * LANES), slice(top, top + 8)

        def gap(kind, i):
            return stack[h, pl.ds(top * rows + depth * (3 * kind + c) + i, 8, stride=rows), :]

        for kind, moved in enumerate((keep[3 + c, group, lanes], vectors[c, group, lanes])):
            gaps = [moved - gap(kind, i) for i in range(depth)] + [moved]
            for i, l in pairs(depth):
                term = gaps[i] * gaps[l]
                sums[i, l] = sums[i, l] + term if (i, l) in sums else term
        push = vectors[3 + c, group, lanes]
        for i in range(depth):
            pushed[i] = pushed[i] + gap(2, i) * push
        pushed_twice = pushed_twice + push * push
    for at, (i, l) in enumerate(pairs(depth)):
        value = sums[i, l] + pushed_twice - pushed[i] - pushed[l]
        rows_sum[at : at + 1, :] = jnp.sum(value, axis=0, keepdims=True)
    count = len(pairs(depth))
    if rows_sum.shape[0] > count:
        rows_sum[count:, :] = jnp.zeros((rows_sum.shape[0] - count, LANES), jnp.float32)
    whole = jnp.broadcast_to(jnp.sum(rows_sum[...], axis=1, keepdims=True), rows_sum.shape)
    lane = lax.broadcasted_iota(jnp.int32, (8, LANES), 1)
    out = whole[0:8]
    for group in range(1, rows_sum.shape[0] // 8):
        out = jnp.where(lane == group, whole[8 * group : 8 * group + 8], out)
    message[6, 0:8, 0:LANES] = out


def solve_kernel(depth, square, *refs):
    parts = refs[:-8]
    keep, past_w, gap_w, past_u, gap_u, new_u, new_w, total = refs[-8:]
    own = new_u.shape[1]
    tile = parts[0][6, 0:8, 0:LANES]
    for other in parts[1:]:
        tile = tile + other[6, 0:8, 0:LANES]
    even = lax.axis_index("sector") % 2 == 0

    def ahead(by, row):
        if square and by in (1, 3):
            return jnp.where(even, parts[by][row], parts[4 - by][row])
        return parts[by][row]

    sectors = len(parts)
    pushes = [[ahead(by, 3 + j) for j in range(3)] for by in range(sectors)]
    cross = sum(ahead(by, j) * pushes[by - 1][j] for by in range(sectors) for j in range(3))
    cross = jnp.sum(jnp.sum(cross, axis=0, keepdims=True), axis=1, keepdims=True)
    last = [keep[6 + j, 0:1] + pushes[-1][j][0:1] for j in range(3)] + [keep[c, 0:1] for c in range(3)]
    for group in range(total.shape[0] // 8):
        total[8 * group : 8 * group + 8, :] = jnp.broadcast_to(tile[:, group : group + 1], (8, LANES))
    matrix = {
        pair: jnp.broadcast_to(total[at : at + 1, :], (depth, LANES)) + 2.0 * cross
        for at, pair in enumerate(pairs(depth))
    }
    ridge = 0.0001 * sum(matrix[i, i] for i in range(depth)) / depth
    for i in range(depth):
        matrix[i, i] = matrix[i, i] + ridge
    inverse = []
    for step in range(depth):
        inverse.append(1.0 / matrix[step, step])
        for i in range(step + 1, depth):
            factor = matrix[step, i] * inverse[step]
            for l in range(i, depth + 1):
                matrix[i, l] = matrix[i, l] - factor * matrix[step, l]
    weights = [None] * depth
    for i in reversed(range(depth)):
        value = matrix[i, depth]
        for l in range(i + 1, depth):
            value = value - matrix[i, l] * weights[l]
        weights[i] = value * inverse[i]
    row = lax.broadcasted_iota(jnp.int32, (depth, LANES), 0)
    weight = weights[0]
    for i in range(1, depth):
        weight = jnp.where(row == i, weights[i], weight)
    for start in range(0, own, LANES):
        lanes = slice(start, start + LANES)
        for at, (past, gap, out) in enumerate(((past_u, gap_u, new_u), (past_w, gap_w, new_w))):
            for c in range(3):
                value = jnp.broadcast_to(last[3 * at + c][:, lanes], (depth, LANES))
                change = weight * (value - past[c, :, lanes] - gap[c, :, lanes])
                out[c : c + 1, lanes] = value[0:1] - jnp.sum(change, axis=0, keepdims=True)


def per_device(
    strain_map,
    corner_nodes,
    counts,
    seam_nodes,
    velocity,
    dual_state,
    nodal_load,
    mobility,
    past_dual,
    past_dual_gap,
    past_velocity,
    past_velocity_gap,
):
    own = velocity.shape[1]
    halves = own // LANES
    blocks = lax.axis_size("dom")
    sectors = lax.axis_size("sector")
    depth = past_dual.shape[0]
    seam_rows = seam_nodes.shape[1] // own
    mobility = mobility.reshape(1, own)
    past_dual, past_dual_gap, past_velocity, past_velocity_gap = (
        value.transpose(1, 0, 2) for value in (past_dual, past_dual_gap, past_velocity, past_velocity_gap)
    )

    def send(value, target):
        return lax.ppermute(value, "sector", [(i, target(i) % sectors) for i in range(sectors)])

    def swap(value, bits):
        return lax.ppermute(value, "dom", [(i, i ^ bits) for i in range(blocks)])

    nodes = (velocity, mobility, seam_nodes)
    ahead = call(
        nodes_kernel,
        f32(8 + seam_rows + 3 * depth, own),
        in_hbm(*nodes, past_velocity_gap),
        loose=len(nodes) + 1,
        scratch=[pltpu.VMEM(value.shape, value.dtype) for value in nodes]
        + [pltpu.SemaphoreType.DMA((len(nodes) + 3,))],
    )
    held = (strain_map, dual_state, velocity, nodal_load, mobility, corner_nodes)
    base, history = call(
        base_kernel,
        (f32(INDEX + 4, own), f32(6, depth, own)),
        (counts, ahead, *in_hbm(*held, past_dual_gap, past_velocity_gap)),
        scalars=1,
        loose=len(held) + 3,
        scratch=[pltpu.VMEM(value.shape, value.dtype) for value in held]
        + [pltpu.SemaphoreType.DMA((len(held) + 2,))],
    )
    ahead = send(ahead, lambda i: i - 1)
    far_ones = list(range(blocks - 2, 2, -2))
    lengths = [max(INDEX + 4, ROWS - place) for place in range(len(far_ones))]
    messages = call(
        functools.partial(message_kernel, own * blocks, depth),
        tuple(f32(rows, own) for rows in sorted(set(lengths), reverse=True)),
        (history, ahead, base),
        loose=1,
    )
    wide = call(wide_kernel, f32(ROWS + 9 * depth, own), (messages[0], history, ahead))
    pieces = {0: wide}
    for bits, rows in zip(far_ones, lengths):
        pieces[bits] = swap(next(value for value in messages if value.shape[0] == rows), bits)
    pieces[2] = swap(wide, 2)
    for even in (0, 2):
        pieces[even + 1] = swap(pieces[even], 1)
    count = len(far_ones)
    crossed = swap(
        call(stack_kernel, f32(count * ROWS, own), tuple(pieces[bits] for bits in far_ones)), 1
    )
    histories, slots = [pieces[block] for block in range(4)], [(block,) for block in range(4)]
    history = call(
        pair_kernel, f32(2, 9 * depth, own), (*(pieces[bits] for bits in far_ones), wide, pieces[2]), loose=len(far_ones)
    )
    known, apart, later = (0, 2), 4, []
    while apart < blocks:
        other = swap(history, apart)
        later.append((other, tuple(slot ^ apart for slot in known)))
        known += later[-1][1]
        apart *= 2
        if apart < blocks:
            history = call(join_kernel, f32(2 * history.shape[0], 9 * depth, own), (history, other))
    order = [(at * ROWS, bits + 1) for at, bits in enumerate(far_ones)]
    order += [(0, block) for block in reversed(range(blocks)) if block in pieces]
    sector = f32(3, blocks, own)
    work = [
        pltpu.VMEM((6, blocks, own), jnp.float32),
        pltpu.VMEM((3 * SPLITS, 4, blocks, own), jnp.float32),
        pltpu.VMEM((3, 4, blocks, own), jnp.float32),
        pltpu.VMEM((blocks * 16 * -(-3 * SPLITS * (halves + 2) // 16), LANES), jnp.float32),
    ]
    state, index, to_near, to_far = call(
        functools.partial(first_kernel, blocks, order),
        (f32(KEPT, blocks, own), jax.ShapeDtypeStruct((4, blocks, own), jnp.int32), sector, sector),
        (*([crossed] * count), *(pieces[block] for _, block in order[count:])),
        scratch=[pltpu.VMEM((halves, blocks * ROWS, LANES), jnp.float32), *work],
    )
    from_far = send(to_far, lambda i: i + 1 if i % 2 else i - 1)
    from_near = send(to_near, lambda i: i ^ 1)
    for other, far in later:
        held_back = call(copy_kernel, f32(*other.shape), (from_near, from_far, other), loose=2)
        histories += [other, swap(held_back, 1)]
        slots += [far, tuple(slot ^ 1 for slot in far)]
    vectors, keep = call(
        second_kernel,
        (f32(6, blocks, own), f32(9, blocks, own)),
        (state, index, to_near, to_far, from_far, from_near),
        scratch=work,
    )
    count = -(-len(pairs(depth)) // 8) * 8
    message = call(
        functools.partial(gram_kernel, depth, tuple(slots)),
        f32(7, blocks, own),
        (vectors, keep, *histories),
        scratch=[
            pltpu.VMEM((halves, blocks * 9 * depth, LANES), jnp.float32),
            pltpu.VMEM((count, LANES), jnp.float32),
        ],
    )
    square = sectors == 4
    parts = [message] + [None] * (sectors - 1)
    for by in sorted(range(1, sectors), key=lambda by: (by != sectors - 1, by)):
        parts[by] = send(message, (lambda i: i ^ by) if square else (lambda i: i - by))
    return call(
        functools.partial(solve_kernel, depth, square),
        (f32(3, own), f32(3, own)),
        (*parts, keep, past_dual, past_dual_gap, past_velocity, past_velocity_gap),
        scratch=[pltpu.VMEM((count, LANES), jnp.float32)],
    )


def solution(mesh):
    in_specs = (
        P(None, ("sector", "dom")),
        P(None, ("sector", "dom")),
        P(("sector", "dom")),
        P("sector", None),
        P(None, ("sector", "dom")),
        P(None, ("sector", "dom")),
        P(None, ("sector", "dom")),
        P(("sector", "dom")),
        P(None, None, ("sector", "dom")),
        P(None, None, ("sector", "dom")),
        P(None, None, ("sector", "dom")),
        P(None, None, ("sector", "dom")),
    )
    out_specs = (P(None, ("sector", "dom")), P(None, ("sector", "dom")))
    return jax.shard_map(
        per_device, mesh=mesh, in_specs=in_specs, out_specs=out_specs, check_vma=False
    )
```
